32 devices in a mesh: batch: 16 (over z, x, core), seq: 2 (over y).
Axes of the slice: x: 2, y: 2, z: 4, core: 2. Of those that a mesh axis runs over, the one named last changes fastest.
Arguments:
- tokens: bfloat16 [16, 2048, 768], P('batch', 'seq'), may hold values from -6 to 6
- cotangent: bfloat16 [16, 2048, 768], P('batch', 'seq'), may hold values from -6 to 6
- segments: int32 [16, 2048], P('batch'), may hold values from 0 to 3, as said below
- adapter_index: int32 [16, 1], P('batch'), may hold values from 0 to 3
- qkv_weight: bfloat16 [1, 3, 768, 768], P(None, None, ('batch', 'seq')), may hold values from -0.21875 to 0.21875
- out_weight: bfloat16 [1, 768, 768], P(None, ('batch', 'seq')), may hold values from -0.875 to 0.875
- ffn_in_weight: bfloat16 [1, 2, 768, 3072], P(None, None, ('batch', 'seq')), may hold values from -0.21875 to 0.21875
- ffn_out_weight: bfloat16 [1, 3072, 768], P(None, ('batch', 'seq')), may hold values from -0.109375 to 0.109375
- norm_gain: float32 [1, 2, 768], replicated, may hold values from 0.1 to 1.9
- norm_bias: float32 [1, 2, 768], replicated, may hold values from -2 to 2
- adapt_in: bfloat16 [1, 4, 6, 768, 16], replicated, may hold values from -0.21875 to 0.21875
- adapt_down: bfloat16 [1, 4, 3072, 16], replicated, may hold values from -0.109375 to 0.109375
- adapt_out: bfloat16 [1, 4, 5, 16, 768], replicated, may hold values from -1.5 to 1.5
- adapt_ffn: bfloat16 [1, 4, 2, 16, 3072], replicated, may hold values from -1.5 to 1.5
Outputs:
- mixed: bfloat16 [16, 2048, 768], P('batch', 'seq')
- input_grad: bfloat16 [16, 2048, 768], P('batch', 'seq')
- grad_adapt_in: float32 [1, 4, 6, 768, 16], replicated
- grad_adapt_down: float32 [1, 4, 3072, 16], replicated
- grad_adapt_out: float32 [1, 4, 5, 16, 768], replicated
- grad_adapt_ffn: float32 [1, 4, 2, 16, 3072], replicated
The draws below stay inside these ranges and needn't reach their ends.
Inputs may be any that keep to these rules, and one draw needn't show every extreme that they name: `segments`: document numbers start at 0 in each sequence and rise by one at each new document; every sequence holds exactly 4 documents, one of which starts before position 1024 and ends at or after position 1024. `adapter_index`: every adapter is used by some sequence.
All inputs are finite; a program needn't handle non-finite values.
Results may differ from the reference program's by a relative error of at most 0.023.
The reference program's roundings to bfloat16 on the way count: a program that leaves them out, or rounds other values in their place, can miss the bound.
Values may be sent and summed in bfloat16 or wider, within the bound.
A program may use at most 320 MiB of HBM per device.

```python
import math
import jax
import jax.numpy as jnp
from jax import lax

D = 768
HEADS = 12
HEAD_DIM = 64
FF = 3072
RANK = 16
ADAPTERS = 4
LAYERS = 1
LEN = 2048
HALF = 512
QBLK = 512
SEQS = 16
TOK_DEV = 1024


def pick_between(key, low_end, high_end):
    width = jnp.maximum(high_end - low_end, 1)
    return low_end + jax.random.randint(key, (SEQS,), 0, 1 << 20) % width


def draw_segments(key, part):
    key = jax.random.fold_in(key, 7)
    side_key, first_key, second_key, extra_key = jax.random.split(key, 4)
    on_left = jax.random.randint(side_key, (SEQS,), 0, 2) == 0
    first_cut = pick_between(first_key, jnp.where(on_left, 2, 1), TOK_DEV + jnp.zeros((SEQS,), jnp.int32))
    second_cut = pick_between(second_key, LEN - TOK_DEV + 1 + jnp.zeros((SEQS,), jnp.int32), jnp.where(on_left, LEN, LEN - 1))
    extra_left = pick_between(extra_key, jnp.ones((SEQS,), jnp.int32), first_cut)
    extra_right = pick_between(extra_key, second_cut + 1, LEN + jnp.zeros((SEQS,), jnp.int32))
    extra_cut = jnp.where(on_left, extra_left, extra_right)
    position_ids = jnp.arange(LEN, dtype=jnp.int32)[None, :]
    boundary = (position_ids == first_cut[:, None]) | (position_ids == second_cut[:, None]) | (position_ids == extra_cut[:, None])
    return jnp.cumsum(boundary.astype(jnp.int32), axis=1).astype(jnp.int32)


def steps_of(stream_key, extent, cuts, low, high):
    def one(axis_at, parts):
        steps = jax.random.uniform(jax.random.fold_in(jax.random.fold_in(stream_key, 6), axis_at), (parts,), jnp.float32, low / len(cuts), high / len(cuts))
        return jnp.repeat(jnp.exp(steps), extent[axis_at] // parts).reshape((-1,) + (1,) * (len(extent) - axis_at - 1))

    factor_of = one(*cuts[0])
    for cut in cuts[1:]:
        factor_of = factor_of * one(*cut)
    return factor_of


def picks_of(stream_key, rows, count, top, lift):
    sequence = jax.random.permutation(jax.random.fold_in(stream_key, 1), count)
    boost = sequence
    for power in range(3):
        boost = boost * boost // count
    boost = boost * lift // count
    tickets = jax.random.randint(jax.random.fold_in(stream_key, 2), (rows, count), 0, 4096) + boost
    fixed_rows = jax.random.permutation(jax.random.fold_in(stream_key, 3), rows)[jnp.arange(count) % rows]
    tickets = jnp.where(jnp.arange(rows)[:, None] == fixed_rows[None, :], 1 << 14, tickets)
    score = tickets * count + jnp.arange(count)
    return lax.top_k(score.astype(jnp.int32), top)[1].astype(jnp.int32)


def gaussian(stream_key, shape, deviation, limit, pieces=(), held_as=jnp.bfloat16):
    drawn = jax.random.normal(stream_key, shape, jnp.float32) * deviation
    if len(pieces) > 0:
        drawn = steps_of(stream_key, shape, pieces, -0.22, 0.18) * drawn
    return jnp.clip(drawn, min=-limit, max=limit).astype(held_as)


def setup_inputs(seed: int = 0) -> dict:
    splits = jax.random.split(jax.random.key(seed), 15)
    tokens = gaussian(splits[0], (SEQS, LEN, D), 1.0, 6.0, ((0, 16), (1, 2)))
    cotangent = gaussian(splits[1], (SEQS, LEN, D), 1.0, 6.0, ((0, 16), (1, 2)))
    segments = draw_segments(jax.random.fold_in(splits[14], 71), 0)
    adapter_index = picks_of(splits[3], SEQS, ADAPTERS, 1, 0)
    qkv_weight = gaussian(splits[4], (LAYERS, 3, D, D), D ** -0.5, 0.21875, ((2, 32),))
    out_weight = gaussian(splits[5], (LAYERS, D, D), (D // 16) ** -0.5, 0.875, ((1, 32),))
    ffn_in_weight = gaussian(splits[6], (LAYERS, 2, D, FF), D ** -0.5, 0.21875, ((2, 32),))
    ffn_out_weight = gaussian(splits[7], (LAYERS, FF, D), FF ** -0.5, 0.109375, ((1, 32),))
    norm_gain = jnp.clip(1.0 + 0.18 * jax.random.normal(splits[8], (LAYERS, 2, D), jnp.float32), 0.1, 1.9)
    norm_bias = gaussian(splits[9], (LAYERS, 2, D), 0.3, 2.0, (), jnp.float32)
    adapt_in = gaussian(splits[10], (LAYERS, ADAPTERS, 6, D, RANK), D ** -0.5, 0.21875)
    adapt_down = gaussian(splits[11], (LAYERS, ADAPTERS, FF, RANK), FF ** -0.5, 0.109375)
    adapt_out = gaussian(splits[12], (LAYERS, ADAPTERS, 5, RANK, D), RANK ** -0.5, 1.5)
    adapt_ffn = gaussian(splits[13], (LAYERS, ADAPTERS, 2, RANK, FF), RANK ** -0.5, 1.5)
    return {"tokens": tokens, "cotangent": cotangent, "segments": segments, "adapter_index": adapter_index, "qkv_weight": qkv_weight, "out_weight": out_weight, "ffn_in_weight": ffn_in_weight, "ffn_out_weight": ffn_out_weight, "norm_gain": norm_gain, "norm_bias": norm_bias, "adapt_in": adapt_in, "adapt_down": adapt_down, "adapt_out": adapt_out, "adapt_ffn": adapt_ffn}


EPSILON = 1e-06
ROPE_BASE = 1000.0
PRECISE = lax.Precision.HIGHEST

@jax.custom_vjp
def low(v):
    return lax.optimization_barrier(v.astype(jnp.bfloat16)).astype(jnp.float32)

@jax.custom_vjp
def low_back(v):
    return v

def low_keep(v):
    return (low(v), None)

def low_pass(kept, grad):
    return (grad,)

def back_keep(v):
    return (v, None)

def back_low(kept, grad):
    return (low(grad),)
low.defvjp(low_keep, low_pass)
low_back.defvjp(back_keep, back_low)

def doc_positions(segment_ids):
    position_ids = jnp.arange(segment_ids.shape[-1], dtype=jnp.int32)
    starts_here = jnp.concatenate([jnp.ones(segment_ids.shape[:-1] + (1,), dtype=jnp.bool_), segment_ids[..., 1:] != segment_ids[..., :-1]], axis=-1)
    doc_start = lax.cummax(jnp.where(starts_here, position_ids, 0), axis=segment_ids.ndim - 1)
    return (position_ids - doc_start).astype(jnp.float32)

def rope_tables(segment_ids):
    positions = doc_positions(segment_ids)
    frequency = jnp.power(ROPE_BASE, -2.0 * jnp.arange(HEAD_DIM // 2, dtype=jnp.float32) / HEAD_DIM)
    angles = positions[..., None] * frequency
    return (jnp.cos(angles), jnp.sin(angles))

def rotate(vectors, cosine_table, sine_table):
    half_dim = vectors.shape[-1] // 2
    first_half = vectors[..., :half_dim]
    second_half = vectors[..., half_dim:]
    cosine_rows = cosine_table[..., None, :]
    sine_rows = sine_table[..., None, :]
    return jnp.concatenate([first_half * cosine_rows - second_half * sine_rows, second_half * cosine_rows + first_half * sine_rows], axis=-1)

def norm_apply(residual, gain_row, bias_row):
    centre = residual - lax.optimization_barrier(jnp.mean(residual, axis=-1, keepdims=True))
    spread = lax.optimization_barrier(jnp.mean(centre * centre, axis=-1, keepdims=True))
    return centre * lax.rsqrt(spread + EPSILON) * gain_row + bias_row

def attend(queries, keys_all, values, segment_ids):
    key_span = QBLK + 2 * HALF
    padded_keys = jnp.pad(keys_all, ((HALF, HALF), (0, 0), (0, 0)))
    padded_values = jnp.pad(values, ((HALF, HALF), (0, 0), (0, 0)))
    padded_ids = jnp.pad(segment_ids, (HALF, HALF), constant_values=-1)
    score_scale = 1.0 / math.sqrt(HEAD_DIM)

    def attend_block(block_start):
        query_block = lax.dynamic_slice_in_dim(queries, block_start, QBLK, 0)
        key_block = lax.dynamic_slice_in_dim(padded_keys, block_start, key_span, 0)
        value_block = lax.dynamic_slice_in_dim(padded_values, block_start, key_span, 0)
        query_ids = lax.dynamic_slice_in_dim(segment_ids, block_start, QBLK, 0)
        key_ids = lax.dynamic_slice_in_dim(padded_ids, block_start, key_span, 0)
        offsets = jnp.arange(QBLK, dtype=jnp.int32)[:, None] - jnp.arange(key_span, dtype=jnp.int32)[None, :] + HALF
        visible = (query_ids[:, None] == key_ids[None, :]) & (jnp.abs(offsets) <= HALF)
        scores = low_back(jnp.einsum('qhd,khd->hqk', query_block, key_block, precision=PRECISE) * score_scale)
        scores = jnp.where(visible[None], scores, -1e+30)
        biggest = lax.optimization_barrier(jnp.max(scores, axis=-1, keepdims=True))
        lifted = jnp.exp(scores - biggest)
        probability = lifted / lax.optimization_barrier(jnp.sum(lifted, axis=-1, keepdims=True))
        return jnp.einsum('hqk,khd->qhd', low(probability), value_block, precision=PRECISE)
    starts = jnp.arange(LEN // QBLK, dtype=jnp.int32) * QBLK
    blocks = lax.map(jax.checkpoint(attend_block), starts)
    return blocks.reshape(LEN, HEADS * HEAD_DIM)

def layer_forward(state, weights, chosen, layer_index, cosine_table, sine_table, segment_ids):
    w_qkv, w_out, w_in, w_down, gains, biases = weights
    chosen_in, chosen_down, chosen_out, chosen_ffn = chosen
    act_one = low(state)
    low_qkv = low_back(low(jnp.einsum('td,pdr->ptr', act_one, chosen_in[layer_index, 0:3], precision=PRECISE)))
    proj = low_back(jnp.einsum('td,pde->pte', act_one, w_qkv[layer_index], precision=PRECISE) + jnp.einsum('ptr,pre->pte', low_qkv, chosen_out[layer_index, 0:3], precision=PRECISE))
    queries = low(rotate(proj[0].reshape(LEN, HEADS, HEAD_DIM), cosine_table, sine_table))
    keys_all = low(rotate(proj[1].reshape(LEN, HEADS, HEAD_DIM), cosine_table, sine_table))
    values = low(proj[2].reshape(LEN, HEADS, HEAD_DIM))
    attended = low_back(low(attend(queries, keys_all, values, segment_ids)))
    low_out = low_back(low(jnp.dot(attended, chosen_in[layer_index, 3], precision=PRECISE)))
    branch = low_back(jnp.dot(attended, w_out[layer_index], precision=PRECISE) + jnp.dot(low_out, chosen_out[layer_index, 3], precision=PRECISE))
    hidden = norm_apply(state + branch, gains[layer_index, 0], biases[layer_index, 0])
    act_two = low(hidden)
    low_ffn = low_back(low(jnp.einsum('td,pdr->ptr', act_two, chosen_in[layer_index, 4:6], precision=PRECISE)))
    gate_up = low_back(jnp.einsum('td,pdf->ptf', act_two, w_in[layer_index], precision=PRECISE) + jnp.einsum('ptr,prf->ptf', low_ffn, chosen_ffn[layer_index], precision=PRECISE))
    inner = low(jax.nn.silu(gate_up[0]) * gate_up[1])
    low_down = low_back(low(jnp.dot(inner, chosen_down[layer_index], precision=PRECISE)))
    branch_two = low_back(jnp.dot(inner, w_down[layer_index], precision=PRECISE) + jnp.dot(low_down, chosen_out[layer_index, 4], precision=PRECISE))
    return norm_apply(hidden + branch_two, gains[layer_index, 1], biases[layer_index, 1])

def reference(tokens, cotangent, segments, adapter_index, qkv_weight, out_weight, ffn_in_weight, ffn_out_weight, norm_gain, norm_bias, adapt_in, adapt_down, adapt_out, adapt_ffn):
    weights = (qkv_weight.astype(jnp.float32), out_weight.astype(jnp.float32), ffn_in_weight.astype(jnp.float32), ffn_out_weight.astype(jnp.float32), norm_gain.astype(jnp.float32), norm_bias.astype(jnp.float32))
    tables = (adapt_in.astype(jnp.float32), adapt_down.astype(jnp.float32), adapt_out.astype(jnp.float32), adapt_ffn.astype(jnp.float32))

    def one_sequence(totals, item):
        token_rows, cot_rows, segment_ids, index_row = item
        slot_index = index_row[0]
        picked = tuple((lax.dynamic_index_in_dim(table, slot_index, 1, keepdims=False) for table in tables))
        cosine_table, sine_table = rope_tables(segment_ids)

        def forward(state, chosen):
            for layer_index in range(LAYERS):
                state = layer_forward(state, weights, chosen, layer_index, cosine_table, sine_table, segment_ids)
            return state
        result, pull_back = jax.vjp(forward, token_rows.astype(jnp.float32), picked)
        d_rows, d_picked = pull_back(cot_rows.astype(jnp.float32))
        totals = tuple((total.at[:, slot_index].add(grad_part) for total, grad_part in zip(totals, d_picked)))
        return (totals, (result.astype(jnp.bfloat16), d_rows.astype(jnp.bfloat16)))
    zero_grads = tuple((jnp.zeros(table.shape, jnp.float32) for table in tables))
    totals, outputs = lax.scan(one_sequence, zero_grads, (tokens, cotangent, segments, adapter_index))
    return (outputs[0], outputs[1], totals[0], totals[1], totals[2], totals[3])
```

```python
import functools
import math

import jax
import jax.numpy as jnp
from jax import lax
from jax.experimental import pallas as pl
from jax.experimental.pallas import tpu as pltpu
from jax.sharding import PartitionSpec as P

HEADS = 12
HEAD_DIM = 64
ADAPTERS = 4
LAYERS = 1
HALF = 512
D = HEADS * HEAD_DIM
FF = 4 * D


EPSILON = 1e-06
ROPE_BASE = 1000.0
PRECISE = lax.Precision.HIGHEST


def shifted(array, axis, by):
    count = lax.axis_size(axis)
    pairs = [(i, i + by) for i in range(count) if 0 <= i + by < count]
    return lax.ppermute(array, axis, pairs)


def doc_positions(segment_ids):
    position_ids = jnp.arange(segment_ids.shape[-1], dtype=jnp.int32)
    starts_here = jnp.concatenate(
        [
            jnp.ones(segment_ids.shape[:-1] + (1,), dtype=jnp.bool_),
            segment_ids[..., 1:] != segment_ids[..., :-1],
        ],
        axis=-1,
    )
    doc_start = lax.cummax(jnp.where(starts_here, position_ids, 0), axis=segment_ids.ndim - 1)
    return (position_ids - doc_start).astype(jnp.float32)


def rope_tables(segment_ids):
    positions = doc_positions(segment_ids)
    frequency = jnp.power(ROPE_BASE, -2.0 * jnp.arange(HEAD_DIM // 2, dtype=jnp.float32) / HEAD_DIM)
    angles = positions[..., None] * frequency
    return (jnp.cos(angles), jnp.sin(angles))


def rotate(vectors, cosine_table, sine_table):
    half_dim = vectors.shape[-1] // 2
    first_half = vectors[..., :half_dim]
    second_half = vectors[..., half_dim:]
    cosine_rows = cosine_table[..., None, :]
    sine_rows = sine_table[..., None, :]
    return jnp.concatenate(
        [
            first_half * cosine_rows - second_half * sine_rows,
            second_half * cosine_rows + first_half * sine_rows,
        ],
        axis=-1,
    )


def norm_apply(residual, gain_row, bias_row):
    centre = residual - jnp.mean(residual, axis=-1, keepdims=True)
    spread = jnp.mean(centre * centre, axis=-1, keepdims=True)
    return centre * lax.rsqrt(spread + EPSILON) * gain_row + bias_row


def split_heads(merged, group_count):
    seqs_here, row_count, _ = merged.shape
    return merged.reshape(seqs_here, row_count, group_count, -1, HEAD_DIM).transpose(2, 0, 1, 3, 4)


def join_heads(grouped):
    group_count, seqs_here, row_count, heads_group, head_size = grouped.shape
    return grouped.transpose(1, 2, 0, 3, 4).reshape(
        seqs_here, row_count, group_count * heads_group * head_size
    )


def shards(
    tokens,
    cotangent,
    segments,
    adapter_index,
    qkv_weight,
    out_weight,
    ffn_in_weight,
    ffn_out_weight,
    norm_gain,
    norm_bias,
    adapt_in,
    adapt_down,
    adapt_out,
    adapt_ffn,
):
    seqs_here, tok_rows, model_width = tokens.shape
    heads_group = math.gcd(HEADS, 4)
    group_count = HEADS // heads_group
    score_scale = 1.0 / math.sqrt(HEAD_DIM)
    seq_count = lax.axis_size("seq")
    row_base = lax.axis_index("seq") * tok_rows
    shift_plan = []
    for distance in range(1, min(seq_count, HALF // tok_rows + 2)):
        row_count = min(tok_rows, HALF - (distance - 1) * tok_rows)
        if row_count > 0:
            shift_plan.append((distance, row_count))
            shift_plan.append((-distance, row_count))
    left_total = sum((plan_item[1] for plan_item in shift_plan if plan_item[0] > 0))
    key_rows = 2 * left_total + tok_rows
    key_places = {}
    passed_rows = 0
    for distance, row_count in shift_plan:
        if distance > 0:
            key_places[distance] = left_total - passed_rows - row_count
            key_places[-distance] = left_total + tok_rows + passed_rows
            passed_rows += row_count
    cosine_all, sine_all = rope_tables(segments)
    cosine_here = lax.dynamic_slice_in_dim(cosine_all, row_base, tok_rows, 1)
    sine_here = lax.dynamic_slice_in_dim(sine_all, row_base, tok_rows, 1)
    padded_ids = jnp.pad(segments, ((0, 0), (HALF, HALF)), constant_values=-1)
    key_ids = lax.dynamic_slice_in_dim(padded_ids, row_base - left_total + HALF, key_rows, 1)
    query_ids = lax.dynamic_slice_in_dim(segments, row_base, tok_rows, 1)
    offsets = (
        jnp.arange(tok_rows, dtype=jnp.int32)[:, None]
        - jnp.arange(key_rows, dtype=jnp.int32)[None, :]
        + left_total
    )
    visible = (query_ids[:, :, None] == key_ids[:, None, :]) & (jnp.abs(offsets) <= HALF)[None]
    slot_hits = adapter_index[:, 0][:, None] == jnp.arange(ADAPTERS, dtype=jnp.int32)[None, :]
    slot_low = slot_hits.astype(jnp.bfloat16)
    slot_full = slot_hits.astype(jnp.float32)

    def select_adapter(table):
        return jnp.einsum(
            "se,le...->ls...", slot_low, table, preferred_element_type=jnp.float32
        ).astype(jnp.bfloat16)

    def spread_slots(per_sequence):
        return jnp.einsum("se,s...->e...", slot_full, per_sequence, precision=PRECISE)

    chosen_in = select_adapter(adapt_in)
    chosen_down = select_adapter(adapt_down)
    chosen_out = select_adapter(adapt_out)
    chosen_ffn = select_adapter(adapt_ffn)

    def forward_group(items):
        query_block, key_block, value_block = items
        scores = (
            jnp.einsum(
                "sqhd,skhd->shqk", query_block, key_block, preferred_element_type=jnp.float32
            )
            * score_scale
        )
        scores = jnp.where(visible[:, None], scores, -1e30)
        biggest = jnp.max(scores, axis=-1, keepdims=True)
        lifted = jnp.exp(scores - biggest)
        row_total = jnp.sum(lifted, axis=-1, keepdims=True)
        probability = (lifted / row_total).astype(jnp.bfloat16)
        result = jnp.einsum(
            "shqk,skhd->sqhd", probability, value_block, preferred_element_type=jnp.float32
        )
        return (result.astype(jnp.bfloat16), (biggest + jnp.log(row_total))[..., 0])

    def backward_group(items):
        query_block, key_block, value_block, grad_block, log_total = items
        scores = (
            jnp.einsum(
                "sqhd,skhd->shqk", query_block, key_block, preferred_element_type=jnp.float32
            )
            * score_scale
        )
        scores = jnp.where(visible[:, None], scores, -1e30)
        probability = jnp.exp(scores - log_total[..., None])
        d_prob = jnp.einsum(
            "sqhd,skhd->shqk", grad_block, value_block, preferred_element_type=jnp.float32
        )
        delta = jnp.sum(probability * d_prob, axis=-1, keepdims=True)
        d_score = (probability * (d_prob - delta)).astype(jnp.bfloat16)
        d_query = (
            jnp.einsum("shqk,skhd->sqhd", d_score, key_block, preferred_element_type=jnp.float32)
            * score_scale
        )
        d_key = (
            jnp.einsum("shqk,sqhd->skhd", d_score, query_block, preferred_element_type=jnp.float32)
            * score_scale
        )
        d_value = jnp.einsum(
            "shqk,sqhd->skhd",
            probability.astype(jnp.bfloat16),
            grad_block,
            preferred_element_type=jnp.float32,
        )
        return (d_query, d_key, d_value)

    state = tokens.astype(jnp.float32)
    layer_index = 0
    w_qkv = lax.all_gather(qkv_weight[layer_index], ("batch", "seq"), axis=1, tiled=True)
    w_out = lax.all_gather(out_weight[layer_index], ("batch", "seq"), axis=0, tiled=True)
    w_in = lax.all_gather(ffn_in_weight[layer_index], ("batch", "seq"), axis=1, tiled=True)
    w_down = lax.all_gather(ffn_out_weight[layer_index], ("batch", "seq"), axis=0, tiled=True)
    held = [(w_qkv, w_out, w_in, w_down)]
    act_one = state.astype(jnp.bfloat16)
    low_qkv = jnp.einsum(
        "std,spdr->pstr",
        act_one,
        chosen_in[layer_index][:, 0:3],
        preferred_element_type=jnp.float32,
    ).astype(jnp.bfloat16)
    proj = jnp.einsum(
        "std,pde->pste", act_one, w_qkv, preferred_element_type=jnp.float32
    ) + jnp.einsum(
        "pstr,spre->pste",
        low_qkv,
        chosen_out[layer_index][:, 0:3],
        preferred_element_type=jnp.float32,
    )
    queries = (
        rotate(proj[0].reshape(seqs_here, tok_rows, HEADS, HEAD_DIM), cosine_here, sine_here)
        .astype(jnp.bfloat16)
        .reshape(seqs_here, tok_rows, model_width)
    )
    key_rot = (
        rotate(proj[1].reshape(seqs_here, tok_rows, HEADS, HEAD_DIM), cosine_here, sine_here)
        .astype(jnp.bfloat16)
        .reshape(seqs_here, tok_rows, model_width)
    )
    key_value = jnp.stack([key_rot, proj[2].astype(jnp.bfloat16)])
    edges = {}
    for step_by, row_count in shift_plan:
        if step_by > 0:
            outgoing = key_value[:, :, tok_rows - row_count :]
        else:
            outgoing = key_value[:, :, :row_count]
        edges[step_by] = shifted(outgoing, "seq", step_by)
    earlier = [edges[distance] for distance, row_count in reversed(shift_plan) if distance > 0]
    later = [edges[-distance] for distance, row_count in shift_plan if distance > 0]
    window = jnp.concatenate(earlier + [key_value] + later, axis=2)
    heads_out, log_total = lax.map(
        forward_group,
        (
            split_heads(queries, group_count),
            split_heads(window[0], group_count),
            split_heads(window[1], group_count),
        ),
    )
    attended = join_heads(heads_out)
    low_out = jnp.einsum(
        "std,sdr->str", attended, chosen_in[layer_index][:, 3], preferred_element_type=jnp.float32
    ).astype(jnp.bfloat16)
    branch = jnp.einsum(
        "std,de->ste", attended, w_out, preferred_element_type=jnp.float32
    ) + jnp.einsum(
        "str,sre->ste", low_out, chosen_out[layer_index][:, 3], preferred_element_type=jnp.float32
    )
    resid_one = state + branch
    hidden = norm_apply(resid_one, norm_gain[layer_index, 0], norm_bias[layer_index, 0])
    act_two = hidden.astype(jnp.bfloat16)
    low_ffn = jnp.einsum(
        "std,spdr->pstr",
        act_two,
        chosen_in[layer_index][:, 4:6],
        preferred_element_type=jnp.float32,
    ).astype(jnp.bfloat16)
    gate_up = jnp.einsum(
        "std,pdf->pstf", act_two, w_in, preferred_element_type=jnp.float32
    ) + jnp.einsum(
        "pstr,sprf->pstf", low_ffn, chosen_ffn[layer_index], preferred_element_type=jnp.float32
    )
    inner = (jax.nn.silu(gate_up[0]) * gate_up[1]).astype(jnp.bfloat16)
    low_down = jnp.einsum(
        "stf,sfr->str", inner, chosen_down[layer_index], preferred_element_type=jnp.float32
    ).astype(jnp.bfloat16)
    branch_two = jnp.einsum(
        "stf,fe->ste", inner, w_down, preferred_element_type=jnp.float32
    ) + jnp.einsum(
        "str,sre->ste", low_down, chosen_out[layer_index][:, 4], preferred_element_type=jnp.float32
    )
    resid_two = hidden + branch_two
    kept = [
        (
            act_one,
            low_qkv,
            queries,
            window,
            log_total,
            attended,
            low_out,
            resid_one,
            act_two,
            low_ffn,
            gate_up,
            inner,
            low_down,
            resid_two,
        )
    ]
    state = norm_apply(resid_two, norm_gain[layer_index, 1], norm_bias[layer_index, 1])
    mixed = state.astype(jnp.bfloat16)
    grad = cotangent.astype(jnp.float32)
    collected = [None] * LAYERS
    for layer_index in reversed(range(LAYERS)):
        (
            act_one,
            low_qkv,
            queries,
            window,
            log_total,
            attended,
            low_out,
            resid_one,
            act_two,
            low_ffn,
            gate_up,
            inner,
            low_down,
            resid_two,
        ) = kept[layer_index]
        w_qkv, w_out, w_in, w_down = held[layer_index]
        gain_two = norm_gain[layer_index, 1]
        bias_two = norm_bias[layer_index, 1]
        _, pull_two = jax.vjp(lambda residual: norm_apply(residual, gain_two, bias_two), resid_two)
        (d_resid_two,) = pull_two(grad)
        d_branch_two = d_resid_two.astype(jnp.bfloat16)
        d_low_down = jnp.einsum(
            "ste,sre->str",
            d_branch_two,
            chosen_out[layer_index][:, 4],
            preferred_element_type=jnp.float32,
        ).astype(jnp.bfloat16)
        g_out_down = jnp.einsum(
            "str,ste->sre", low_down, d_branch_two, preferred_element_type=jnp.float32
        )
        g_down = jnp.einsum("stf,str->sfr", inner, d_low_down, preferred_element_type=jnp.float32)
        d_inner = jnp.einsum(
            "ste,fe->stf", d_branch_two, w_down, preferred_element_type=jnp.float32
        ) + jnp.einsum(
            "str,sfr->stf", d_low_down, chosen_down[layer_index], preferred_element_type=jnp.float32
        )
        _, pull_act = jax.vjp(
            lambda gate_part, up_part: jax.nn.silu(gate_part) * up_part, gate_up[0], gate_up[1]
        )
        d_gate, d_up = pull_act(d_inner)
        d_gate_up = jnp.stack([d_gate, d_up]).astype(jnp.bfloat16)
        d_low_ffn = jnp.einsum(
            "pstf,sprf->pstr",
            d_gate_up,
            chosen_ffn[layer_index],
            preferred_element_type=jnp.float32,
        ).astype(jnp.bfloat16)
        g_ffn = jnp.einsum(
            "pstr,pstf->sprf", low_ffn, d_gate_up, preferred_element_type=jnp.float32
        )
        g_in_ffn = jnp.einsum(
            "std,pstr->spdr", act_two, d_low_ffn, preferred_element_type=jnp.float32
        )
        ffn_in_sum = spread_slots(g_in_ffn)
        ffn_down_sum = spread_slots(g_down)
        ffn_out_sum = spread_slots(g_out_down[:, None])
        ffn_ffn_sum = spread_slots(g_ffn)
        d_hidden = (
            d_resid_two
            + jnp.einsum("pstf,pdf->std", d_gate_up, w_in, preferred_element_type=jnp.float32)
            + jnp.einsum(
                "pstr,spdr->std",
                d_low_ffn,
                chosen_in[layer_index][:, 4:6],
                preferred_element_type=jnp.float32,
            )
        )
        gain_one = norm_gain[layer_index, 0]
        bias_one = norm_bias[layer_index, 0]
        _, pull_one = jax.vjp(lambda residual: norm_apply(residual, gain_one, bias_one), resid_one)
        (d_resid_one,) = pull_one(d_hidden)
        d_branch = d_resid_one.astype(jnp.bfloat16)
        d_low_out = jnp.einsum(
            "ste,sre->str",
            d_branch,
            chosen_out[layer_index][:, 3],
            preferred_element_type=jnp.float32,
        ).astype(jnp.bfloat16)
        g_out_att = jnp.einsum(
            "str,ste->sre", low_out, d_branch, preferred_element_type=jnp.float32
        )
        g_in_att = jnp.einsum(
            "std,str->sdr", attended, d_low_out, preferred_element_type=jnp.float32
        )
        d_attended = (
            jnp.einsum("ste,de->std", d_branch, w_out, preferred_element_type=jnp.float32)
            + jnp.einsum(
                "str,sdr->std",
                d_low_out,
                chosen_in[layer_index][:, 3],
                preferred_element_type=jnp.float32,
            )
        ).astype(jnp.bfloat16)
        d_query_heads, d_key_heads, d_value_heads = lax.map(
            backward_group,
            (
                split_heads(queries, group_count),
                split_heads(window[0], group_count),
                split_heads(window[1], group_count),
                split_heads(d_attended, group_count),
                log_total,
            ),
        )
        d_query = join_heads(d_query_heads)
        d_window = jnp.stack([join_heads(d_key_heads), join_heads(d_value_heads)])
        d_pair = d_window[:, :, left_total : left_total + tok_rows]
        for step_by, row_count in shift_plan:
            returning = lax.slice_in_dim(
                d_window, key_places[step_by], key_places[step_by] + row_count, axis=2
            )
            arrived = shifted(returning.astype(jnp.bfloat16), "seq", -step_by).astype(
                returning.dtype
            )
            if step_by > 0:
                d_pair = d_pair.at[:, :, tok_rows - row_count :].add(arrived)
            else:
                d_pair = d_pair.at[:, :, :row_count].add(arrived)
        d_query_rot = rotate(
            d_query.reshape(seqs_here, tok_rows, HEADS, HEAD_DIM), cosine_here, -sine_here
        ).reshape(seqs_here, tok_rows, model_width)
        d_key_rot = rotate(
            d_pair[0].reshape(seqs_here, tok_rows, HEADS, HEAD_DIM), cosine_here, -sine_here
        ).reshape(seqs_here, tok_rows, model_width)
        d_proj = jnp.stack([d_query_rot, d_key_rot, d_pair[1]]).astype(jnp.bfloat16)
        d_low_qkv = jnp.einsum(
            "pste,spre->pstr",
            d_proj,
            chosen_out[layer_index][:, 0:3],
            preferred_element_type=jnp.float32,
        ).astype(jnp.bfloat16)
        g_out_qkv = jnp.einsum(
            "pstr,pste->spre", low_qkv, d_proj, preferred_element_type=jnp.float32
        )
        g_in_qkv = jnp.einsum(
            "std,pstr->spdr", act_one, d_low_qkv, preferred_element_type=jnp.float32
        )
        grad = (
            d_resid_one
            + jnp.einsum("pste,pde->std", d_proj, w_qkv, preferred_element_type=jnp.float32)
            + jnp.einsum(
                "pstr,spdr->std",
                d_low_qkv,
                chosen_in[layer_index][:, 0:3],
                preferred_element_type=jnp.float32,
            )
        )
        att_in_sum = spread_slots(jnp.concatenate([g_in_qkv, g_in_att[:, None]], axis=1))
        att_out_sum = spread_slots(jnp.concatenate([g_out_qkv, g_out_att[:, None]], axis=1))
        collected[layer_index] = (
            jnp.concatenate([att_in_sum, ffn_in_sum], axis=1),
            ffn_down_sum,
            jnp.concatenate([att_out_sum, ffn_out_sum], axis=1),
            ffn_ffn_sum,
        )
    input_grad = grad.astype(jnp.bfloat16)
    stack_in = jnp.stack([collected[0][0]])
    stack_down = jnp.stack([collected[0][1]])
    stack_out = jnp.stack([collected[0][2]])
    stack_ffn = jnp.stack([collected[0][3]])
    stack_in, stack_down, stack_out, stack_ffn = lax.psum(
        (stack_in, stack_down, stack_out, stack_ffn), ("batch", "seq")
    )
    return (mixed, input_grad, stack_in, stack_down, stack_out, stack_ffn)


BF = jnp.bfloat16
F32 = jnp.float32
QB = 256
PLAN = ((0, 3, False, True), (0, 4, False, True), (0, 5, True, True), (1, 5, True, True))
HALO_PLAN = ((2, 2), (3, 1))
NEG = -1e30
VMEM_LIMIT = int(63.9 * 2**20)


def nn(a, b):
    return jnp.dot(a, b, preferred_element_type=F32)


def nt(a, b):
    return lax.dot_general(a, b, (((1,), (1,)), ((), ())), preferred_element_type=F32)


def tn(a, b):
    return lax.dot_general(a, b, (((0,), (0,)), ((), ())), preferred_element_type=F32)


def iota(shape, dim):
    return lax.broadcasted_iota(jnp.int32, shape, dim)


def block_at(flip, block):
    return pl.multiple_of(jnp.where(flip == 1, 3 - block, block) * QB, QB)


def rope(vectors, cosine, sine):
    lane = iota((1, 128), 1)
    first = lax.rem(lane, HEAD_DIM) < HEAD_DIM // 2
    out = []
    for c in range(vectors.shape[1] // 128):
        part = vectors[:, c * 128 : (c + 1) * 128]
        other = jnp.where(first, pltpu.roll(part, 96, 1), pltpu.roll(part, 32, 1))
        out.append(part * cosine + other * sine)
    return jnp.concatenate(out, axis=1)


def fill_tables(flip, seg_ref, freq_ref, cos_ref, sin_ref, fq_ref, fk_ref, bias_ref):
    lane = iota((1, 128), 1)
    seg_row = seg_ref[...].astype(F32)
    starts = [
        jnp.sum((seg_row < float(d)).astype(F32), axis=1, keepdims=True) for d in (1, 2, 3)
    ]
    sign = jnp.where(lax.rem(lane, HEAD_DIM) < HEAD_DIM // 2, -1.0, 1.0)
    for w in range(12):
        block, part = divmod(w, 2)
        base = jnp.where(flip == 1, 7 - block, block) * QB + part * 128
        row = seg_ref[:, pl.ds(pl.multiple_of(base, 128), 128)].astype(F32)
        seg = jnp.broadcast_to(row, (128, 128)).T
        start = jnp.where(
            seg >= 3.0,
            starts[2],
            jnp.where(seg >= 2.0, starts[1], jnp.where(seg >= 1.0, starts[0], 0.0)),
        )
        pos = (iota((128, 128), 0) + base).astype(F32) - start
        angle = pos * freq_ref[...]
        rows = pl.ds(w * 128, 128)
        cos_ref[rows, :] = jnp.cos(angle)
        sin_ref[rows, :] = jnp.sin(angle) * sign
        hit = seg == lane.astype(F32)
        fq_ref[rows, :] = jnp.where(hit, 1.0, 0.0).astype(BF)
        fk_ref[rows, :] = jnp.where(hit | (lane >= 4), 0.0, NEG).astype(BF)
    gap = iota((QB, QB), 0) - iota((QB, QB), 1)
    gap = jnp.where(flip == 1, -gap, gap)
    bias_ref[0] = jnp.where(gap >= 0, 0.0, NEG)
    bias_ref[1] = jnp.where(gap <= 0, 0.0, NEG)


def qkv_rows(rb, xw, wq, aqkv, bblk, cos_ref, sin_ref, q_ref, k_ref, v_ref, low_ref):
    rows = pl.ds(pl.multiple_of(rb * QB, QB), QB)
    x = xw[rows, :]
    low = nt(x, aqkv[...]).astype(BF)
    low_ref[rows, :] = low
    cosine = cos_ref[rows, :]
    sine = sin_ref[rows, :]
    for p, dest in enumerate((q_ref, k_ref, v_ref)):
        proj = nn(x, wq[p].reshape(D, D)) + nn(low, bblk[p])
        if p == 0:
            value = rope(proj, cosine, sine).astype(BF) * jnp.asarray(0.125, BF)
        elif p == 1:
            value = rope(proj, cosine, sine).astype(BF)
        else:
            value = proj.astype(BF)
        dest[rb] = value


def attend_pair(
    qb, pair, step, q_ref, k_ref, v_ref, fq_ref, fk_ref, bias_ref, att_ref, linv_ref, mf_ref, p_hbm, stage, sem
):
    k0, n, tri_first, tri_last = PLAN[qb]
    rows = pl.ds(qb * QB, QB)
    kblocks = pl.ds(k0, n)
    krows = pl.ds(k0 * QB, n * QB)
    half = iota((1, 128), 1) >= HEAD_DIM
    lane = iota((1, 128), 1)
    slot = lax.rem(step, 2)

    def copy(s):
        return pltpu.make_async_copy(stage.at[pl.ds(s * 4, 4)], p_hbm.at[qb, pair], sem.at[s])

    @pl.when(pair >= 2)
    def _():
        copy(slot).wait()

    lanes = pl.ds(pl.multiple_of(pair * 128, 128), 128)
    q2 = q_ref[qb, :, lanes]
    fq = fq_ref[rows, :]
    keys = jnp.concatenate([k_ref[kblocks, :, lanes].reshape(n * QB, 128), fk_ref[krows, :]], axis=1)
    v2 = v_ref[kblocks, :, lanes].reshape(n * QB, 128)
    outs = []
    for h in range(2):
        mine = half if h == 1 else jnp.logical_not(half)
        qm = jnp.where(mine, q2, jnp.zeros_like(q2))
        s = nt(jnp.concatenate([qm, fq], axis=1), keys)
        parts = [s[:, t * QB : (t + 1) * QB] for t in range(n)]
        if tri_last:
            parts[n - 1] = parts[n - 1] + bias_ref[0]
        if tri_first:
            parts[0] = parts[0] + bias_ref[1]
        s = jnp.concatenate(parts, axis=1)
        m = jnp.max(s, axis=1, keepdims=True)
        p = jnp.exp(s - m).astype(BF)
        for g in range((n + 2) // 3):
            part = p[:, g * D : min(g * D + D, n * QB)]
            stage[slot * 4 + h * 2 + g, :, 0 : part.shape[1]] = part
        if qb >= 2:
            low = 4 + 3 * (2 * pair + h)
            mf_ref[rows, :] = jnp.where((lane >= low) & (lane < low + 3), -m, mf_ref[rows, :])
        outs.append(nn(p, jnp.where(mine, v2, jnp.ones_like(v2))))
    inv = 1.0 / pltpu.roll(jnp.where(half, outs[0], outs[1]), HEAD_DIM, 1)
    att_ref[rows, lanes] = (jnp.where(half, outs[1], outs[0]) * inv).astype(BF)
    linv_ref[rows, lanes] = inv
    copy(slot).start()


def drain_pairs(qb, p_hbm, stage, sem):
    for s in range(2):
        pltpu.make_async_copy(stage.at[pl.ds(s * 4, 4)], p_hbm.at[qb, 0], sem.at[s]).wait()


def norm_stats(r):
    centre = r - jnp.mean(r, axis=1, keepdims=True)
    rstd = lax.rsqrt(jnp.mean(centre * centre, axis=1, keepdims=True) + EPSILON)
    return centre * rstd, rstd


def norm_back(grad, xhat, rstd):
    return rstd * (
        grad
        - jnp.mean(grad, axis=1, keepdims=True)
        - xhat * jnp.mean(grad * xhat, axis=1, keepdims=True)
    )


def out_rows(rb, xw, att_ref, wo, ao, bo, gb, aff, xhat_ref, rstd_ref, act_ref, lowo_ref, lowf_ref):
    rows = pl.ds(pl.multiple_of(rb * QB, QB), QB)
    att = att_ref[rows, :]
    low = nt(att, ao[...]).astype(BF)
    lowo_ref[rows, :] = low
    branch = nn(att, wo[...].reshape(D, D)) + nn(low, bo[...])
    xhat, rstd = norm_stats(xw[rows, :].astype(F32) + branch)
    xhat_ref[rows, :] = xhat
    rstd_ref[rows, :] = jnp.broadcast_to(rstd, (QB, 128))
    act = (xhat * gb[0:1, :] + gb[1:2, :]).astype(BF)
    act_ref[rows, :] = act
    lowf_ref[rows, :] = nt(act, aff[...]).astype(BF)


def ffn_in_tile(n, rb, size, act_ref, lowf_ref, wi, wd, bg, bu, adn, big, lowd_ref, total_ref):
    start = pl.multiple_of(rb * size, size)
    rows = pl.ds(start, size)
    act = act_ref[rows, :]
    low = lowf_ref[rows, :]
    gate = nn(act, wi[n, 0].reshape(D, D)) + nn(low, bg[n])
    up = nn(act, wi[n, 1].reshape(D, D)) + nn(low, bu[n])
    inner = (gate * (1.0 / (1.0 + jnp.exp(-gate))) * up).astype(BF)
    blocks = size // QB
    here = n * 4 + rb * blocks
    big[pl.ds(here, blocks)] = gate.astype(BF).reshape(blocks, QB, D)
    big[pl.ds(here + 16, blocks)] = up.astype(BF).reshape(blocks, QB, D)
    lowd_ref[rows, 0:16] += nt(inner, adn[n])
    total_ref[rows, :] += nn(inner, wd[pl.ds(n * 8, 8)].reshape(D, D))


def ffn_out_rows(
    rb, flip, lowd_ref, bdn, xhat_ref, gb, cot, dtwo_ref, db2_ref, dlow_ref, mixed_ref, gbdn_ref
):
    start = pl.multiple_of(rb * QB, QB)
    rows = pl.ds(start, QB)
    low = lowd_ref[rows, 0:16].astype(BF)
    total = nn(low, bdn[...]) + dtwo_ref[rows, :]
    r = xhat_ref[rows, :] * gb[0:1, :] + gb[1:2, :] + total
    xhat, rstd = norm_stats(r)
    mixed_ref[pl.ds(block_at(flip, rb), QB), :] = (xhat * gb[2:3, :] + gb[3:4, :]).astype(BF)
    dtwo = norm_back(cot[rows, :].astype(F32) * gb[2:3, :], xhat, rstd)
    dtwo_ref[rows, :] = dtwo
    db2 = dtwo.astype(BF)
    db2_ref[rows, :] = db2
    dlow_ref[rows, :] = nt(db2, bdn[...]).astype(BF)
    gbdn_ref[...] += tn(low, db2)


def ffn_back_tile(
    n, start, size, db2_ref, dlow_ref, wd, wi, adn, bg, bu, big, lowf_ref, acc, dlf_ref, gadn_ref, gbf_ref
):
    rows = pl.ds(start, size)
    db2 = db2_ref[rows, :]
    dlow = dlow_ref[rows, :]
    dinner = nt(db2, wd[pl.ds(n * 8, 8)].reshape(D, D)) + nn(dlow, adn[n])
    blocks = size // QB
    here = n * 4 + lax.div(start, QB)
    gate = big[pl.ds(here, blocks)].reshape(size, D).astype(F32)
    up = big[pl.ds(here + 16, blocks)].reshape(size, D).astype(F32)
    sig = 1.0 / (1.0 + jnp.exp(-gate))
    silu = gate * sig
    inner = (silu * up).astype(BF)
    dg = (dinner * up * (sig + silu * (1.0 - sig))).astype(BF)
    du = (dinner * silu).astype(BF)
    acc[...] += nt(dg, wi[n, 0].reshape(D, D)) + nt(du, wi[n, 1].reshape(D, D))
    dlf_ref[...] += nt(dg, bg[n]) + nt(du, bu[n])
    gadn_ref[n] += tn(dlow, inner)
    low = lowf_ref[rows, :]
    gbf_ref[n] += jnp.where(iota((32, 1), 0) < 16, tn(low, dg), tn(low, du))


def hidden_back_rows(
    rb, off, acc, dlf_ref, aff, act_ref, dtwo_ref, xhat_ref, rstd_ref, gb, bo, ao, lowo_ref, att_ref,
    wo, linv_ref, h2, mf_ref, do_ref, hf_ref, gaff_ref, gbo_ref, gao_ref,
):
    start = pl.multiple_of(rb * QB, QB)
    rows = pl.ds(start, QB)
    local = pl.ds(pl.multiple_of(start - off, QB), QB)
    dlf = dlf_ref[local, :].astype(BF)
    dhid = dtwo_ref[rows, :] + acc[local, :] + nn(dlf, aff[...])
    gaff_ref[...] += tn(dlf, act_ref[rows, :])
    done = norm_back(dhid * gb[0:1, :], xhat_ref[rows, :], rstd_ref[rows, 0:1])
    dtwo_ref[rows, :] = done
    dbr = done.astype(BF)
    dlo = nt(dbr, bo[...]).astype(BF)
    att = att_ref[rows, :]
    gbo_ref[...] += tn(lowo_ref[rows, :], dbr)
    gao_ref[...] += tn(dlo, att)
    datt = (nt(dbr, wo[...].reshape(D, D)) + nn(dlo, ao[...])).astype(BF)
    do = (datt.astype(F32) * linv_ref[rows, :]).astype(BF)
    do_ref[rows, :] = do
    value = nn(do * att, h2[...]) + mf_ref[rows, :]
    lane = iota((1, 128), 1)
    role = jnp.where(lane < 40, lax.rem(lane + 2, 3), lax.rem(lane, 2))
    high = value.astype(BF)
    rest = value - high.astype(F32)
    mid = rest.astype(BF)
    last = (rest - mid.astype(F32)).astype(BF)
    hf_ref[rows, :] = jnp.where(role == 0, high, jnp.where(role == 1, mid, last))


def kf_kernel(
    x_hbm, xh_hbm, cot_hbm, seg_ref, freq_ref, aqkv, bqkv, ao, bo, aff, bff, adn, bdn, gb,
    wq_hbm, wo_hbm, wi_hbm, wd_hbm,
    q_hbm, k_hbm, v_hbm, p_hbm, mixed_ref, do_ref, hf_ref, lowq_hbm, done_hbm, cos_hbm, sin_hbm, fq_hbm, fk_hbm,
    gao_ref, gaff_ref, gadn_ref, gbo_ref, gbdn_ref, gbf_ref,
    wq, wo, wi, wd, big, xw, att, linv, xhat, dtwo, act, db2, cos, sin, fq, fk, bias, mf,
    lowq, lowo, lowf, dlow, acc, dlf, bblk, bg, bu, h2, wsem, xsem, osem, psem,
):
    flip = lax.axis_index("seq")
    cot = db2
    rstd = cos
    lowd = sin
    loads = []
    for i in range(4):
        loads.append(
            pltpu.make_async_copy(
                x_hbm.at[pl.ds(block_at(flip, i), QB)], xw.at[pl.ds(i * QB, QB)], xsem.at[i]
            )
        )
        loads.append(
            pltpu.make_async_copy(
                cot_hbm.at[pl.ds(block_at(flip, i), QB)], cot.at[pl.ds(i * QB, QB)], xsem.at[4 + i]
            )
        )
    for i in range(2):
        at = pl.multiple_of(jnp.where(flip == 1, 1 - i, i) * QB, QB)
        loads.append(
            pltpu.make_async_copy(xh_hbm.at[pl.ds(at, QB)], xw.at[pl.ds(1024 + i * QB, QB)], xsem.at[8 + i])
        )
    weights = [
        pltpu.make_async_copy(a, b, wsem.at[i])
        for i, (a, b) in enumerate(((wq_hbm, wq), (wo_hbm, wo), (wi_hbm, wi), (wd_hbm, wd)))
    ]
    for copy in loads + weights:
        copy.start()
    fill_tables(flip, seg_ref, freq_ref, cos, sin, fq, fk, bias)
    rank = iota((48, 1), 0)
    for p in range(3):
        keep = (rank >= 16 * p) & (rank < 16 * p + 16)
        bblk[p] = jnp.where(keep, bqkv[...], jnp.zeros_like(bqkv[...]))
    rank = iota((32, 1), 0)
    for n in range(4):
        piece = bff[:, n * D : (n + 1) * D]
        bg[n] = jnp.where(rank < 16, piece, jnp.zeros_like(piece))
        bu[n] = jnp.where(rank >= 16, piece, jnp.zeros_like(piece))
    head = lax.div(iota((D, 128), 0), HEAD_DIM)
    spot = iota((D, 128), 1)
    h2[...] = jnp.where(lax.div(spot - 40, 2) == head, jnp.where(spot >= 40, -1.0, 0.0), 0.0).astype(BF)
    mf[...] = jnp.zeros_like(mf)
    dtwo[...] = jnp.zeros_like(dtwo)
    for g in (gao_ref, gaff_ref, gadn_ref, gbo_ref, gbdn_ref, gbf_ref):
        g[...] = jnp.zeros_like(g)
    for copy in loads:
        copy.wait()
    weights[0].wait()
    q_ref, k_ref, v_ref = (big.at[pl.ds(i * 6, 6)] for i in range(3))
    stage = big.at[pl.ds(18, 8)]

    def qkv_step(rb, _):
        qkv_rows(rb, xw, wq, aqkv, bblk, cos, sin, q_ref, k_ref, v_ref, lowq)
        return 0

    lax.fori_loop(0, 6, qkv_step, 0)
    saves = [
        pltpu.make_async_copy(a, b, osem.at[i])
        for i, (a, b) in enumerate(
            ((q_ref, q_hbm), (k_ref, k_hbm), (v_ref, v_hbm), (lowq, lowq_hbm), (cos, cos_hbm), (sin, sin_hbm), (fq, fq_hbm), (fk, fk_hbm))
        )
    ]
    for copy in saves:
        copy.start()
    for qb in range(4):

        def pair_step(pair, _, qb=qb):
            attend_pair(qb, pair, pair, q_ref, k_ref, v_ref, fq, fk, bias, att, linv, mf, p_hbm, stage, psem)
            return 0

        lax.fori_loop(0, 6, pair_step, 0)
        drain_pairs(qb, p_hbm, stage, psem)
    for copy in saves:
        copy.wait()
    lowd[...] = jnp.zeros_like(lowd)
    weights[1].wait()

    def out_step(rb, _):
        out_rows(rb, xw, att, wo, ao, bo, gb, aff, xhat, rstd, act, lowo, lowf)
        return 0

    lax.fori_loop(0, 4, out_step, 0)
    weights[2].wait()
    weights[3].wait()

    def in_step(i, _):
        ffn_in_tile(lax.div(i, 2), lax.rem(i, 2), 512, act, lowf, wi, wd, bg, bu, adn, big, lowd, dtwo)
        return 0

    lax.fori_loop(0, 8, in_step, 0)

    def down_step(rb, _):
        ffn_out_rows(rb, flip, lowd, bdn, xhat, gb, cot, dtwo, db2, dlow, mixed_ref, gbdn_ref)
        return 0

    lax.fori_loop(0, 4, down_step, 0)

    def back_step(half, _):
        off = pl.multiple_of(half * 512, 512)
        acc[...] = jnp.zeros_like(acc)
        dlf[...] = jnp.zeros_like(dlf)

        def tile(n, _):
            ffn_back_tile(
                n, off, 512, db2, dlow, wd, wi, adn, bg, bu, big, lowf, acc, dlf, gadn_ref, gbf_ref
            )
            return 0

        lax.fori_loop(0, 4, tile, 0)

        def rows(i, _):
            hidden_back_rows(
                half * 2 + i, off, acc, dlf, aff, act, dtwo, xhat, rstd, gb, bo, ao, lowo, att, wo, linv, h2, mf,
                do_ref, hf_ref, gaff_ref, gbo_ref, gao_ref,
            )
            return 0

        lax.fori_loop(0, 2, rows, 0)
        return 0

    lax.fori_loop(0, 2, back_step, 0)
    last = pltpu.make_async_copy(dtwo, done_hbm, osem.at[8])
    last.start()
    last.wait()


def k3_kernel(
    x_hbm, q_hbm, k_hbm, v_hbm, p_hbm, do_hbm, hf_hbm, doh_hbm, hfh_hbm, lowq_hbm, done_hbm, cos_hbm, sin_hbm,
    fq_hbm, fk_hbm, aqkv, bqkv, wq_hbm,
    dx_ref, ga_ref, gbq_ref,
    xw, q, k, v, do, hf, lowq, done, cos, sin, fq, fk, wq, stage, dq, dkT, dvT, bias, sem, psem,
):
    flip = lax.axis_index("seq")
    table = (
        (q_hbm, q), (k_hbm, k), (v_hbm, v), (do_hbm, do.at[pl.ds(0, 1024)]), (hf_hbm, hf.at[pl.ds(0, 1024)]),
        (doh_hbm.at[pl.ds(256, 256)], do.at[pl.ds(1024, 256)]), (doh_hbm.at[pl.ds(0, 256)], do.at[pl.ds(1280, 256)]),
        (hfh_hbm.at[pl.ds(256, 256)], hf.at[pl.ds(1024, 256)]), (hfh_hbm.at[pl.ds(0, 256)], hf.at[pl.ds(1280, 256)]),
        (lowq_hbm, lowq), (done_hbm, done), (cos_hbm, cos), (sin_hbm, sin), (fq_hbm, fq), (fk_hbm, fk), (wq_hbm, wq),
    )
    loads = [pltpu.make_async_copy(a, b, sem.at[i]) for i, (a, b) in enumerate(table)]
    for i in range(4):
        loads.append(
            pltpu.make_async_copy(
                x_hbm.at[pl.ds(block_at(flip, i), QB)], xw.at[pl.ds(i * QB, QB)], sem.at[16 + i]
            )
        )
    for copy in loads:
        copy.start()
    dkT[...] = jnp.zeros_like(dkT)
    dvT[...] = jnp.zeros_like(dvT)
    ga_ref[...] = jnp.zeros_like(ga_ref)
    gbq_ref[...] = jnp.zeros_like(gbq_ref)
    gap = iota((QB, QB), 0) - iota((QB, QB), 1)
    gap = jnp.where(flip == 1, -gap, gap)
    bias[...] = jnp.where(gap <= 0, 0.0, NEG)
    half = iota((1, 128), 1) >= HEAD_DIM
    for copy in loads:
        copy.wait()

    def picks(pair, first, width):
        head = 2 * pair + lax.div(iota((128, 256), 1), 128)
        row = iota((128, 256), 0) - first - width * head
        return jnp.where((row >= 0) & (row < width), 1.0, 0.0).astype(BF)

    for qb in range(4):
        k0, n, _, _ = PLAN[qb]
        own = min(4 - k0, n)
        rows = pl.ds(qb * QB, QB)
        krows = pl.ds(k0 * QB, n * QB)

        def fetch(pair, s, qb=qb, n=n):
            return pltpu.make_async_copy(p_hbm.at[qb, pair], stage.at[s], psem.at[s])

        fetch(0, 0).start()

        def pair_step(pair, _, k0=k0, n=n, own=own, rows=rows, krows=krows, fetch=fetch):
            slot = lax.rem(pair, 2)
            fetch(pair, slot).wait()

            @pl.when(pair < 5)
            def _():
                fetch(pair + 1, 1 - slot).start()

            lanes = pl.ds(pl.multiple_of(pair * 128, 128), 128)
            do2 = do[rows, lanes]
            ndl = nn(hf[rows, :], picks(pair, 40, 2))
            k2 = k[krows, lanes]
            v2 = v[krows, lanes]
            qT = q[rows, lanes].T
            doT = do2.T
            dqs = []
            for h in range(2):
                mine = half if h == 1 else jnp.logical_not(half)
                p = stage[slot, 2 * h, :, 0 : min(D, n * QB)]
                if n > 3:
                    p = jnp.concatenate([p, stage[slot, 2 * h + 1, :, 0 : n * QB - D]], axis=1)
                dp = nt(jnp.where(mine, do2, jnp.zeros_like(do2)), v2)
                d = ndl[:, h * 128 : (h + 1) * 128]
                ds = (p.astype(F32) * (dp + jnp.concatenate([d] * (2 * n), axis=1))).astype(BF)
                dqs.append(nn(ds, k2))
                hr = pl.ds(pl.multiple_of(pair * 128 + h * 64, 64), 64)
                kc = pl.ds(k0 * QB, own * QB)
                dkT[hr, kc] += nn(qT[h * 64 : (h + 1) * 64], ds[:, 0 : own * QB])
                dvT[hr, kc] += nn(doT[h * 64 : (h + 1) * 64], p[:, 0 : own * QB])
            dq[rows, lanes] = jnp.where(half, dqs[1], dqs[0]) * 0.125
            return 0

        lax.fori_loop(0, 6, pair_step, 0)

    for i, (k0, n) in enumerate(HALO_PLAN):
        rows = pl.ds(1024 + i * QB, QB)
        krows = pl.ds(k0 * QB, n * QB)

        def halo_step(pair, _, k0=k0, n=n, rows=rows, krows=krows):
            lanes = pl.ds(pl.multiple_of(pair * 128, 128), 128)
            do2 = do[rows, lanes]
            q2 = q[rows, lanes]
            feats = hf[rows, :]
            ndl = nn(feats, picks(pair, 40, 2))
            nm = nn(feats, picks(pair, 4, 3))
            keys = jnp.concatenate([k[krows, lanes], fk[krows, :]], axis=1)
            v2 = v[krows, lanes]
            qT = q2.T
            doT = do2.T
            for h in range(2):
                mine = half if h == 1 else jnp.logical_not(half)
                s = nt(jnp.concatenate([jnp.where(mine, q2, jnp.zeros_like(q2)), fq[rows, :]], axis=1), keys)
                parts = [s[:, t * QB : (t + 1) * QB] for t in range(n)]
                parts[0] = parts[0] + bias[...]
                s = jnp.concatenate(parts, axis=1)
                m = nm[:, h * 128 : (h + 1) * 128]
                p = jnp.exp(s + jnp.concatenate([m] * (2 * n), axis=1))
                dp = nt(jnp.where(mine, do2, jnp.zeros_like(do2)), v2)
                d = ndl[:, h * 128 : (h + 1) * 128]
                ds = (p * (dp + jnp.concatenate([d] * (2 * n), axis=1))).astype(BF)
                hr = pl.ds(pl.multiple_of(pair * 128 + h * 64, 64), 64)
                kc = pl.ds(k0 * QB, n * QB)
                dkT[hr, kc] += nn(qT[h * 64 : (h + 1) * 64], ds)
                dvT[hr, kc] += nn(doT[h * 64 : (h + 1) * 64], p.astype(BF))
            return 0

        lax.fori_loop(0, 6, halo_step, 0)

    def row_step(rb, _):
        start = pl.multiple_of(rb * QB, QB)
        rows = pl.ds(start, QB)
        cosine = cos[rows, :]
        sine = -sin[rows, :]
        x = xw[rows, :]
        low = lowq[rows, :]
        dlow = jnp.zeros((QB, 48), F32)
        lane = lax.div(iota((1, 48), 1), 16)
        rank = lax.div(iota((48, 1), 0), 16)
        total = done[rows, :]
        for p in range(3):
            if p == 0:
                d = rope(dq[rows, :], cosine, sine)
            else:
                src = (dkT, dvT)[p - 1]
                d = jnp.concatenate(
                    [src[pl.ds(c * 128, 128), rows].T for c in range(6)], axis=1
                )
                if p == 1:
                    d = rope(d, cosine, sine)
            d = d.astype(BF)
            dlow += jnp.where(lane == p, nt(d, bqkv[...]), 0.0)
            gbq_ref[...] += jnp.where(rank == p, tn(low, d), 0.0)
            total += nt(d, wq[p].reshape(D, D))
        dlow = dlow.astype(BF)
        ga_ref[...] += tn(dlow, x)
        total += nn(dlow, aqkv[...])
        dx_ref[pl.ds(block_at(flip, rb), QB), :] = total.astype(BF)
        return 0

    lax.fori_loop(0, 4, row_step, 0)


MESH = pl.DeviceIdType.MESH
NCHUNK = 8


class Gather:
    def __init__(self, refs, sems):
        self.wq, self.wo, self.wi, self.wd = refs
        (self.zs, self.zr, self.xs, self.xr, self.ys, self.yr, self.ds, self.dr, self.es, self.er, self.cs, self.cr) = sems
        b = lax.axis_index("batch")
        self.s = lax.axis_index("seq")
        self.core = lax.rem(b, 2)
        self.x = lax.rem(lax.div(b, 2), 2)
        self.z = lax.div(b, 4)
        self.devx = (b + 2 - 4 * self.x, self.s)
        self.devy = (b, 1 - self.s)
        self.devc = (b + 1 - 2 * self.core, self.s)
        self.me = self.owner(self.z, 0, 0, 0)

    def owner(self, z, dx, dy, dc):
        x = 1 - self.x if dx else self.x
        y = 1 - self.s if dy else self.s
        c = 1 - self.core if dc else self.core
        return (z * 4 + x * 2 + c) * 2 + y

    def devz(self, z):
        return (z * 4 + self.x * 2 + self.core, self.s)

    def zof(self, d):
        return lax.rem(self.z + d, 4)

    def view(self, c, j, half=None):
        lanes = slice(None) if half is None else pl.ds(half * 384, 384)
        if c == 0:
            return self.wq.at[:, j, :, lanes]
        if c == 1:
            return self.wo.at[j, :, lanes]
        if c < 6:
            return self.wi.at[c - 2, :, j, :, lanes]
        return self.wd.at[j, pl.ds((c - 6) * 48, 48), lanes]

    def copy(self, c, j, half, dev, send, recv):
        v = self.view(c, j, half)
        return pltpu.make_async_remote_copy(v, v, send, recv, device_id=dev, device_id_type=MESH)

    def to_z(self, c, z):
        return self.copy(c, self.me, None, self.devz(z), self.zs.at[c, z], self.zr.at[c, self.z])

    def from_z(self, c, z):
        return self.copy(c, self.owner(z, 0, 0, 0), None, self.devz(z), self.zs.at[c, z], self.zr.at[c, z])

    def on_x(self, c, z, arriving):
        return self.copy(c, self.owner(z, arriving, 0, 0), None, self.devx, self.xs.at[c, z], self.xr.at[c, z])

    def on_y(self, c, z, arriving):
        return self.copy(c, self.owner(z, 0, arriving, 0), None, self.devy, self.ys.at[c, z], self.yr.at[c, z])

    def corner_x(self, c, z, arriving):
        return self.copy(c, self.owner(z, arriving, 1, 0), 0, self.devx, self.ds.at[c, z], self.dr.at[c, z])

    def corner_y(self, c, z, arriving):
        return self.copy(c, self.owner(z, 1, arriving, 0), 1, self.devy, self.es.at[c, z], self.er.at[c, z])

    def on_core(self, c, kind, z, arriving):
        j = self.owner(z, kind & 1, kind >> 1, arriving)
        k = kind * 4 + z
        return self.copy(c, j, None, self.devc, self.cs.at[c, k], self.cr.at[c, k])

    def barrier(self):
        bar = pltpu.get_barrier_semaphore()
        for dev in (self.devx, self.devy, self.devc, self.devz(self.zof(1)), self.devz(self.zof(2)), self.devz(self.zof(3))):
            pl.semaphore_signal(bar, inc=1, device_id=dev, device_id_type=MESH)
        pl.semaphore_wait(bar, 6)

    def stage_own(self, c):
        self.on_x(c, self.z, 0).start()
        self.on_y(c, self.z, 0).start()
        for d in (1, 3, 2):
            self.to_z(c, self.zof(d)).start()
        self.on_core(c, 0, self.z, 0).start()

    def stage_z(self, c):
        for d in (1, 3, 2):
            z = self.zof(d)
            self.from_z(c, z).wait_recv()
            self.on_x(c, z, 0).start()
            self.on_y(c, z, 0).start()
            self.on_core(c, 0, z, 0).start()

    def stage_xy(self, c):
        for d in range(4):
            z = self.zof(d)
            self.on_x(c, z, 1).wait_recv()
            self.corner_y(c, z, 0).start()
            self.on_core(c, 1, z, 0).start()
            self.on_y(c, z, 1).wait_recv()
            self.corner_x(c, z, 0).start()
            self.on_core(c, 2, z, 0).start()

    def stage_corner(self, c):
        for d in range(4):
            z = self.zof(d)
            self.corner_x(c, z, 1).wait_recv()
            self.corner_y(c, z, 1).wait_recv()
            self.on_core(c, 3, z, 0).start()

    def stage_core(self, c):
        for kind in range(4):
            for z in range(4):
                self.on_core(c, kind, z, 1).wait_recv()

    def finish(self, c):
        for d in (1, 2, 3):
            self.to_z(c, self.zof(d)).wait_send()
        for z in range(4):
            self.on_x(c, z, 0).wait_send()
            self.on_y(c, z, 0).wait_send()
            self.corner_x(c, z, 0).wait_send()
            self.corner_y(c, z, 0).wait_send()
            for kind in range(4):
                self.on_core(c, kind, z, 0).wait_send()


def gather_kernel(q, o, i, d, wq, wo, wi, wd, *rest):
    g = Gather((wq, wo, wi, wd), rest[:12])
    lsem = rest[12]
    local = [
        pltpu.make_async_copy(q, wq.at[:, g.me], lsem.at[0]),
        pltpu.make_async_copy(o, wo.at[g.me], lsem.at[1]),
        pltpu.make_async_copy(d, wd.at[g.me], lsem.at[2]),
    ]
    for n in range(4):
        local.append(pltpu.make_async_copy(i.at[:, :, pl.ds(D * n, D)], wi.at[n, :, g.me], lsem.at[3 + n]))
    for copy in local:
        copy.start()
    g.barrier()
    for copy in local:
        copy.wait()
    for t in range(NCHUNK + 4):
        for lag, stage in enumerate((g.stage_own, g.stage_z, g.stage_xy, g.stage_corner, g.stage_core)):
            if 0 <= t - lag < NCHUNK:
                stage(t - lag)
    for c in range(NCHUNK):
        g.finish(c)


def sds(shape, dtype):
    return jax.ShapeDtypeStruct(shape, dtype)


ANY = functools.partial(pl.BlockSpec, memory_space=pl.ANY)
INV = functools.partial(pl.BlockSpec, memory_space=pltpu.VMEM)


def gather_call(q, o, i, d):
    return pl.pallas_call(
        gather_kernel,
        out_shape=[sds(s, BF) for s in ((3, 32, 24, D), (32, 24, D), (4, 2, 32, 24, D), (32, 96, D))],
        in_specs=[ANY()] * 4,
        out_specs=[ANY()] * 4,
        scratch_shapes=[pltpu.SemaphoreType.DMA((NCHUNK, 4))] * 10
        + [pltpu.SemaphoreType.DMA((NCHUNK, 16))] * 2
        + [pltpu.SemaphoreType.DMA((7,))],
        compiler_params=pltpu.CompilerParams(collective_id=1, has_side_effects=True),
    )(q, o, i, d)


def kf_call(*args):
    outs = [
        (ANY, (6, QB, D), BF), (ANY, (6, QB, D), BF), (ANY, (6, QB, D), BF), (ANY, (4, 6, 4, QB, D), BF),
        (INV, (1024, D), BF), (INV, (1024, D), BF), (INV, (1024, 128), BF),
        (ANY, (1536, 48), BF), (ANY, (1024, D), F32), (ANY, (1536, 128), F32), (ANY, (1536, 128), F32),
        (ANY, (1536, 128), BF), (ANY, (1536, 128), BF),
        (INV, (16, D), F32), (INV, (32, D), F32), (INV, (4, 16, D), F32), (INV, (16, D), F32), (INV, (16, D), F32),
        (INV, (4, 32, D), F32),
    ]
    V = pltpu.VMEM
    scratch = [
        V((3, 32, 24, D), BF), V((32, 24, D), BF), V((4, 2, 32, 24, D), BF), V((32, 96, D), BF),
        V((32, QB, D), BF), V((1536, D), BF), V((1024, D), BF), V((1024, D), F32),
        V((1024, D), F32), V((1024, D), F32), V((1024, D), BF), V((1024, D), BF),
        V((1536, 128), F32), V((1536, 128), F32), V((1536, 128), BF), V((1536, 128), BF), V((2, QB, QB), F32),
        V((1024, 128), F32), V((1536, 48), BF), V((1024, 16), BF), V((1024, 32), BF),
        V((1024, 16), BF), V((512, D), F32), V((512, 32), F32), V((3, 48, D), BF),
        V((4, 32, D), BF), V((4, 32, D), BF), V((D, 128), BF),
        pltpu.SemaphoreType.DMA((4,)), pltpu.SemaphoreType.DMA((10,)), pltpu.SemaphoreType.DMA((9,)),
        pltpu.SemaphoreType.DMA((2,)),
    ]
    return pl.pallas_call(
        kf_kernel,
        out_shape=[sds(s, t) for _, s, t in outs],
        in_specs=[ANY()] * 3 + [INV()] * 11 + [ANY()] * 4,
        out_specs=[m() for m, _, _ in outs],
        scratch_shapes=scratch,
        compiler_params=pltpu.CompilerParams(vmem_limit_bytes=VMEM_LIMIT),
    )(*args)


def k3_call(*args):
    V = pltpu.VMEM
    scratch = [
        V((1024, D), BF), V((1536, D), BF), V((1536, D), BF), V((1536, D), BF), V((1536, D), BF), V((1536, 128), BF),
        V((1536, 48), BF), V((1024, D), F32), V((1536, 128), F32), V((1536, 128), F32), V((1536, 128), BF),
        V((1536, 128), BF), V((3, 32, 24, D), BF), V((2, 4, QB, D), BF), V((1024, D), F32), V((D, 1024), F32),
        V((D, 1024), F32), V((QB, QB), F32), pltpu.SemaphoreType.DMA((20,)), pltpu.SemaphoreType.DMA((2,)),
    ]
    return pl.pallas_call(
        k3_kernel,
        out_shape=[sds((1024, D), BF), sds((48, D), F32), sds((48, D), F32)],
        in_specs=[ANY()] * 15 + [INV()] * 2 + [ANY()],
        out_specs=[INV()] * 3,
        scratch_shapes=scratch,
        compiler_params=pltpu.CompilerParams(vmem_limit_bytes=VMEM_LIMIT),
    )(*args)


def fast(
    tokens, cotangent, segments, adapter_index, qkv_weight, out_weight, ffn_in_weight, ffn_out_weight,
    norm_gain, norm_bias, adapt_in, adapt_down, adapt_out, adapt_ffn,
):
    side = lax.axis_index("seq")
    x = tokens[0]
    swap = [(0, 1), (1, 0)]
    edge = lax.dynamic_slice_in_dim(x, jnp.where(side == 0, 512, 0), 512, 0)
    halo = lax.ppermute(edge, "seq", swap)
    e = adapter_index[0, 0]
    pick = lambda table: lax.dynamic_index_in_dim(table[0], e, 0, False)
    a_in = pick(adapt_in).transpose(0, 2, 1)
    aqkv, ao, aff = a_in[0:3].reshape(48, D), a_in[3], a_in[4:6].reshape(32, D)
    adn = pick(adapt_down).T.reshape(16, 4, D).transpose(1, 0, 2)
    b_out = pick(adapt_out)
    bqkv, bo, bdn = b_out[0:3].reshape(48, D), b_out[3], b_out[4]
    bff = pick(adapt_ffn).reshape(32, FF)
    gb = jnp.stack([norm_gain[0, 0], norm_bias[0, 0], norm_gain[0, 1], norm_bias[0, 1]])
    freq = jnp.power(ROPE_BASE, -2.0 * jnp.arange(HEAD_DIM // 2, dtype=F32) / HEAD_DIM)
    freq = jnp.tile(freq, 4)[None]
    wq, wo, wi, wd = gather_call(qkv_weight[0], out_weight[0], ffn_in_weight[0], ffn_out_weight[0])
    (
        q, k, v, p, mixed, do, hf, lowq, done, cos, sin, fq, fk, gao, gaff, gadn, gbo, gbdn, gbf,
    ) = kf_call(x, halo, cotangent[0], segments, freq, aqkv, bqkv, ao, bo, aff, bff, adn, bdn, gb, wq, wo, wi, wd)
    q, k, v = (a.reshape(1536, D) for a in (q, k, v))
    doh = lax.ppermute(do[512:], "seq", swap)
    hfh = lax.ppermute(hf[512:], "seq", swap)
    dx, gaq, gbq = k3_call(x, q, k, v, p, do, hf, doh, hfh, lowq, done, cos, sin, fq, fk, aqkv, bqkv, wq)
    g_in = jnp.concatenate([gaq, gao, gaff]).reshape(6, 16, D)
    g_dn = gadn.transpose(1, 0, 2).reshape(16, FF)
    g_out = jnp.concatenate([gbq, gbo, gbdn]).reshape(5, 16, D)
    g_ff = gbf.reshape(4, 2, 16, D).transpose(1, 2, 0, 3).reshape(2, 16, FF)
    slot = (jnp.arange(ADAPTERS) == e).astype(F32)
    spread = lambda g: slot.reshape((ADAPTERS,) + (1,) * g.ndim) * g[None]
    g_in, g_dn, g_out, g_ff = lax.psum(tuple(spread(g) for g in (g_in, g_dn, g_out, g_ff)), ("batch", "seq"))
    return (
        mixed[None], dx[None], g_in.transpose(0, 1, 3, 2)[None], g_dn.transpose(0, 2, 1)[None], g_out[None], g_ff[None],
    )


def solution(mesh):
    here = fast if dict(mesh.shape) == {"batch": 16, "seq": 2} else shards
    return jax.shard_map(
        here,
        mesh=mesh,
        in_specs=(
            P("batch", "seq", None),
            P("batch", "seq", None),
            P("batch", None),
            P("batch", None),
            P(None, None, ("batch", "seq"), None),
            P(None, ("batch", "seq"), None),
            P(None, None, ("batch", "seq"), None),
            P(None, ("batch", "seq"), None),
            P(),
            P(),
            P(),
            P(),
            P(),
            P(),
        ),
        out_specs=(P("batch", "seq", None), P("batch", "seq", None), P(), P(), P(), P()),
        check_vma=False,
    )
```

```python
import functools
import math

import jax
import jax.numpy as jnp
from jax import lax
from jax.experimental import pallas as pl
from jax.experimental.pallas import tpu as pltpu
from jax.sharding import PartitionSpec as P

HEADS = 12
HEAD_DIM = 64
ADAPTERS = 4
LAYERS = 1
HALF = 512
D = HEADS * HEAD_DIM
FF = 4 * D


EPSILON = 1e-06
ROPE_BASE = 1000.0
PRECISE = lax.Precision.HIGHEST


def shifted(array, axis, by):
    count = lax.axis_size(axis)
    pairs = [(i, i + by) for i in range(count) if 0 <= i + by < count]
    return lax.ppermute(array, axis, pairs)


def doc_positions(segment_ids):
    position_ids = jnp.arange(segment_ids.shape[-1], dtype=jnp.int32)
    starts_here = jnp.concatenate(
        [
            jnp.ones(segment_ids.shape[:-1] + (1,), dtype=jnp.bool_),
            segment_ids[..., 1:] != segment_ids[..., :-1],
        ],
        axis=-1,
    )
    doc_start = lax.cummax(jnp.where(starts_here, position_ids, 0), axis=segment_ids.ndim - 1)
    return (position_ids - doc_start).astype(jnp.float32)


def rope_tables(segment_ids):
    positions = doc_positions(segment_ids)
    frequency = jnp.power(ROPE_BASE, -2.0 * jnp.arange(HEAD_DIM // 2, dtype=jnp.float32) / HEAD_DIM)
    angles = positions[..., None] * frequency
    return (jnp.cos(angles), jnp.sin(angles))


def rotate(vectors, cosine_table, sine_table):
    half_dim = vectors.shape[-1] // 2
    first_half = vectors[..., :half_dim]
    second_half = vectors[..., half_dim:]
    cosine_rows = cosine_table[..., None, :]
    sine_rows = sine_table[..., None, :]
    return jnp.concatenate(
        [
            first_half * cosine_rows - second_half * sine_rows,
            second_half * cosine_rows + first_half * sine_rows,
        ],
        axis=-1,
    )


def norm_apply(residual, gain_row, bias_row):
    centre = residual - jnp.mean(residual, axis=-1, keepdims=True)
    spread = jnp.mean(centre * centre, axis=-1, keepdims=True)
    return centre * lax.rsqrt(spread + EPSILON) * gain_row + bias_row


def split_heads(merged, group_count):
    seqs_here, row_count, _ = merged.shape
    return merged.reshape(seqs_here, row_count, group_count, -1, HEAD_DIM).transpose(2, 0, 1, 3, 4)


def join_heads(grouped):
    group_count, seqs_here, row_count, heads_group, head_size = grouped.shape
    return grouped.transpose(1, 2, 0, 3, 4).reshape(
        seqs_here, row_count, group_count * heads_group * head_size
    )


def shards(
    tokens,
    cotangent,
    segments,
    adapter_index,
    qkv_weight,
    out_weight,
    ffn_in_weight,
    ffn_out_weight,
    norm_gain,
    norm_bias,
    adapt_in,
    adapt_down,
    adapt_out,
    adapt_ffn,
):
    seqs_here, tok_rows, model_width = tokens.shape
    heads_group = math.gcd(HEADS, 4)
    group_count = HEADS // heads_group
    score_scale = 1.0 / math.sqrt(HEAD_DIM)
    seq_count = lax.axis_size("seq")
    row_base = lax.axis_index("seq") * tok_rows
    shift_plan = []
    for distance in range(1, min(seq_count, HALF // tok_rows + 2)):
        row_count = min(tok_rows, HALF - (distance - 1) * tok_rows)
        if row_count > 0:
            shift_plan.append((distance, row_count))
            shift_plan.append((-distance, row_count))
    left_total = sum((plan_item[1] for plan_item in shift_plan if plan_item[0] > 0))
    key_rows = 2 * left_total + tok_rows
    key_places = {}
    passed_rows = 0
    for distance, row_count in shift_plan:
        if distance > 0:
            key_places[distance] = left_total - passed_rows - row_count
            key_places[-distance] = left_total + tok_rows + passed_rows
            passed_rows += row_count
    cosine_all, sine_all = rope_tables(segments)
    cosine_here = lax.dynamic_slice_in_dim(cosine_all, row_base, tok_rows, 1)
    sine_here = lax.dynamic_slice_in_dim(sine_all, row_base, tok_rows, 1)
    padded_ids = jnp.pad(segments, ((0, 0), (HALF, HALF)), constant_values=-1)
    key_ids = lax.dynamic_slice_in_dim(padded_ids, row_base - left_total + HALF, key_rows, 1)
    query_ids = lax.dynamic_slice_in_dim(segments, row_base, tok_rows, 1)
    offsets = (
        jnp.arange(tok_rows, dtype=jnp.int32)[:, None]
        - jnp.arange(key_rows, dtype=jnp.int32)[None, :]
        + left_total
    )
    visible = (query_ids[:, :, None] == key_ids[:, None, :]) & (jnp.abs(offsets) <= HALF)[None]
    slot_hits = adapter_index[:, 0][:, None] == jnp.arange(ADAPTERS, dtype=jnp.int32)[None, :]
    slot_low = slot_hits.astype(jnp.bfloat16)
    slot_full = slot_hits.astype(jnp.float32)

    def select_adapter(table):
        return jnp.einsum(
            "se,le...->ls...", slot_low, table, preferred_element_type=jnp.float32
        ).astype(jnp.bfloat16)

    def spread_slots(per_sequence):
        return jnp.einsum("se,s...->e...", slot_full, per_sequence, precision=PRECISE)

    chosen_in = select_adapter(adapt_in)
    chosen_down = select_adapter(adapt_down)
    chosen_out = select_adapter(adapt_out)
    chosen_ffn = select_adapter(adapt_ffn)

    def forward_group(items):
        query_block, key_block, value_block = items
        scores = (
            jnp.einsum(
                "sqhd,skhd->shqk", query_block, key_block, preferred_element_type=jnp.float32
            )
            * score_scale
        )
        scores = jnp.where(visible[:, None], scores, -1e30)
        biggest = jnp.max(scores, axis=-1, keepdims=True)
        lifted = jnp.exp(scores - biggest)
        row_total = jnp.sum(lifted, axis=-1, keepdims=True)
        probability = (lifted / row_total).astype(jnp.bfloat16)
        result = jnp.einsum(
            "shqk,skhd->sqhd", probability, value_block, preferred_element_type=jnp.float32
        )
        return (result.astype(jnp.bfloat16), (biggest + jnp.log(row_total))[..., 0])

    def backward_group(items):
        query_block, key_block, value_block, grad_block, log_total = items
        scores = (
            jnp.einsum(
                "sqhd,skhd->shqk", query_block, key_block, preferred_element_type=jnp.float32
            )
            * score_scale
        )
        scores = jnp.where(visible[:, None], scores, -1e30)
        probability = jnp.exp(scores - log_total[..., None])
        d_prob = jnp.einsum(
            "sqhd,skhd->shqk", grad_block, value_block, preferred_element_type=jnp.float32
        )
        delta = jnp.sum(probability * d_prob, axis=-1, keepdims=True)
        d_score = (probability * (d_prob - delta)).astype(jnp.bfloat16)
        d_query = (
            jnp.einsum("shqk,skhd->sqhd", d_score, key_block, preferred_element_type=jnp.float32)
            * score_scale
        )
        d_key = (
            jnp.einsum("shqk,sqhd->skhd", d_score, query_block, preferred_element_type=jnp.float32)
            * score_scale
        )
        d_value = jnp.einsum(
            "shqk,sqhd->skhd",
            probability.astype(jnp.bfloat16),
            grad_block,
            preferred_element_type=jnp.float32,
        )
        return (d_query, d_key, d_value)

    state = tokens.astype(jnp.float32)
    layer_index = 0
    w_qkv = lax.all_gather(qkv_weight[layer_index], ("batch", "seq"), axis=1, tiled=True)
    w_out = lax.all_gather(out_weight[layer_index], ("batch", "seq"), axis=0, tiled=True)
    w_in = lax.all_gather(ffn_in_weight[layer_index], ("batch", "seq"), axis=1, tiled=True)
    w_down = lax.all_gather(ffn_out_weight[layer_index], ("batch", "seq"), axis=0, tiled=True)
    held = [(w_qkv, w_out, w_in, w_down)]
    act_one = state.astype(jnp.bfloat16)
    low_qkv = jnp.einsum(
        "std,spdr->pstr",
        act_one,
        chosen_in[layer_index][:, 0:3],
        preferred_element_type=jnp.float32,
    ).astype(jnp.bfloat16)
    proj = jnp.einsum(
        "std,pde->pste", act_one, w_qkv, preferred_element_type=jnp.float32
    ) + jnp.einsum(
        "pstr,spre->pste",
        low_qkv,
        chosen_out[layer_index][:, 0:3],
        preferred_element_type=jnp.float32,
    )
    queries = (
        rotate(proj[0].reshape(seqs_here, tok_rows, HEADS, HEAD_DIM), cosine_here, sine_here)
        .astype(jnp.bfloat16)
        .reshape(seqs_here, tok_rows, model_width)
    )
    key_rot = (
        rotate(proj[1].reshape(seqs_here, tok_rows, HEADS, HEAD_DIM), cosine_here, sine_here)
        .astype(jnp.bfloat16)
        .reshape(seqs_here, tok_rows, model_width)
    )
    key_value = jnp.stack([key_rot, proj[2].astype(jnp.bfloat16)])
    edges = {}
    for step_by, row_count in shift_plan:
        if step_by > 0:
            outgoing = key_value[:, :, tok_rows - row_count :]
        else:
            outgoing = key_value[:, :, :row_count]
        edges[step_by] = shifted(outgoing, "seq", step_by)
    earlier = [edges[distance] for distance, row_count in reversed(shift_plan) if distance > 0]
    later = [edges[-distance] for distance, row_count in shift_plan if distance > 0]
    window = jnp.concatenate(earlier + [key_value] + later, axis=2)
    heads_out, log_total = lax.map(
        forward_group,
        (
            split_heads(queries, group_count),
            split_heads(window[0], group_count),
            split_heads(window[1], group_count),
        ),
    )
    attended = join_heads(heads_out)
    low_out = jnp.einsum(
        "std,sdr->str", attended, chosen_in[layer_index][:, 3], preferred_element_type=jnp.float32
    ).astype(jnp.bfloat16)
    branch = jnp.einsum(
        "std,de->ste", attended, w_out, preferred_element_type=jnp.float32
    ) + jnp.einsum(
        "str,sre->ste", low_out, chosen_out[layer_index][:, 3], preferred_element_type=jnp.float32
    )
    resid_one = state + branch
    hidden = norm_apply(resid_one, norm_gain[layer_index, 0], norm_bias[layer_index, 0])
    act_two = hidden.astype(jnp.bfloat16)
    low_ffn = jnp.einsum(
        "std,spdr->pstr",
        act_two,
        chosen_in[layer_index][:, 4:6],
        preferred_element_type=jnp.float32,
    ).astype(jnp.bfloat16)
    gate_up = jnp.einsum(
        "std,pdf->pstf", act_two, w_in, preferred_element_type=jnp.float32
    ) + jnp.einsum(
        "pstr,sprf->pstf", low_ffn, chosen_ffn[layer_index], preferred_element_type=jnp.float32
    )
    inner = (jax.nn.silu(gate_up[0]) * gate_up[1]).astype(jnp.bfloat16)
    low_down = jnp.einsum(
        "stf,sfr->str", inner, chosen_down[layer_index], preferred_element_type=jnp.float32
    ).astype(jnp.bfloat16)
    branch_two = jnp.einsum(
        "stf,fe->ste", inner, w_down, preferred_element_type=jnp.float32
    ) + jnp.einsum(
        "str,sre->ste", low_down, chosen_out[layer_index][:, 4], preferred_element_type=jnp.float32
    )
    resid_two = hidden + branch_two
    kept = [
        (
            act_one,
            low_qkv,
            queries,
            window,
            log_total,
            attended,
            low_out,
            resid_one,
            act_two,
            low_ffn,
            gate_up,
            inner,
            low_down,
            resid_two,
        )
    ]
    state = norm_apply(resid_two, norm_gain[layer_index, 1], norm_bias[layer_index, 1])
    mixed = state.astype(jnp.bfloat16)
    grad = cotangent.astype(jnp.float32)
    collected = [None] * LAYERS
    for layer_index in reversed(range(LAYERS)):
        (
            act_one,
            low_qkv,
            queries,
            window,
            log_total,
            attended,
            low_out,
            resid_one,
            act_two,
            low_ffn,
            gate_up,
            inner,
            low_down,
            resid_two,
        ) = kept[layer_index]
        w_qkv, w_out, w_in, w_down = held[layer_index]
        gain_two = norm_gain[layer_index, 1]
        bias_two = norm_bias[layer_index, 1]
        _, pull_two = jax.vjp(lambda residual: norm_apply(residual, gain_two, bias_two), resid_two)
        (d_resid_two,) = pull_two(grad)
        d_branch_two = d_resid_two.astype(jnp.bfloat16)
        d_low_down = jnp.einsum(
            "ste,sre->str",
            d_branch_two,
            chosen_out[layer_index][:, 4],
            preferred_element_type=jnp.float32,
        ).astype(jnp.bfloat16)
        g_out_down = jnp.einsum(
            "str,ste->sre", low_down, d_branch_two, preferred_element_type=jnp.float32
        )
        g_down = jnp.einsum("stf,str->sfr", inner, d_low_down, preferred_element_type=jnp.float32)
        d_inner = jnp.einsum(
            "ste,fe->stf", d_branch_two, w_down, preferred_element_type=jnp.float32
        ) + jnp.einsum(
            "str,sfr->stf", d_low_down, chosen_down[layer_index], preferred_element_type=jnp.float32
        )
        _, pull_act = jax.vjp(
            lambda gate_part, up_part: jax.nn.silu(gate_part) * up_part, gate_up[0], gate_up[1]
        )
        d_gate, d_up = pull_act(d_inner)
        d_gate_up = jnp.stack([d_gate, d_up]).astype(jnp.bfloat16)
        d_low_ffn = jnp.einsum(
            "pstf,sprf->pstr",
            d_gate_up,
            chosen_ffn[layer_index],
            preferred_element_type=jnp.float32,
        ).astype(jnp.bfloat16)
        g_ffn = jnp.einsum(
            "pstr,pstf->sprf", low_ffn, d_gate_up, preferred_element_type=jnp.float32
        )
        g_in_ffn = jnp.einsum(
            "std,pstr->spdr", act_two, d_low_ffn, preferred_element_type=jnp.float32
        )
        ffn_in_sum = spread_slots(g_in_ffn)
        ffn_down_sum = spread_slots(g_down)
        ffn_out_sum = spread_slots(g_out_down[:, None])
        ffn_ffn_sum = spread_slots(g_ffn)
        d_hidden = (
            d_resid_two
            + jnp.einsum("pstf,pdf->std", d_gate_up, w_in, preferred_element_type=jnp.float32)
            + jnp.einsum(
                "pstr,spdr->std",
                d_low_ffn,
                chosen_in[layer_index][:, 4:6],
                preferred_element_type=jnp.float32,
            )
        )
        gain_one = norm_gain[layer_index, 0]
        bias_one = norm_bias[layer_index, 0]
        _, pull_one = jax.vjp(lambda residual: norm_apply(residual, gain_one, bias_one), resid_one)
        (d_resid_one,) = pull_one(d_hidden)
        d_branch = d_resid_one.astype(jnp.bfloat16)
        d_low_out = jnp.einsum(
            "ste,sre->str",
            d_branch,
            chosen_out[layer_index][:, 3],
            preferred_element_type=jnp.float32,
        ).astype(jnp.bfloat16)
        g_out_att = jnp.einsum(
            "str,ste->sre", low_out, d_branch, preferred_element_type=jnp.float32
        )
        g_in_att = jnp.einsum(
            "std,str->sdr", attended, d_low_out, preferred_element_type=jnp.float32
        )
        d_attended = (
            jnp.einsum("ste,de->std", d_branch, w_out, preferred_element_type=jnp.float32)
            + jnp.einsum(
                "str,sdr->std",
                d_low_out,
                chosen_in[layer_index][:, 3],
                preferred_element_type=jnp.float32,
            )
        ).astype(jnp.bfloat16)
        d_query_heads, d_key_heads, d_value_heads = lax.map(
            backward_group,
            (
                split_heads(queries, group_count),
                split_heads(window[0], group_count),
                split_heads(window[1], group_count),
                split_heads(d_attended, group_count),
                log_total,
            ),
        )
        d_query = join_heads(d_query_heads)
        d_window = jnp.stack([join_heads(d_key_heads), join_heads(d_value_heads)])
        d_pair = d_window[:, :, left_total : left_total + tok_rows]
        for step_by, row_count in shift_plan:
            returning = lax.slice_in_dim(
                d_window, key_places[step_by], key_places[step_by] + row_count, axis=2
            )
            arrived = shifted(returning.astype(jnp.bfloat16), "seq", -step_by).astype(
                returning.dtype
            )
            if step_by > 0:
                d_pair = d_pair.at[:, :, tok_rows - row_count :].add(arrived)
            else:
                d_pair = d_pair.at[:, :, :row_count].add(arrived)
        d_query_rot = rotate(
            d_query.reshape(seqs_here, tok_rows, HEADS, HEAD_DIM), cosine_here, -sine_here
        ).reshape(seqs_here, tok_rows, model_width)
        d_key_rot = rotate(
            d_pair[0].reshape(seqs_here, tok_rows, HEADS, HEAD_DIM), cosine_here, -sine_here
        ).reshape(seqs_here, tok_rows, model_width)
        d_proj = jnp.stack([d_query_rot, d_key_rot, d_pair[1]]).astype(jnp.bfloat16)
        d_low_qkv = jnp.einsum(
            "pste,spre->pstr",
            d_proj,
            chosen_out[layer_index][:, 0:3],
            preferred_element_type=jnp.float32,
        ).astype(jnp.bfloat16)
        g_out_qkv = jnp.einsum(
            "pstr,pste->spre", low_qkv, d_proj, preferred_element_type=jnp.float32
        )
        g_in_qkv = jnp.einsum(
            "std,pstr->spdr", act_one, d_low_qkv, preferred_element_type=jnp.float32
        )
        grad = (
            d_resid_one
            + jnp.einsum("pste,pde->std", d_proj, w_qkv, preferred_element_type=jnp.float32)
            + jnp.einsum(
                "pstr,spdr->std",
                d_low_qkv,
                chosen_in[layer_index][:, 0:3],
                preferred_element_type=jnp.float32,
            )
        )
        att_in_sum = spread_slots(jnp.concatenate([g_in_qkv, g_in_att[:, None]], axis=1))
        att_out_sum = spread_slots(jnp.concatenate([g_out_qkv, g_out_att[:, None]], axis=1))
        collected[layer_index] = (
            jnp.concatenate([att_in_sum, ffn_in_sum], axis=1),
            ffn_down_sum,
            jnp.concatenate([att_out_sum, ffn_out_sum], axis=1),
            ffn_ffn_sum,
        )
    input_grad = grad.astype(jnp.bfloat16)
    stack_in = jnp.stack([collected[0][0]])
    stack_down = jnp.stack([collected[0][1]])
    stack_out = jnp.stack([collected[0][2]])
    stack_ffn = jnp.stack([collected[0][3]])
    stack_in, stack_down, stack_out, stack_ffn = lax.psum(
        (stack_in, stack_down, stack_out, stack_ffn), ("batch", "seq")
    )
    return (mixed, input_grad, stack_in, stack_down, stack_out, stack_ffn)


BF = jnp.bfloat16
F32 = jnp.float32
QB = 256
PLAN = ((0, 3, False, True), (0, 4, False, True), (0, 5, True, True), (1, 5, True, True))
HALO_PLAN = ((2, 2), (3, 1))
NEG = -1e30
VMEM_LIMIT = int(63.9 * 2**20)


def nn(a, b):
    return jnp.dot(a, b, preferred_element_type=F32)


def nt(a, b):
    return lax.dot_general(a, b, (((1,), (1,)), ((), ())), preferred_element_type=F32)


def tn(a, b):
    return lax.dot_general(a, b, (((0,), (0,)), ((), ())), preferred_element_type=F32)


def iota(shape, dim):
    return lax.broadcasted_iota(jnp.int32, shape, dim)


def block_at(flip, block):
    return pl.multiple_of(jnp.where(flip == 1, 3 - block, block) * QB, QB)


def rope(vectors, cosine, sine):
    lane = iota((1, 128), 1)
    first = lax.rem(lane, HEAD_DIM) < HEAD_DIM // 2
    out = []
    for c in range(vectors.shape[1] // 128):
        part = vectors[:, c * 128 : (c + 1) * 128]
        other = jnp.where(first, pltpu.roll(part, 96, 1), pltpu.roll(part, 32, 1))
        out.append(part * cosine + other * sine)
    return jnp.concatenate(out, axis=1)


def fill_tables(flip, seg_ref, freq_ref, cos_ref, sin_ref, fq_ref, fk_ref, bias_ref):
    lane = iota((1, 128), 1)
    seg_row = seg_ref[...].astype(F32)
    starts = [
        jnp.sum((seg_row < float(d)).astype(F32), axis=1, keepdims=True) for d in (1, 2, 3)
    ]
    sign = jnp.where(lax.rem(lane, HEAD_DIM) < HEAD_DIM // 2, -1.0, 1.0)
    for w in range(12):
        block, part = divmod(w, 2)
        base = jnp.where(flip == 1, 7 - block, block) * QB + part * 128
        row = seg_ref[:, pl.ds(pl.multiple_of(base, 128), 128)].astype(F32)
        seg = jnp.broadcast_to(row, (128, 128)).T
        start = jnp.where(
            seg >= 3.0,
            starts[2],
            jnp.where(seg >= 2.0, starts[1], jnp.where(seg >= 1.0, starts[0], 0.0)),
        )
        pos = (iota((128, 128), 0) + base).astype(F32) - start
        angle = pos * freq_ref[...]
        rows = pl.ds(w * 128, 128)
        cos_ref[rows, :] = jnp.cos(angle)
        sin_ref[rows, :] = jnp.sin(angle) * sign
        hit = seg == lane.astype(F32)
        fq_ref[rows, :] = jnp.where(hit, 1.0, 0.0).astype(BF)
        fk_ref[rows, :] = jnp.where(hit | (lane >= 4), 0.0, NEG).astype(BF)
    gap = iota((QB, QB), 0) - iota((QB, QB), 1)
    gap = jnp.where(flip == 1, -gap, gap)
    bias_ref[0] = jnp.where(gap >= 0, 0.0, NEG)
    bias_ref[1] = jnp.where(gap <= 0, 0.0, NEG)


def qkv_rows(rb, xw, wq, aqkv, bblk, cos_ref, sin_ref, q_ref, k_ref, v_ref, low_ref):
    rows = pl.ds(pl.multiple_of(rb * QB, QB), QB)
    x = xw[rows, :]
    low = nt(x, aqkv[...]).astype(BF)
    low_ref[rows, :] = low
    cosine = cos_ref[rows, :]
    sine = sin_ref[rows, :]
    for p, dest in enumerate((q_ref, k_ref, v_ref)):
        proj = nn(x, wq[p].reshape(D, D)) + nn(low, bblk[p])
        if p == 0:
            value = rope(proj, cosine, sine).astype(BF) * jnp.asarray(0.125, BF)
        elif p == 1:
            value = rope(proj, cosine, sine).astype(BF)
        else:
            value = proj.astype(BF)
        dest[rb] = value


def attend_pair(
    qb, pair, step, q_ref, k_ref, v_ref, fq_ref, fk_ref, bias_ref, att_ref, linv_ref, mf_ref, p_hbm, stage, sem
):
    k0, n, tri_first, tri_last = PLAN[qb]
    rows = pl.ds(qb * QB, QB)
    kblocks = pl.ds(k0, n)
    krows = pl.ds(k0 * QB, n * QB)
    half = iota((1, 128), 1) >= HEAD_DIM
    lane = iota((1, 128), 1)
    slot = lax.rem(step, 2)

    def copy(s):
        return pltpu.make_async_copy(stage.at[pl.ds(s * 4, 4)], p_hbm.at[qb, pair], sem.at[s])

    @pl.when(pair >= 2)
    def _():
        copy(slot).wait()

    lanes = pl.ds(pl.multiple_of(pair * 128, 128), 128)
    q2 = q_ref[qb, :, lanes]
    fq = fq_ref[rows, :]
    keys = jnp.concatenate([k_ref[kblocks, :, lanes].reshape(n * QB, 128), fk_ref[krows, :]], axis=1)
    v2 = v_ref[kblocks, :, lanes].reshape(n * QB, 128)
    outs = []
    for h in range(2):
        mine = half if h == 1 else jnp.logical_not(half)
        qm = jnp.where(mine, q2, jnp.zeros_like(q2))
        s = nt(jnp.concatenate([qm, fq], axis=1), keys)
        parts = [s[:, t * QB : (t + 1) * QB] for t in range(n)]
        if tri_last:
            parts[n - 1] = parts[n - 1] + bias_ref[0]
        if tri_first:
            parts[0] = parts[0] + bias_ref[1]
        s = jnp.concatenate(parts, axis=1)
        m = jnp.max(s, axis=1, keepdims=True)
        p = jnp.exp(s - m).astype(BF)
        for g in range((n + 2) // 3):
            part = p[:, g * D : min(g * D + D, n * QB)]
            stage[slot * 4 + h * 2 + g, :, 0 : part.shape[1]] = part
        if qb >= 2:
            low = 4 + 3 * (2 * pair + h)
            mf_ref[rows, :] = jnp.where((lane >= low) & (lane < low + 3), -m, mf_ref[rows, :])
        outs.append(nn(p, jnp.where(mine, v2, jnp.ones_like(v2))))
    inv = 1.0 / pltpu.roll(jnp.where(half, outs[0], outs[1]), HEAD_DIM, 1)
    att_ref[rows, lanes] = (jnp.where(half, outs[1], outs[0]) * inv).astype(BF)
    linv_ref[rows, lanes] = inv
    copy(slot).start()


def drain_pairs(qb, p_hbm, stage, sem):
    for s in range(2):
        pltpu.make_async_copy(stage.at[pl.ds(s * 4, 4)], p_hbm.at[qb, 0], sem.at[s]).wait()


def norm_stats(r):
    centre = r - jnp.mean(r, axis=1, keepdims=True)
    rstd = lax.rsqrt(jnp.mean(centre * centre, axis=1, keepdims=True) + EPSILON)
    return centre * rstd, rstd


def norm_back(grad, xhat, rstd):
    return rstd * (
        grad
        - jnp.mean(grad, axis=1, keepdims=True)
        - xhat * jnp.mean(grad * xhat, axis=1, keepdims=True)
    )


def out_rows(rb, xw, att_ref, wo, ao, bo, gb, aff, xhat_ref, rstd_ref, act_ref, lowo_ref, lowf_ref):
    rows = pl.ds(pl.multiple_of(rb * QB, QB), QB)
    att = att_ref[rows, :]
    low = nt(att, ao[...]).astype(BF)
    lowo_ref[rows, :] = low
    branch = nn(att, wo[...].reshape(D, D)) + nn(low, bo[...])
    xhat, rstd = norm_stats(xw[rows, :].astype(F32) + branch)
    xhat_ref[rows, :] = xhat
    rstd_ref[rows, :] = jnp.broadcast_to(rstd, (QB, 128))
    act = (xhat * gb[0:1, :] + gb[1:2, :]).astype(BF)
    act_ref[rows, :] = act
    lowf_ref[rows, :] = nt(act, aff[...]).astype(BF)


def ffn_in_tile(n, rb, size, act_ref, lowf_ref, wi, wd, bg, bu, adn, big, lowd_ref, total_ref):
    start = pl.multiple_of(rb * size, size)
    rows = pl.ds(start, size)
    act = act_ref[rows, :]
    low = lowf_ref[rows, :]
    gate = nn(act, wi[n, 0].reshape(D, D)) + nn(low, bg[n])
    up = nn(act, wi[n, 1].reshape(D, D)) + nn(low, bu[n])
    inner = (gate * (1.0 / (1.0 + jnp.exp(-gate))) * up).astype(BF)
    blocks = size // QB
    here = n * 4 + rb * blocks
    big[pl.ds(here, blocks)] = gate.astype(BF).reshape(blocks, QB, D)
    big[pl.ds(here + 16, blocks)] = up.astype(BF).reshape(blocks, QB, D)
    lowd_ref[rows, 0:16] += nt(inner, adn[n])
    total_ref[rows, :] += nn(inner, wd[pl.ds(n * 8, 8)].reshape(D, D))


def ffn_out_rows(
    rb, flip, lowd_ref, bdn, xhat_ref, gb, cot, dtwo_ref, db2_ref, dlow_ref, mixed_ref, gbdn_ref
):
    start = pl.multiple_of(rb * QB, QB)
    rows = pl.ds(start, QB)
    low = lowd_ref[rows, 0:16].astype(BF)
    total = nn(low, bdn[...]) + dtwo_ref[rows, :]
    r = xhat_ref[rows, :] * gb[0:1, :] + gb[1:2, :] + total
    xhat, rstd = norm_stats(r)
    mixed_ref[pl.ds(block_at(flip, rb), QB), :] = (xhat * gb[2:3, :] + gb[3:4, :]).astype(BF)
    dtwo = norm_back(cot[rows, :].astype(F32) * gb[2:3, :], xhat, rstd)
    dtwo_ref[rows, :] = dtwo
    db2 = dtwo.astype(BF)
    db2_ref[rows, :] = db2
    dlow_ref[rows, :] = nt(db2, bdn[...]).astype(BF)
    gbdn_ref[...] += tn(low, db2)


def ffn_back_tile(
    n, start, size, db2_ref, dlow_ref, wd, wi, adn, bg, bu, big, lowf_ref, acc, dlf_ref, gadn_ref, gbf_ref
):
    rows = pl.ds(start, size)
    db2 = db2_ref[rows, :]
    dlow = dlow_ref[rows, :]
    dinner = nt(db2, wd[pl.ds(n * 8, 8)].reshape(D, D)) + nn(dlow, adn[n])
    blocks = size // QB
    here = n * 4 + lax.div(start, QB)
    gate = big[pl.ds(here, blocks)].reshape(size, D).astype(F32)
    up = big[pl.ds(here + 16, blocks)].reshape(size, D).astype(F32)
    sig = 1.0 / (1.0 + jnp.exp(-gate))
    silu = gate * sig
    inner = (silu * up).astype(BF)
    dg = (dinner * up * (sig + silu * (1.0 - sig))).astype(BF)
    du = (dinner * silu).astype(BF)
    acc[...] += nt(dg, wi[n, 0].reshape(D, D)) + nt(du, wi[n, 1].reshape(D, D))
    dlf_ref[...] += nt(dg, bg[n]) + nt(du, bu[n])
    gadn_ref[n] += tn(dlow, inner)
    low = lowf_ref[rows, :]
    gbf_ref[n] += jnp.where(iota((32, 1), 0) < 16, tn(low, dg), tn(low, du))


def hidden_back_rows(
    rb, off, acc, dlf_ref, aff, act_ref, dtwo_ref, xhat_ref, rstd_ref, gb, bo, ao, lowo_ref, att_ref,
    wo, linv_ref, h2, mf_ref, do_ref, hf_ref, gaff_ref, gbo_ref, gao_ref,
):
    start = pl.multiple_of(rb * QB, QB)
    rows = pl.ds(start, QB)
    local = pl.ds(pl.multiple_of(start - off, QB), QB)
    dlf = dlf_ref[local, :].astype(BF)
    dhid = dtwo_ref[rows, :] + acc[local, :] + nn(dlf, aff[...])
    gaff_ref[...] += tn(dlf, act_ref[rows, :])
    done = norm_back(dhid * gb[0:1, :], xhat_ref[rows, :], rstd_ref[rows, 0:1])
    dtwo_ref[rows, :] = done
    dbr = done.astype(BF)
    dlo = nt(dbr, bo[...]).astype(BF)
    att = att_ref[rows, :]
    gbo_ref[...] += tn(lowo_ref[rows, :], dbr)
    gao_ref[...] += tn(dlo, att)
    datt = (nt(dbr, wo[...].reshape(D, D)) + nn(dlo, ao[...])).astype(BF)
    do = (datt.astype(F32) * linv_ref[rows, :]).astype(BF)
    do_ref[rows, :] = do
    value = nn(do * att, h2[...]) + mf_ref[rows, :]
    lane = iota((1, 128), 1)
    role = jnp.where(lane < 40, lax.rem(lane + 2, 3), lax.rem(lane, 2))
    high = value.astype(BF)
    rest = value - high.astype(F32)
    mid = rest.astype(BF)
    last = (rest - mid.astype(F32)).astype(BF)
    hf_ref[rows, :] = jnp.where(role == 0, high, jnp.where(role == 1, mid, last))


def kf_kernel(
    x_hbm, xh_hbm, cot_hbm, seg_ref, freq_ref, aqkv, bqkv, ao, bo, aff, bff, adn, bdn, gb, tag,
    wq_hbm, wo_hbm, wi_hbm, wd_hbm,
    q_hbm, k_hbm, v_hbm, p_hbm, mixed_ref, do_ref, hf_ref, lowq_hbm, done_hbm, cos_hbm, sin_hbm, fq_hbm, fk_hbm,
    ge_ref,
    gao_ref, gaff_ref, gadn_ref, gbo_ref, gbdn_ref, gbf_ref,
    wq, wo, wi, wd, big, xw, att, linv, xhat, dtwo, act, db2, cos, sin, fq, fk, bias, mf,
    lowq, lowo, lowf, dlow, acc, dlf, bblk, bg, bu, h2, wsem, xsem, osem, psem,
):
    flip = lax.axis_index("seq")
    cot = db2
    rstd = cos
    lowd = sin
    loads = []
    for i in range(4):
        loads.append(
            pltpu.make_async_copy(
                x_hbm.at[pl.ds(block_at(flip, i), QB)], xw.at[pl.ds(i * QB, QB)], xsem.at[i]
            )
        )
        loads.append(
            pltpu.make_async_copy(
                cot_hbm.at[pl.ds(block_at(flip, i), QB)], cot.at[pl.ds(i * QB, QB)], xsem.at[4 + i]
            )
        )
    for i in range(2):
        at = pl.multiple_of(jnp.where(flip == 1, 1 - i, i) * QB, QB)
        loads.append(
            pltpu.make_async_copy(xh_hbm.at[pl.ds(at, QB)], xw.at[pl.ds(1024 + i * QB, QB)], xsem.at[8 + i])
        )
    weights = [
        pltpu.make_async_copy(a, b, wsem.at[i])
        for i, (a, b) in enumerate(((wq_hbm, wq), (wo_hbm, wo), (wi_hbm, wi), (wd_hbm, wd)))
    ]
    for copy in loads + weights:
        copy.start()
    fill_tables(flip, seg_ref, freq_ref, cos, sin, fq, fk, bias)
    rank = iota((48, 1), 0)
    for p in range(3):
        keep = (rank >= 16 * p) & (rank < 16 * p + 16)
        bblk[p] = jnp.where(keep, bqkv[...], jnp.zeros_like(bqkv[...]))
    rank = iota((32, 1), 0)
    for n in range(4):
        piece = bff[:, n * D : (n + 1) * D]
        bg[n] = jnp.where(rank < 16, piece, jnp.zeros_like(piece))
        bu[n] = jnp.where(rank >= 16, piece, jnp.zeros_like(piece))
    head = lax.div(iota((D, 128), 0), HEAD_DIM)
    spot = iota((D, 128), 1)
    h2[...] = jnp.where(lax.div(spot - 40, 2) == head, jnp.where(spot >= 40, -1.0, 0.0), 0.0).astype(BF)
    mf[...] = jnp.zeros_like(mf)
    dtwo[...] = jnp.zeros_like(dtwo)
    for g in (gao_ref, gaff_ref, gadn_ref, gbo_ref, gbdn_ref, gbf_ref):
        g[...] = jnp.zeros_like(g)
    for copy in loads:
        copy.wait()
    weights[0].wait()
    q_ref, k_ref, v_ref = (big.at[pl.ds(i * 6, 6)] for i in range(3))
    stage = big.at[pl.ds(18, 8)]

    def qkv_step(rb, _):
        qkv_rows(rb, xw, wq, aqkv, bblk, cos, sin, q_ref, k_ref, v_ref, lowq)
        return 0

    lax.fori_loop(0, 6, qkv_step, 0)
    saves = [
        pltpu.make_async_copy(a, b, osem.at[i])
        for i, (a, b) in enumerate(
            ((q_ref, q_hbm), (k_ref, k_hbm), (v_ref, v_hbm), (lowq, lowq_hbm), (cos, cos_hbm), (sin, sin_hbm), (fq, fq_hbm), (fk, fk_hbm))
        )
    ]
    for copy in saves:
        copy.start()
    for qb in range(4):

        def pair_step(pair, _, qb=qb):
            attend_pair(qb, pair, pair, q_ref, k_ref, v_ref, fq, fk, bias, att, linv, mf, p_hbm, stage, psem)
            return 0

        lax.fori_loop(0, 6, pair_step, 0)
        drain_pairs(qb, p_hbm, stage, psem)
    for copy in saves:
        copy.wait()
    lowd[...] = jnp.zeros_like(lowd)
    weights[1].wait()

    def out_step(rb, _):
        out_rows(rb, xw, att, wo, ao, bo, gb, aff, xhat, rstd, act, lowo, lowf)
        return 0

    lax.fori_loop(0, 4, out_step, 0)
    weights[2].wait()
    weights[3].wait()

    def in_step(i, _):
        ffn_in_tile(lax.div(i, 2), lax.rem(i, 2), 512, act, lowf, wi, wd, bg, bu, adn, big, lowd, dtwo)
        return 0

    lax.fori_loop(0, 8, in_step, 0)

    def down_step(rb, _):
        ffn_out_rows(rb, flip, lowd, bdn, xhat, gb, cot, dtwo, db2, dlow, mixed_ref, gbdn_ref)
        return 0

    lax.fori_loop(0, 4, down_step, 0)

    def back_step(half, _):
        off = pl.multiple_of(half * 512, 512)
        acc[...] = jnp.zeros_like(acc)
        dlf[...] = jnp.zeros_like(dlf)

        def tile(n, _):
            ffn_back_tile(
                n, off, 512, db2, dlow, wd, wi, adn, bg, bu, big, lowf, acc, dlf, gadn_ref, gbf_ref
            )
            return 0

        lax.fori_loop(0, 4, tile, 0)

        def rows(i, _):
            hidden_back_rows(
                half * 2 + i, off, acc, dlf, aff, act, dtwo, xhat, rstd, gb, bo, ao, lowo, att, wo, linv, h2, mf,
                do_ref, hf_ref, gaff_ref, gbo_ref, gao_ref,
            )
            return 0

        lax.fori_loop(0, 2, rows, 0)
        return 0

    lax.fori_loop(0, 2, back_step, 0)
    last = pltpu.make_async_copy(dtwo, done_hbm, osem.at[8])
    last.start()
    ge_ref[0:16] = gao_ref[...].astype(BF)
    ge_ref[16:48] = gaff_ref[...].astype(BF)
    ge_ref[48:64] = gbo_ref[...].astype(BF)
    ge_ref[64:80] = gbdn_ref[...].astype(BF)
    ge_ref[80:144] = gadn_ref[...].reshape(64, D).astype(BF)
    ge_ref[144:272] = gbf_ref[...].reshape(128, D).astype(BF)
    ge_ref[272:288] = tag[...]
    last.wait()


MESH = pl.DeviceIdType.MESH
NCHUNK = 8


class Gather:
    def __init__(self, sems):
        (self.zs, self.zr, self.xs, self.xr, self.ys, self.yr, self.ds, self.dr, self.es, self.er, self.cs, self.cr) = sems
        b = lax.axis_index("batch")
        self.s = lax.axis_index("seq")
        self.core = lax.rem(b, 2)
        self.x = lax.rem(lax.div(b, 2), 2)
        self.z = lax.div(b, 4)
        self.devx = (b + 2 - 4 * self.x, self.s)
        self.devy = (b, 1 - self.s)
        self.devc = (b + 1 - 2 * self.core, self.s)
        self.me = self.owner(self.z, 0, 0, 0)

    def owner(self, z, dx, dy, dc):
        x = 1 - self.x if dx else self.x
        y = 1 - self.s if dy else self.s
        c = 1 - self.core if dc else self.core
        return (z * 4 + x * 2 + c) * 2 + y

    def devz(self, z):
        return (z * 4 + self.x * 2 + self.core, self.s)

    def zof(self, d):
        return lax.rem(self.z + d, 4)

    def copy(self, c, j, half, dev, send, recv):
        v = self.view(c, j, half)
        return pltpu.make_async_remote_copy(v, v, send, recv, device_id=dev, device_id_type=MESH)

    def to_z(self, c, z):
        return self.copy(c, self.me, None, self.devz(z), self.zs.at[c, z], self.zr.at[c, self.z])

    def from_z(self, c, z):
        return self.copy(c, self.owner(z, 0, 0, 0), None, self.devz(z), self.zs.at[c, z], self.zr.at[c, z])

    def on_x(self, c, z, arriving):
        return self.copy(c, self.owner(z, arriving, 0, 0), None, self.devx, self.xs.at[c, z], self.xr.at[c, z])

    def on_y(self, c, z, arriving):
        return self.copy(c, self.owner(z, 0, arriving, 0), None, self.devy, self.ys.at[c, z], self.yr.at[c, z])

    def corner_x(self, c, z, arriving):
        return self.copy(c, self.owner(z, arriving, 1, 0), 0, self.devx, self.ds.at[c, z], self.dr.at[c, z])

    def corner_y(self, c, z, arriving):
        return self.copy(c, self.owner(z, 1, arriving, 0), 1, self.devy, self.es.at[c, z], self.er.at[c, z])

    def on_core(self, c, kind, z, arriving):
        j = self.owner(z, kind & 1, kind >> 1, arriving)
        k = kind * 4 + z
        return self.copy(c, j, None, self.devc, self.cs.at[c, k], self.cr.at[c, k])

    def barrier(self):
        bar = pltpu.get_barrier_semaphore()
        for dev in (self.devx, self.devy, self.devc, self.devz(self.zof(1)), self.devz(self.zof(2)), self.devz(self.zof(3))):
            pl.semaphore_signal(bar, inc=1, device_id=dev, device_id_type=MESH)
        pl.semaphore_wait(bar, 6)

    def stage_own(self, c):
        self.on_x(c, self.z, 0).start()
        self.on_y(c, self.z, 0).start()
        for d in (1, 3, 2):
            self.to_z(c, self.zof(d)).start()
        self.on_core(c, 0, self.z, 0).start()

    def stage_z(self, c):
        for d in (1, 3, 2):
            z = self.zof(d)
            self.from_z(c, z).wait_recv()
            self.on_x(c, z, 0).start()
            self.on_y(c, z, 0).start()
            self.on_core(c, 0, z, 0).start()

    def stage_xy(self, c):
        for d in range(4):
            z = self.zof(d)
            self.on_x(c, z, 1).wait_recv()
            self.corner_y(c, z, 0).start()
            self.on_core(c, 1, z, 0).start()
            self.on_y(c, z, 1).wait_recv()
            self.corner_x(c, z, 0).start()
            self.on_core(c, 2, z, 0).start()

    def stage_corner(self, c):
        for d in range(4):
            z = self.zof(d)
            self.corner_x(c, z, 1).wait_recv()
            self.corner_y(c, z, 1).wait_recv()
            self.on_core(c, 3, z, 0).start()

    def stage_core(self, c):
        for kind in range(4):
            for z in range(4):
                self.on_core(c, kind, z, 1).wait_recv()

    def finish(self, c):
        for d in (1, 2, 3):
            self.to_z(c, self.zof(d)).wait_send()
        for z in range(4):
            self.on_x(c, z, 0).wait_send()
            self.on_y(c, z, 0).wait_send()
            self.corner_x(c, z, 0).wait_send()
            self.corner_y(c, z, 0).wait_send()
            for kind in range(4):
                self.on_core(c, kind, z, 0).wait_send()


def k3_kernel(
    x_hbm, q_hbm, k_hbm, v_hbm, p_hbm, do_hbm, hf_hbm, ge, lowq_hbm, done_hbm, cos_hbm, sin_hbm,
    fq_hbm, fk_hbm, aqkv, bqkv, wq_hbm,
    dx_ref, sum_e_ref, sum_l_ref,
    ga_ref, gbq_ref, dproj, eg, lg, ge_in, gl_out, gl_in,
    xw, q, k, v, do, hf, lowq, done, cos, sin, fq, fk, wq, stage, dq, dkT, dvT, bias, sem, psem, hs, hr, *sems,
):
    flip = lax.axis_index("seq")
    g = Gather(sems)
    table = (
        (q_hbm, q), (k_hbm, k), (v_hbm, v), (do_hbm, do.at[pl.ds(0, 1024)]), (hf_hbm, hf.at[pl.ds(0, 1024)]),
        (lowq_hbm, lowq), (done_hbm, done), (cos_hbm, cos), (sin_hbm, sin), (fq_hbm, fq), (fk_hbm, fk), (wq_hbm, wq),
    )
    loads = [pltpu.make_async_copy(a, b, sem.at[i]) for i, (a, b) in enumerate(table)]
    for i in range(4):
        loads.append(
            pltpu.make_async_copy(
                x_hbm.at[pl.ds(block_at(flip, i), QB)], xw.at[pl.ds(i * QB, QB)], sem.at[12 + i]
            )
        )
    for copy in loads:
        copy.start()

    def early(c, j, half):
        lanes = slice(None) if half is None else pl.ds(half * 384, 384)
        return eg.at[j, :, lanes]

    def late(c, j, half):
        lanes = slice(None) if half is None else pl.ds(half * 384, 384)
        return lg.at[j, :, lanes]

    g.barrier()
    halo = []
    for i, (src, dst) in enumerate(
        (
            (do_hbm.at[pl.ds(768, QB)], do.at[pl.ds(1024, QB)]),
            (do_hbm.at[pl.ds(512, QB)], do.at[pl.ds(1280, QB)]),
            (hf_hbm.at[pl.ds(768, QB)], hf.at[pl.ds(1024, QB)]),
            (hf_hbm.at[pl.ds(512, QB)], hf.at[pl.ds(1280, QB)]),
            (ge.at[pl.ds(pl.multiple_of((1 - flip) * 144, 16), 144)], ge_in),
            (gl_out.at[pl.ds(pl.multiple_of((1 - flip) * 48, 16), 48)], gl_in),
        )
    ):
        halo.append(
            pltpu.make_async_remote_copy(
                src, dst, hs.at[i], hr.at[i], device_id=g.devy, device_id_type=MESH
            )
        )
    for copy in (halo[4], halo[0], halo[1], halo[2], halo[3]):
        copy.start()
    dkT[...] = jnp.zeros_like(dkT)
    dvT[...] = jnp.zeros_like(dvT)
    ga_ref[...] = jnp.zeros_like(ga_ref)
    gbq_ref[...] = jnp.zeros_like(gbq_ref)
    gap = iota((QB, QB), 0) - iota((QB, QB), 1)
    gap = jnp.where(flip == 1, -gap, gap)
    bias[...] = jnp.where(gap <= 0, 0.0, NEG)
    half = iota((1, 128), 1) >= HEAD_DIM
    for copy in loads[:5]:
        copy.wait()

    def picks(pair, first, width):
        head = 2 * pair + lax.div(iota((128, 256), 1), 128)
        row = iota((128, 256), 0) - first - width * head
        return jnp.where((row >= 0) & (row < width), 1.0, 0.0).astype(BF)

    for qb in range(4):
        k0, n, _, _ = PLAN[qb]
        own = min(4 - k0, n)
        rows = pl.ds(qb * QB, QB)
        krows = pl.ds(k0 * QB, n * QB)

        def fetch(pair, s, qb=qb, n=n):
            return pltpu.make_async_copy(p_hbm.at[qb, pair], stage.at[s], psem.at[s])

        fetch(0, 0).start()

        def pair_step(pair, _, k0=k0, n=n, own=own, rows=rows, krows=krows, fetch=fetch):
            slot = lax.rem(pair, 2)
            fetch(pair, slot).wait()

            @pl.when(pair < 5)
            def _():
                fetch(pair + 1, 1 - slot).start()

            lanes = pl.ds(pl.multiple_of(pair * 128, 128), 128)
            do2 = do[rows, lanes]
            ndl = nn(hf[rows, :], picks(pair, 40, 2))
            k2 = k[krows, lanes]
            v2 = v[krows, lanes]
            qT = q[rows, lanes].T
            doT = do2.T
            dqs = []
            for h in range(2):
                mine = half if h == 1 else jnp.logical_not(half)
                p = stage[slot, 2 * h, :, 0 : min(D, n * QB)]
                if n > 3:
                    p = jnp.concatenate([p, stage[slot, 2 * h + 1, :, 0 : n * QB - D]], axis=1)
                dp = nt(jnp.where(mine, do2, jnp.zeros_like(do2)), v2)
                d = ndl[:, h * 128 : (h + 1) * 128]
                ds = (p.astype(F32) * (dp + jnp.concatenate([d] * (2 * n), axis=1))).astype(BF)
                dqs.append(nn(ds, k2))
                hr = pl.ds(pl.multiple_of(pair * 128 + h * 64, 64), 64)
                kc = pl.ds(k0 * QB, own * QB)
                dkT[hr, kc] += nn(qT[h * 64 : (h + 1) * 64], ds[:, 0 : own * QB])
                dvT[hr, kc] += nn(doT[h * 64 : (h + 1) * 64], p[:, 0 : own * QB])
            dq[rows, lanes] = jnp.where(half, dqs[1], dqs[0]) * 0.125
            return 0

        lax.fori_loop(0, 6, pair_step, 0)
        g.view = early
        if qb == 0:
            halo[4].wait_recv()
            mine = ge[pl.ds(pl.multiple_of(flip * 144, 16), 144)]
            total = mine.astype(F32) + ge_in[...].astype(F32)
            row = iota((144, 1), 0)
            eg[g.me] = jnp.where((row >= 128) & (flip == 1), mine.astype(F32), total).astype(BF)
            g.stage_own(0)
        elif qb == 1:
            g.stage_z(0)
        elif qb == 2:
            g.stage_xy(0)
        else:
            g.stage_corner(0)

    for copy in loads[5:]:
        copy.wait()
    for copy in halo[:4]:
        copy.wait_recv()
    for i, (k0, n) in enumerate(HALO_PLAN):
        rows = pl.ds(1024 + i * QB, QB)
        krows = pl.ds(k0 * QB, n * QB)

        def halo_step(pair, _, k0=k0, n=n, rows=rows, krows=krows):
            lanes = pl.ds(pl.multiple_of(pair * 128, 128), 128)
            do2 = do[rows, lanes]
            q2 = q[rows, lanes]
            feats = hf[rows, :]
            ndl = nn(feats, picks(pair, 40, 2))
            nm = nn(feats, picks(pair, 4, 3))
            keys = jnp.concatenate([k[krows, lanes], fk[krows, :]], axis=1)
            v2 = v[krows, lanes]
            qT = q2.T
            doT = do2.T
            for h in range(2):
                mine = half if h == 1 else jnp.logical_not(half)
                s = nt(jnp.concatenate([jnp.where(mine, q2, jnp.zeros_like(q2)), fq[rows, :]], axis=1), keys)
                parts = [s[:, t * QB : (t + 1) * QB] for t in range(n)]
                parts[0] = parts[0] + bias[...]
                s = jnp.concatenate(parts, axis=1)
                m = nm[:, h * 128 : (h + 1) * 128]
                p = jnp.exp(s + jnp.concatenate([m] * (2 * n), axis=1))
                dp = nt(jnp.where(mine, do2, jnp.zeros_like(do2)), v2)
                d = ndl[:, h * 128 : (h + 1) * 128]
                ds = (p * (dp + jnp.concatenate([d] * (2 * n), axis=1))).astype(BF)
                hr = pl.ds(pl.multiple_of(pair * 128 + h * 64, 64), 64)
                kc = pl.ds(k0 * QB, n * QB)
                dkT[hr, kc] += nn(qT[h * 64 : (h + 1) * 64], ds)
                dvT[hr, kc] += nn(doT[h * 64 : (h + 1) * 64], p.astype(BF))
            return 0

        lax.fori_loop(0, 6, halo_step, 0)

    g.stage_core(0)

    def weights_of(b, e):
        return eg[2 * b + 1, 128 + e : 129 + e, :].astype(F32)

    def sum_step(i, _):
        y = lax.div(i, 9)
        r = pl.multiple_of(lax.rem(i, 9) * 16, 16)
        totals = [jnp.zeros((16, D), F32) for _ in range(ADAPTERS)]
        for b in range(16):
            part = eg[2 * b + y, pl.ds(r, 16), :].astype(F32)
            for e in range(ADAPTERS):
                totals[e] += part * weights_of(b, e)
        for e in range(ADAPTERS):
            sum_e_ref[e, pl.ds(pl.multiple_of(i * 16, 16), 16), :] = totals[e]
        return 0

    lane = lax.div(iota((1, 48), 1), 16)
    rank = lax.div(iota((48, 1), 0), 16)

    def proj_step(rb, _):
        start = pl.multiple_of(rb * QB, QB)
        rows = pl.ds(start, QB)
        cosine = cos[rows, :]
        sine = -sin[rows, :]
        low = lowq[rows, :]
        dlow = jnp.zeros((QB, 48), F32)
        for p in range(3):
            if p == 0:
                d = rope(dq[rows, :], cosine, sine)
            else:
                src = (dkT, dvT)[p - 1]
                d = jnp.concatenate([src[pl.ds(c * 128, 128), rows].T for c in range(6)], axis=1)
                if p == 1:
                    d = rope(d, cosine, sine)
            d = d.astype(BF)
            dproj[p, rows, :] = d
            dlow += jnp.where(lane == p, nt(d, bqkv[...]), 0.0)
            gbq_ref[...] += jnp.where(rank == p, tn(low, d), 0.0)
        dlow = dlow.astype(BF)
        lowq[rows, :] = dlow
        ga_ref[...] += tn(dlow, xw[rows, :])
        return 0

    lax.fori_loop(0, 4, proj_step, 0)
    gl_out[0:48] = ga_ref[...].astype(BF)
    gl_out[48:96] = gbq_ref[...].astype(BF)
    halo[5].start()
    g.view = late

    def dx_rows(rb):
        rows = pl.ds(rb * QB, QB)
        total = done[rows, :] + nn(lowq[rows, :], aqkv[...])
        for p in range(3):
            total += nt(dproj[p, rows, :], wq[p].reshape(D, D))
        dx_ref[pl.ds(block_at(flip, rb), QB), :] = total.astype(BF)

    lax.fori_loop(0, 18, sum_step, 0)
    halo[5].wait_recv()
    lg[g.me] = (
        gl_out[pl.ds(pl.multiple_of(flip * 48, 16), 48)].astype(F32) + gl_in[...].astype(F32)
    ).astype(BF)
    g.stage_own(1)
    dx_rows(0)
    g.stage_z(1)
    dx_rows(1)
    g.stage_xy(1)
    dx_rows(2)
    g.stage_corner(1)
    dx_rows(3)
    g.stage_core(1)

    def late_step(i, _):
        y = lax.div(i, 3)
        r = pl.multiple_of(lax.rem(i, 3) * 16, 16)
        totals = [jnp.zeros((16, D), F32) for _ in range(ADAPTERS)]
        for b in range(16):
            part = lg[2 * b + y, pl.ds(r, 16), :].astype(F32)
            for e in range(ADAPTERS):
                totals[e] += part * weights_of(b, e)
        for e in range(ADAPTERS):
            sum_l_ref[e, pl.ds(pl.multiple_of(i * 16, 16), 16), :] = totals[e]
        return 0

    lax.fori_loop(0, 6, late_step, 0)
    for copy in halo:
        copy.wait_send()
    for c, view in enumerate((early, late)):
        g.view = view
        g.finish(c)


def gather_kernel(q, o, i, d, wq, wo, wi, wd, *rest):
    g = Gather(rest[:12])

    def view(c, j, half):
        lanes = slice(None) if half is None else pl.ds(half * 384, 384)
        if c == 0:
            return wq.at[:, j, :, lanes]
        if c == 1:
            return wo.at[j, :, lanes]
        if c < 6:
            return wi.at[c - 2, :, j, :, lanes]
        return wd.at[j, pl.ds((c - 6) * 48, 48), lanes]

    g.view = view
    lsem = rest[12]
    local = [
        pltpu.make_async_copy(q, wq.at[:, g.me], lsem.at[0]),
        pltpu.make_async_copy(o, wo.at[g.me], lsem.at[1]),
        pltpu.make_async_copy(d, wd.at[g.me], lsem.at[2]),
    ]
    for n in range(4):
        local.append(pltpu.make_async_copy(i.at[:, :, pl.ds(D * n, D)], wi.at[n, :, g.me], lsem.at[3 + n]))
    for copy in local:
        copy.start()
    g.barrier()
    for copy in local:
        copy.wait()
    for t in range(NCHUNK + 4):
        for lag, stage in enumerate((g.stage_own, g.stage_z, g.stage_xy, g.stage_corner, g.stage_core)):
            if 0 <= t - lag < NCHUNK:
                stage(t - lag)
    for c in range(NCHUNK):
        g.finish(c)


def sds(shape, dtype):
    return jax.ShapeDtypeStruct(shape, dtype)


ANY = functools.partial(pl.BlockSpec, memory_space=pl.ANY)
INV = functools.partial(pl.BlockSpec, memory_space=pltpu.VMEM)


def gather_call(q, o, i, d):
    return pl.pallas_call(
        gather_kernel,
        out_shape=[sds(s, BF) for s in ((3, 32, 24, D), (32, 24, D), (4, 2, 32, 24, D), (32, 96, D))],
        in_specs=[ANY()] * 4,
        out_specs=[ANY()] * 4,
        scratch_shapes=[pltpu.SemaphoreType.DMA((NCHUNK, 4))] * 10
        + [pltpu.SemaphoreType.DMA((NCHUNK, 16))] * 2
        + [pltpu.SemaphoreType.DMA((7,))],
        compiler_params=pltpu.CompilerParams(collective_id=1, has_side_effects=True),
    )(q, o, i, d)


def kf_call(*args):
    outs = [
        (ANY, (6, QB, D), BF), (ANY, (6, QB, D), BF), (ANY, (6, QB, D), BF), (ANY, (4, 6, 4, QB, D), BF),
        (INV, (1024, D), BF), (INV, (1024, D), BF), (INV, (1024, 128), BF),
        (ANY, (1536, 48), BF), (ANY, (1024, D), F32), (ANY, (1536, 128), F32), (ANY, (1536, 128), F32),
        (ANY, (1536, 128), BF), (ANY, (1536, 128), BF),
        (INV, (288, D), BF),
    ]
    V = pltpu.VMEM
    scratch = [
        V((16, D), F32), V((32, D), F32), V((4, 16, D), F32), V((16, D), F32), V((16, D), F32), V((4, 32, D), F32),
        V((3, 32, 24, D), BF), V((32, 24, D), BF), V((4, 2, 32, 24, D), BF), V((32, 96, D), BF),
        V((32, QB, D), BF), V((1536, D), BF), V((1024, D), BF), V((1024, D), F32),
        V((1024, D), F32), V((1024, D), F32), V((1024, D), BF), V((1024, D), BF),
        V((1536, 128), F32), V((1536, 128), F32), V((1536, 128), BF), V((1536, 128), BF), V((2, QB, QB), F32),
        V((1024, 128), F32), V((1536, 48), BF), V((1024, 16), BF), V((1024, 32), BF),
        V((1024, 16), BF), V((512, D), F32), V((512, 32), F32), V((3, 48, D), BF),
        V((4, 32, D), BF), V((4, 32, D), BF), V((D, 128), BF),
        pltpu.SemaphoreType.DMA((4,)), pltpu.SemaphoreType.DMA((10,)), pltpu.SemaphoreType.DMA((9,)),
        pltpu.SemaphoreType.DMA((2,)),
    ]
    return pl.pallas_call(
        kf_kernel,
        out_shape=[sds(s, t) for _, s, t in outs],
        in_specs=[ANY()] * 3 + [INV()] * 12 + [ANY()] * 4,
        out_specs=[m() for m, _, _ in outs],
        scratch_shapes=scratch,
        compiler_params=pltpu.CompilerParams(vmem_limit_bytes=VMEM_LIMIT),
    )(*args)


def k3_call(*args):
    V = pltpu.VMEM
    scratch = [
        V((48, D), F32), V((48, D), F32), V((3, 1024, D), BF), V((32, 144, D), BF), V((32, 48, D), BF),
        V((144, D), BF), V((96, D), BF), V((48, D), BF),
        V((1024, D), BF), V((1536, D), BF), V((1536, D), BF), V((1536, D), BF), V((1536, D), BF), V((1536, 128), BF),
        V((1536, 48), BF), V((1024, D), F32), V((1536, 128), F32), V((1536, 128), F32), V((1536, 128), BF),
        V((1536, 128), BF), V((3, 32, 24, D), BF), V((2, 4, QB, D), BF), V((1024, D), F32), V((D, 1024), F32),
        V((D, 1024), F32), V((QB, QB), F32), pltpu.SemaphoreType.DMA((16,)), pltpu.SemaphoreType.DMA((2,)),
        pltpu.SemaphoreType.DMA((6,)), pltpu.SemaphoreType.DMA((6,)),
    ]
    scratch += [pltpu.SemaphoreType.DMA((2, 4))] * 10 + [pltpu.SemaphoreType.DMA((2, 16))] * 2
    return pl.pallas_call(
        k3_kernel,
        out_shape=[sds((1024, D), BF), sds((4, 288, D), F32), sds((4, 96, D), F32)],
        in_specs=[ANY()] * 7 + [INV()] + [ANY()] * 6 + [INV()] * 2 + [ANY()],
        out_specs=[INV()] * 3,
        scratch_shapes=scratch,
        compiler_params=pltpu.CompilerParams(
            vmem_limit_bytes=VMEM_LIMIT, collective_id=2, has_side_effects=True
        ),
    )(*args)


def fast(
    tokens, cotangent, segments, adapter_index, qkv_weight, out_weight, ffn_in_weight, ffn_out_weight,
    norm_gain, norm_bias, adapt_in, adapt_down, adapt_out, adapt_ffn,
):
    side = lax.axis_index("seq")
    x = tokens[0]
    swap = [(0, 1), (1, 0)]
    edge = lax.dynamic_slice_in_dim(x, jnp.where(side == 0, 512, 0), 512, 0)
    halo = lax.ppermute(edge, "seq", swap)
    e = adapter_index[0, 0]
    pick = lambda table: lax.dynamic_index_in_dim(table[0], e, 0, False)
    a_in = pick(adapt_in).transpose(0, 2, 1)
    aqkv, ao, aff = a_in[0:3].reshape(48, D), a_in[3], a_in[4:6].reshape(32, D)
    adn = pick(adapt_down).T.reshape(16, 4, D).transpose(1, 0, 2)
    b_out = pick(adapt_out)
    bqkv, bo, bdn = b_out[0:3].reshape(48, D), b_out[3], b_out[4]
    bff = pick(adapt_ffn).reshape(32, FF)
    gb = jnp.stack([norm_gain[0, 0], norm_bias[0, 0], norm_gain[0, 1], norm_bias[0, 1]])
    freq = jnp.power(ROPE_BASE, -2.0 * jnp.arange(HEAD_DIM // 2, dtype=F32) / HEAD_DIM)
    freq = jnp.tile(freq, 4)[None]
    wq, wo, wi, wd = gather_call(qkv_weight[0], out_weight[0], ffn_in_weight[0], ffn_out_weight[0])
    tag = jnp.where(jnp.arange(16)[:, None] == e, 1.0, jnp.zeros((1, D))).astype(BF)
    q, k, v, p, mixed, do, hf, lowq, done, cos, sin, fq, fk, ge = kf_call(
        x, halo, cotangent[0], segments, freq, aqkv, bqkv, ao, bo, aff, bff, adn, bdn, gb, tag, wq, wo, wi, wd
    )
    q, k, v = (a.reshape(1536, D) for a in (q, k, v))
    dx, se, sl = k3_call(x, q, k, v, p, do, hf, ge, lowq, done, cos, sin, fq, fk, aqkv, bqkv, wq)
    g_in = jnp.concatenate([sl[:, :48], se[:, :48]], axis=1).reshape(4, 6, 16, D)
    g_dn = se[:, 80:144].reshape(4, 4, 16, D).transpose(0, 2, 1, 3).reshape(4, 16, FF)
    g_out = jnp.concatenate([sl[:, 48:], se[:, 48:80]], axis=1).reshape(4, 5, 16, D)
    g_ff = se[:, 144:272].reshape(4, 4, 2, 16, D).transpose(0, 2, 3, 1, 4).reshape(4, 2, 16, FF)
    return (
        mixed[None], dx[None], g_in.transpose(0, 1, 3, 2)[None], g_dn.transpose(0, 2, 1)[None], g_out[None], g_ff[None],
    )


def solution(mesh):
    here = fast if dict(mesh.shape) == {"batch": 16, "seq": 2} else shards
    return jax.shard_map(
        here,
        mesh=mesh,
        in_specs=(
            P("batch", "seq", None),
            P("batch", "seq", None),
            P("batch", None),
            P("batch", None),
            P(None, None, ("batch", "seq"), None),
            P(None, ("batch", "seq"), None),
            P(None, None, ("batch", "seq"), None),
            P(None, ("batch", "seq"), None),
            P(),
            P(),
            P(),
            P(),
            P(),
            P(),
        ),
        out_specs=(P("batch", "seq", None), P("batch", "seq", None), P(), P(), P(), P()),
        check_vma=False,
    )
```

```python
import functools
import math

import jax
import jax.numpy as jnp
from jax import lax
from jax.experimental import pallas as pl
from jax.experimental.pallas import tpu as pltpu
from jax.sharding import PartitionSpec as P

HEADS = 12
HEAD_DIM = 64
ADAPTERS = 4
LAYERS = 1
HALF = 512
D = HEADS * HEAD_DIM
FF = 4 * D


EPSILON = 1e-06
ROPE_BASE = 1000.0
PRECISE = lax.Precision.HIGHEST


def shifted(array, axis, by):
    count = lax.axis_size(axis)
    pairs = [(i, i + by) for i in range(count) if 0 <= i + by < count]
    return lax.ppermute(array, axis, pairs)


def doc_positions(segment_ids):
    position_ids = jnp.arange(segment_ids.shape[-1], dtype=jnp.int32)
    starts_here = jnp.concatenate(
        [
            jnp.ones(segment_ids.shape[:-1] + (1,), dtype=jnp.bool_),
            segment_ids[..., 1:] != segment_ids[..., :-1],
        ],
        axis=-1,
    )
    doc_start = lax.cummax(jnp.where(starts_here, position_ids, 0), axis=segment_ids.ndim - 1)
    return (position_ids - doc_start).astype(jnp.float32)


def rope_tables(segment_ids):
    positions = doc_positions(segment_ids)
    frequency = jnp.power(ROPE_BASE, -2.0 * jnp.arange(HEAD_DIM // 2, dtype=jnp.float32) / HEAD_DIM)
    angles = positions[..., None] * frequency
    return (jnp.cos(angles), jnp.sin(angles))


def rotate(vectors, cosine_table, sine_table):
    half_dim = vectors.shape[-1] // 2
    first_half = vectors[..., :half_dim]
    second_half = vectors[..., half_dim:]
    cosine_rows = cosine_table[..., None, :]
    sine_rows = sine_table[..., None, :]
    return jnp.concatenate(
        [
            first_half * cosine_rows - second_half * sine_rows,
            second_half * cosine_rows + first_half * sine_rows,
        ],
        axis=-1,
    )


def norm_apply(residual, gain_row, bias_row):
    centre = residual - jnp.mean(residual, axis=-1, keepdims=True)
    spread = jnp.mean(centre * centre, axis=-1, keepdims=True)
    return centre * lax.rsqrt(spread + EPSILON) * gain_row + bias_row


def split_heads(merged, group_count):
    seqs_here, row_count, _ = merged.shape
    return merged.reshape(seqs_here, row_count, group_count, -1, HEAD_DIM).transpose(2, 0, 1, 3, 4)


def join_heads(grouped):
    group_count, seqs_here, row_count, heads_group, head_size = grouped.shape
    return grouped.transpose(1, 2, 0, 3, 4).reshape(
        seqs_here, row_count, group_count * heads_group * head_size
    )


def shards(
    tokens,
    cotangent,
    segments,
    adapter_index,
    qkv_weight,
    out_weight,
    ffn_in_weight,
    ffn_out_weight,
    norm_gain,
    norm_bias,
    adapt_in,
    adapt_down,
    adapt_out,
    adapt_ffn,
):
    seqs_here, tok_rows, model_width = tokens.shape
    heads_group = math.gcd(HEADS, 4)
    group_count = HEADS // heads_group
    score_scale = 1.0 / math.sqrt(HEAD_DIM)
    seq_count = lax.axis_size("seq")
    row_base = lax.axis_index("seq") * tok_rows
    shift_plan = []
    for distance in range(1, min(seq_count, HALF // tok_rows + 2)):
        row_count = min(tok_rows, HALF - (distance - 1) * tok_rows)
        if row_count > 0:
            shift_plan.append((distance, row_count))
            shift_plan.append((-distance, row_count))
    left_total = sum((plan_item[1] for plan_item in shift_plan if plan_item[0] > 0))
    key_rows = 2 * left_total + tok_rows
    key_places = {}
    passed_rows = 0
    for distance, row_count in shift_plan:
        if distance > 0:
            key_places[distance] = left_total - passed_rows - row_count
            key_places[-distance] = left_total + tok_rows + passed_rows
            passed_rows += row_count
    cosine_all, sine_all = rope_tables(segments)
    cosine_here = lax.dynamic_slice_in_dim(cosine_all, row_base, tok_rows, 1)
    sine_here = lax.dynamic_slice_in_dim(sine_all, row_base, tok_rows, 1)
    padded_ids = jnp.pad(segments, ((0, 0), (HALF, HALF)), constant_values=-1)
    key_ids = lax.dynamic_slice_in_dim(padded_ids, row_base - left_total + HALF, key_rows, 1)
    query_ids = lax.dynamic_slice_in_dim(segments, row_base, tok_rows, 1)
    offsets = (
        jnp.arange(tok_rows, dtype=jnp.int32)[:, None]
        - jnp.arange(key_rows, dtype=jnp.int32)[None, :]
        + left_total
    )
    visible = (query_ids[:, :, None] == key_ids[:, None, :]) & (jnp.abs(offsets) <= HALF)[None]
    slot_hits = adapter_index[:, 0][:, None] == jnp.arange(ADAPTERS, dtype=jnp.int32)[None, :]
    slot_low = slot_hits.astype(jnp.bfloat16)
    slot_full = slot_hits.astype(jnp.float32)

    def select_adapter(table):
        return jnp.einsum(
            "se,le...->ls...", slot_low, table, preferred_element_type=jnp.float32
        ).astype(jnp.bfloat16)

    def spread_slots(per_sequence):
        return jnp.einsum("se,s...->e...", slot_full, per_sequence, precision=PRECISE)

    chosen_in = select_adapter(adapt_in)
    chosen_down = select_adapter(adapt_down)
    chosen_out = select_adapter(adapt_out)
    chosen_ffn = select_adapter(adapt_ffn)

    def forward_group(items):
        query_block, key_block, value_block = items
        scores = (
            jnp.einsum(
                "sqhd,skhd->shqk", query_block, key_block, preferred_element_type=jnp.float32
            )
            * score_scale
        )
        scores = jnp.where(visible[:, None], scores, -1e30)
        biggest = jnp.max(scores, axis=-1, keepdims=True)
        lifted = jnp.exp(scores - biggest)
        row_total = jnp.sum(lifted, axis=-1, keepdims=True)
        probability = (lifted / row_total).astype(jnp.bfloat16)
        result = jnp.einsum(
            "shqk,skhd->sqhd", probability, value_block, preferred_element_type=jnp.float32
        )
        return (result.astype(jnp.bfloat16), (biggest + jnp.log(row_total))[..., 0])

    def backward_group(items):
        query_block, key_block, value_block, grad_block, log_total = items
        scores = (
            jnp.einsum(
                "sqhd,skhd->shqk", query_block, key_block, preferred_element_type=jnp.float32
            )
            * score_scale
        )
        scores = jnp.where(visible[:, None], scores, -1e30)
        probability = jnp.exp(scores - log_total[..., None])
        d_prob = jnp.einsum(
            "sqhd,skhd->shqk", grad_block, value_block, preferred_element_type=jnp.float32
        )
        delta = jnp.sum(probability * d_prob, axis=-1, keepdims=True)
        d_score = (probability * (d_prob - delta)).astype(jnp.bfloat16)
        d_query = (
            jnp.einsum("shqk,skhd->sqhd", d_score, key_block, preferred_element_type=jnp.float32)
            * score_scale
        )
        d_key = (
            jnp.einsum("shqk,sqhd->skhd", d_score, query_block, preferred_element_type=jnp.float32)
            * score_scale
        )
        d_value = jnp.einsum(
            "shqk,sqhd->skhd",
            probability.astype(jnp.bfloat16),
            grad_block,
            preferred_element_type=jnp.float32,
        )
        return (d_query, d_key, d_value)

    state = tokens.astype(jnp.float32)
    layer_index = 0
    w_qkv = lax.all_gather(qkv_weight[layer_index], ("batch", "seq"), axis=1, tiled=True)
    w_out = lax.all_gather(out_weight[layer_index], ("batch", "seq"), axis=0, tiled=True)
    w_in = lax.all_gather(ffn_in_weight[layer_index], ("batch", "seq"), axis=1, tiled=True)
    w_down = lax.all_gather(ffn_out_weight[layer_index], ("batch", "seq"), axis=0, tiled=True)
    held = [(w_qkv, w_out, w_in, w_down)]
    act_one = state.astype(jnp.bfloat16)
    low_qkv = jnp.einsum(
        "std,spdr->pstr",
        act_one,
        chosen_in[layer_index][:, 0:3],
        preferred_element_type=jnp.float32,
    ).astype(jnp.bfloat16)
    proj = jnp.einsum(
        "std,pde->pste", act_one, w_qkv, preferred_element_type=jnp.float32
    ) + jnp.einsum(
        "pstr,spre->pste",
        low_qkv,
        chosen_out[layer_index][:, 0:3],
        preferred_element_type=jnp.float32,
    )
    queries = (
        rotate(proj[0].reshape(seqs_here, tok_rows, HEADS, HEAD_DIM), cosine_here, sine_here)
        .astype(jnp.bfloat16)
        .reshape(seqs_here, tok_rows, model_width)
    )
    key_rot = (
        rotate(proj[1].reshape(seqs_here, tok_rows, HEADS, HEAD_DIM), cosine_here, sine_here)
        .astype(jnp.bfloat16)
        .reshape(seqs_here, tok_rows, model_width)
    )
    key_value = jnp.stack([key_rot, proj[2].astype(jnp.bfloat16)])
    edges = {}
    for step_by, row_count in shift_plan:
        if step_by > 0:
            outgoing = key_value[:, :, tok_rows - row_count :]
        else:
            outgoing = key_value[:, :, :row_count]
        edges[step_by] = shifted(outgoing, "seq", step_by)
    earlier = [edges[distance] for distance, row_count in reversed(shift_plan) if distance > 0]
    later = [edges[-distance] for distance, row_count in shift_plan if distance > 0]
    window = jnp.concatenate(earlier + [key_value] + later, axis=2)
    heads_out, log_total = lax.map(
        forward_group,
        (
            split_heads(queries, group_count),
            split_heads(window[0], group_count),
            split_heads(window[1], group_count),
        ),
    )
    attended = join_heads(heads_out)
    low_out = jnp.einsum(
        "std,sdr->str", attended, chosen_in[layer_index][:, 3], preferred_element_type=jnp.float32
    ).astype(jnp.bfloat16)
    branch = jnp.einsum(
        "std,de->ste", attended, w_out, preferred_element_type=jnp.float32
    ) + jnp.einsum(
        "str,sre->ste", low_out, chosen_out[layer_index][:, 3], preferred_element_type=jnp.float32
    )
    resid_one = state + branch
    hidden = norm_apply(resid_one, norm_gain[layer_index, 0], norm_bias[layer_index, 0])
    act_two = hidden.astype(jnp.bfloat16)
    low_ffn = jnp.einsum(
        "std,spdr->pstr",
        act_two,
        chosen_in[layer_index][:, 4:6],
        preferred_element_type=jnp.float32,
    ).astype(jnp.bfloat16)
    gate_up = jnp.einsum(
        "std,pdf->pstf", act_two, w_in, preferred_element_type=jnp.float32
    ) + jnp.einsum(
        "pstr,sprf->pstf", low_ffn, chosen_ffn[layer_index], preferred_element_type=jnp.float32
    )
    inner = (jax.nn.silu(gate_up[0]) * gate_up[1]).astype(jnp.bfloat16)
    low_down = jnp.einsum(
        "stf,sfr->str", inner, chosen_down[layer_index], preferred_element_type=jnp.float32
    ).astype(jnp.bfloat16)
    branch_two = jnp.einsum(
        "stf,fe->ste", inner, w_down, preferred_element_type=jnp.float32
    ) + jnp.einsum(
        "str,sre->ste", low_down, chosen_out[layer_index][:, 4], preferred_element_type=jnp.float32
    )
    resid_two = hidden + branch_two
    kept = [
        (
            act_one,
            low_qkv,
            queries,
            window,
            log_total,
            attended,
            low_out,
            resid_one,
            act_two,
            low_ffn,
            gate_up,
            inner,
            low_down,
            resid_two,
        )
    ]
    state = norm_apply(resid_two, norm_gain[layer_index, 1], norm_bias[layer_index, 1])
    mixed = state.astype(jnp.bfloat16)
    grad = cotangent.astype(jnp.float32)
    collected = [None] * LAYERS
    for layer_index in reversed(range(LAYERS)):
        (
            act_one,
            low_qkv,
            queries,
            window,
            log_total,
            attended,
            low_out,
            resid_one,
            act_two,
            low_ffn,
            gate_up,
            inner,
            low_down,
            resid_two,
        ) = kept[layer_index]
        w_qkv, w_out, w_in, w_down = held[layer_index]
        gain_two = norm_gain[layer_index, 1]
        bias_two = norm_bias[layer_index, 1]
        _, pull_two = jax.vjp(lambda residual: norm_apply(residual, gain_two, bias_two), resid_two)
        (d_resid_two,) = pull_two(grad)
        d_branch_two = d_resid_two.astype(jnp.bfloat16)
        d_low_down = jnp.einsum(
            "ste,sre->str",
            d_branch_two,
            chosen_out[layer_index][:, 4],
            preferred_element_type=jnp.float32,
        ).astype(jnp.bfloat16)
        g_out_down = jnp.einsum(
            "str,ste->sre", low_down, d_branch_two, preferred_element_type=jnp.float32
        )
        g_down = jnp.einsum("stf,str->sfr", inner, d_low_down, preferred_element_type=jnp.float32)
        d_inner = jnp.einsum(
            "ste,fe->stf", d_branch_two, w_down, preferred_element_type=jnp.float32
        ) + jnp.einsum(
            "str,sfr->stf", d_low_down, chosen_down[layer_index], preferred_element_type=jnp.float32
        )
        _, pull_act = jax.vjp(
            lambda gate_part, up_part: jax.nn.silu(gate_part) * up_part, gate_up[0], gate_up[1]
        )
        d_gate, d_up = pull_act(d_inner)
        d_gate_up = jnp.stack([d_gate, d_up]).astype(jnp.bfloat16)
        d_low_ffn = jnp.einsum(
            "pstf,sprf->pstr",
            d_gate_up,
            chosen_ffn[layer_index],
            preferred_element_type=jnp.float32,
        ).astype(jnp.bfloat16)
        g_ffn = jnp.einsum(
            "pstr,pstf->sprf", low_ffn, d_gate_up, preferred_element_type=jnp.float32
        )
        g_in_ffn = jnp.einsum(
            "std,pstr->spdr", act_two, d_low_ffn, preferred_element_type=jnp.float32
        )
        ffn_in_sum = spread_slots(g_in_ffn)
        ffn_down_sum = spread_slots(g_down)
        ffn_out_sum = spread_slots(g_out_down[:, None])
        ffn_ffn_sum = spread_slots(g_ffn)
        d_hidden = (
            d_resid_two
            + jnp.einsum("pstf,pdf->std", d_gate_up, w_in, preferred_element_type=jnp.float32)
            + jnp.einsum(
                "pstr,spdr->std",
                d_low_ffn,
                chosen_in[layer_index][:, 4:6],
                preferred_element_type=jnp.float32,
            )
        )
        gain_one = norm_gain[layer_index, 0]
        bias_one = norm_bias[layer_index, 0]
        _, pull_one = jax.vjp(lambda residual: norm_apply(residual, gain_one, bias_one), resid_one)
        (d_resid_one,) = pull_one(d_hidden)
        d_branch = d_resid_one.astype(jnp.bfloat16)
        d_low_out = jnp.einsum(
            "ste,sre->str",
            d_branch,
            chosen_out[layer_index][:, 3],
            preferred_element_type=jnp.float32,
        ).astype(jnp.bfloat16)
        g_out_att = jnp.einsum(
            "str,ste->sre", low_out, d_branch, preferred_element_type=jnp.float32
        )
        g_in_att = jnp.einsum(
            "std,str->sdr", attended, d_low_out, preferred_element_type=jnp.float32
        )
        d_attended = (
            jnp.einsum("ste,de->std", d_branch, w_out, preferred_element_type=jnp.float32)
            + jnp.einsum(
                "str,sdr->std",
                d_low_out,
                chosen_in[layer_index][:, 3],
                preferred_element_type=jnp.float32,
            )
        ).astype(jnp.bfloat16)
        d_query_heads, d_key_heads, d_value_heads = lax.map(
            backward_group,
            (
                split_heads(queries, group_count),
                split_heads(window[0], group_count),
                split_heads(window[1], group_count),
                split_heads(d_attended, group_count),
                log_total,
            ),
        )
        d_query = join_heads(d_query_heads)
        d_window = jnp.stack([join_heads(d_key_heads), join_heads(d_value_heads)])
        d_pair = d_window[:, :, left_total : left_total + tok_rows]
        for step_by, row_count in shift_plan:
            returning = lax.slice_in_dim(
                d_window, key_places[step_by], key_places[step_by] + row_count, axis=2
            )
            arrived = shifted(returning.astype(jnp.bfloat16), "seq", -step_by).astype(
                returning.dtype
            )
            if step_by > 0:
                d_pair = d_pair.at[:, :, tok_rows - row_count :].add(arrived)
            else:
                d_pair = d_pair.at[:, :, :row_count].add(arrived)
        d_query_rot = rotate(
            d_query.reshape(seqs_here, tok_rows, HEADS, HEAD_DIM), cosine_here, -sine_here
        ).reshape(seqs_here, tok_rows, model_width)
        d_key_rot = rotate(
            d_pair[0].reshape(seqs_here, tok_rows, HEADS, HEAD_DIM), cosine_here, -sine_here
        ).reshape(seqs_here, tok_rows, model_width)
        d_proj = jnp.stack([d_query_rot, d_key_rot, d_pair[1]]).astype(jnp.bfloat16)
        d_low_qkv = jnp.einsum(
            "pste,spre->pstr",
            d_proj,
            chosen_out[layer_index][:, 0:3],
            preferred_element_type=jnp.float32,
        ).astype(jnp.bfloat16)
        g_out_qkv = jnp.einsum(
            "pstr,pste->spre", low_qkv, d_proj, preferred_element_type=jnp.float32
        )
        g_in_qkv = jnp.einsum(
            "std,pstr->spdr", act_one, d_low_qkv, preferred_element_type=jnp.float32
        )
        grad = (
            d_resid_one
            + jnp.einsum("pste,pde->std", d_proj, w_qkv, preferred_element_type=jnp.float32)
            + jnp.einsum(
                "pstr,spdr->std",
                d_low_qkv,
                chosen_in[layer_index][:, 0:3],
                preferred_element_type=jnp.float32,
            )
        )
        att_in_sum = spread_slots(jnp.concatenate([g_in_qkv, g_in_att[:, None]], axis=1))
        att_out_sum = spread_slots(jnp.concatenate([g_out_qkv, g_out_att[:, None]], axis=1))
        collected[layer_index] = (
            jnp.concatenate([att_in_sum, ffn_in_sum], axis=1),
            ffn_down_sum,
            jnp.concatenate([att_out_sum, ffn_out_sum], axis=1),
            ffn_ffn_sum,
        )
    input_grad = grad.astype(jnp.bfloat16)
    stack_in = jnp.stack([collected[0][0]])
    stack_down = jnp.stack([collected[0][1]])
    stack_out = jnp.stack([collected[0][2]])
    stack_ffn = jnp.stack([collected[0][3]])
    stack_in, stack_down, stack_out, stack_ffn = lax.psum(
        (stack_in, stack_down, stack_out, stack_ffn), ("batch", "seq")
    )
    return (mixed, input_grad, stack_in, stack_down, stack_out, stack_ffn)


MESH = pl.DeviceIdType.MESH
NCHUNK = 10


class Gather:
    def __init__(self, sems, direct=()):
        self.direct = direct
        (
            self.zs, self.zr, self.xs, self.xr, self.ys, self.yr, self.ds, self.dr, self.es, self.er, self.fs, self.fr,
            self.cs, self.cr,
        ) = sems
        b = lax.axis_index("batch")
        self.s = lax.axis_index("seq")
        self.core = lax.rem(b, 2)
        self.x = lax.rem(lax.div(b, 2), 2)
        self.z = lax.div(b, 4)
        self.devx = (b + 2 - 4 * self.x, self.s)
        self.devy = (b, 1 - self.s)
        self.devc = (b + 1 - 2 * self.core, self.s)
        self.pair = self.z + 1 - 2 * lax.rem(self.z, 2)
        self.me = self.owner(self.z, 0, 0, 0)

    def owner(self, z, dx, dy, dc):
        x = 1 - self.x if dx else self.x
        y = 1 - self.s if dy else self.s
        c = 1 - self.core if dc else self.core
        return (z * 4 + x * 2 + c) * 2 + y

    def devz(self, z):
        return (z * 4 + self.x * 2 + self.core, self.s)

    def zof(self, d):
        return lax.rem(self.z + d, 4)

    def copy(self, c, j, half, dev, send, recv):
        v = self.view(c, j, half)
        return pltpu.make_async_remote_copy(v, v, send, recv, device_id=dev, device_id_type=MESH)

    def to_z(self, c, z):
        return self.copy(c, self.me, None, self.devz(z), self.zs.at[c, z], self.zr.at[c, self.z])

    def from_z(self, c, z):
        return self.copy(c, self.owner(z, 0, 0, 0), None, self.devz(z), self.zs.at[c, z], self.zr.at[c, z])

    def on_x(self, c, z, arriving):
        return self.copy(c, self.owner(z, arriving, 0, 0), None, self.devx, self.xs.at[c, z], self.xr.at[c, z])

    def on_y(self, c, z, arriving):
        return self.copy(c, self.owner(z, 0, arriving, 0), None, self.devy, self.ys.at[c, z], self.yr.at[c, z])

    def corner_x(self, c, z, arriving):
        return self.copy(c, self.owner(z, arriving, 1, 0), 0, self.devx, self.ds.at[c, z], self.dr.at[c, z])

    def corner_y(self, c, z, arriving):
        return self.copy(c, self.owner(z, 1, arriving, 0), 1, self.devy, self.es.at[c, z], self.er.at[c, z])

    def corner_z(self, c, z):
        return self.copy(c, self.owner(z, 1, 1, 0), None, self.devz(self.pair), self.fs.at[c, z], self.fr.at[c, z])

    def on_core(self, c, kind, z, arriving):
        j = self.owner(z, kind & 1, kind >> 1, arriving)
        k = kind * 4 + z
        return self.copy(c, j, None, self.devc, self.cs.at[c, k], self.cr.at[c, k])

    def barrier(self):
        bar = pltpu.get_barrier_semaphore()
        for dev in (self.devx, self.devy, self.devc, self.devz(self.zof(1)), self.devz(self.zof(2)), self.devz(self.zof(3))):
            pl.semaphore_signal(bar, inc=1, device_id=dev, device_id_type=MESH)
        pl.semaphore_wait(bar, 6)

    def others(self):
        z = self.z
        first = jnp.where(z == 0, 1, z - 1)
        second = jnp.where(z == 0, 2, jnp.where(z == 3, 1, z + 1))
        third = jnp.where(z <= 1, 3, 0)
        return first, second, third

    def corners(self, c):
        return (0, 1, 2, 3) if c in self.direct else (0, 2)

    def send_z(self, c):
        for z in self.others():
            self.to_z(c, z).start()

    def send_xy(self, c):
        self.on_x(c, self.z, 0).start()
        self.on_y(c, self.z, 0).start()
        self.on_core(c, 0, self.z, 0).start()

    def stage_own(self, c):
        self.send_z(c)
        self.send_xy(c)

    def stage_z(self, c):
        for z in self.others():
            self.from_z(c, z).wait_recv()
            self.on_x(c, z, 0).start()
            self.on_y(c, z, 0).start()
            self.on_core(c, 0, z, 0).start()

    def stage_xy(self, c):
        for d in (0, 2, 1, 3):
            z = self.zof(d)
            self.on_x(c, z, 1).wait_recv()
            if d in self.corners(c):
                self.corner_y(c, z, 0).start()
            self.on_core(c, 1, z, 0).start()
            self.on_y(c, z, 1).wait_recv()
            if d in self.corners(c):
                self.corner_x(c, z, 0).start()
            self.on_core(c, 2, z, 0).start()

    def stage_corner(self, c):
        for d in self.corners(c):
            z = self.zof(d)
            self.corner_x(c, z, 1).wait_recv()
            self.corner_y(c, z, 1).wait_recv()
            if c not in self.direct:
                self.corner_z(c, z).start()
            self.on_core(c, 3, z, 0).start()

    def stage_pair(self, c):
        if c in self.direct:
            return
        for d in (1, 3):
            z = self.zof(d)
            self.corner_z(c, z).wait_recv()
            self.on_core(c, 3, z, 0).start()

    def stage_core(self, c):
        for kind in range(4):
            for z in range(4):
                self.on_core(c, kind, z, 1).wait_recv()

    def finish(self, c):
        for d in (1, 2, 3):
            self.to_z(c, self.zof(d)).wait_send()
        for z in range(4):
            self.on_x(c, z, 0).wait_send()
            self.on_y(c, z, 0).wait_send()
            for kind in range(4):
                self.on_core(c, kind, z, 0).wait_send()
        for d in self.corners(c):
            z = self.zof(d)
            self.corner_x(c, z, 0).wait_send()
            self.corner_y(c, z, 0).wait_send()
            if c not in self.direct:
                self.corner_z(c, z).wait_send()


def gather_sems(chunks):
    return [pltpu.SemaphoreType.DMA((chunks, 4))] * 12 + [pltpu.SemaphoreType.DMA((chunks, 16))] * 2


BF = jnp.bfloat16
F32 = jnp.float32
QB = 256
PLAN = ((0, 3, False, True), (0, 4, False, True), (0, 5, True, True), (1, 5, True, True))
HALO_PLAN = ((2, 2), (3, 1))
NEG = -1e30
VMEM_LIMIT = int(63.9 * 2**20)


def nn(a, b):
    return jnp.dot(a, b, preferred_element_type=F32)


def nt(a, b):
    return lax.dot_general(a, b, (((1,), (1,)), ((), ())), preferred_element_type=F32)


def tn(a, b):
    return lax.dot_general(a, b, (((0,), (0,)), ((), ())), preferred_element_type=F32)


def iota(shape, dim):
    return lax.broadcasted_iota(jnp.int32, shape, dim)


def block_at(flip, block):
    return pl.multiple_of(jnp.where(flip == 1, 3 - block, block) * QB, QB)


def rope(vectors, cosine, sine):
    lane = iota((1, 128), 1)
    first = lax.rem(lane, HEAD_DIM) < HEAD_DIM // 2
    out = []
    for c in range(vectors.shape[1] // 128):
        part = vectors[:, c * 128 : (c + 1) * 128]
        other = jnp.where(first, pltpu.roll(part, 96, 1), pltpu.roll(part, 32, 1))
        out.append(part * cosine + other * sine)
    return jnp.concatenate(out, axis=1)


def fill_tables(flip, seg_ref, freq_ref, cos_ref, sin_ref, fq_ref, fk_ref, bias_ref):
    lane = iota((1, 128), 1)
    seg_row = seg_ref[...].astype(F32)
    starts = [
        jnp.sum((seg_row < float(d)).astype(F32), axis=1, keepdims=True) for d in (1, 2, 3)
    ]
    sign = jnp.where(lax.rem(lane, HEAD_DIM) < HEAD_DIM // 2, -1.0, 1.0)
    for w in range(12):
        block, part = divmod(w, 2)
        base = jnp.where(flip == 1, 7 - block, block) * QB + part * 128
        row = seg_ref[:, pl.ds(pl.multiple_of(base, 128), 128)].astype(F32)
        seg = jnp.broadcast_to(row, (128, 128)).T
        start = jnp.where(
            seg >= 3.0,
            starts[2],
            jnp.where(seg >= 2.0, starts[1], jnp.where(seg >= 1.0, starts[0], 0.0)),
        )
        pos = (iota((128, 128), 0) + base).astype(F32) - start
        angle = pos * freq_ref[...]
        rows = pl.ds(w * 128, 128)
        cos_ref[rows, :] = jnp.cos(angle)
        sin_ref[rows, :] = jnp.sin(angle) * sign
        hit = seg == lane.astype(F32)
        fq_ref[rows, :] = jnp.where(hit, 1.0, 0.0).astype(BF)
        fk_ref[rows, :] = jnp.where(hit | (lane >= 4), 0.0, NEG).astype(BF)
    gap = iota((QB, QB), 0) - iota((QB, QB), 1)
    gap = jnp.where(flip == 1, -gap, gap)
    bias_ref[0] = jnp.where(gap >= 0, 0.0, NEG)
    bias_ref[1] = jnp.where(gap <= 0, 0.0, NEG)


def qkv_rows(p, rb, xw, wq, aqkv, bblk, cos_ref, sin_ref, dest, low_ref):
    rows = pl.ds(pl.multiple_of(rb * QB, QB), QB)
    x = xw[rows, :]
    if p == 0:
        low = nt(x, aqkv[...]).astype(BF)
        low_ref[rows, :] = low
    else:
        low = low_ref[rows, :]
    proj = nn(x, wq[p].reshape(D, D)) + nn(low, bblk[p])
    if p < 2:
        proj = rope(proj, cos_ref[rows, :], sin_ref[rows, :])
    value = proj.astype(BF)
    if p == 0:
        value = value * jnp.asarray(0.125, BF)
    dest[rb] = value


def attend_pair(
    qb, pair, step, q_ref, k_ref, v_ref, fq_ref, fk_ref, bias_ref, att_ref, linv_ref, mf_ref, p_hbm, stage, sem
):
    k0, n, tri_first, tri_last = PLAN[qb]
    rows = pl.ds(qb * QB, QB)
    kblocks = pl.ds(k0, n)
    krows = pl.ds(k0 * QB, n * QB)
    half = iota((1, 128), 1) >= HEAD_DIM
    lane = iota((1, 128), 1)
    slot = lax.rem(step, 2)

    def copy(s):
        return pltpu.make_async_copy(stage.at[pl.ds(s * 4, 4)], p_hbm.at[qb, pair], sem.at[s])

    @pl.when(pair >= 2)
    def _():
        copy(slot).wait()

    lanes = pl.ds(pl.multiple_of(pair * 128, 128), 128)
    q2 = q_ref[qb, :, lanes]
    fq = fq_ref[rows, :]
    keys = jnp.concatenate([k_ref[kblocks, :, lanes].reshape(n * QB, 128), fk_ref[krows, :]], axis=1)
    v2 = v_ref[kblocks, :, lanes].reshape(n * QB, 128)
    outs = []
    for h in range(2):
        mine = half if h == 1 else jnp.logical_not(half)
        qm = jnp.where(mine, q2, jnp.zeros_like(q2))
        s = nt(jnp.concatenate([qm, fq], axis=1), keys)
        parts = [s[:, t * QB : (t + 1) * QB] for t in range(n)]
        if tri_last:
            parts[n - 1] = parts[n - 1] + bias_ref[0]
        if tri_first:
            parts[0] = parts[0] + bias_ref[1]
        s = jnp.concatenate(parts, axis=1)
        m = jnp.max(s, axis=1, keepdims=True)
        p = jnp.exp(s - m).astype(BF)
        for g in range((n + 2) // 3):
            part = p[:, g * D : min(g * D + D, n * QB)]
            stage[slot * 4 + h * 2 + g, :, 0 : part.shape[1]] = part
        if qb >= 2:
            low = 4 + 3 * (2 * pair + h)
            mf_ref[rows, :] = jnp.where((lane >= low) & (lane < low + 3), -m, mf_ref[rows, :])
        outs.append(nn(p, jnp.where(mine, v2, jnp.ones_like(v2))))
    inv = 1.0 / pltpu.roll(jnp.where(half, outs[0], outs[1]), HEAD_DIM, 1)
    att_ref[rows, lanes] = (jnp.where(half, outs[1], outs[0]) * inv).astype(BF)
    linv_ref[rows, lanes] = inv
    copy(slot).start()


def drain_pairs(qb, p_hbm, stage, sem):
    for s in range(2):
        pltpu.make_async_copy(stage.at[pl.ds(s * 4, 4)], p_hbm.at[qb, 0], sem.at[s]).wait()


def norm_stats(r):
    centre = r - jnp.mean(r, axis=1, keepdims=True)
    rstd = lax.rsqrt(jnp.mean(centre * centre, axis=1, keepdims=True) + EPSILON)
    return centre * rstd, rstd


def norm_back(grad, xhat, rstd):
    return rstd * (
        grad
        - jnp.mean(grad, axis=1, keepdims=True)
        - xhat * jnp.mean(grad * xhat, axis=1, keepdims=True)
    )


def out_rows(rb, xw, att_ref, wo, ao, bo, gb, aff, xhat_ref, rstd_ref, act_ref, lowo_ref, lowf_ref):
    rows = pl.ds(pl.multiple_of(rb * QB, QB), QB)
    att = att_ref[rows, :]
    low = nt(att, ao[...]).astype(BF)
    lowo_ref[rows, :] = low
    branch = nn(att, wo[...].reshape(D, D)) + nn(low, bo[...])
    xhat, rstd = norm_stats(xw[rows, :].astype(F32) + branch)
    xhat_ref[rows, :] = xhat
    rstd_ref[rows, :] = jnp.broadcast_to(rstd, (QB, 128))
    act = (xhat * gb[0:1, :] + gb[1:2, :]).astype(BF)
    act_ref[rows, :] = act
    lowf_ref[rows, :] = nt(act, aff[...]).astype(BF)


def ffn_in_tile(n, rb, size, act_ref, lowf_ref, wi, wd, bg, bu, adn, big, lowd_ref, total_ref):
    start = pl.multiple_of(rb * size, size)
    rows = pl.ds(start, size)
    act = act_ref[rows, :]
    low = lowf_ref[rows, :]
    gate = nn(act, wi[n, 0].reshape(D, D)) + nn(low, bg[n])
    up = nn(act, wi[n, 1].reshape(D, D)) + nn(low, bu[n])
    inner = (gate * (1.0 / (1.0 + jnp.exp(-gate))) * up).astype(BF)
    blocks = size // QB
    here = n * 4 + rb * blocks
    big[pl.ds(here, blocks)] = gate.astype(BF).reshape(blocks, QB, D)
    big[pl.ds(here + 16, blocks)] = up.astype(BF).reshape(blocks, QB, D)
    lowd_ref[rows, 0:16] += nt(inner, adn[n])
    total_ref[rows, :] += nn(inner, wd[pl.ds(n * 8, 8)].reshape(D, D))


def ffn_out_rows(
    rb, flip, lowd_ref, bdn, xhat_ref, gb, cot, dtwo_ref, db2_ref, dlow_ref, mixed_ref, gbdn_ref
):
    start = pl.multiple_of(rb * QB, QB)
    rows = pl.ds(start, QB)
    low = lowd_ref[rows, 0:16].astype(BF)
    total = nn(low, bdn[...]) + dtwo_ref[rows, :]
    r = xhat_ref[rows, :] * gb[0:1, :] + gb[1:2, :] + total
    xhat, rstd = norm_stats(r)
    mixed_ref[pl.ds(block_at(flip, rb), QB), :] = (xhat * gb[2:3, :] + gb[3:4, :]).astype(BF)
    dtwo = norm_back(cot[rows, :].astype(F32) * gb[2:3, :], xhat, rstd)
    dtwo_ref[rows, :] = dtwo
    db2 = dtwo.astype(BF)
    db2_ref[rows, :] = db2
    dlow_ref[rows, :] = nt(db2, bdn[...]).astype(BF)
    gbdn_ref[...] += tn(low, db2)


def ffn_back_tile(
    n, start, size, db2_ref, dlow_ref, wd, wi, adn, bg, bu, big, lowf_ref, acc, dlf_ref, gadn_ref, gbf_ref
):
    rows = pl.ds(start, size)
    db2 = db2_ref[rows, :]
    dlow = dlow_ref[rows, :]
    dinner = nt(db2, wd[pl.ds(n * 8, 8)].reshape(D, D)) + nn(dlow, adn[n])
    blocks = size // QB
    here = n * 4 + lax.div(start, QB)
    gate = big[pl.ds(here, blocks)].reshape(size, D).astype(F32)
    up = big[pl.ds(here + 16, blocks)].reshape(size, D).astype(F32)
    sig = 1.0 / (1.0 + jnp.exp(-gate))
    silu = gate * sig
    inner = (silu * up).astype(BF)
    dg = (dinner * up * (sig + silu * (1.0 - sig))).astype(BF)
    du = (dinner * silu).astype(BF)
    acc[...] += nt(dg, wi[n, 0].reshape(D, D)) + nt(du, wi[n, 1].reshape(D, D))
    dlf_ref[...] += nt(dg, bg[n]) + nt(du, bu[n])
    gadn_ref[n] += tn(dlow, inner)
    low = lowf_ref[rows, :]
    gbf_ref[n] += jnp.where(iota((32, 1), 0) < 16, tn(low, dg), tn(low, du))


def hidden_back_rows(
    rb, off, acc, dlf_ref, aff, act_ref, dtwo_ref, xhat_ref, rstd_ref, gb, bo, ao, lowo_ref, att_ref,
    wo, linv_ref, h2, mf_ref, do_ref, hf_ref, gaff_ref, gbo_ref, gao_ref,
):
    start = pl.multiple_of(rb * QB, QB)
    rows = pl.ds(start, QB)
    local = pl.ds(pl.multiple_of(start - off, QB), QB)
    dlf = dlf_ref[local, :].astype(BF)
    dhid = dtwo_ref[rows, :] + acc[local, :] + nn(dlf, aff[...])
    gaff_ref[...] += tn(dlf, act_ref[rows, :])
    done = norm_back(dhid * gb[0:1, :], xhat_ref[rows, :], rstd_ref[rows, 0:1])
    dtwo_ref[rows, :] = done
    dbr = done.astype(BF)
    dlo = nt(dbr, bo[...]).astype(BF)
    att = att_ref[rows, :]
    gbo_ref[...] += tn(lowo_ref[rows, :], dbr)
    gao_ref[...] += tn(dlo, att)
    datt = (nt(dbr, wo[...].reshape(D, D)) + nn(dlo, ao[...])).astype(BF)
    do = (datt.astype(F32) * linv_ref[rows, :]).astype(BF)
    do_ref[rows, :] = do
    value = nn(do * att, h2[...]) + mf_ref[rows, :]
    lane = iota((1, 128), 1)
    role = jnp.where(lane < 40, lax.rem(lane + 2, 3), lax.rem(lane, 2))
    high = value.astype(BF)
    rest = value - high.astype(F32)
    mid = rest.astype(BF)
    last = (rest - mid.astype(F32)).astype(BF)
    hf_ref[rows, :] = jnp.where(role == 0, high, jnp.where(role == 1, mid, last))


def kf_kernel(
    x_hbm, cot_hbm, seg_ref, freq_ref, aqkv, bqkv, ao, bo, aff, bff, adn, bdn, gb, tag,
    wq_hbm, wo_hbm, wi_hbm, wd_hbm,
    q_hbm, k_hbm, v_hbm, p_hbm, mixed_hbm, do_hbm, hf_ref, lowq_hbm, done_hbm, cos_hbm, sin_hbm, fq_hbm, fk_hbm,
    ge_ref, wq_out,
    gao_ref, gaff_ref, gadn_ref, gbo_ref, gbdn_ref, gbf_ref,
    wq, wo, wi, wd, big, xw, att, linv, xhat, dtwo, act, db2, cos, sin, fq, fk, bias, mf,
    lowq, lowo, lowf, dlow, acc, dlf, bblk, bg, bu, h2, mixed_ref, do_ref, rsem, wsem, xsem, osem, psem, hs, hr, *sems,
):
    flip = lax.axis_index("seq")
    cot = db2
    rstd = cos
    lowd = sin
    loads = []
    for i in range(4):
        loads.append(
            pltpu.make_async_copy(
                x_hbm.at[pl.ds(block_at(flip, i), QB)], xw.at[pl.ds(i * QB, QB)], xsem.at[i]
            )
        )
        loads.append(
            pltpu.make_async_copy(
                cot_hbm.at[pl.ds(block_at(flip, i), QB)], cot.at[pl.ds(i * QB, QB)], xsem.at[4 + i]
            )
        )
    g = Gather(sems, direct=(0, 1, 2))

    def view(c, j, half):
        cut = 384 if c < 3 else 640
        lanes = slice(None) if half is None else pl.ds(0, cut) if half == 0 else pl.ds(cut, D - cut)
        if c < 3:
            return wq.at[c, j, :, lanes]
        if c == 3:
            return wo.at[j, :, lanes]
        if c < 6:
            return wd.at[j, pl.ds((c - 4) * 48, 48), lanes]
        return wi.at[c - 6, :, j, :, lanes]

    g.view = view
    weights = [
        pltpu.make_async_copy(a, b, wsem.at[i])
        for i, (a, b) in enumerate(
            [(wq_hbm, wq.at[:, g.me]), (wo_hbm, wo.at[g.me]), (wd_hbm, wd.at[g.me])]
            + [(wi_hbm.at[:, :, pl.ds(D * n, D)], wi.at[n, :, g.me]) for n in range(4)]
        )
    ]
    for copy in weights:
        copy.start()
    g.barrier()
    for copy in weights:
        copy.wait()
    for c in range(3):
        g.stage_own(c)
    for c in range(3, NCHUNK):
        g.send_z(c)
    halo = [
        pltpu.make_async_remote_copy(
            x_hbm.at[pl.ds(block_at(flip, 3 - i), QB)], xw.at[pl.ds(1024 + i * QB, QB)], hs.at[i], hr.at[i],
            device_id=g.devy, device_id_type=MESH,
        )
        for i in range(2)
    ]

    kinds = {
        "z": g.stage_z, "x": g.stage_xy, "c": g.stage_corner, "p": g.stage_pair, "k": g.stage_core, "s": g.send_xy,
    }

    def tick(*steps):
        for step in steps:
            kinds[step[0]](int(step[1]))

    for copy in loads:
        copy.start()
    fill_tables(flip, seg_ref, freq_ref, cos, sin, fq, fk, bias)
    rank = iota((48, 1), 0)
    for p in range(3):
        keep = (rank >= 16 * p) & (rank < 16 * p + 16)
        bblk[p] = jnp.where(keep, bqkv[...], jnp.zeros_like(bqkv[...]))
    rank = iota((32, 1), 0)
    for n in range(4):
        piece = bff[:, n * D : (n + 1) * D]
        bg[n] = jnp.where(rank < 16, piece, jnp.zeros_like(piece))
        bu[n] = jnp.where(rank >= 16, piece, jnp.zeros_like(piece))
    head = lax.div(iota((D, 128), 0), HEAD_DIM)
    spot = iota((D, 128), 1)
    h2[...] = jnp.where(lax.div(spot - 40, 2) == head, jnp.where(spot >= 40, -1.0, 0.0), 0.0).astype(BF)
    mf[...] = jnp.zeros_like(mf)
    dtwo[...] = jnp.zeros_like(dtwo)
    for ref in (gao_ref, gaff_ref, gadn_ref, gbo_ref, gbdn_ref, gbf_ref):
        ref[...] = jnp.zeros_like(ref)
    tick("z0", "z1", "z2", "s3", "x0", "x1", "x2")
    for copy in halo:
        copy.start()
    for copy in loads:
        copy.wait()
    tick("s4", "c0", "k0")
    q_ref, k_ref, v_ref = (big.at[pl.ds(i * 6, 6)] for i in range(3))
    stage = big.at[pl.ds(18, 8)]

    def qkv_page(p, first, last):
        def step(rb, _):
            qkv_rows(p, rb, xw, wq, aqkv, bblk, cos, sin, (q_ref, k_ref, v_ref)[p], lowq)
            return 0

        lax.fori_loop(first, last, step, 0)

    qkv_page(0, 0, 4)
    tick("c1", "k1", "z3", "s5")
    qkv_page(1, 0, 4)
    tick("c2", "k2", "x3", "z4")
    qkv_page(2, 0, 4)
    tick("c3", "x4", "z5", "s6")
    keep_wq = pltpu.make_async_copy(wq, wq_out, osem.at[9])
    keep_wq.start()
    for qb in range(4):

        def pair_step(pair, _, qb=qb):
            attend_pair(qb, pair, pair, q_ref, k_ref, v_ref, fq, fk, bias, att, linv, mf, p_hbm, stage, psem)
            return 0

        if qb < 2:
            lax.fori_loop(0, 6, pair_step, 0)
        else:
            lax.fori_loop(0, 3, pair_step, 0)
            tick(*(("c6", "x7", "s9") if qb == 2 else ("c7", "x8")))
            lax.fori_loop(3, 6, pair_step, 0)
        drain_pairs(qb, p_hbm, stage, psem)
        tick(
            *(
                ("p3", "c4", "x5", "z6", "s7"),
                ("k3", "p4", "c5", "x6", "z7", "s8"),
                ("k5", "p6", "z9"),
                ("k6", "p7", "x9"),
            )[qb]
        )
        if qb == 1:
            for copy in halo:
                copy.wait_recv()
            for p in range(3):
                qkv_page(p, 4, 6)
            tick("p5", "k4", "z8")
            saves = [
                pltpu.make_async_copy(a, b, osem.at[i])
                for i, (a, b) in enumerate(
                    ((q_ref, q_hbm), (k_ref, k_hbm), (v_ref, v_hbm), (lowq, lowq_hbm), (cos, cos_hbm), (sin, sin_hbm), (fq, fq_hbm), (fk, fk_hbm))
                )
            ]
            for copy in saves:
                copy.start()
    for copy in saves:
        copy.wait()
    lowd[...] = jnp.zeros_like(lowd)

    def out_step(rb, _):
        out_rows(rb, xw, att, wo, ao, bo, gb, aff, xhat, rstd, act, lowo, lowf)
        return 0

    lax.fori_loop(0, 4, out_step, 0)
    tick("c8")

    def in_step(i, _):
        ffn_in_tile(lax.div(i, 2), lax.rem(i, 2), 512, act, lowf, wi, wd, bg, bu, adn, big, lowd, dtwo)
        return 0

    lax.fori_loop(0, 2, in_step, 0)
    tick("k7", "p8", "c9")
    lax.fori_loop(2, 4, in_step, 0)
    tick("k8", "p9")
    lax.fori_loop(4, 6, in_step, 0)
    tick("k9")
    lax.fori_loop(6, 8, in_step, 0)

    def down_step(rb, _):
        ffn_out_rows(rb, flip, lowd, bdn, xhat, gb, cot, dtwo, db2, dlow, mixed_ref, gbdn_ref)
        return 0

    lax.fori_loop(0, 4, down_step, 0)
    outs = [pltpu.make_async_copy(mixed_ref, mixed_hbm, rsem.at[0])]
    outs[0].start()

    def row_copies(rb):
        rows = pl.ds(pl.multiple_of(rb * QB, QB), QB)
        return (
            pltpu.make_async_copy(do_ref.at[rows], do_hbm.at[rows], rsem.at[1 + rb]),
            pltpu.make_async_copy(dtwo.at[rows], done_hbm.at[rows], rsem.at[5 + rb]),
        )

    def back_step(half, _):
        off = pl.multiple_of(half * 512, 512)
        acc[...] = jnp.zeros_like(acc)
        dlf[...] = jnp.zeros_like(dlf)

        def tile(n, _):
            ffn_back_tile(
                n, off, 512, db2, dlow, wd, wi, adn, bg, bu, big, lowf, acc, dlf, gadn_ref, gbf_ref
            )
            return 0

        lax.fori_loop(0, 4, tile, 0)

        def rows(i, _):
            hidden_back_rows(
                half * 2 + i, off, acc, dlf, aff, act, dtwo, xhat, rstd, gb, bo, ao, lowo, att, wo, linv, h2, mf,
                do_ref, hf_ref, gaff_ref, gbo_ref, gao_ref,
            )
            for copy in row_copies(half * 2 + i):
                copy.start()
            return 0

        lax.fori_loop(0, 2, rows, 0)
        return 0

    lax.fori_loop(0, 2, back_step, 0)
    for rb in range(4):
        outs.extend(row_copies(rb))
    ge_ref[0:16] = gao_ref[...].astype(BF)
    ge_ref[16:48] = gaff_ref[...].astype(BF)
    ge_ref[48:64] = gbo_ref[...].astype(BF)
    ge_ref[64:80] = gbdn_ref[...].astype(BF)
    ge_ref[80:144] = gadn_ref[...].reshape(64, D).astype(BF)
    ge_ref[144:272] = gbf_ref[...].reshape(128, D).astype(BF)
    ge_ref[272:288] = tag[...]
    keep_wq.wait()
    for copy in outs:
        copy.wait()
    for copy in halo:
        copy.wait_send()
    for c in range(NCHUNK):
        g.finish(c)


def k3_kernel(
    x_hbm, q_hbm, k_hbm, v_hbm, p_hbm, do_hbm, hf_hbm, ge, lowq_hbm, done_hbm, cos_hbm, sin_hbm,
    fq_hbm, fk_hbm, aqkv, bqkv, wq_hbm,
    dx_ref, sum_e_ref, sum_l_ref,
    ga_ref, gbq_ref, dproj, eg, lg, ge_in, gl_out, gl_in,
    xw, q, k, v, do, hf, lowq, done, cos, sin, fq, fk, wq, stage, dq, dkT, dvT, bias, sem, psem, hs, hr, *sems,
):
    flip = lax.axis_index("seq")
    g = Gather(sems)
    table = (
        (q_hbm, q), (k_hbm, k), (v_hbm, v), (do_hbm, do.at[pl.ds(0, 1024)]), (hf_hbm, hf.at[pl.ds(0, 1024)]),
        (lowq_hbm, lowq), (done_hbm, done), (cos_hbm, cos), (sin_hbm, sin), (fq_hbm, fq), (fk_hbm, fk), (wq_hbm, wq),
    )
    loads = [pltpu.make_async_copy(a, b, sem.at[i]) for i, (a, b) in enumerate(table)]
    for i in range(4):
        loads.append(
            pltpu.make_async_copy(
                x_hbm.at[pl.ds(block_at(flip, i), QB)], xw.at[pl.ds(i * QB, QB)], sem.at[12 + i]
            )
        )
    for copy in loads:
        copy.start()

    def early(c, j, half):
        lanes = slice(None) if half is None else pl.ds(half * 384, 384)
        return eg.at[j, :, lanes]

    def late(c, j, half):
        lanes = slice(None) if half is None else pl.ds(half * 384, 384)
        return lg.at[j, :, lanes]

    g.barrier()
    halo = []
    for i, (src, dst) in enumerate(
        (
            (do_hbm.at[pl.ds(768, QB)], do.at[pl.ds(1024, QB)]),
            (do_hbm.at[pl.ds(512, QB)], do.at[pl.ds(1280, QB)]),
            (hf_hbm.at[pl.ds(768, QB)], hf.at[pl.ds(1024, QB)]),
            (hf_hbm.at[pl.ds(512, QB)], hf.at[pl.ds(1280, QB)]),
            (ge.at[pl.ds(pl.multiple_of((1 - flip) * 144, 16), 144)], ge_in),
            (gl_out.at[pl.ds(pl.multiple_of((1 - flip) * 48, 16), 48)], gl_in),
        )
    ):
        halo.append(
            pltpu.make_async_remote_copy(
                src, dst, hs.at[i], hr.at[i], device_id=g.devy, device_id_type=MESH
            )
        )
    for copy in (halo[4], halo[0], halo[1], halo[2], halo[3]):
        copy.start()
    dkT[...] = jnp.zeros_like(dkT)
    dvT[...] = jnp.zeros_like(dvT)
    ga_ref[...] = jnp.zeros_like(ga_ref)
    gbq_ref[...] = jnp.zeros_like(gbq_ref)
    gap = iota((QB, QB), 0) - iota((QB, QB), 1)
    gap = jnp.where(flip == 1, -gap, gap)
    bias[...] = jnp.where(gap <= 0, 0.0, NEG)
    half = iota((1, 128), 1) >= HEAD_DIM
    for copy in loads[:5]:
        copy.wait()

    def picks(pair, first, width):
        head = 2 * pair + lax.div(iota((128, 256), 1), 128)
        row = iota((128, 256), 0) - first - width * head
        return jnp.where((row >= 0) & (row < width), 1.0, 0.0).astype(BF)

    for qb in range(4):
        k0, n, _, _ = PLAN[qb]
        own = min(4 - k0, n)
        rows = pl.ds(qb * QB, QB)
        krows = pl.ds(k0 * QB, n * QB)

        def fetch(pair, s, qb=qb, n=n):
            return pltpu.make_async_copy(p_hbm.at[qb, pair], stage.at[s], psem.at[s])

        fetch(0, 0).start()

        def pair_step(pair, _, k0=k0, n=n, own=own, rows=rows, krows=krows, fetch=fetch):
            slot = lax.rem(pair, 2)
            fetch(pair, slot).wait()

            @pl.when(pair < 5)
            def _():
                fetch(pair + 1, 1 - slot).start()

            lanes = pl.ds(pl.multiple_of(pair * 128, 128), 128)
            do2 = do[rows, lanes]
            ndl = nn(hf[rows, :], picks(pair, 40, 2))
            k2 = k[krows, lanes]
            v2 = v[krows, lanes]
            qT = q[rows, lanes].T
            doT = do2.T
            dqs = []
            for h in range(2):
                mine = half if h == 1 else jnp.logical_not(half)
                p = stage[slot, 2 * h, :, 0 : min(D, n * QB)]
                if n > 3:
                    p = jnp.concatenate([p, stage[slot, 2 * h + 1, :, 0 : n * QB - D]], axis=1)
                dp = nt(jnp.where(mine, do2, jnp.zeros_like(do2)), v2)
                d = ndl[:, h * 128 : (h + 1) * 128]
                ds = (p.astype(F32) * (dp + jnp.concatenate([d] * (2 * n), axis=1))).astype(BF)
                dqs.append(nn(ds, k2))
                hr = pl.ds(pl.multiple_of(pair * 128 + h * 64, 64), 64)
                kc = pl.ds(k0 * QB, own * QB)
                dkT[hr, kc] += nn(qT[h * 64 : (h + 1) * 64], ds[:, 0 : own * QB])
                dvT[hr, kc] += nn(doT[h * 64 : (h + 1) * 64], p[:, 0 : own * QB])
            dq[rows, lanes] = jnp.where(half, dqs[1], dqs[0]) * 0.125
            return 0

        lax.fori_loop(0, 6, pair_step, 0)
        g.view = early
        if qb == 0:
            halo[4].wait_recv()
            mine = ge[pl.ds(pl.multiple_of(flip * 144, 16), 144)]
            total = mine.astype(F32) + ge_in[...].astype(F32)
            row = iota((144, 1), 0)
            eg[g.me] = jnp.where((row >= 128) & (flip == 1), mine.astype(F32), total).astype(BF)
            g.stage_own(0)
        elif qb == 1:
            g.stage_z(0)
        elif qb == 2:
            g.stage_xy(0)
        else:
            g.stage_corner(0)
            g.stage_pair(0)

    for copy in loads[5:]:
        copy.wait()
    for copy in halo[:4]:
        copy.wait_recv()
    for i, (k0, n) in enumerate(HALO_PLAN):
        rows = pl.ds(1024 + i * QB, QB)
        krows = pl.ds(k0 * QB, n * QB)

        def halo_step(pair, _, k0=k0, n=n, rows=rows, krows=krows):
            lanes = pl.ds(pl.multiple_of(pair * 128, 128), 128)
            do2 = do[rows, lanes]
            q2 = q[rows, lanes]
            feats = hf[rows, :]
            ndl = nn(feats, picks(pair, 40, 2))
            nm = nn(feats, picks(pair, 4, 3))
            keys = jnp.concatenate([k[krows, lanes], fk[krows, :]], axis=1)
            v2 = v[krows, lanes]
            qT = q2.T
            doT = do2.T
            for h in range(2):
                mine = half if h == 1 else jnp.logical_not(half)
                s = nt(jnp.concatenate([jnp.where(mine, q2, jnp.zeros_like(q2)), fq[rows, :]], axis=1), keys)
                parts = [s[:, t * QB : (t + 1) * QB] for t in range(n)]
                parts[0] = parts[0] + bias[...]
                s = jnp.concatenate(parts, axis=1)
                m = nm[:, h * 128 : (h + 1) * 128]
                p = jnp.exp(s + jnp.concatenate([m] * (2 * n), axis=1))
                dp = nt(jnp.where(mine, do2, jnp.zeros_like(do2)), v2)
                d = ndl[:, h * 128 : (h + 1) * 128]
                ds = (p * (dp + jnp.concatenate([d] * (2 * n), axis=1))).astype(BF)
                hr = pl.ds(pl.multiple_of(pair * 128 + h * 64, 64), 64)
                kc = pl.ds(k0 * QB, n * QB)
                dkT[hr, kc] += nn(qT[h * 64 : (h + 1) * 64], ds)
                dvT[hr, kc] += nn(doT[h * 64 : (h + 1) * 64], p.astype(BF))
            return 0

        lax.fori_loop(0, 6, halo_step, 0)

    g.stage_core(0)

    def weights_of(b, e):
        return eg[2 * b + 1, 128 + e : 129 + e, :].astype(F32)

    def sum_step(i, _):
        y = lax.div(i, 9)
        r = pl.multiple_of(lax.rem(i, 9) * 16, 16)
        totals = [jnp.zeros((16, D), F32) for _ in range(ADAPTERS)]
        for b in range(16):
            part = eg[2 * b + y, pl.ds(r, 16), :].astype(F32)
            for e in range(ADAPTERS):
                totals[e] += part * weights_of(b, e)
        for e in range(ADAPTERS):
            sum_e_ref[e, pl.ds(pl.multiple_of(i * 16, 16), 16), :] = totals[e]
        return 0

    lane = lax.div(iota((1, 48), 1), 16)
    rank = lax.div(iota((48, 1), 0), 16)

    def proj_step(rb, _):
        start = pl.multiple_of(rb * QB, QB)
        rows = pl.ds(start, QB)
        cosine = cos[rows, :]
        sine = -sin[rows, :]
        low = lowq[rows, :]
        dlow = jnp.zeros((QB, 48), F32)
        for p in range(3):
            if p == 0:
                d = rope(dq[rows, :], cosine, sine)
            else:
                src = (dkT, dvT)[p - 1]
                d = jnp.concatenate([src[pl.ds(c * 128, 128), rows].T for c in range(6)], axis=1)
                if p == 1:
                    d = rope(d, cosine, sine)
            d = d.astype(BF)
            dproj[p, rows, :] = d
            dlow += jnp.where(lane == p, nt(d, bqkv[...]), 0.0)
            gbq_ref[...] += jnp.where(rank == p, tn(low, d), 0.0)
        dlow = dlow.astype(BF)
        lowq[rows, :] = dlow
        ga_ref[...] += tn(dlow, xw[rows, :])
        return 0

    lax.fori_loop(0, 4, proj_step, 0)
    gl_out[0:48] = ga_ref[...].astype(BF)
    gl_out[48:96] = gbq_ref[...].astype(BF)
    halo[5].start()
    g.view = late

    def dx_rows(rb):
        rows = pl.ds(rb * QB, QB)
        total = done[rows, :] + nn(lowq[rows, :], aqkv[...])
        for p in range(3):
            total += nt(dproj[p, rows, :], wq[p].reshape(D, D))
        dx_ref[pl.ds(block_at(flip, rb), QB), :] = total.astype(BF)

    lax.fori_loop(0, 18, sum_step, 0)
    halo[5].wait_recv()
    lg[g.me] = (
        gl_out[pl.ds(pl.multiple_of(flip * 48, 16), 48)].astype(F32) + gl_in[...].astype(F32)
    ).astype(BF)
    g.stage_own(1)
    dx_rows(0)
    g.stage_z(1)
    dx_rows(1)
    g.stage_xy(1)
    dx_rows(2)
    g.stage_corner(1)
    dx_rows(3)
    g.stage_pair(1)
    g.stage_core(1)

    def late_step(i, _):
        y = lax.div(i, 3)
        r = pl.multiple_of(lax.rem(i, 3) * 16, 16)
        totals = [jnp.zeros((16, D), F32) for _ in range(ADAPTERS)]
        for b in range(16):
            part = lg[2 * b + y, pl.ds(r, 16), :].astype(F32)
            for e in range(ADAPTERS):
                totals[e] += part * weights_of(b, e)
        for e in range(ADAPTERS):
            sum_l_ref[e, pl.ds(pl.multiple_of(i * 16, 16), 16), :] = totals[e]
        return 0

    lax.fori_loop(0, 6, late_step, 0)
    for copy in halo:
        copy.wait_send()
    for c, view in enumerate((early, late)):
        g.view = view
        g.finish(c)


def sds(shape, dtype):
    return jax.ShapeDtypeStruct(shape, dtype)


ANY = functools.partial(pl.BlockSpec, memory_space=pl.ANY)
INV = functools.partial(pl.BlockSpec, memory_space=pltpu.VMEM)


def kf_call(*args):
    outs = [
        (ANY, (6, QB, D), BF), (ANY, (6, QB, D), BF), (ANY, (6, QB, D), BF), (ANY, (4, 6, 4, QB, D), BF),
        (ANY, (1024, D), BF), (ANY, (1024, D), BF), (INV, (1024, 128), BF),
        (ANY, (1536, 48), BF), (ANY, (1024, D), F32), (ANY, (1536, 128), F32), (ANY, (1536, 128), F32),
        (ANY, (1536, 128), BF), (ANY, (1536, 128), BF),
        (INV, (288, D), BF), (ANY, (3, 32, 24, D), BF),
    ]
    V = pltpu.VMEM
    scratch = [
        V((16, D), F32), V((32, D), F32), V((4, 16, D), F32), V((16, D), F32), V((16, D), F32), V((4, 32, D), F32),
        V((3, 32, 24, D), BF), V((32, 24, D), BF), V((4, 2, 32, 24, D), BF), V((32, 96, D), BF),
        V((32, QB, D), BF), V((1536, D), BF), V((1024, D), BF), V((1024, D), F32),
        V((1024, D), F32), V((1024, D), F32), V((1024, D), BF), V((1024, D), BF),
        V((1536, 128), F32), V((1536, 128), F32), V((1536, 128), BF), V((1536, 128), BF), V((2, QB, QB), F32),
        V((1024, 128), F32), V((1536, 48), BF), V((1024, 16), BF), V((1024, 32), BF),
        V((1024, 16), BF), V((512, D), F32), V((512, 32), F32), V((3, 48, D), BF),
        V((4, 32, D), BF), V((4, 32, D), BF), V((D, 128), BF), V((1024, D), BF), V((1024, D), BF),
        pltpu.SemaphoreType.DMA((9,)), pltpu.SemaphoreType.DMA((7,)), pltpu.SemaphoreType.DMA((8,)), pltpu.SemaphoreType.DMA((10,)),
        pltpu.SemaphoreType.DMA((2,)), pltpu.SemaphoreType.DMA((2,)), pltpu.SemaphoreType.DMA((2,)),
    ]
    scratch += gather_sems(NCHUNK)
    return pl.pallas_call(
        kf_kernel,
        out_shape=[sds(s, t) for _, s, t in outs],
        in_specs=[ANY()] * 2 + [INV()] * 12 + [ANY()] * 4,
        out_specs=[m() for m, _, _ in outs],
        scratch_shapes=scratch,
        compiler_params=pltpu.CompilerParams(
            vmem_limit_bytes=VMEM_LIMIT, collective_id=1, has_side_effects=True
        ),
    )(*args)


def k3_call(*args):
    V = pltpu.VMEM
    scratch = [
        V((48, D), F32), V((48, D), F32), V((3, 1024, D), BF), V((32, 144, D), BF), V((32, 48, D), BF),
        V((144, D), BF), V((96, D), BF), V((48, D), BF),
        V((1024, D), BF), V((1536, D), BF), V((1536, D), BF), V((1536, D), BF), V((1536, D), BF), V((1536, 128), BF),
        V((1536, 48), BF), V((1024, D), F32), V((1536, 128), F32), V((1536, 128), F32), V((1536, 128), BF),
        V((1536, 128), BF), V((3, 32, 24, D), BF), V((2, 4, QB, D), BF), V((1024, D), F32), V((D, 1024), F32),
        V((D, 1024), F32), V((QB, QB), F32), pltpu.SemaphoreType.DMA((16,)), pltpu.SemaphoreType.DMA((2,)),
        pltpu.SemaphoreType.DMA((6,)), pltpu.SemaphoreType.DMA((6,)),
    ]
    scratch += gather_sems(2)
    return pl.pallas_call(
        k3_kernel,
        out_shape=[sds((1024, D), BF), sds((4, 288, D), F32), sds((4, 96, D), F32)],
        in_specs=[ANY()] * 7 + [INV()] + [ANY()] * 6 + [INV()] * 2 + [ANY()],
        out_specs=[INV()] * 3,
        scratch_shapes=scratch,
        compiler_params=pltpu.CompilerParams(
            vmem_limit_bytes=VMEM_LIMIT, collective_id=2, has_side_effects=True
        ),
    )(*args)


def fast(
    tokens, cotangent, segments, adapter_index, qkv_weight, out_weight, ffn_in_weight, ffn_out_weight,
    norm_gain, norm_bias, adapt_in, adapt_down, adapt_out, adapt_ffn,
):
    x = tokens[0]
    e = adapter_index[0, 0]
    pick = lambda table: lax.dynamic_index_in_dim(table[0], e, 0, False)
    a_in = pick(adapt_in).transpose(0, 2, 1)
    aqkv, ao, aff = a_in[0:3].reshape(48, D), a_in[3], a_in[4:6].reshape(32, D)
    adn = pick(adapt_down).T.reshape(16, 4, D).transpose(1, 0, 2)
    b_out = pick(adapt_out)
    bqkv, bo, bdn = b_out[0:3].reshape(48, D), b_out[3], b_out[4]
    bff = pick(adapt_ffn).reshape(32, FF)
    gb = jnp.stack([norm_gain[0, 0], norm_bias[0, 0], norm_gain[0, 1], norm_bias[0, 1]])
    freq = jnp.power(ROPE_BASE, -2.0 * jnp.arange(HEAD_DIM // 2, dtype=F32) / HEAD_DIM)
    freq = jnp.tile(freq, 4)[None]
    tag = jnp.where(jnp.arange(16)[:, None] == e, 1.0, jnp.zeros((1, D))).astype(BF)
    q, k, v, p, mixed, do, hf, lowq, done, cos, sin, fq, fk, ge, wq = kf_call(
        x, cotangent[0], segments, freq, aqkv, bqkv, ao, bo, aff, bff, adn, bdn, gb, tag,
        qkv_weight[0], out_weight[0], ffn_in_weight[0], ffn_out_weight[0],
    )
    q, k, v = (a.reshape(1536, D) for a in (q, k, v))
    dx, se, sl = k3_call(x, q, k, v, p, do, hf, ge, lowq, done, cos, sin, fq, fk, aqkv, bqkv, wq)
    g_in = jnp.concatenate([sl[:, :48], se[:, :48]], axis=1).reshape(4, 6, 16, D)
    g_dn = se[:, 80:144].reshape(4, 4, 16, D).transpose(0, 2, 1, 3).reshape(4, 16, FF)
    g_out = jnp.concatenate([sl[:, 48:], se[:, 48:80]], axis=1).reshape(4, 5, 16, D)
    g_ff = se[:, 144:272].reshape(4, 4, 2, 16, D).transpose(0, 2, 3, 1, 4).reshape(4, 2, 16, FF)
    return (
        mixed[None], dx[None], g_in.transpose(0, 1, 3, 2)[None], g_dn.transpose(0, 2, 1)[None], g_out[None], g_ff[None],
    )


def solution(mesh):
    here = fast if dict(mesh.shape) == {"batch": 16, "seq": 2} else shards
    return jax.shard_map(
        here,
        mesh=mesh,
        in_specs=(
            P("batch", "seq", None),
            P("batch", "seq", None),
            P("batch", None),
            P("batch", None),
            P(None, None, ("batch", "seq"), None),
            P(None, ("batch", "seq"), None),
            P(None, None, ("batch", "seq"), None),
            P(None, ("batch", "seq"), None),
            P(),
            P(),
            P(),
            P(),
            P(),
            P(),
        ),
        out_specs=(P("batch", "seq", None), P("batch", "seq", None), P(), P(), P(), P()),
        check_vma=False,
    )
```

```python
import functools
import math

import jax
import jax.numpy as jnp
import numpy as np
from jax import lax
from jax.experimental import pallas as pl
from jax.experimental.pallas import tpu as pltpu
from jax.sharding import PartitionSpec as P

HEADS = 12
HEAD_DIM = 64
ADAPTERS = 4
LAYERS = 1
HALF = 512
D = HEADS * HEAD_DIM
FF = 4 * D


EPSILON = 1e-06
ROPE_BASE = 1000.0
PRECISE = lax.Precision.HIGHEST


def shifted(array, axis, by):
    count = lax.axis_size(axis)
    pairs = [(i, i + by) for i in range(count) if 0 <= i + by < count]
    return lax.ppermute(array, axis, pairs)


def doc_positions(segment_ids):
    position_ids = jnp.arange(segment_ids.shape[-1], dtype=jnp.int32)
    starts_here = jnp.concatenate(
        [
            jnp.ones(segment_ids.shape[:-1] + (1,), dtype=jnp.bool_),
            segment_ids[..., 1:] != segment_ids[..., :-1],
        ],
        axis=-1,
    )
    doc_start = lax.cummax(jnp.where(starts_here, position_ids, 0), axis=segment_ids.ndim - 1)
    return (position_ids - doc_start).astype(jnp.float32)


def rope_tables(segment_ids):
    positions = doc_positions(segment_ids)
    frequency = jnp.power(ROPE_BASE, -2.0 * jnp.arange(HEAD_DIM // 2, dtype=jnp.float32) / HEAD_DIM)
    angles = positions[..., None] * frequency
    return (jnp.cos(angles), jnp.sin(angles))


def rotate(vectors, cosine_table, sine_table):
    half_dim = vectors.shape[-1] // 2
    first_half = vectors[..., :half_dim]
    second_half = vectors[..., half_dim:]
    cosine_rows = cosine_table[..., None, :]
    sine_rows = sine_table[..., None, :]
    return jnp.concatenate(
        [
            first_half * cosine_rows - second_half * sine_rows,
            second_half * cosine_rows + first_half * sine_rows,
        ],
        axis=-1,
    )


def norm_apply(residual, gain_row, bias_row):
    centre = residual - jnp.mean(residual, axis=-1, keepdims=True)
    spread = jnp.mean(centre * centre, axis=-1, keepdims=True)
    return centre * lax.rsqrt(spread + EPSILON) * gain_row + bias_row


def split_heads(merged, group_count):
    seqs_here, row_count, _ = merged.shape
    return merged.reshape(seqs_here, row_count, group_count, -1, HEAD_DIM).transpose(2, 0, 1, 3, 4)


def join_heads(grouped):
    group_count, seqs_here, row_count, heads_group, head_size = grouped.shape
    return grouped.transpose(1, 2, 0, 3, 4).reshape(
        seqs_here, row_count, group_count * heads_group * head_size
    )


def shards(
    tokens,
    cotangent,
    segments,
    adapter_index,
    qkv_weight,
    out_weight,
    ffn_in_weight,
    ffn_out_weight,
    norm_gain,
    norm_bias,
    adapt_in,
    adapt_down,
    adapt_out,
    adapt_ffn,
):
    seqs_here, tok_rows, model_width = tokens.shape
    heads_group = math.gcd(HEADS, 4)
    group_count = HEADS // heads_group
    score_scale = 1.0 / math.sqrt(HEAD_DIM)
    seq_count = lax.axis_size("seq")
    row_base = lax.axis_index("seq") * tok_rows
    shift_plan = []
    for distance in range(1, min(seq_count, HALF // tok_rows + 2)):
        row_count = min(tok_rows, HALF - (distance - 1) * tok_rows)
        if row_count > 0:
            shift_plan.append((distance, row_count))
            shift_plan.append((-distance, row_count))
    left_total = sum((plan_item[1] for plan_item in shift_plan if plan_item[0] > 0))
    key_rows = 2 * left_total + tok_rows
    key_places = {}
    passed_rows = 0
    for distance, row_count in shift_plan:
        if distance > 0:
            key_places[distance] = left_total - passed_rows - row_count
            key_places[-distance] = left_total + tok_rows + passed_rows
            passed_rows += row_count
    cosine_all, sine_all = rope_tables(segments)
    cosine_here = lax.dynamic_slice_in_dim(cosine_all, row_base, tok_rows, 1)
    sine_here = lax.dynamic_slice_in_dim(sine_all, row_base, tok_rows, 1)
    padded_ids = jnp.pad(segments, ((0, 0), (HALF, HALF)), constant_values=-1)
    key_ids = lax.dynamic_slice_in_dim(padded_ids, row_base - left_total + HALF, key_rows, 1)
    query_ids = lax.dynamic_slice_in_dim(segments, row_base, tok_rows, 1)
    offsets = (
        jnp.arange(tok_rows, dtype=jnp.int32)[:, None]
        - jnp.arange(key_rows, dtype=jnp.int32)[None, :]
        + left_total
    )
    visible = (query_ids[:, :, None] == key_ids[:, None, :]) & (jnp.abs(offsets) <= HALF)[None]
    slot_hits = adapter_index[:, 0][:, None] == jnp.arange(ADAPTERS, dtype=jnp.int32)[None, :]
    slot_low = slot_hits.astype(jnp.bfloat16)
    slot_full = slot_hits.astype(jnp.float32)

    def select_adapter(table):
        return jnp.einsum(
            "se,le...->ls...", slot_low, table, preferred_element_type=jnp.float32
        ).astype(jnp.bfloat16)

    def spread_slots(per_sequence):
        return jnp.einsum("se,s...->e...", slot_full, per_sequence, precision=PRECISE)

    chosen_in = select_adapter(adapt_in)
    chosen_down = select_adapter(adapt_down)
    chosen_out = select_adapter(adapt_out)
    chosen_ffn = select_adapter(adapt_ffn)

    def forward_group(items):
        query_block, key_block, value_block = items
        scores = (
            jnp.einsum(
                "sqhd,skhd->shqk", query_block, key_block, preferred_element_type=jnp.float32
            )
            * score_scale
        )
        scores = jnp.where(visible[:, None], scores, -1e30)
        biggest = jnp.max(scores, axis=-1, keepdims=True)
        lifted = jnp.exp(scores - biggest)
        row_total = jnp.sum(lifted, axis=-1, keepdims=True)
        probability = (lifted / row_total).astype(jnp.bfloat16)
        result = jnp.einsum(
            "shqk,skhd->sqhd", probability, value_block, preferred_element_type=jnp.float32
        )
        return (result.astype(jnp.bfloat16), (biggest + jnp.log(row_total))[..., 0])

    def backward_group(items):
        query_block, key_block, value_block, grad_block, log_total = items
        scores = (
            jnp.einsum(
                "sqhd,skhd->shqk", query_block, key_block, preferred_element_type=jnp.float32
            )
            * score_scale
        )
        scores = jnp.where(visible[:, None], scores, -1e30)
        probability = jnp.exp(scores - log_total[..., None])
        d_prob = jnp.einsum(
            "sqhd,skhd->shqk", grad_block, value_block, preferred_element_type=jnp.float32
        )
        delta = jnp.sum(probability * d_prob, axis=-1, keepdims=True)
        d_score = (probability * (d_prob - delta)).astype(jnp.bfloat16)
        d_query = (
            jnp.einsum("shqk,skhd->sqhd", d_score, key_block, preferred_element_type=jnp.float32)
            * score_scale
        )
        d_key = (
            jnp.einsum("shqk,sqhd->skhd", d_score, query_block, preferred_element_type=jnp.float32)
            * score_scale
        )
        d_value = jnp.einsum(
            "shqk,sqhd->skhd",
            probability.astype(jnp.bfloat16),
            grad_block,
            preferred_element_type=jnp.float32,
        )
        return (d_query, d_key, d_value)

    state = tokens.astype(jnp.float32)
    layer_index = 0
    w_qkv = lax.all_gather(qkv_weight[layer_index], ("batch", "seq"), axis=1, tiled=True)
    w_out = lax.all_gather(out_weight[layer_index], ("batch", "seq"), axis=0, tiled=True)
    w_in = lax.all_gather(ffn_in_weight[layer_index], ("batch", "seq"), axis=1, tiled=True)
    w_down = lax.all_gather(ffn_out_weight[layer_index], ("batch", "seq"), axis=0, tiled=True)
    held = [(w_qkv, w_out, w_in, w_down)]
    act_one = state.astype(jnp.bfloat16)
    low_qkv = jnp.einsum(
        "std,spdr->pstr",
        act_one,
        chosen_in[layer_index][:, 0:3],
        preferred_element_type=jnp.float32,
    ).astype(jnp.bfloat16)
    proj = jnp.einsum(
        "std,pde->pste", act_one, w_qkv, preferred_element_type=jnp.float32
    ) + jnp.einsum(
        "pstr,spre->pste",
        low_qkv,
        chosen_out[layer_index][:, 0:3],
        preferred_element_type=jnp.float32,
    )
    queries = (
        rotate(proj[0].reshape(seqs_here, tok_rows, HEADS, HEAD_DIM), cosine_here, sine_here)
        .astype(jnp.bfloat16)
        .reshape(seqs_here, tok_rows, model_width)
    )
    key_rot = (
        rotate(proj[1].reshape(seqs_here, tok_rows, HEADS, HEAD_DIM), cosine_here, sine_here)
        .astype(jnp.bfloat16)
        .reshape(seqs_here, tok_rows, model_width)
    )
    key_value = jnp.stack([key_rot, proj[2].astype(jnp.bfloat16)])
    edges = {}
    for step_by, row_count in shift_plan:
        if step_by > 0:
            outgoing = key_value[:, :, tok_rows - row_count :]
        else:
            outgoing = key_value[:, :, :row_count]
        edges[step_by] = shifted(outgoing, "seq", step_by)
    earlier = [edges[distance] for distance, row_count in reversed(shift_plan) if distance > 0]
    later = [edges[-distance] for distance, row_count in shift_plan if distance > 0]
    window = jnp.concatenate(earlier + [key_value] + later, axis=2)
    heads_out, log_total = lax.map(
        forward_group,
        (
            split_heads(queries, group_count),
            split_heads(window[0], group_count),
            split_heads(window[1], group_count),
        ),
    )
    attended = join_heads(heads_out)
    low_out = jnp.einsum(
        "std,sdr->str", attended, chosen_in[layer_index][:, 3], preferred_element_type=jnp.float32
    ).astype(jnp.bfloat16)
    branch = jnp.einsum(
        "std,de->ste", attended, w_out, preferred_element_type=jnp.float32
    ) + jnp.einsum(
        "str,sre->ste", low_out, chosen_out[layer_index][:, 3], preferred_element_type=jnp.float32
    )
    resid_one = state + branch
    hidden = norm_apply(resid_one, norm_gain[layer_index, 0], norm_bias[layer_index, 0])
    act_two = hidden.astype(jnp.bfloat16)
    low_ffn = jnp.einsum(
        "std,spdr->pstr",
        act_two,
        chosen_in[layer_index][:, 4:6],
        preferred_element_type=jnp.float32,
    ).astype(jnp.bfloat16)
    gate_up = jnp.einsum(
        "std,pdf->pstf", act_two, w_in, preferred_element_type=jnp.float32
    ) + jnp.einsum(
        "pstr,sprf->pstf", low_ffn, chosen_ffn[layer_index], preferred_element_type=jnp.float32
    )
    inner = (jax.nn.silu(gate_up[0]) * gate_up[1]).astype(jnp.bfloat16)
    low_down = jnp.einsum(
        "stf,sfr->str", inner, chosen_down[layer_index], preferred_element_type=jnp.float32
    ).astype(jnp.bfloat16)
    branch_two = jnp.einsum(
        "stf,fe->ste", inner, w_down, preferred_element_type=jnp.float32
    ) + jnp.einsum(
        "str,sre->ste", low_down, chosen_out[layer_index][:, 4], preferred_element_type=jnp.float32
    )
    resid_two = hidden + branch_two
    kept = [
        (
            act_one,
            low_qkv,
            queries,
            window,
            log_total,
            attended,
            low_out,
            resid_one,
            act_two,
            low_ffn,
            gate_up,
            inner,
            low_down,
            resid_two,
        )
    ]
    state = norm_apply(resid_two, norm_gain[layer_index, 1], norm_bias[layer_index, 1])
    mixed = state.astype(jnp.bfloat16)
    grad = cotangent.astype(jnp.float32)
    collected = [None] * LAYERS
    for layer_index in reversed(range(LAYERS)):
        (
            act_one,
            low_qkv,
            queries,
            window,
            log_total,
            attended,
            low_out,
            resid_one,
            act_two,
            low_ffn,
            gate_up,
            inner,
            low_down,
            resid_two,
        ) = kept[layer_index]
        w_qkv, w_out, w_in, w_down = held[layer_index]
        gain_two = norm_gain[layer_index, 1]
        bias_two = norm_bias[layer_index, 1]
        _, pull_two = jax.vjp(lambda residual: norm_apply(residual, gain_two, bias_two), resid_two)
        (d_resid_two,) = pull_two(grad)
        d_branch_two = d_resid_two.astype(jnp.bfloat16)
        d_low_down = jnp.einsum(
            "ste,sre->str",
            d_branch_two,
            chosen_out[layer_index][:, 4],
            preferred_element_type=jnp.float32,
        ).astype(jnp.bfloat16)
        g_out_down = jnp.einsum(
            "str,ste->sre", low_down, d_branch_two, preferred_element_type=jnp.float32
        )
        g_down = jnp.einsum("stf,str->sfr", inner, d_low_down, preferred_element_type=jnp.float32)
        d_inner = jnp.einsum(
            "ste,fe->stf", d_branch_two, w_down, preferred_element_type=jnp.float32
        ) + jnp.einsum(
            "str,sfr->stf", d_low_down, chosen_down[layer_index], preferred_element_type=jnp.float32
        )
        _, pull_act = jax.vjp(
            lambda gate_part, up_part: jax.nn.silu(gate_part) * up_part, gate_up[0], gate_up[1]
        )
        d_gate, d_up = pull_act(d_inner)
        d_gate_up = jnp.stack([d_gate, d_up]).astype(jnp.bfloat16)
        d_low_ffn = jnp.einsum(
            "pstf,sprf->pstr",
            d_gate_up,
            chosen_ffn[layer_index],
            preferred_element_type=jnp.float32,
        ).astype(jnp.bfloat16)
        g_ffn = jnp.einsum(
            "pstr,pstf->sprf", low_ffn, d_gate_up, preferred_element_type=jnp.float32
        )
        g_in_ffn = jnp.einsum(
            "std,pstr->spdr", act_two, d_low_ffn, preferred_element_type=jnp.float32
        )
        ffn_in_sum = spread_slots(g_in_ffn)
        ffn_down_sum = spread_slots(g_down)
        ffn_out_sum = spread_slots(g_out_down[:, None])
        ffn_ffn_sum = spread_slots(g_ffn)
        d_hidden = (
            d_resid_two
            + jnp.einsum("pstf,pdf->std", d_gate_up, w_in, preferred_element_type=jnp.float32)
            + jnp.einsum(
                "pstr,spdr->std",
                d_low_ffn,
                chosen_in[layer_index][:, 4:6],
                preferred_element_type=jnp.float32,
            )
        )
        gain_one = norm_gain[layer_index, 0]
        bias_one = norm_bias[layer_index, 0]
        _, pull_one = jax.vjp(lambda residual: norm_apply(residual, gain_one, bias_one), resid_one)
        (d_resid_one,) = pull_one(d_hidden)
        d_branch = d_resid_one.astype(jnp.bfloat16)
        d_low_out = jnp.einsum(
            "ste,sre->str",
            d_branch,
            chosen_out[layer_index][:, 3],
            preferred_element_type=jnp.float32,
        ).astype(jnp.bfloat16)
        g_out_att = jnp.einsum(
            "str,ste->sre", low_out, d_branch, preferred_element_type=jnp.float32
        )
        g_in_att = jnp.einsum(
            "std,str->sdr", attended, d_low_out, preferred_element_type=jnp.float32
        )
        d_attended = (
            jnp.einsum("ste,de->std", d_branch, w_out, preferred_element_type=jnp.float32)
            + jnp.einsum(
                "str,sdr->std",
                d_low_out,
                chosen_in[layer_index][:, 3],
                preferred_element_type=jnp.float32,
            )
        ).astype(jnp.bfloat16)
        d_query_heads, d_key_heads, d_value_heads = lax.map(
            backward_group,
            (
                split_heads(queries, group_count),
                split_heads(window[0], group_count),
                split_heads(window[1], group_count),
                split_heads(d_attended, group_count),
                log_total,
            ),
        )
        d_query = join_heads(d_query_heads)
        d_window = jnp.stack([join_heads(d_key_heads), join_heads(d_value_heads)])
        d_pair = d_window[:, :, left_total : left_total + tok_rows]
        for step_by, row_count in shift_plan:
            returning = lax.slice_in_dim(
                d_window, key_places[step_by], key_places[step_by] + row_count, axis=2
            )
            arrived = shifted(returning.astype(jnp.bfloat16), "seq", -step_by).astype(
                returning.dtype
            )
            if step_by > 0:
                d_pair = d_pair.at[:, :, tok_rows - row_count :].add(arrived)
            else:
                d_pair = d_pair.at[:, :, :row_count].add(arrived)
        d_query_rot = rotate(
            d_query.reshape(seqs_here, tok_rows, HEADS, HEAD_DIM), cosine_here, -sine_here
        ).reshape(seqs_here, tok_rows, model_width)
        d_key_rot = rotate(
            d_pair[0].reshape(seqs_here, tok_rows, HEADS, HEAD_DIM), cosine_here, -sine_here
        ).reshape(seqs_here, tok_rows, model_width)
        d_proj = jnp.stack([d_query_rot, d_key_rot, d_pair[1]]).astype(jnp.bfloat16)
        d_low_qkv = jnp.einsum(
            "pste,spre->pstr",
            d_proj,
            chosen_out[layer_index][:, 0:3],
            preferred_element_type=jnp.float32,
        ).astype(jnp.bfloat16)
        g_out_qkv = jnp.einsum(
            "pstr,pste->spre", low_qkv, d_proj, preferred_element_type=jnp.float32
        )
        g_in_qkv = jnp.einsum(
            "std,pstr->spdr", act_one, d_low_qkv, preferred_element_type=jnp.float32
        )
        grad = (
            d_resid_one
            + jnp.einsum("pste,pde->std", d_proj, w_qkv, preferred_element_type=jnp.float32)
            + jnp.einsum(
                "pstr,spdr->std",
                d_low_qkv,
                chosen_in[layer_index][:, 0:3],
                preferred_element_type=jnp.float32,
            )
        )
        att_in_sum = spread_slots(jnp.concatenate([g_in_qkv, g_in_att[:, None]], axis=1))
        att_out_sum = spread_slots(jnp.concatenate([g_out_qkv, g_out_att[:, None]], axis=1))
        collected[layer_index] = (
            jnp.concatenate([att_in_sum, ffn_in_sum], axis=1),
            ffn_down_sum,
            jnp.concatenate([att_out_sum, ffn_out_sum], axis=1),
            ffn_ffn_sum,
        )
    input_grad = grad.astype(jnp.bfloat16)
    stack_in = jnp.stack([collected[0][0]])
    stack_down = jnp.stack([collected[0][1]])
    stack_out = jnp.stack([collected[0][2]])
    stack_ffn = jnp.stack([collected[0][3]])
    stack_in, stack_down, stack_out, stack_ffn = lax.psum(
        (stack_in, stack_down, stack_out, stack_ffn), ("batch", "seq")
    )
    return (mixed, input_grad, stack_in, stack_down, stack_out, stack_ffn)


MESH = pl.DeviceIdType.MESH
NCHUNK = 10
ALL = slice(None)


class Gather:
    def __init__(self, sems, direct=(), diagonal=()):
        self.direct = direct
        self.diagonal = diagonal
        (
            self.zs, self.zr, self.xs, self.xr, self.ys, self.yr, self.ds, self.dr, self.es, self.er, self.fs, self.fr,
            self.cs, self.cr,
        ) = sems
        b = lax.axis_index("batch")
        self.b = b
        self.s = lax.axis_index("seq")
        self.core = lax.rem(b, 2)
        self.x = lax.rem(lax.div(b, 2), 2)
        self.z = lax.div(b, 4)
        self.za = lax.div(self.z, 2)
        self.zb = lax.rem(self.z, 2)
        self.devx = (b + 2 - 4 * self.x, self.s)
        self.devy = (b, 1 - self.s)
        self.devd = (b + 2 - 4 * self.x, 1 - self.s)
        self.devc = (b + 1 - 2 * self.core, self.s)
        self.devp = (b + 4 - 8 * self.zb, self.s)

    def column(self, dx, dy, dc):
        x = 1 - self.x if dx else self.x
        y = 1 - self.s if dy else self.s
        c = 1 - self.core if dc else self.core
        return (x * 2 + c) * 2 + y

    def devz(self, z):
        return (z * 4 + self.x * 2 + self.core, self.s)

    def copy(self, c, za, zb, k, half, dev, send, recv):
        v = self.view(c, za, zb, k, half)
        return pltpu.make_async_remote_copy(v, v, send, recv, device_id=dev, device_id_type=MESH)

    def to_z(self, c, z):
        return self.copy(
            c, self.za, self.zb, self.column(0, 0, 0), None, self.devz(z), self.zs.at[c, z], self.zr.at[c, self.z]
        )

    def from_z(self, c, z):
        return self.copy(
            c, lax.div(z, 2), lax.rem(z, 2), self.column(0, 0, 0), None, self.devz(z), self.zs.at[c, z], self.zr.at[c, z]
        )

    def on_x(self, c, arriving):
        return self.copy(c, ALL, ALL, self.column(arriving, 0, 0), None, self.devx, self.xs.at[c], self.xr.at[c])

    def on_y(self, c, arriving):
        return self.copy(c, ALL, ALL, self.column(0, arriving, 0), None, self.devy, self.ys.at[c], self.yr.at[c])

    def on_diagonal(self, c, arriving):
        return self.copy(c, ALL, ALL, self.column(arriving, arriving, 0), None, self.devd, self.ds.at[c], self.dr.at[c])

    def parity(self, c):
        return ALL if c in self.direct else self.zb

    def corner_x(self, c, arriving):
        k = self.column(arriving, 1, 0)
        return self.copy(c, ALL, self.parity(c), k, 0, self.devx, self.ds.at[c], self.dr.at[c])

    def corner_y(self, c, arriving):
        k = self.column(1, arriving, 0)
        return self.copy(c, ALL, self.parity(c), k, 1, self.devy, self.es.at[c], self.er.at[c])

    def corner_z(self, c, arriving):
        zb = 1 - self.zb if arriving else self.zb
        return self.copy(c, ALL, zb, self.column(1, 1, 0), None, self.devp, self.fs.at[c], self.fr.at[c])

    def on_core(self, c, kind, arriving):
        k = self.column(kind & 1, kind >> 1, arriving)
        return self.copy(c, ALL, ALL, k, None, self.devc, self.cs.at[c, kind], self.cr.at[c, kind])

    def others(self):
        z = self.z
        first = jnp.where(z == 0, 1, z - 1)
        second = jnp.where(z == 0, 2, jnp.where(z == 3, 1, z + 1))
        third = jnp.where(z <= 1, 3, 0)
        return first, second, third

    def partners(self):
        return [self.devx, self.devy, self.devc] + [self.devz(z) for z in self.others()]

    def barrier(self, devices):
        bar = pltpu.get_barrier_semaphore()
        for dev in devices:
            pl.semaphore_signal(bar, inc=1, device_id=dev, device_id_type=MESH)
        pl.semaphore_wait(bar, len(devices))

    def send_z(self, c):
        for z in self.others():
            self.to_z(c, z).start()

    def stage_z(self, c):
        for z in self.others():
            self.from_z(c, z).wait_recv()
        self.on_x(c, 0).start()
        self.on_y(c, 0).start()
        if c in self.diagonal:
            self.on_diagonal(c, 0).start()
        self.on_core(c, 0, 0).start()

    def stage_xy(self, c):
        self.on_x(c, 1).wait_recv()
        if c not in self.diagonal:
            self.corner_y(c, 0).start()
        self.on_core(c, 1, 0).start()
        self.on_y(c, 1).wait_recv()
        if c not in self.diagonal:
            self.corner_x(c, 0).start()
        self.on_core(c, 2, 0).start()
        if c in self.diagonal:
            self.on_diagonal(c, 1).wait_recv()
            self.on_core(c, 3, 0).start()

    def stage_corner(self, c):
        self.corner_x(c, 1).wait_recv()
        self.corner_y(c, 1).wait_recv()
        if c in self.direct:
            self.on_core(c, 3, 0).start()
        else:
            self.corner_z(c, 0).start()

    def stage_pair(self, c):
        self.corner_z(c, 1).wait_recv()
        self.on_core(c, 3, 0).start()

    def stage_core(self, c):
        for kind in range(4):
            self.on_core(c, kind, 1).wait_recv()

    def finish(self, c):
        for z in self.others():
            self.to_z(c, z).wait_send()
        self.on_x(c, 0).wait_send()
        self.on_y(c, 0).wait_send()
        for kind in range(4):
            self.on_core(c, kind, 0).wait_send()
        if c in self.diagonal:
            self.on_diagonal(c, 0).wait_send()
        else:
            self.corner_x(c, 0).wait_send()
            self.corner_y(c, 0).wait_send()
            if c not in self.direct:
                self.corner_z(c, 0).wait_send()


def gather_sems(chunks):
    one = pltpu.SemaphoreType.DMA((chunks,))
    four = pltpu.SemaphoreType.DMA((chunks, 4))
    return [four] * 2 + [one] * 10 + [four] * 2


BF = jnp.bfloat16
F32 = jnp.float32
QB = 256
PLAN = ((0, 3, False, True), (0, 4, False, True), (0, 5, True, True), (1, 5, True, True))
HALO_PLAN = ((2, 2), (3, 1))
NEG = -1e30
VMEM_LIMIT = int(63.9 * 2**20)


def nn(a, b):
    return jnp.dot(a, b, preferred_element_type=F32)


def nt(a, b):
    return lax.dot_general(a, b, (((1,), (1,)), ((), ())), preferred_element_type=F32)


def tn(a, b):
    return lax.dot_general(a, b, (((0,), (0,)), ((), ())), preferred_element_type=F32)


def iota(shape, dim):
    return lax.broadcasted_iota(jnp.int32, shape, dim)


def block_at(flip, block):
    return pl.multiple_of(jnp.where(flip == 1, 3 - block, block) * QB, QB)


def rope(vectors, cosine, sine):
    lane = iota((1, 128), 1)
    first = lax.rem(lane, HEAD_DIM) < HEAD_DIM // 2
    out = []
    for c in range(vectors.shape[1] // 128):
        part = vectors[:, c * 128 : (c + 1) * 128]
        other = jnp.where(first, pltpu.roll(part, 96, 1), pltpu.roll(part, 32, 1))
        out.append(part * cosine + other * sine)
    return jnp.concatenate(out, axis=1)


def fill_tables(flip, seg_ref, freq_ref, cos_ref, sin_ref, fq_ref, fk_ref, bias_ref):
    lane = iota((1, 128), 1)
    seg_row = seg_ref[...].astype(F32)
    starts = [
        jnp.sum((seg_row < float(d)).astype(F32), axis=1, keepdims=True) for d in (1, 2, 3)
    ]
    sign = jnp.where(lax.rem(lane, HEAD_DIM) < HEAD_DIM // 2, -1.0, 1.0)
    for w in range(12):
        block, part = divmod(w, 2)
        base = jnp.where(flip == 1, 7 - block, block) * QB + part * 128
        row = seg_ref[:, pl.ds(pl.multiple_of(base, 128), 128)].astype(F32)
        seg = jnp.broadcast_to(row, (128, 128)).T
        start = jnp.where(
            seg >= 3.0,
            starts[2],
            jnp.where(seg >= 2.0, starts[1], jnp.where(seg >= 1.0, starts[0], 0.0)),
        )
        pos = (iota((128, 128), 0) + base).astype(F32) - start
        angle = pos * freq_ref[...]
        rows = pl.ds(w * 128, 128)
        cos_ref[rows, :] = jnp.cos(angle)
        sin_ref[rows, :] = jnp.sin(angle) * sign
        hit = seg == lane.astype(F32)
        fq_ref[rows, :] = jnp.where(hit, 1.0, 0.0).astype(BF)
        fk_ref[rows, :] = jnp.where(hit | (lane >= 4), 0.0, NEG).astype(BF)
    gap = iota((QB, QB), 0) - iota((QB, QB), 1)
    gap = jnp.where(flip == 1, -gap, gap)
    bias_ref[0] = jnp.where(gap >= 0, 0.0, NEG)
    bias_ref[1] = jnp.where(gap <= 0, 0.0, NEG)


def qkv_rows(p, rb, xw, wq, aqkv, bblk, cos_ref, sin_ref, dest, low_ref):
    rows = pl.ds(pl.multiple_of(rb * 512, 512), 512)
    x = xw[rows, :]
    if p == 0:
        low = nt(x, aqkv[...]).astype(BF)
        low_ref[rows, :] = low
    else:
        low = low_ref[rows, :]
    proj = nn(x, wq[p].reshape(D, D)) + nn(low, bblk[p])
    if p < 2:
        proj = rope(proj, cos_ref[rows, :], sin_ref[rows, :])
    value = proj.astype(BF)
    if p == 0:
        value = value * jnp.asarray(0.125, BF)
    dest[pl.ds(rb * 2, 2)] = value.reshape(2, QB, D)


def prob_copies(n, src, dst, sem, s):
    full = (2 * n + 2) // 3
    cuts = ((0, 2), (2, full)) if full > 2 else ((0, 1), (1, 2))
    return [
        pltpu.make_async_copy(src.at[pl.ds(a, b - a)], dst.at[pl.ds(a, b - a)], sem.at[2 * s + i])
        for i, (a, b) in enumerate(cuts)
    ]


def attend_pair(
    qb, pair, step, q_ref, k_ref, v_ref, fq_ref, fk_ref, bias_ref, att_ref, linv_ref, mf_ref, p_hbm, stage, sem
):
    k0, n, tri_first, tri_last = PLAN[qb]
    rows = pl.ds(qb * QB, QB)
    kblocks = pl.ds(k0, n)
    krows = pl.ds(k0 * QB, n * QB)
    half = iota((1, 128), 1) >= HEAD_DIM
    lane = iota((1, 128), 1)
    slot = lax.rem(step, 2)

    def copy(s):
        return prob_copies(n, stage.at[pl.ds(s * 4, 4)], p_hbm.at[qb, pair], sem, s)

    @pl.when(pair >= 2)
    def _():
        for one in copy(slot):
            one.wait()

    lanes = pl.ds(pl.multiple_of(pair * 128, 128), 128)
    q2 = q_ref[qb, :, lanes]
    fq = fq_ref[rows, :]
    keys = jnp.concatenate([k_ref[kblocks, :, lanes].reshape(n * QB, 128), fk_ref[krows, :]], axis=1)
    v2 = v_ref[kblocks, :, lanes].reshape(n * QB, 128)
    outs = []
    for h in range(2):
        mine = half if h == 1 else jnp.logical_not(half)
        qm = jnp.where(mine, q2, jnp.zeros_like(q2))
        s = nt(jnp.concatenate([qm, fq], axis=1), keys)
        parts = [s[:, t * QB : (t + 1) * QB] for t in range(n)]
        if tri_last:
            parts[n - 1] = parts[n - 1] + bias_ref[0]
        if tri_first:
            parts[0] = parts[0] + bias_ref[1]
        s = jnp.concatenate(parts, axis=1)
        m = jnp.max(s, axis=1, keepdims=True)
        p = jnp.exp(s - m).astype(BF)
        for t in range(n):
            block, lane0 = divmod(h * n + t, 3)
            stage[slot * 4 + block, :, lane0 * QB : lane0 * QB + QB] = p[:, t * QB : (t + 1) * QB]
        if qb >= 2:
            low = 4 + 3 * (2 * pair + h)
            mf_ref[rows, :] = jnp.where((lane >= low) & (lane < low + 3), -m, mf_ref[rows, :])
        outs.append(nn(p, jnp.where(mine, v2, jnp.ones_like(v2))))
    inv = 1.0 / pltpu.roll(jnp.where(half, outs[0], outs[1]), HEAD_DIM, 1)
    att_ref[rows, lanes] = (jnp.where(half, outs[1], outs[0]) * inv).astype(BF)
    linv_ref[rows, lanes] = inv
    for one in copy(slot):
        one.start()


def drain_pairs(qb, p_hbm, stage, sem):
    for s in range(2):
        for one in prob_copies(PLAN[qb][1], stage.at[pl.ds(s * 4, 4)], p_hbm.at[qb, 0], sem, s):
            one.wait()


def norm_stats(r):
    centre = r - jnp.mean(r, axis=1, keepdims=True)
    rstd = lax.rsqrt(jnp.mean(centre * centre, axis=1, keepdims=True) + EPSILON)
    return centre * rstd, rstd


def norm_back(grad, xhat, rstd):
    return rstd * (
        grad
        - jnp.mean(grad, axis=1, keepdims=True)
        - xhat * jnp.mean(grad * xhat, axis=1, keepdims=True)
    )


def out_rows(rb, xw, att_ref, wo, ao, bo, gb, aff, xhat_ref, rstd_ref, act_ref, lowo_ref, lowf_ref):
    rows = pl.ds(pl.multiple_of(rb * QB, QB), QB)
    att = att_ref[rows, :]
    low = nt(att, ao[...]).astype(BF)
    lowo_ref[rows, :] = low
    branch = nn(att, wo[...].reshape(D, D)) + nn(low, bo[...])
    xhat, rstd = norm_stats(xw[rows, :].astype(F32) + branch)
    xhat_ref[rows, :] = xhat
    rstd_ref[rows, :] = jnp.broadcast_to(rstd, (QB, 128))
    act = (xhat * gb[0:1, :] + gb[1:2, :]).astype(BF)
    act_ref[rows, :] = act
    lowf_ref[rows, :] = nt(act, aff[...]).astype(BF)


def ffn_in_tile(n, rb, size, act_ref, lowf_ref, wi, wd, bg, bu, adn, big, lowd_ref, total_ref):
    start = pl.multiple_of(rb * size, size)
    rows = pl.ds(start, size)
    act = act_ref[rows, :]
    low = lowf_ref[rows, :]
    blocks = size // QB
    here = n * 4 + rb * blocks
    parts = []
    for c in range(3):
        lanes = slice(c * 256, c * 256 + 256)
        gate = nn(act, wi[n, 0, :, :, :, :, lanes].reshape(D, 256)) + nn(low, bg[n, :, lanes])
        up = nn(act, wi[n, 1, :, :, :, :, lanes].reshape(D, 256)) + nn(low, bu[n, :, lanes])
        parts.append((gate * (1.0 / (1.0 + jnp.exp(-gate))) * up).astype(BF))
        big[pl.ds(here, blocks), :, lanes] = gate.astype(BF).reshape(blocks, QB, 256)
        big[pl.ds(here + 16, blocks), :, lanes] = up.astype(BF).reshape(blocks, QB, 256)
    inner = jnp.concatenate(parts, axis=1)
    lowd_ref[rows, 0:16] += nt(inner, adn[n])
    total_ref[rows, :] += nn(inner, wd[lax.div(n, 2), lax.rem(n, 2)].reshape(D, D))


def ffn_out_rows(
    rb, flip, lowd_ref, bdn, xhat_ref, gb, cot, dtwo_ref, db2_ref, dlow_ref, mixed_ref, gbdn_ref
):
    start = pl.multiple_of(rb * QB, QB)
    rows = pl.ds(start, QB)
    low = lowd_ref[rows, 0:16].astype(BF)
    total = nn(low, bdn[...]) + dtwo_ref[rows, :]
    r = xhat_ref[rows, :] * gb[0:1, :] + gb[1:2, :] + total
    xhat, rstd = norm_stats(r)
    mixed_ref[pl.ds(block_at(flip, rb), QB), :] = (xhat * gb[2:3, :] + gb[3:4, :]).astype(BF)
    dtwo = norm_back(cot[rows, :].astype(F32) * gb[2:3, :], xhat, rstd)
    dtwo_ref[rows, :] = dtwo
    db2 = dtwo.astype(BF)
    db2_ref[rows, :] = db2
    dlow_ref[rows, :] = nt(db2, bdn[...]).astype(BF)
    gbdn_ref[...] += tn(low, db2)


def ffn_back_tile(
    n, start, size, db2_ref, dlow_ref, wd, wi, adn, bg, bu, big, lowf_ref, acc, dlf_ref, gadn_ref, gbf_ref
):
    rows = pl.ds(start, size)
    db2 = db2_ref[rows, :]
    dlow = dlow_ref[rows, :]
    blocks = size // QB
    here = n * 4 + lax.div(start, QB)
    down = wd[lax.div(n, 2), lax.rem(n, 2)].reshape(D, D)
    dgs, dus, inners = [], [], []
    for c in range(3):
        lanes = slice(c * 256, c * 256 + 256)
        dinner = nt(db2, down[lanes]) + nn(dlow, adn[n, :, lanes])
        gate = big[pl.ds(here, blocks), :, lanes].reshape(size, 256).astype(F32)
        up = big[pl.ds(here + 16, blocks), :, lanes].reshape(size, 256).astype(F32)
        sig = 1.0 / (1.0 + jnp.exp(-gate))
        silu = gate * sig
        inners.append((silu * up).astype(BF))
        dgs.append((dinner * up * (sig + silu * (1.0 - sig))).astype(BF))
        dus.append((dinner * silu).astype(BF))
    dg, du, inner = (jnp.concatenate(v, axis=1) for v in (dgs, dus, inners))
    acc[...] += nt(dg, wi[n, 0].reshape(D, D)) + nt(du, wi[n, 1].reshape(D, D))
    dlf_ref[...] += nt(dg, bg[n]) + nt(du, bu[n])
    gadn_ref[n] += tn(dlow, inner)
    low = lowf_ref[rows, :]
    gbf_ref[n] += jnp.where(iota((32, 1), 0) < 16, tn(low, dg), tn(low, du))


def hidden_back_rows(
    rb, off, acc, dlf_ref, aff, act_ref, dtwo_ref, xhat_ref, rstd_ref, gb, bo, ao, lowo_ref, att_ref,
    wo, linv_ref, h2, mf_ref, do_ref, hf_ref, gaff_ref, gbo_ref, gao_ref,
):
    start = pl.multiple_of(rb * QB, QB)
    rows = pl.ds(start, QB)
    local = pl.ds(pl.multiple_of(start - off, QB), QB)
    dlf = dlf_ref[local, :].astype(BF)
    dhid = dtwo_ref[rows, :] + acc[local, :] + nn(dlf, aff[...])
    gaff_ref[...] += tn(dlf, act_ref[rows, :])
    done = norm_back(dhid * gb[0:1, :], xhat_ref[rows, :], rstd_ref[rows, 0:1])
    dtwo_ref[rows, :] = done
    dbr = done.astype(BF)
    dlo = nt(dbr, bo[...]).astype(BF)
    att = att_ref[rows, :]
    gbo_ref[...] += tn(lowo_ref[rows, :], dbr)
    gao_ref[...] += tn(dlo, att)
    datt = (nt(dbr, wo[...].reshape(D, D)) + nn(dlo, ao[...])).astype(BF)
    do = (datt.astype(F32) * linv_ref[rows, :]).astype(BF)
    do_ref[rows, :] = do
    value = nn(do * att, h2[...]) + mf_ref[rows, :]
    lane = iota((1, 128), 1)
    role = jnp.where(lane < 40, lax.rem(lane + 2, 3), lax.rem(lane, 2))
    high = value.astype(BF)
    rest = value - high.astype(F32)
    mid = rest.astype(BF)
    last = (rest - mid.astype(F32)).astype(BF)
    hf_ref[rows, :] = jnp.where(role == 0, high, jnp.where(role == 1, mid, last))


def kf_kernel(
    x_hbm, cot_hbm, seg_ref, freq_ref, pick_ref, gain_ref, shift_ref, tin_hbm, tdn_hbm, tout_hbm, tff_hbm,
    wq_hbm, wo_hbm, wi_hbm, wd_hbm,
    q_hbm, k_hbm, v_hbm, p_hbm, mixed_hbm, do_hbm, hf_ref, lowq_hbm, done_hbm, cos_hbm, sin_hbm, fq_hbm, fk_hbm,
    ge_ref, gao_ref, tag_ref, aqkv, bqkv, wq_out,
    ao, bo, aff, adn, bdn, gb,
    gaff_ref, gadn_ref, gbo_ref, gbdn_ref, gbf_ref,
    wq, wo, wi, wd, big, xw, att, linv, xhat, dtwo, act, db2, cos, sin, fq, fk, bias, mf,
    lowq, lowo, lowf, dlow, acc, dlf, bblk, bg, bu, h2, mixed_ref, do_ref, rsem, tsem, wsem, xsem, osem, psem, hs, hr, *sems,
):
    flip = lax.axis_index("seq")
    cot = db2
    rstd = cos
    lowd = sin
    loads = []
    for i in range(4):
        loads.append(
            pltpu.make_async_copy(
                x_hbm.at[pl.ds(block_at(flip, i), QB)], xw.at[pl.ds(i * QB, QB)], xsem.at[i]
            )
        )
        loads.append(
            pltpu.make_async_copy(
                cot_hbm.at[pl.ds(block_at(flip, i), QB)], cot.at[pl.ds(i * QB, QB)], xsem.at[4 + i]
            )
        )
    tables = [
        (tin_hbm, big.at[pl.ds(0, ADAPTERS), pl.ds(0, 96)]),
        (tout_hbm, big.at[pl.ds(4, ADAPTERS), pl.ds(0, 80)]),
    ]
    for n in range(4):
        lanes = pl.ds(n * D, D)
        tables.append((tdn_hbm.at[:, :, lanes], big.at[pl.ds(8, ADAPTERS), pl.ds(16 * n, 16)]))
        tables.append((tff_hbm.at[:, :, lanes], big.at[pl.ds(12, ADAPTERS), pl.ds(32 * n, 32)]))
    tables = [pltpu.make_async_copy(a, b, tsem.at[i]) for i, (a, b) in enumerate(tables)]
    g = Gather(sems, direct=(0, 1, 2))

    def view(c, za, zb, k, half):
        cut = 384 if c < 3 else 640
        lanes = ALL if half is None else pl.ds(0, cut) if half == 0 else pl.ds(cut, D - cut)
        if c < 3:
            return wq.at[c, za, zb, k, :, lanes]
        if c == 3:
            return wo.at[za, zb, k, :, lanes]
        if c < 6:
            return wd.at[za, zb, k, pl.ds((c - 4) * 48, 48), lanes]
        return wi.at[c - 6, :, za, zb, k, :, lanes]

    g.view = view
    here = g.column(0, 0, 0)
    weights = [
        pltpu.make_async_copy(a, b, wsem.at[i])
        for i, (a, b) in enumerate(
            [(wq_hbm, wq.at[:, g.za, g.zb, here]), (wo_hbm, wo.at[g.za, g.zb, here]), (wd_hbm, wd.at[g.za, g.zb, here])]
            + [(wi_hbm.at[:, :, pl.ds(D * n, D)], wi.at[n, :, g.za, g.zb, here]) for n in range(4)]
        )
    ]
    for copy in weights:
        copy.start()
    g.barrier(g.partners())
    for copy in weights:
        copy.wait()
    for c in range(NCHUNK):
        g.send_z(c)
    halo = [
        pltpu.make_async_remote_copy(
            x_hbm.at[pl.ds(block_at(flip, 3 - i // 2) + i % 2 * 128, 128)], xw.at[pl.ds(1024 + i * 128, 128)],
            hs.at[i], hr.at[i], device_id=g.devy, device_id_type=MESH,
        )
        for i in range(4)
    ]

    kinds = {
        "z": g.stage_z, "x": g.stage_xy, "c": g.stage_corner, "p": g.stage_pair, "k": g.stage_core,
    }

    def tick(*steps):
        for step in steps:
            if step[0] == "h":
                halo[int(step[1])].start()
            else:
                kinds[step[0]](int(step[1]))

    tick("h0")
    for copy in loads + tables:
        copy.start()
    fill_tables(flip, seg_ref, freq_ref, cos, sin, fq, fk, bias)
    for copy in tables:
        copy.wait()
    e = pick_ref[0, 0]
    aqkv[...] = big[e, 0:48, :]
    ao[...] = big[e, 48:64, :]
    aff[...] = big[e, 64:96, :]
    bqkv[...] = big[4 + e, 0:48, :]
    bo[...] = big[4 + e, 48:64, :]
    bdn[...] = big[4 + e, 64:80, :]
    for n in range(4):
        adn[n] = big[8 + e, 16 * n : 16 * n + 16, :]
    tag_ref[...] = jnp.where(iota((16, 128), 0) == e, 1.0, 0.0).astype(BF)
    for i in range(2):
        gb[2 * i : 2 * i + 1, :] = gain_ref[i : i + 1, :]
        gb[2 * i + 1 : 2 * i + 2, :] = shift_ref[i : i + 1, :]
    rank = iota((48, 1), 0)
    for p in range(3):
        keep = (rank >= 16 * p) & (rank < 16 * p + 16)
        bblk[p] = jnp.where(keep, bqkv[...], jnp.zeros_like(bqkv[...]))
    rank = iota((32, 1), 0)
    for n in range(4):
        piece = big[12 + e, 32 * n : 32 * n + 32, :]
        bg[n] = jnp.where(rank < 16, piece, jnp.zeros_like(piece))
        bu[n] = jnp.where(rank >= 16, piece, jnp.zeros_like(piece))
    head = lax.div(iota((D, 128), 0), HEAD_DIM)
    spot = iota((D, 128), 1)
    h2[...] = jnp.where(lax.div(spot - 40, 2) == head, jnp.where(spot >= 40, -1.0, 0.0), 0.0).astype(BF)
    mf[...] = jnp.zeros_like(mf)
    dtwo[...] = jnp.zeros_like(dtwo)
    for ref in (gao_ref, gaff_ref, gadn_ref, gbo_ref, gbdn_ref, gbf_ref):
        ref[...] = jnp.zeros_like(ref)
    tick("z0", "z1", "x0", "z2", "x1", "h1", "z3")
    for copy in loads:
        copy.wait()
    tick("c0", "k0")
    q_ref, k_ref, v_ref = (big.at[pl.ds(i * 6, 6)] for i in range(3))
    stage = big.at[pl.ds(18, 8)]

    def qkv_page(p, first, last):
        def step(rb, _):
            qkv_rows(p, rb, xw, wq, aqkv, bblk, cos, sin, (q_ref, k_ref, v_ref)[p], lowq)
            return 0

        lax.fori_loop(first, last, step, 0)

    qkv_page(0, 0, 2)
    tick("x2", "z4", "c1", "k1")
    qkv_page(1, 0, 2)
    tick("h2", "z5", "x3", "c2", "k2")
    qkv_page(2, 0, 2)
    tick("h3", "z6")
    keep_wq = pltpu.make_async_copy(wq, wq_out, osem.at[9])
    keep_wq.start()
    for qb in range(4):

        def pair_step(pair, _, qb=qb):
            attend_pair(qb, pair, pair, q_ref, k_ref, v_ref, fq, fk, bias, att, linv, mf, p_hbm, stage, psem)
            return 0

        parts = 2 if qb < 2 else 3
        for part in range(parts):
            lax.fori_loop(part * 6 // parts, (part + 1) * 6 // parts, pair_step, 0)
            if part == parts - 1:
                drain_pairs(qb, p_hbm, stage, psem)
            tick(
                *(
                    (("x4", "z7", "c3"), ("p3",)),
                    (("x5", "z8", "c4"), ("z9", "k3", "p4")),
                    (("p5",), ("x7", "c6", "k5"), ()),
                    (("x8", "c7", "p6"), (), ("x9", "p7", "k6")),
                )[qb][part]
            )
        if qb == 1:
            for copy in halo:
                copy.wait_recv()
            for p in range(3):
                qkv_page(p, 2, 3)
            tick("x6", "c5", "k4")
            saves = [
                pltpu.make_async_copy(a, b, osem.at[i])
                for i, (a, b) in enumerate(
                    ((q_ref, q_hbm), (k_ref, k_hbm), (v_ref, v_hbm), (lowq, lowq_hbm), (cos, cos_hbm), (sin, sin_hbm), (fq, fq_hbm), (fk, fk_hbm))
                )
            ]
            for copy in saves:
                copy.start()
    for copy in saves:
        copy.wait()
    lowd[...] = jnp.zeros_like(lowd)

    def out_step(rb, _):
        out_rows(rb, xw, att, wo, ao, bo, gb, aff, xhat, rstd, act, lowo, lowf)
        return 0

    lax.fori_loop(0, 4, out_step, 0)
    tick("c8")

    def in_step(i, _):
        ffn_in_tile(lax.div(i, 2), lax.rem(i, 2), 512, act, lowf, wi, wd, bg, bu, adn, big, lowd, dtwo)
        return 0

    lax.fori_loop(0, 2, in_step, 0)
    tick("k7", "p8", "c9")
    lax.fori_loop(2, 4, in_step, 0)
    tick("k8", "p9")
    lax.fori_loop(4, 6, in_step, 0)
    tick("k9")
    lax.fori_loop(6, 8, in_step, 0)

    def down_step(rb, _):
        ffn_out_rows(rb, flip, lowd, bdn, xhat, gb, cot, dtwo, db2, dlow, mixed_ref, gbdn_ref)
        return 0

    lax.fori_loop(0, 4, down_step, 0)
    outs = [pltpu.make_async_copy(mixed_ref, mixed_hbm, rsem.at[0])]
    outs[0].start()

    def row_copies(rb):
        rows = pl.ds(pl.multiple_of(rb * QB, QB), QB)
        return (
            pltpu.make_async_copy(do_ref.at[rows], do_hbm.at[rows], rsem.at[1 + rb]),
            pltpu.make_async_copy(dtwo.at[rows], done_hbm.at[rows], rsem.at[5 + rb]),
        )

    def back_step(half, _):
        off = pl.multiple_of(half * 512, 512)
        acc[...] = jnp.zeros_like(acc)
        dlf[...] = jnp.zeros_like(dlf)

        def tile(n, _):
            ffn_back_tile(
                n, off, 512, db2, dlow, wd, wi, adn, bg, bu, big, lowf, acc, dlf, gadn_ref, gbf_ref
            )
            return 0

        lax.fori_loop(0, 4, tile, 0)

        def rows(i, _):
            hidden_back_rows(
                half * 2 + i, off, acc, dlf, aff, act, dtwo, xhat, rstd, gb, bo, ao, lowo, att, wo, linv, h2, mf,
                do_ref, hf_ref, gaff_ref, gbo_ref, gao_ref,
            )
            for copy in row_copies(half * 2 + i):
                copy.start()
            return 0

        lax.fori_loop(0, 2, rows, 0)
        return 0

    lax.fori_loop(0, 2, back_step, 0)
    for rb in range(4):
        outs.extend(row_copies(rb))
    ge_ref[0:32] = gaff_ref[...].astype(BF)
    ge_ref[32:48] = gbo_ref[...].astype(BF)
    ge_ref[48:64] = gbdn_ref[...].astype(BF)
    ge_ref[64:128] = gadn_ref[...].reshape(64, D).astype(BF)
    ge_ref[128:256] = gbf_ref[...].reshape(128, D).astype(BF)
    keep_wq.wait()
    for copy in outs:
        copy.wait()
    for copy in halo:
        copy.wait_send()
    for c in range(NCHUNK):
        g.finish(c)


def k3_kernel(
    x_hbm, q_hbm, k_hbm, v_hbm, p_hbm, do_hbm, hf_hbm, ge, gao, tag, lowq_hbm, done_hbm, cos_hbm, sin_hbm,
    fq_hbm, fk_hbm, aqkv, bqkv, wq_hbm,
    dx_hbm, gin_ref, gdn_ref, gout_ref, gff_ref,
    ga_ref, gbq_ref, dproj, eg, lg, e_in, e_half, rs_e, rs_t, gl_out, gl_in, l_half, rs_l, dx_ref,
    xw, q, k, v, do, hf, lowq, done, cos, sin, fq, fk, wq, stage, dq, dkT, dvT, bias, sem, psem, hs, hr,
    es, er, ts, tr, ls, lr, dsem, *sems,
):
    flip = lax.axis_index("seq")
    g = Gather(sems, diagonal=(1,))

    def part(src, dst, start, size):
        return src.at[pl.ds(start, size)], dst.at[pl.ds(start, size)]

    table = (
        part(q_hbm, q, 0, 256), part(k_hbm, k, 0, 768), part(v_hbm, v, 0, 768), part(do_hbm, do, 0, 256),
        part(hf_hbm, hf, 0, 1024),
        part(q_hbm, q, 256, 1280), part(k_hbm, k, 768, 768), part(v_hbm, v, 768, 768), part(do_hbm, do, 256, 768),
        (lowq_hbm, lowq), (done_hbm, done), (cos_hbm, cos), (sin_hbm, sin), (fq_hbm, fq), (fk_hbm, fk), (wq_hbm, wq),
    )
    loads = [pltpu.make_async_copy(a, b, sem.at[i]) for i, (a, b) in enumerate(table)]
    for i in range(4):
        loads.append(
            pltpu.make_async_copy(
                x_hbm.at[pl.ds(block_at(flip, i), QB)], xw.at[pl.ds(i * QB, QB)], sem.at[16 + i]
            )
        )
    for copy in loads:
        copy.start()

    def view(c, za, zb, k, half):
        lanes = ALL if half is None else pl.ds(0, 256) if half == 0 else pl.ds(256, 128)
        return (eg, lg)[c].at[za, zb, k, :, lanes]

    g.view = view

    def plane(d):
        return lax.rem(g.b + d, 16)

    def scatter(src, dst, send, recv):
        def copy(d):
            to = plane(d)
            return pltpu.make_async_remote_copy(
                src(to), dst.at[g.b], send.at[d], recv.at[d], device_id=(to, g.s), device_id_type=MESH
            )

        def arrival(d):
            return pltpu.make_async_remote_copy(
                src(0), dst.at[plane(16 - d)], send.at[d], recv.at[d], device_id=(plane(d), g.s), device_id_type=MESH
            )

        def each(what):
            def step(d, _):
                what(d)
                return 0

            lax.fori_loop(1, 16, step, 0)

        return (
            lambda: each(lambda d: copy(d).start()),
            lambda: each(lambda d: arrival(d).wait_recv()),
            lambda: each(lambda d: copy(d).wait_send()),
        )

    def piece(ref, size):
        def at(to):
            rows = pl.ds(pl.multiple_of(lax.div(to, 2) * size, size), size)
            return ref.at[rows, pl.ds(pl.multiple_of(lax.rem(to, 2) * 384, 128), 384)]

        return at

    send_e, wait_e, end_e = scatter(piece(e_half, 16), rs_e, es, er)
    send_t, wait_t, end_t = scatter(lambda to: tag, rs_t, ts, tr)
    send_l, wait_l, end_l = scatter(piece(l_half, 8), rs_l, ls, lr)

    bar = pltpu.get_barrier_semaphore()

    def greet(d, _):
        pl.semaphore_signal(bar, inc=1, device_id=(plane(d), g.s), device_id_type=MESH)
        return 0

    lax.fori_loop(1, 16, greet, 0)
    for dev in (g.devy, g.devd):
        pl.semaphore_signal(bar, inc=1, device_id=dev, device_id_type=MESH)
    pl.semaphore_wait(bar, 17)
    halo = []
    for i, (src, dst) in enumerate(
        (
            (do_hbm.at[pl.ds(768, QB)], do.at[pl.ds(1024, QB)]),
            (do_hbm.at[pl.ds(512, QB)], do.at[pl.ds(1280, QB)]),
            (hf_hbm.at[pl.ds(768, QB)], hf.at[pl.ds(1024, QB)]),
            (hf_hbm.at[pl.ds(512, QB)], hf.at[pl.ds(1280, QB)]),
            (ge.at[pl.ds(pl.multiple_of((1 - flip) * 128, 16), 128)], e_in),
            (gl_out.at[pl.ds(pl.multiple_of((1 - flip) * 64, 16), 64)], gl_in),
        )
    ):
        halo.append(
            pltpu.make_async_remote_copy(
                src, dst, hs.at[i], hr.at[i], device_id=g.devy, device_id_type=MESH
            )
        )
    for copy in (halo[4], halo[0], halo[1], halo[2], halo[3]):
        copy.start()
    send_t()

    def total_of(ref):
        totals = [0.0] * ADAPTERS
        for b in range(16):
            value = ref[b].astype(F32)
            for e in range(ADAPTERS):
                weight = rs_t[b, e : e + 1, :].astype(F32)
                totals[e] = totals[e] + value * jnp.concatenate([weight] * 3, axis=1)
        return jnp.concatenate(totals, axis=0).astype(BF)

    def own_piece(ref, size):
        rows = pl.ds(pl.multiple_of(lax.div(g.b, 2) * size, size), size)
        return ref[rows, pl.ds(pl.multiple_of(g.core * 384, 128), 384)]

    dkT[...] = jnp.zeros_like(dkT)
    dvT[...] = jnp.zeros_like(dvT)
    ga_ref[...] = jnp.zeros_like(ga_ref)
    gbq_ref[...] = jnp.zeros_like(gbq_ref)
    gap = iota((QB, QB), 0) - iota((QB, QB), 1)
    gap = jnp.where(flip == 1, -gap, gap)
    bias[...] = jnp.where(gap <= 0, 0.0, NEG)
    half = iota((1, 128), 1) >= HEAD_DIM
    for copy in loads[:5]:
        copy.wait()

    def picks(pair, first, width):
        head = 2 * pair + lax.div(iota((128, 256), 1), 128)
        row = iota((128, 256), 0) - first - width * head
        return jnp.where((row >= 0) & (row < width), 1.0, 0.0).astype(BF)

    for qb in range(4):
        k0, n, _, _ = PLAN[qb]
        own = min(4 - k0, n)
        rows = pl.ds(qb * QB, QB)
        krows = pl.ds(k0 * QB, n * QB)

        def fetch(pair, s, qb=qb, n=n):
            return prob_copies(n, p_hbm.at[qb, pair], stage.at[s], psem, s)

        for one in fetch(0, 0):
            one.start()

        def pair_step(pair, _, k0=k0, n=n, own=own, rows=rows, krows=krows, fetch=fetch):
            slot = lax.rem(pair, 2)
            for one in fetch(pair, slot):
                one.wait()

            @pl.when(pair < 5)
            def _():
                for one in fetch(pair + 1, 1 - slot):
                    one.start()

            lanes = pl.ds(pl.multiple_of(pair * 128, 128), 128)
            do2 = do[rows, lanes]
            ndl = nn(hf[rows, :], picks(pair, 40, 2))
            k2 = k[krows, lanes]
            v2 = v[krows, lanes]
            qT = q[rows, lanes].T
            doT = do2.T
            dqs = []
            for h in range(2):
                mine = half if h == 1 else jnp.logical_not(half)
                spots = [divmod(h * n + t, 3) for t in range(n)]
                p = jnp.concatenate([stage[slot, i, :, j * QB : j * QB + QB] for i, j in spots], axis=1)
                dp = nt(jnp.where(mine, do2, jnp.zeros_like(do2)), v2)
                d = ndl[:, h * 128 : (h + 1) * 128]
                ds = (p.astype(F32) * (dp + jnp.concatenate([d] * (2 * n), axis=1))).astype(BF)
                dqs.append(nn(ds, k2))
                hr = pl.ds(pl.multiple_of(pair * 128 + h * 64, 64), 64)
                kc = pl.ds(k0 * QB, own * QB)
                dkT[hr, kc] += nn(qT[h * 64 : (h + 1) * 64], ds[:, 0 : own * QB])
                dvT[hr, kc] += nn(doT[h * 64 : (h + 1) * 64], p[:, 0 : own * QB])
            dq[rows, lanes] = jnp.where(half, dqs[1], dqs[0]) * 0.125
            return 0

        lax.fori_loop(0, 6, pair_step, 0)
        if qb == 0:
            halo[4].wait_recv()
            mine = ge[pl.ds(pl.multiple_of(flip * 128, 16), 128), :]
            e_half[...] = (mine.astype(F32) + e_in[...].astype(F32)).astype(BF)
            send_e()
            for copy in loads[5:9]:
                copy.wait()
        elif qb == 1:
            rs_e[g.b] = own_piece(e_half, 16)
            rs_t[g.b] = tag[...]
            wait_e()
            wait_t()
            eg[g.za, g.zb, g.column(0, 0, 0)] = total_of(rs_e)
            g.send_z(0)
        elif qb == 2:
            g.stage_z(0)
        else:
            g.stage_xy(0)

    for copy in loads[9:]:
        copy.wait()
    for copy in halo[:4]:
        copy.wait_recv()
    for i, (k0, n) in enumerate(HALO_PLAN):
        rows = pl.ds(1024 + i * QB, QB)
        krows = pl.ds(k0 * QB, n * QB)

        def halo_step(pair, _, k0=k0, n=n, rows=rows, krows=krows):
            lanes = pl.ds(pl.multiple_of(pair * 128, 128), 128)
            do2 = do[rows, lanes]
            q2 = q[rows, lanes]
            feats = hf[rows, :]
            ndl = nn(feats, picks(pair, 40, 2))
            nm = nn(feats, picks(pair, 4, 3))
            keys = jnp.concatenate([k[krows, lanes], fk[krows, :]], axis=1)
            v2 = v[krows, lanes]
            qT = q2.T
            doT = do2.T
            for h in range(2):
                mine = half if h == 1 else jnp.logical_not(half)
                s = nt(jnp.concatenate([jnp.where(mine, q2, jnp.zeros_like(q2)), fq[rows, :]], axis=1), keys)
                parts = [s[:, t * QB : (t + 1) * QB] for t in range(n)]
                parts[0] = parts[0] + bias[...]
                s = jnp.concatenate(parts, axis=1)
                m = nm[:, h * 128 : (h + 1) * 128]
                p = jnp.exp(s + jnp.concatenate([m] * (2 * n), axis=1))
                dp = nt(jnp.where(mine, do2, jnp.zeros_like(do2)), v2)
                d = ndl[:, h * 128 : (h + 1) * 128]
                ds = (p * (dp + jnp.concatenate([d] * (2 * n), axis=1))).astype(BF)
                hr = pl.ds(pl.multiple_of(pair * 128 + h * 64, 64), 64)
                kc = pl.ds(k0 * QB, n * QB)
                dkT[hr, kc] += nn(qT[h * 64 : (h + 1) * 64], ds)
                dvT[hr, kc] += nn(doT[h * 64 : (h + 1) * 64], p.astype(BF))
            return 0

        lax.fori_loop(0, 6, halo_step, 0)
        (g.stage_corner, g.stage_pair)[i](0)

    lane = lax.div(iota((1, 48), 1), 16)
    rank = lax.div(iota((48, 1), 0), 16)

    def proj_step(rb, _):
        start = pl.multiple_of(rb * QB, QB)
        rows = pl.ds(start, QB)
        cosine = cos[rows, :]
        sine = -sin[rows, :]
        low = lowq[rows, :]
        dlow = jnp.zeros((QB, 48), F32)
        for p in range(3):
            if p == 0:
                d = rope(dq[rows, :], cosine, sine)
            else:
                src = (dkT, dvT)[p - 1]
                d = jnp.concatenate([src[pl.ds(c * 128, 128), rows].T for c in range(6)], axis=1)
                if p == 1:
                    d = rope(d, cosine, sine)
            d = d.astype(BF)
            dproj[p, rows, :] = d
            dlow += jnp.where(lane == p, nt(d, bqkv[...]), 0.0)
            gbq_ref[...] += jnp.where(rank == p, tn(low, d), 0.0)
        dlow = dlow.astype(BF)
        lowq[rows, :] = dlow
        ga_ref[...] += tn(dlow, xw[rows, :])
        return 0

    lax.fori_loop(0, 4, proj_step, 0)
    gl_out[0:48] = ga_ref[...].astype(BF)
    gl_out[48:96] = gbq_ref[...].astype(BF)
    gl_out[96:112] = gao[...].astype(BF)
    gl_out[112:128] = jnp.zeros((16, D), BF)
    halo[5].start()

    def dx_rows(rb):
        rows = pl.ds(rb * QB, QB)
        total = done[rows, :] + nn(lowq[rows, :], aqkv[...])
        for p in range(3):
            total += nt(dproj[p, rows, :], wq[p].reshape(D, D))
        dx_ref[rows, :] = total.astype(BF)
        copy = pltpu.make_async_copy(dx_ref.at[rows], dx_hbm.at[pl.ds(block_at(flip, rb), QB)], dsem.at[rb])
        copy.start()
        return copy

    def blocks(ref):
        for z in range(4):
            for xx in range(2):
                for core in range(2):
                    for y in range(2):
                        yield (
                            y * 8 + z * 2 + xx, core * 384,
                            ref[z // 2, z % 2, (xx * 2 + core) * 2 + y].astype(F32),
                        )

    def place_early():
        for group, lane0, value in blocks(eg):
            lanes = slice(lane0, lane0 + 384)
            for e in range(ADAPTERS):
                rows = value[16 * e : 16 * e + 16]
                if group < 2:
                    gin_ref[e, 64 + 16 * group : 80 + 16 * group, lanes] = rows
                elif group < 4:
                    gout_ref[e, 16 + 16 * group : 32 + 16 * group, lanes] = rows
                elif group < 8:
                    at = (group - 4) * D + lane0
                    gdn_ref[e, :, at : at + 384] = rows
                else:
                    at = (group - 8) // 2 * D + lane0
                    first = 16 * (group % 2)
                    gff_ref[e, first : first + 16, at : at + 384] = rows

    def place_late():
        for group, lane0, value in blocks(lg):
            lanes = slice(lane0, lane0 + 384)
            for e in range(ADAPTERS):
                rows = value[8 * e : 8 * e + 8]
                if group < 6:
                    gin_ref[e, 8 * group : 8 * group + 8, lanes] = rows
                elif group < 12:
                    gout_ref[e, 8 * group - 48 : 8 * group - 40, lanes] = rows
                elif group < 14:
                    gin_ref[e, 8 * group - 48 : 8 * group - 40, lanes] = rows

    tails = [dx_rows(0)]
    halo[5].wait_recv()
    mine = gl_out[pl.ds(pl.multiple_of(flip * 64, 16), 64), :]
    l_half[...] = mine.astype(F32) + gl_in[...].astype(F32)
    send_l()
    tails.append(dx_rows(1))
    rs_l[g.b] = own_piece(l_half, 8)
    wait_l()
    lg[g.za, g.zb, g.column(0, 0, 0)] = total_of(rs_l)
    g.send_z(1)
    tails.append(dx_rows(2))
    g.stage_z(1)
    tails.append(dx_rows(3))
    g.stage_core(0)
    place_early()
    g.stage_xy(1)
    for copy in halo:
        copy.wait_send()
    end_e()
    end_t()
    end_l()
    g.finish(0)
    g.stage_core(1)
    place_late()
    g.finish(1)
    for copy in tails:
        copy.wait()


def sds(shape, dtype):
    return jax.ShapeDtypeStruct(shape, dtype)


ANY = functools.partial(pl.BlockSpec, memory_space=pl.ANY)
INV = functools.partial(pl.BlockSpec, memory_space=pltpu.VMEM)


def kf_call(*args):
    outs = [
        (ANY, (6, QB, D), BF), (ANY, (6, QB, D), BF), (ANY, (6, QB, D), BF), (ANY, (4, 6, 4, QB, D), BF),
        (ANY, (1024, D), BF), (ANY, (1024, D), BF), (INV, (1024, 128), BF),
        (ANY, (1536, 48), BF), (ANY, (1024, D), F32), (ANY, (1536, 128), F32), (ANY, (1536, 128), F32),
        (ANY, (1536, 128), BF), (ANY, (1536, 128), BF),
        (INV, (256, D), BF), (INV, (16, D), F32), (INV, (16, 128), BF), (INV, (48, D), BF), (INV, (48, D), BF),
        (ANY, (3, 2, 2, 8, 24, D), BF),
    ]
    V = pltpu.VMEM
    scratch = [
        V((16, D), BF), V((16, D), BF), V((32, D), BF), V((4, 16, D), BF), V((16, D), BF), V((4, D), F32),
        V((32, D), F32), V((4, 16, D), F32), V((16, D), F32), V((16, D), F32), V((4, 32, D), F32),
        V((3, 2, 2, 8, 24, D), BF), V((2, 2, 8, 24, D), BF), V((4, 2, 2, 2, 8, 24, D), BF), V((2, 2, 8, 96, D), BF),
        V((32, QB, D), BF), V((1536, D), BF), V((1024, D), BF), V((1024, D), F32),
        V((1024, D), F32), V((1024, D), F32), V((1024, D), BF), V((1024, D), BF),
        V((1536, 128), F32), V((1536, 128), F32), V((1536, 128), BF), V((1536, 128), BF), V((2, QB, QB), F32),
        V((1024, 128), F32), V((1536, 48), BF), V((1024, 16), BF), V((1024, 32), BF),
        V((1024, 16), BF), V((512, D), F32), V((512, 32), F32), V((3, 48, D), BF),
        V((4, 32, D), BF), V((4, 32, D), BF), V((D, 128), BF), V((1024, D), BF), V((1024, D), BF),
        pltpu.SemaphoreType.DMA((9,)), pltpu.SemaphoreType.DMA((10,)), pltpu.SemaphoreType.DMA((7,)), pltpu.SemaphoreType.DMA((8,)), pltpu.SemaphoreType.DMA((10,)),
        pltpu.SemaphoreType.DMA((4,)), pltpu.SemaphoreType.DMA((4,)), pltpu.SemaphoreType.DMA((4,)),
    ]
    scratch += gather_sems(NCHUNK)
    return pl.pallas_call(
        kf_kernel,
        out_shape=[sds(s, t) for _, s, t in outs],
        in_specs=[ANY()] * 2 + [INV()] * 2 + [pl.BlockSpec(memory_space=pltpu.SMEM)] + [INV()] * 2 + [ANY()] * 8,
        out_specs=[m() for m, _, _ in outs],
        scratch_shapes=scratch,
        compiler_params=pltpu.CompilerParams(
            vmem_limit_bytes=VMEM_LIMIT, collective_id=1, has_side_effects=True
        ),
    )(*args)


def k3_call(*args):
    V = pltpu.VMEM
    S = pltpu.SemaphoreType.DMA
    scratch = [
        V((48, D), F32), V((48, D), F32), V((3, 1024, D), BF), V((2, 2, 8, 64, 384), BF), V((2, 2, 8, 32, 384), BF),
        V((128, D), BF), V((128, D), BF), V((16, 16, 384), BF), V((16, 16, 128), BF), V((128, D), BF), V((64, D), BF),
        V((64, D), F32), V((16, 8, 384), F32), V((1024, D), BF),
        V((1024, D), BF), V((1536, D), BF), V((1536, D), BF), V((1536, D), BF), V((1536, D), BF), V((1536, 128), BF),
        V((1536, 48), BF), V((1024, D), F32), V((1536, 128), F32), V((1536, 128), F32), V((1536, 128), BF),
        V((1536, 128), BF), V((3, 2, 2, 8, 24, D), BF), V((2, 4, QB, D), BF), V((1024, D), F32), V((D, 1024), F32),
        V((D, 1024), F32), V((QB, QB), F32), S((20,)), S((4,)), S((6,)), S((6,)),
        S((16,)), S((16,)), S((16,)), S((16,)), S((16,)), S((16,)), S((4,)),
    ]
    return pl.pallas_call(
        k3_kernel,
        out_shape=[
            sds((1024, D), BF), sds((4, 96, D), F32), sds((4, 16, FF), F32), sds((4, 80, D), F32), sds((4, 32, FF), F32),
        ],
        in_specs=[ANY()] * 7 + [INV()] * 3 + [ANY()] * 6 + [INV()] * 2 + [ANY()],
        out_specs=[ANY()] + [INV()] * 4,
        scratch_shapes=scratch + gather_sems(2),
        compiler_params=pltpu.CompilerParams(
            vmem_limit_bytes=VMEM_LIMIT, collective_id=2, has_side_effects=True
        ),
    )(*args)


def fast(
    tokens, cotangent, segments, adapter_index, qkv_weight, out_weight, ffn_in_weight, ffn_out_weight,
    norm_gain, norm_bias, adapt_in, adapt_down, adapt_out, adapt_ffn,
):
    x = tokens[0]
    freq = np.power(np.float32(ROPE_BASE), np.float32(-2.0 / HEAD_DIM) * np.arange(HEAD_DIM // 2, dtype=np.float32))
    freq = np.tile(freq.astype(np.float32), 4)[None]
    q, k, v, p, mixed, do, hf, lowq, done, cos, sin, fq, fk, ge, gao, tag, aqkv, bqkv, wq = kf_call(
        x, cotangent[0], segments, freq, adapter_index, norm_gain[0], norm_bias[0],
        adapt_in[0].transpose(0, 1, 3, 2).reshape(ADAPTERS, 96, D), adapt_down[0].transpose(0, 2, 1),
        adapt_out[0].reshape(ADAPTERS, 80, D), adapt_ffn[0].reshape(ADAPTERS, 32, FF),
        qkv_weight[0], out_weight[0], ffn_in_weight[0], ffn_out_weight[0],
    )
    q, k, v = (a.reshape(1536, D) for a in (q, k, v))
    dx, g_in, g_dn, g_out, g_ff = k3_call(
        x, q, k, v, p, do, hf, ge, gao, tag, lowq, done, cos, sin, fq, fk, aqkv, bqkv, wq
    )
    return (
        mixed[None], dx[None], g_in.reshape(ADAPTERS, 6, 16, D).transpose(0, 1, 3, 2)[None],
        g_dn.transpose(0, 2, 1)[None], g_out.reshape(ADAPTERS, 5, 16, D)[None], g_ff.reshape(ADAPTERS, 2, 16, FF)[None],
    )


def solution(mesh):
    here = fast if dict(mesh.shape) == {"batch": 16, "seq": 2} else shards
    return jax.shard_map(
        here,
        mesh=mesh,
        in_specs=(
            P("batch", "seq", None),
            P("batch", "seq", None),
            P("batch", None),
            P("batch", None),
            P(None, None, ("batch", "seq"), None),
            P(None, ("batch", "seq"), None),
            P(None, None, ("batch", "seq"), None),
            P(None, ("batch", "seq"), None),
            P(),
            P(),
            P(),
            P(),
            P(),
            P(),
        ),
        out_specs=(P("batch", "seq", None), P("batch", "seq", None), P(), P(), P(), P()),
        check_vma=False,
    )
```

```python
import functools
import math

import jax
import jax.numpy as jnp
import numpy as np
from jax import lax
from jax.experimental import pallas as pl
from jax.experimental.pallas import tpu as pltpu
from jax.sharding import PartitionSpec as P

HEADS = 12
HEAD_DIM = 64
ADAPTERS = 4
LAYERS = 1
HALF = 512
D = HEADS * HEAD_DIM
FF = 4 * D


EPSILON = 1e-06
ROPE_BASE = 1000.0
PRECISE = lax.Precision.HIGHEST


def shifted(array, axis, by):
    count = lax.axis_size(axis)
    pairs = [(i, i + by) for i in range(count) if 0 <= i + by < count]
    return lax.ppermute(array, axis, pairs)


def doc_positions(segment_ids):
    position_ids = jnp.arange(segment_ids.shape[-1], dtype=jnp.int32)
    starts_here = jnp.concatenate(
        [
            jnp.ones(segment_ids.shape[:-1] + (1,), dtype=jnp.bool_),
            segment_ids[..., 1:] != segment_ids[..., :-1],
        ],
        axis=-1,
    )
    doc_start = lax.cummax(jnp.where(starts_here, position_ids, 0), axis=segment_ids.ndim - 1)
    return (position_ids - doc_start).astype(jnp.float32)


def rope_tables(segment_ids):
    positions = doc_positions(segment_ids)
    frequency = jnp.power(ROPE_BASE, -2.0 * jnp.arange(HEAD_DIM // 2, dtype=jnp.float32) / HEAD_DIM)
    angles = positions[..., None] * frequency
    return (jnp.cos(angles), jnp.sin(angles))


def rotate(vectors, cosine_table, sine_table):
    half_dim = vectors.shape[-1] // 2
    first_half = vectors[..., :half_dim]
    second_half = vectors[..., half_dim:]
    cosine_rows = cosine_table[..., None, :]
    sine_rows = sine_table[..., None, :]
    return jnp.concatenate(
        [
            first_half * cosine_rows - second_half * sine_rows,
            second_half * cosine_rows + first_half * sine_rows,
        ],
        axis=-1,
    )


def norm_apply(residual, gain_row, bias_row):
    centre = residual - jnp.mean(residual, axis=-1, keepdims=True)
    spread = jnp.mean(centre * centre, axis=-1, keepdims=True)
    return centre * lax.rsqrt(spread + EPSILON) * gain_row + bias_row


def split_heads(merged, group_count):
    seqs_here, row_count, _ = merged.shape
    return merged.reshape(seqs_here, row_count, group_count, -1, HEAD_DIM).transpose(2, 0, 1, 3, 4)


def join_heads(grouped):
    group_count, seqs_here, row_count, heads_group, head_size = grouped.shape
    return grouped.transpose(1, 2, 0, 3, 4).reshape(
        seqs_here, row_count, group_count * heads_group * head_size
    )


def shards(
    tokens,
    cotangent,
    segments,
    adapter_index,
    qkv_weight,
    out_weight,
    ffn_in_weight,
    ffn_out_weight,
    norm_gain,
    norm_bias,
    adapt_in,
    adapt_down,
    adapt_out,
    adapt_ffn,
):
    seqs_here, tok_rows, model_width = tokens.shape
    heads_group = math.gcd(HEADS, 4)
    group_count = HEADS // heads_group
    score_scale = 1.0 / math.sqrt(HEAD_DIM)
    seq_count = lax.axis_size("seq")
    row_base = lax.axis_index("seq") * tok_rows
    shift_plan = []
    for distance in range(1, min(seq_count, HALF // tok_rows + 2)):
        row_count = min(tok_rows, HALF - (distance - 1) * tok_rows)
        if row_count > 0:
            shift_plan.append((distance, row_count))
            shift_plan.append((-distance, row_count))
    left_total = sum((plan_item[1] for plan_item in shift_plan if plan_item[0] > 0))
    key_rows = 2 * left_total + tok_rows
    key_places = {}
    passed_rows = 0
    for distance, row_count in shift_plan:
        if distance > 0:
            key_places[distance] = left_total - passed_rows - row_count
            key_places[-distance] = left_total + tok_rows + passed_rows
            passed_rows += row_count
    cosine_all, sine_all = rope_tables(segments)
    cosine_here = lax.dynamic_slice_in_dim(cosine_all, row_base, tok_rows, 1)
    sine_here = lax.dynamic_slice_in_dim(sine_all, row_base, tok_rows, 1)
    padded_ids = jnp.pad(segments, ((0, 0), (HALF, HALF)), constant_values=-1)
    key_ids = lax.dynamic_slice_in_dim(padded_ids, row_base - left_total + HALF, key_rows, 1)
    query_ids = lax.dynamic_slice_in_dim(segments, row_base, tok_rows, 1)
    offsets = (
        jnp.arange(tok_rows, dtype=jnp.int32)[:, None]
        - jnp.arange(key_rows, dtype=jnp.int32)[None, :]
        + left_total
    )
    visible = (query_ids[:, :, None] == key_ids[:, None, :]) & (jnp.abs(offsets) <= HALF)[None]
    slot_hits = adapter_index[:, 0][:, None] == jnp.arange(ADAPTERS, dtype=jnp.int32)[None, :]
    slot_low = slot_hits.astype(jnp.bfloat16)
    slot_full = slot_hits.astype(jnp.float32)

    def select_adapter(table):
        return jnp.einsum(
            "se,le...->ls...", slot_low, table, preferred_element_type=jnp.float32
        ).astype(jnp.bfloat16)

    def spread_slots(per_sequence):
        return jnp.einsum("se,s...->e...", slot_full, per_sequence, precision=PRECISE)

    chosen_in = select_adapter(adapt_in)
    chosen_down = select_adapter(adapt_down)
    chosen_out = select_adapter(adapt_out)
    chosen_ffn = select_adapter(adapt_ffn)

    def forward_group(items):
        query_block, key_block, value_block = items
        scores = (
            jnp.einsum(
                "sqhd,skhd->shqk", query_block, key_block, preferred_element_type=jnp.float32
            )
            * score_scale
        )
        scores = jnp.where(visible[:, None], scores, -1e30)
        biggest = jnp.max(scores, axis=-1, keepdims=True)
        lifted = jnp.exp(scores - biggest)
        row_total = jnp.sum(lifted, axis=-1, keepdims=True)
        probability = (lifted / row_total).astype(jnp.bfloat16)
        result = jnp.einsum(
            "shqk,skhd->sqhd", probability, value_block, preferred_element_type=jnp.float32
        )
        return (result.astype(jnp.bfloat16), (biggest + jnp.log(row_total))[..., 0])

    def backward_group(items):
        query_block, key_block, value_block, grad_block, log_total = items
        scores = (
            jnp.einsum(
                "sqhd,skhd->shqk", query_block, key_block, preferred_element_type=jnp.float32
            )
            * score_scale
        )
        scores = jnp.where(visible[:, None], scores, -1e30)
        probability = jnp.exp(scores - log_total[..., None])
        d_prob = jnp.einsum(
            "sqhd,skhd->shqk", grad_block, value_block, preferred_element_type=jnp.float32
        )
        delta = jnp.sum(probability * d_prob, axis=-1, keepdims=True)
        d_score = (probability * (d_prob - delta)).astype(jnp.bfloat16)
        d_query = (
            jnp.einsum("shqk,skhd->sqhd", d_score, key_block, preferred_element_type=jnp.float32)
            * score_scale
        )
        d_key = (
            jnp.einsum("shqk,sqhd->skhd", d_score, query_block, preferred_element_type=jnp.float32)
            * score_scale
        )
        d_value = jnp.einsum(
            "shqk,sqhd->skhd",
            probability.astype(jnp.bfloat16),
            grad_block,
            preferred_element_type=jnp.float32,
        )
        return (d_query, d_key, d_value)

    state = tokens.astype(jnp.float32)
    layer_index = 0
    w_qkv = lax.all_gather(qkv_weight[layer_index], ("batch", "seq"), axis=1, tiled=True)
    w_out = lax.all_gather(out_weight[layer_index], ("batch", "seq"), axis=0, tiled=True)
    w_in = lax.all_gather(ffn_in_weight[layer_index], ("batch", "seq"), axis=1, tiled=True)
    w_down = lax.all_gather(ffn_out_weight[layer_index], ("batch", "seq"), axis=0, tiled=True)
    held = [(w_qkv, w_out, w_in, w_down)]
    act_one = state.astype(jnp.bfloat16)
    low_qkv = jnp.einsum(
        "std,spdr->pstr",
        act_one,
        chosen_in[layer_index][:, 0:3],
        preferred_element_type=jnp.float32,
    ).astype(jnp.bfloat16)
    proj = jnp.einsum(
        "std,pde->pste", act_one, w_qkv, preferred_element_type=jnp.float32
    ) + jnp.einsum(
        "pstr,spre->pste",
        low_qkv,
        chosen_out[layer_index][:, 0:3],
        preferred_element_type=jnp.float32,
    )
    queries = (
        rotate(proj[0].reshape(seqs_here, tok_rows, HEADS, HEAD_DIM), cosine_here, sine_here)
        .astype(jnp.bfloat16)
        .reshape(seqs_here, tok_rows, model_width)
    )
    key_rot = (
        rotate(proj[1].reshape(seqs_here, tok_rows, HEADS, HEAD_DIM), cosine_here, sine_here)
        .astype(jnp.bfloat16)
        .reshape(seqs_here, tok_rows, model_width)
    )
    key_value = jnp.stack([key_rot, proj[2].astype(jnp.bfloat16)])
    edges = {}
    for step_by, row_count in shift_plan:
        if step_by > 0:
            outgoing = key_value[:, :, tok_rows - row_count :]
        else:
            outgoing = key_value[:, :, :row_count]
        edges[step_by] = shifted(outgoing, "seq", step_by)
    earlier = [edges[distance] for distance, row_count in reversed(shift_plan) if distance > 0]
    later = [edges[-distance] for distance, row_count in shift_plan if distance > 0]
    window = jnp.concatenate(earlier + [key_value] + later, axis=2)
    heads_out, log_total = lax.map(
        forward_group,
        (
            split_heads(queries, group_count),
            split_heads(window[0], group_count),
            split_heads(window[1], group_count),
        ),
    )
    attended = join_heads(heads_out)
    low_out = jnp.einsum(
        "std,sdr->str", attended, chosen_in[layer_index][:, 3], preferred_element_type=jnp.float32
    ).astype(jnp.bfloat16)
    branch = jnp.einsum(
        "std,de->ste", attended, w_out, preferred_element_type=jnp.float32
    ) + jnp.einsum(
        "str,sre->ste", low_out, chosen_out[layer_index][:, 3], preferred_element_type=jnp.float32
    )
    resid_one = state + branch
    hidden = norm_apply(resid_one, norm_gain[layer_index, 0], norm_bias[layer_index, 0])
    act_two = hidden.astype(jnp.bfloat16)
    low_ffn = jnp.einsum(
        "std,spdr->pstr",
        act_two,
        chosen_in[layer_index][:, 4:6],
        preferred_element_type=jnp.float32,
    ).astype(jnp.bfloat16)
    gate_up = jnp.einsum(
        "std,pdf->pstf", act_two, w_in, preferred_element_type=jnp.float32
    ) + jnp.einsum(
        "pstr,sprf->pstf", low_ffn, chosen_ffn[layer_index], preferred_element_type=jnp.float32
    )
    inner = (jax.nn.silu(gate_up[0]) * gate_up[1]).astype(jnp.bfloat16)
    low_down = jnp.einsum(
        "stf,sfr->str", inner, chosen_down[layer_index], preferred_element_type=jnp.float32
    ).astype(jnp.bfloat16)
    branch_two = jnp.einsum(
        "stf,fe->ste", inner, w_down, preferred_element_type=jnp.float32
    ) + jnp.einsum(
        "str,sre->ste", low_down, chosen_out[layer_index][:, 4], preferred_element_type=jnp.float32
    )
    resid_two = hidden + branch_two
    kept = [
        (
            act_one,
            low_qkv,
            queries,
            window,
            log_total,
            attended,
            low_out,
            resid_one,
            act_two,
            low_ffn,
            gate_up,
            inner,
            low_down,
            resid_two,
        )
    ]
    state = norm_apply(resid_two, norm_gain[layer_index, 1], norm_bias[layer_index, 1])
    mixed = state.astype(jnp.bfloat16)
    grad = cotangent.astype(jnp.float32)
    collected = [None] * LAYERS
    for layer_index in reversed(range(LAYERS)):
        (
            act_one,
            low_qkv,
            queries,
            window,
            log_total,
            attended,
            low_out,
            resid_one,
            act_two,
            low_ffn,
            gate_up,
            inner,
            low_down,
            resid_two,
        ) = kept[layer_index]
        w_qkv, w_out, w_in, w_down = held[layer_index]
        gain_two = norm_gain[layer_index, 1]
        bias_two = norm_bias[layer_index, 1]
        _, pull_two = jax.vjp(lambda residual: norm_apply(residual, gain_two, bias_two), resid_two)
        (d_resid_two,) = pull_two(grad)
        d_branch_two = d_resid_two.astype(jnp.bfloat16)
        d_low_down = jnp.einsum(
            "ste,sre->str",
            d_branch_two,
            chosen_out[layer_index][:, 4],
            preferred_element_type=jnp.float32,
        ).astype(jnp.bfloat16)
        g_out_down = jnp.einsum(
            "str,ste->sre", low_down, d_branch_two, preferred_element_type=jnp.float32
        )
        g_down = jnp.einsum("stf,str->sfr", inner, d_low_down, preferred_element_type=jnp.float32)
        d_inner = jnp.einsum(
            "ste,fe->stf", d_branch_two, w_down, preferred_element_type=jnp.float32
        ) + jnp.einsum(
            "str,sfr->stf", d_low_down, chosen_down[layer_index], preferred_element_type=jnp.float32
        )
        _, pull_act = jax.vjp(
            lambda gate_part, up_part: jax.nn.silu(gate_part) * up_part, gate_up[0], gate_up[1]
        )
        d_gate, d_up = pull_act(d_inner)
        d_gate_up = jnp.stack([d_gate, d_up]).astype(jnp.bfloat16)
        d_low_ffn = jnp.einsum(
            "pstf,sprf->pstr",
            d_gate_up,
            chosen_ffn[layer_index],
            preferred_element_type=jnp.float32,
        ).astype(jnp.bfloat16)
        g_ffn = jnp.einsum(
            "pstr,pstf->sprf", low_ffn, d_gate_up, preferred_element_type=jnp.float32
        )
        g_in_ffn = jnp.einsum(
            "std,pstr->spdr", act_two, d_low_ffn, preferred_element_type=jnp.float32
        )
        ffn_in_sum = spread_slots(g_in_ffn)
        ffn_down_sum = spread_slots(g_down)
        ffn_out_sum = spread_slots(g_out_down[:, None])
        ffn_ffn_sum = spread_slots(g_ffn)
        d_hidden = (
            d_resid_two
            + jnp.einsum("pstf,pdf->std", d_gate_up, w_in, preferred_element_type=jnp.float32)
            + jnp.einsum(
                "pstr,spdr->std",
                d_low_ffn,
                chosen_in[layer_index][:, 4:6],
                preferred_element_type=jnp.float32,
            )
        )
        gain_one = norm_gain[layer_index, 0]
        bias_one = norm_bias[layer_index, 0]
        _, pull_one = jax.vjp(lambda residual: norm_apply(residual, gain_one, bias_one), resid_one)
        (d_resid_one,) = pull_one(d_hidden)
        d_branch = d_resid_one.astype(jnp.bfloat16)
        d_low_out = jnp.einsum(
            "ste,sre->str",
            d_branch,
            chosen_out[layer_index][:, 3],
            preferred_element_type=jnp.float32,
        ).astype(jnp.bfloat16)
        g_out_att = jnp.einsum(
            "str,ste->sre", low_out, d_branch, preferred_element_type=jnp.float32
        )
        g_in_att = jnp.einsum(
            "std,str->sdr", attended, d_low_out, preferred_element_type=jnp.float32
        )
        d_attended = (
            jnp.einsum("ste,de->std", d_branch, w_out, preferred_element_type=jnp.float32)
            + jnp.einsum(
                "str,sdr->std",
                d_low_out,
                chosen_in[layer_index][:, 3],
                preferred_element_type=jnp.float32,
            )
        ).astype(jnp.bfloat16)
        d_query_heads, d_key_heads, d_value_heads = lax.map(
            backward_group,
            (
                split_heads(queries, group_count),
                split_heads(window[0], group_count),
                split_heads(window[1], group_count),
                split_heads(d_attended, group_count),
                log_total,
            ),
        )
        d_query = join_heads(d_query_heads)
        d_window = jnp.stack([join_heads(d_key_heads), join_heads(d_value_heads)])
        d_pair = d_window[:, :, left_total : left_total + tok_rows]
        for step_by, row_count in shift_plan:
            returning = lax.slice_in_dim(
                d_window, key_places[step_by], key_places[step_by] + row_count, axis=2
            )
            arrived = shifted(returning.astype(jnp.bfloat16), "seq", -step_by).astype(
                returning.dtype
            )
            if step_by > 0:
                d_pair = d_pair.at[:, :, tok_rows - row_count :].add(arrived)
            else:
                d_pair = d_pair.at[:, :, :row_count].add(arrived)
        d_query_rot = rotate(
            d_query.reshape(seqs_here, tok_rows, HEADS, HEAD_DIM), cosine_here, -sine_here
        ).reshape(seqs_here, tok_rows, model_width)
        d_key_rot = rotate(
            d_pair[0].reshape(seqs_here, tok_rows, HEADS, HEAD_DIM), cosine_here, -sine_here
        ).reshape(seqs_here, tok_rows, model_width)
        d_proj = jnp.stack([d_query_rot, d_key_rot, d_pair[1]]).astype(jnp.bfloat16)
        d_low_qkv = jnp.einsum(
            "pste,spre->pstr",
            d_proj,
            chosen_out[layer_index][:, 0:3],
            preferred_element_type=jnp.float32,
        ).astype(jnp.bfloat16)
        g_out_qkv = jnp.einsum(
            "pstr,pste->spre", low_qkv, d_proj, preferred_element_type=jnp.float32
        )
        g_in_qkv = jnp.einsum(
            "std,pstr->spdr", act_one, d_low_qkv, preferred_element_type=jnp.float32
        )
        grad = (
            d_resid_one
            + jnp.einsum("pste,pde->std", d_proj, w_qkv, preferred_element_type=jnp.float32)
            + jnp.einsum(
                "pstr,spdr->std",
                d_low_qkv,
                chosen_in[layer_index][:, 0:3],
                preferred_element_type=jnp.float32,
            )
        )
        att_in_sum = spread_slots(jnp.concatenate([g_in_qkv, g_in_att[:, None]], axis=1))
        att_out_sum = spread_slots(jnp.concatenate([g_out_qkv, g_out_att[:, None]], axis=1))
        collected[layer_index] = (
            jnp.concatenate([att_in_sum, ffn_in_sum], axis=1),
            ffn_down_sum,
            jnp.concatenate([att_out_sum, ffn_out_sum], axis=1),
            ffn_ffn_sum,
        )
    input_grad = grad.astype(jnp.bfloat16)
    stack_in = jnp.stack([collected[0][0]])
    stack_down = jnp.stack([collected[0][1]])
    stack_out = jnp.stack([collected[0][2]])
    stack_ffn = jnp.stack([collected[0][3]])
    stack_in, stack_down, stack_out, stack_ffn = lax.psum(
        (stack_in, stack_down, stack_out, stack_ffn), ("batch", "seq")
    )
    return (mixed, input_grad, stack_in, stack_down, stack_out, stack_ffn)


MESH = pl.DeviceIdType.MESH
NCHUNK = 10
ALL = slice(None)


class Gather:
    def __init__(self, sems, direct=(), diagonal=()):
        self.direct = direct
        self.diagonal = diagonal
        (
            self.zs, self.zr, self.xs, self.xr, self.ys, self.yr, self.ds, self.dr, self.es, self.er, self.fs, self.fr,
            self.cs, self.cr,
        ) = sems
        b = lax.axis_index("batch")
        self.b = b
        self.s = lax.axis_index("seq")
        self.core = lax.rem(b, 2)
        self.x = lax.rem(lax.div(b, 2), 2)
        self.z = lax.div(b, 4)
        self.za = lax.div(self.z, 2)
        self.zb = lax.rem(self.z, 2)
        self.devx = (b + 2 - 4 * self.x, self.s)
        self.devy = (b, 1 - self.s)
        self.devd = (b + 2 - 4 * self.x, 1 - self.s)
        self.devc = (b + 1 - 2 * self.core, self.s)
        self.devp = (b + 4 - 8 * self.zb, self.s)

    def column(self, dx, dy, dc):
        x = 1 - self.x if dx else self.x
        y = 1 - self.s if dy else self.s
        c = 1 - self.core if dc else self.core
        return (x * 2 + c) * 2 + y

    def devz(self, z):
        return (z * 4 + self.x * 2 + self.core, self.s)

    def copy(self, c, za, zb, k, half, dev, send, recv):
        v = self.view(c, za, zb, k, half)
        return pltpu.make_async_remote_copy(v, v, send, recv, device_id=dev, device_id_type=MESH)

    def to_z(self, c, z):
        return self.copy(
            c, self.za, self.zb, self.column(0, 0, 0), None, self.devz(z), self.zs.at[c, z], self.zr.at[c, self.z]
        )

    def from_z(self, c, z):
        return self.copy(
            c, lax.div(z, 2), lax.rem(z, 2), self.column(0, 0, 0), None, self.devz(z), self.zs.at[c, z], self.zr.at[c, z]
        )

    def on_x(self, c, arriving):
        return self.copy(c, ALL, ALL, self.column(arriving, 0, 0), None, self.devx, self.xs.at[c], self.xr.at[c])

    def on_y(self, c, arriving):
        return self.copy(c, ALL, ALL, self.column(0, arriving, 0), None, self.devy, self.ys.at[c], self.yr.at[c])

    def on_diagonal(self, c, arriving):
        return self.copy(c, ALL, ALL, self.column(arriving, arriving, 0), None, self.devd, self.ds.at[c], self.dr.at[c])

    def parity(self, c):
        return ALL if c in self.direct else self.zb

    def corner_x(self, c, arriving):
        k = self.column(arriving, 1, 0)
        return self.copy(c, ALL, self.parity(c), k, 0, self.devx, self.ds.at[c], self.dr.at[c])

    def corner_y(self, c, arriving):
        k = self.column(1, arriving, 0)
        return self.copy(c, ALL, self.parity(c), k, 1, self.devy, self.es.at[c], self.er.at[c])

    def corner_z(self, c, arriving):
        zb = 1 - self.zb if arriving else self.zb
        return self.copy(c, ALL, zb, self.column(1, 1, 0), None, self.devp, self.fs.at[c], self.fr.at[c])

    def on_core(self, c, kind, arriving):
        k = self.column(kind & 1, kind >> 1, arriving)
        return self.copy(c, ALL, ALL, k, None, self.devc, self.cs.at[c, kind], self.cr.at[c, kind])

    def others(self):
        z = self.z
        first = jnp.where(z == 0, 1, z - 1)
        second = jnp.where(z == 0, 2, jnp.where(z == 3, 1, z + 1))
        third = jnp.where(z <= 1, 3, 0)
        return first, second, third

    def partners(self):
        return [self.devx, self.devy, self.devc] + [self.devz(z) for z in self.others()]

    def barrier(self, devices):
        bar = pltpu.get_barrier_semaphore()
        for dev in devices:
            pl.semaphore_signal(bar, inc=1, device_id=dev, device_id_type=MESH)
        pl.semaphore_wait(bar, len(devices))

    def send_z(self, c):
        for z in self.others():
            self.to_z(c, z).start()

    def stage_z(self, c):
        for z in self.others():
            self.from_z(c, z).wait_recv()
        self.on_x(c, 0).start()
        self.on_y(c, 0).start()
        if c in self.diagonal:
            self.on_diagonal(c, 0).start()
        self.on_core(c, 0, 0).start()

    def stage_xy(self, c):
        self.on_x(c, 1).wait_recv()
        if c not in self.diagonal:
            self.corner_y(c, 0).start()
        self.on_core(c, 1, 0).start()
        self.on_y(c, 1).wait_recv()
        if c not in self.diagonal:
            self.corner_x(c, 0).start()
        self.on_core(c, 2, 0).start()
        if c in self.diagonal:
            self.on_diagonal(c, 1).wait_recv()
            self.on_core(c, 3, 0).start()

    def stage_corner(self, c):
        self.corner_x(c, 1).wait_recv()
        self.corner_y(c, 1).wait_recv()
        if c in self.direct:
            self.on_core(c, 3, 0).start()
        else:
            self.corner_z(c, 0).start()

    def stage_pair(self, c):
        self.corner_z(c, 1).wait_recv()
        self.on_core(c, 3, 0).start()

    def stage_core(self, c):
        for kind in range(4):
            self.on_core(c, kind, 1).wait_recv()

    def finish(self, c):
        for z in self.others():
            self.to_z(c, z).wait_send()
        self.on_x(c, 0).wait_send()
        self.on_y(c, 0).wait_send()
        for kind in range(4):
            self.on_core(c, kind, 0).wait_send()
        if c in self.diagonal:
            self.on_diagonal(c, 0).wait_send()
        else:
            self.corner_x(c, 0).wait_send()
            self.corner_y(c, 0).wait_send()
            if c not in self.direct:
                self.corner_z(c, 0).wait_send()


def gather_sems(chunks):
    one = pltpu.SemaphoreType.DMA((chunks,))
    four = pltpu.SemaphoreType.DMA((chunks, 4))
    return [four] * 2 + [one] * 10 + [four] * 2


BF = jnp.bfloat16
F32 = jnp.float32
QB = 256
PLAN = ((0, 3, False, True), (0, 4, False, True), (0, 5, True, True), (1, 5, True, True))
HALO_PLAN = ((2, 2), (3, 1))
NEG = -1e30
VMEM_LIMIT = int(63.9 * 2**20)
ORDER = (
    "h0", "z0", "z1", "z2", "x0", "T", "x1", "x2", "c0", "z4", "h2", "c2", "c1", "k0",
    "h3", "k2", "z3", "P0", "k1", "x4", "z6", "h1", "P1", "P2", "A003", "z5", "A036", "c4",
    "A103", "x6", "z7", "A136", "H", "x5", "x3", "p4", "c6", "z8", "A202", "A224", "p6", "c5",
    "A246", "x7", "c3", "k6", "z9", "A302", "p5", "x8", "c7", "k3", "k4", "A324", "A346", "p7",
    "k5", "O", "x9", "c8", "k7", "F0", "c9", "p8", "F1", "k8", "p9", "F2", "k9", "F3",
)


def nn(a, b):
    return jnp.dot(a, b, preferred_element_type=F32)


def nt(a, b):
    return lax.dot_general(a, b, (((1,), (1,)), ((), ())), preferred_element_type=F32)


def tn(a, b):
    return lax.dot_general(a, b, (((0,), (0,)), ((), ())), preferred_element_type=F32)


def iota(shape, dim):
    return lax.broadcasted_iota(jnp.int32, shape, dim)


def block_at(flip, block):
    return pl.multiple_of(jnp.where(flip == 1, 3 - block, block) * QB, QB)


def rope(vectors, cosine, sine):
    lane = iota((1, 128), 1)
    first = lax.rem(lane, HEAD_DIM) < HEAD_DIM // 2
    out = []
    for c in range(vectors.shape[1] // 128):
        part = vectors[:, c * 128 : (c + 1) * 128]
        other = jnp.where(first, pltpu.roll(part, 96, 1), pltpu.roll(part, 32, 1))
        out.append(part * cosine + other * sine)
    return jnp.concatenate(out, axis=1)


def fill_tables(flip, seg_ref, freq_ref, cos_ref, sin_ref, fq_ref, fk_ref, bias_ref):
    lane = iota((1, 128), 1)
    seg_row = seg_ref[...].astype(F32)
    starts = [
        jnp.sum((seg_row < float(d)).astype(F32), axis=1, keepdims=True) for d in (1, 2, 3)
    ]
    sign = jnp.where(lax.rem(lane, HEAD_DIM) < HEAD_DIM // 2, -1.0, 1.0)
    for w in range(12):
        block, part = divmod(w, 2)
        base = jnp.where(flip == 1, 7 - block, block) * QB + part * 128
        row = seg_ref[:, pl.ds(pl.multiple_of(base, 128), 128)].astype(F32)
        seg = jnp.broadcast_to(row, (128, 128)).T
        start = jnp.where(
            seg >= 3.0,
            starts[2],
            jnp.where(seg >= 2.0, starts[1], jnp.where(seg >= 1.0, starts[0], 0.0)),
        )
        pos = (iota((128, 128), 0) + base).astype(F32) - start
        angle = pos * freq_ref[...]
        rows = pl.ds(w * 128, 128)
        cos_ref[rows, :] = jnp.cos(angle)
        sin_ref[rows, :] = jnp.sin(angle) * sign
        hit = seg == lane.astype(F32)
        fq_ref[rows, :] = jnp.where(hit, 1.0, 0.0).astype(BF)
        fk_ref[rows, :] = jnp.where(hit | (lane >= 4), 0.0, NEG).astype(BF)
    gap = iota((QB, QB), 0) - iota((QB, QB), 1)
    gap = jnp.where(flip == 1, -gap, gap)
    bias_ref[0] = jnp.where(gap >= 0, 0.0, NEG)
    bias_ref[1] = jnp.where(gap <= 0, 0.0, NEG)


def qkv_rows(p, rb, xw, wq, aqkv, bblk, cos_ref, sin_ref, dest, low_ref):
    rows = pl.ds(pl.multiple_of(rb * 512, 512), 512)
    x = xw[rows, :]
    if p == 0:
        low = nt(x, aqkv[...]).astype(BF)
        low_ref[rows, :] = low
    else:
        low = low_ref[rows, :]
    proj = nn(x, wq[p].reshape(D, D)) + nn(low, bblk[p])
    if p < 2:
        proj = rope(proj, cos_ref[rows, :], sin_ref[rows, :])
    value = proj.astype(BF)
    if p == 0:
        value = value * jnp.asarray(0.125, BF)
    dest[pl.ds(rb * 2, 2)] = value.reshape(2, QB, D)


def prob_copies(n, src, dst, sem, s):
    full = (2 * n + 2) // 3
    cuts = ((0, 2), (2, full)) if full > 2 else ((0, 1), (1, 2))
    return [
        pltpu.make_async_copy(src.at[pl.ds(a, b - a)], dst.at[pl.ds(a, b - a)], sem.at[2 * s + i])
        for i, (a, b) in enumerate(cuts)
    ]


def attend_pair(
    qb, pair, step, q_ref, k_ref, v_ref, fq_ref, fk_ref, bias_ref, att_ref, linv_ref, mf_ref, p_hbm, stage, sem
):
    k0, n, tri_first, tri_last = PLAN[qb]
    rows = pl.ds(qb * QB, QB)
    kblocks = pl.ds(k0, n)
    krows = pl.ds(k0 * QB, n * QB)
    half = iota((1, 128), 1) >= HEAD_DIM
    lane = iota((1, 128), 1)
    slot = lax.rem(step, 2)

    def copy(s):
        return prob_copies(n, stage.at[pl.ds(s * 4, 4)], p_hbm.at[qb, pair], sem, s)

    @pl.when(pair >= 2)
    def _():
        for one in copy(slot):
            one.wait()

    lanes = pl.ds(pl.multiple_of(pair * 128, 128), 128)
    q2 = q_ref[qb, :, lanes]
    fq = fq_ref[rows, :]
    keys = jnp.concatenate([k_ref[kblocks, :, lanes].reshape(n * QB, 128), fk_ref[krows, :]], axis=1)
    v2 = v_ref[kblocks, :, lanes].reshape(n * QB, 128)
    masks = (jnp.logical_not(half), half)
    scores = [
        nt(jnp.concatenate([jnp.where(mine, q2, jnp.zeros_like(q2)), fq], axis=1), keys) for mine in masks
    ]
    outs = []
    for h, (mine, s) in enumerate(zip(masks, scores)):
        parts = [s[:, t * QB : (t + 1) * QB] for t in range(n)]
        if tri_last:
            parts[n - 1] = parts[n - 1] + bias_ref[0]
        if tri_first:
            parts[0] = parts[0] + bias_ref[1]
        s = jnp.concatenate(parts, axis=1)
        m = jnp.max(s, axis=1, keepdims=True)
        p = jnp.exp(s - m).astype(BF)
        for t in range(n):
            block, lane0 = divmod(h * n + t, 3)
            stage[slot * 4 + block, :, lane0 * QB : lane0 * QB + QB] = p[:, t * QB : (t + 1) * QB]
        if qb >= 2:
            low = 4 + 3 * (2 * pair + h)
            mf_ref[rows, :] = jnp.where((lane >= low) & (lane < low + 3), -m, mf_ref[rows, :])
        outs.append(nn(p, jnp.where(mine, v2, jnp.ones_like(v2))))
    inv = 1.0 / pltpu.roll(jnp.where(half, outs[0], outs[1]), HEAD_DIM, 1)
    att_ref[rows, lanes] = (jnp.where(half, outs[1], outs[0]) * inv).astype(BF)
    linv_ref[rows, lanes] = inv
    for one in copy(slot):
        one.start()


def drain_pairs(qb, p_hbm, stage, sem):
    for s in range(2):
        for one in prob_copies(PLAN[qb][1], stage.at[pl.ds(s * 4, 4)], p_hbm.at[qb, 0], sem, s):
            one.wait()


def norm_stats(r):
    centre = r - jnp.mean(r, axis=1, keepdims=True)
    rstd = lax.rsqrt(jnp.mean(centre * centre, axis=1, keepdims=True) + EPSILON)
    return centre * rstd, rstd


def norm_back(grad, xhat, rstd):
    return rstd * (
        grad
        - jnp.mean(grad, axis=1, keepdims=True)
        - xhat * jnp.mean(grad * xhat, axis=1, keepdims=True)
    )


def out_rows(rb, xw, att_ref, wo, ao, bo, gb, aff, xhat_ref, rstd_ref, act_ref, lowo_ref, lowf_ref):
    rows = pl.ds(pl.multiple_of(rb * QB, QB), QB)
    att = att_ref[rows, :]
    low = nt(att, ao[...]).astype(BF)
    lowo_ref[rows, :] = low
    branch = nn(att, wo[...].reshape(D, D)) + nn(low, bo[...])
    xhat, rstd = norm_stats(xw[rows, :].astype(F32) + branch)
    xhat_ref[rows, :] = xhat
    rstd_ref[rows, :] = jnp.broadcast_to(rstd, (QB, 128))
    act = (xhat * gb[0:1, :] + gb[1:2, :]).astype(BF)
    act_ref[rows, :] = act
    lowf_ref[rows, :] = nt(act, aff[...]).astype(BF)


def ffn_in_tile(n, rb, size, act_ref, lowf_ref, wi, wd, bg, bu, adn, big, lowd_ref, total_ref):
    start = pl.multiple_of(rb * size, size)
    rows = pl.ds(start, size)
    act = act_ref[rows, :]
    low = lowf_ref[rows, :]
    blocks = size // QB
    here = n * 4 + rb * blocks
    parts = []
    for c in range(3):
        lanes = slice(c * 256, c * 256 + 256)
        gate = nn(act, wi[n, 0, :, :, :, :, lanes].reshape(D, 256)) + nn(low, bg[n, :, lanes])
        up = nn(act, wi[n, 1, :, :, :, :, lanes].reshape(D, 256)) + nn(low, bu[n, :, lanes])
        parts.append((gate * (1.0 / (1.0 + jnp.exp(-gate))) * up).astype(BF))
        big[pl.ds(here, blocks), :, lanes] = gate.astype(BF).reshape(blocks, QB, 256)
        big[pl.ds(here + 16, blocks), :, lanes] = up.astype(BF).reshape(blocks, QB, 256)
    inner = jnp.concatenate(parts, axis=1)
    lowd_ref[rows, 0:16] += nt(inner, adn[n])
    total_ref[rows, :] += nn(inner, wd[lax.div(n, 2), lax.rem(n, 2)].reshape(D, D))


def ffn_out_rows(
    rb, flip, lowd_ref, bdn, xhat_ref, gb, cot, dtwo_ref, db2_ref, dlow_ref, mixed_ref, gbdn_ref
):
    start = pl.multiple_of(rb * QB, QB)
    rows = pl.ds(start, QB)
    low = lowd_ref[rows, 0:16].astype(BF)
    total = nn(low, bdn[...]) + dtwo_ref[rows, :]
    r = xhat_ref[rows, :] * gb[0:1, :] + gb[1:2, :] + total
    xhat, rstd = norm_stats(r)
    mixed_ref[pl.ds(block_at(flip, rb), QB), :] = (xhat * gb[2:3, :] + gb[3:4, :]).astype(BF)
    dtwo = norm_back(cot[rows, :].astype(F32) * gb[2:3, :], xhat, rstd)
    dtwo_ref[rows, :] = dtwo
    db2 = dtwo.astype(BF)
    db2_ref[rows, :] = db2
    dlow_ref[rows, :] = nt(db2, bdn[...]).astype(BF)
    gbdn_ref[...] += tn(low, db2)


def ffn_back_tile(
    n, start, size, db2_ref, dlow_ref, wd, wi, adn, bg, bu, big, lowf_ref, acc, dlf_ref, gadn_ref, gbf_ref
):
    rows = pl.ds(start, size)
    db2 = db2_ref[rows, :]
    dlow = dlow_ref[rows, :]
    blocks = size // QB
    here = n * 4 + lax.div(start, QB)
    down = wd[lax.div(n, 2), lax.rem(n, 2)].reshape(D, D)
    dgs, dus, inners = [], [], []
    for c in range(3):
        lanes = slice(c * 256, c * 256 + 256)
        dinner = nt(db2, down[lanes]) + nn(dlow, adn[n, :, lanes])
        gate = big[pl.ds(here, blocks), :, lanes].reshape(size, 256).astype(F32)
        up = big[pl.ds(here + 16, blocks), :, lanes].reshape(size, 256).astype(F32)
        sig = 1.0 / (1.0 + jnp.exp(-gate))
        silu = gate * sig
        inners.append((silu * up).astype(BF))
        dgs.append((dinner * up * (sig + silu * (1.0 - sig))).astype(BF))
        dus.append((dinner * silu).astype(BF))
    dg, du, inner = (jnp.concatenate(v, axis=1) for v in (dgs, dus, inners))
    acc[...] += nt(dg, wi[n, 0].reshape(D, D)) + nt(du, wi[n, 1].reshape(D, D))
    dlf_ref[...] += nt(dg, bg[n]) + nt(du, bu[n])
    gadn_ref[n] += tn(dlow, inner)
    low = lowf_ref[rows, :]
    gbf_ref[n] += jnp.where(iota((32, 1), 0) < 16, tn(low, dg), tn(low, du))


def hidden_back_rows(
    rb, off, acc, dlf_ref, aff, act_ref, dtwo_ref, xhat_ref, rstd_ref, gb, bo, ao, lowo_ref, att_ref,
    wo, linv_ref, h2, mf_ref, do_ref, hf_ref, gaff_ref, gbo_ref, gao_ref,
):
    start = pl.multiple_of(rb * QB, QB)
    rows = pl.ds(start, QB)
    local = pl.ds(pl.multiple_of(start - off, QB), QB)
    dlf = dlf_ref[local, :].astype(BF)
    dhid = dtwo_ref[rows, :] + acc[local, :] + nn(dlf, aff[...])
    gaff_ref[...] += tn(dlf, act_ref[rows, :])
    done = norm_back(dhid * gb[0:1, :], xhat_ref[rows, :], rstd_ref[rows, 0:1])
    dtwo_ref[rows, :] = done
    dbr = done.astype(BF)
    dlo = nt(dbr, bo[...]).astype(BF)
    att = att_ref[rows, :]
    gbo_ref[...] += tn(lowo_ref[rows, :], dbr)
    gao_ref[...] += tn(dlo, att)
    datt = (nt(dbr, wo[...].reshape(D, D)) + nn(dlo, ao[...])).astype(BF)
    do = (datt.astype(F32) * linv_ref[rows, :]).astype(BF)
    do_ref[rows, :] = do
    value = nn(do * att, h2[...]) + mf_ref[rows, :]
    lane = iota((1, 128), 1)
    role = jnp.where(lane < 40, lax.rem(lane + 2, 3), lax.rem(lane, 2))
    high = value.astype(BF)
    rest = value - high.astype(F32)
    mid = rest.astype(BF)
    last = (rest - mid.astype(F32)).astype(BF)
    hf_ref[rows, :] = jnp.where(role == 0, high, jnp.where(role == 1, mid, last))


def kf_kernel(
    x_hbm, cot_hbm, seg_hbm, freq_hbm, pick_hbm, gain_hbm, shift_hbm, tin_hbm, tdn_hbm, tout_hbm, tff_hbm,
    wq_hbm, wo_hbm, wi_hbm, wd_hbm,
    q_hbm, k_hbm, v_hbm, p_hbm, mixed_hbm, do_hbm, hf_hbm, lowq_hbm, done_hbm, cos_hbm, sin_hbm, fq_hbm, fk_hbm,
    ge_hbm, gao_hbm, tag_hbm, aqkv_hbm, bqkv_hbm, wq_out,
    seg_ref, freq_ref, pick_ref, gain_ref, shift_ref, hf_ref, ge_ref, gao_ref, tag_ref, aqkv, bqkv, ssem, fsem,
    ao, bo, aff, adn, bdn, gb,
    gaff_ref, gadn_ref, gbo_ref, gbdn_ref, gbf_ref,
    wq, wo, wi, wd, big, xw, att, linv, xhat, dtwo, act, db2, cos, sin, fq, fk, bias, mf,
    lowq, lowo, lowf, dlow, acc, dlf, bblk, bg, bu, h2, mixed_ref, do_ref, rsem, tsem, wsem, xsem, osem, psem, hs, hr, *sems,
):
    flip = lax.axis_index("seq")
    cot = db2
    rstd = cos
    lowd = sin
    loads = []
    for i in range(4):
        loads.append(
            pltpu.make_async_copy(
                x_hbm.at[pl.ds(block_at(flip, i), QB)], xw.at[pl.ds(i * QB, QB)], xsem.at[i]
            )
        )
        loads.append(
            pltpu.make_async_copy(
                cot_hbm.at[pl.ds(block_at(flip, i), QB)], cot.at[pl.ds(i * QB, QB)], xsem.at[4 + i]
            )
        )
    small = [
        pltpu.make_async_copy(a, b, ssem.at[i])
        for i, (a, b) in enumerate(
            ((seg_hbm, seg_ref), (freq_hbm, freq_ref), (pick_hbm, pick_ref), (gain_hbm, gain_ref), (shift_hbm, shift_ref))
        )
    ]
    for copy in small:
        copy.start()
    facts = [
        pltpu.make_async_copy(a, b, fsem.at[i])
        for i, (a, b) in enumerate(
            ((tag_ref, tag_hbm), (aqkv, aqkv_hbm), (bqkv, bqkv_hbm), (ge_ref, ge_hbm), (gao_ref, gao_hbm))
        )
    ]
    tables = [
        (tin_hbm, big.at[pl.ds(0, ADAPTERS), pl.ds(0, 96)]),
        (tout_hbm, big.at[pl.ds(4, ADAPTERS), pl.ds(0, 80)]),
    ]
    for n in range(4):
        lanes = pl.ds(n * D, D)
        tables.append((tdn_hbm.at[:, :, lanes], big.at[pl.ds(8, ADAPTERS), pl.ds(16 * n, 16)]))
        tables.append((tff_hbm.at[:, :, lanes], big.at[pl.ds(12, ADAPTERS), pl.ds(32 * n, 32)]))
    tables = [pltpu.make_async_copy(a, b, tsem.at[i]) for i, (a, b) in enumerate(tables)]
    g = Gather(sems, direct=(0, 1, 2, 3))

    def view(c, za, zb, k, half):
        cut = 384 if c < 4 else 640
        lanes = ALL if half is None else pl.ds(0, cut) if half == 0 else pl.ds(cut, D - cut)
        if c < 3:
            return wq.at[c, za, zb, k, :, lanes]
        if c == 3:
            return wo.at[za, zb, k, :, lanes]
        if c < 6:
            return wd.at[za, zb, k, pl.ds((c - 4) * 48, 48), lanes]
        return wi.at[c - 6, :, za, zb, k, :, lanes]

    g.view = view
    here = g.column(0, 0, 0)
    weights = [
        pltpu.make_async_copy(a, b, wsem.at[i])
        for i, (a, b) in enumerate(
            [(wq_hbm, wq.at[:, g.za, g.zb, here]), (wo_hbm, wo.at[g.za, g.zb, here]), (wd_hbm, wd.at[g.za, g.zb, here])]
            + [(wi_hbm.at[:, :, pl.ds(D * n, D)], wi.at[n, :, g.za, g.zb, here]) for n in range(4)]
        )
    ]
    for copy in weights:
        copy.start()
    g.barrier(g.partners())
    for copy in weights:
        copy.wait()
    for c in range(NCHUNK):
        g.send_z(c)
    halo = [
        pltpu.make_async_remote_copy(
            x_hbm.at[pl.ds(block_at(flip, 3 - i // 2) + i % 2 * 128, 128)], xw.at[pl.ds(1024 + i * 128, 128)],
            hs.at[i], hr.at[i], device_id=g.devy, device_id_type=MESH,
        )
        for i in range(4)
    ]

    kinds = {
        "z": g.stage_z, "x": g.stage_xy, "c": g.stage_corner, "p": g.stage_pair, "k": g.stage_core,
    }

    for copy in loads + tables:
        copy.start()

    def prepare():
        for copy in small:
            copy.wait()
        fill_tables(flip, seg_ref, freq_ref, cos, sin, fq, fk, bias)
        for copy in tables:
            copy.wait()
        e = pick_ref[0, 0]
        aqkv[...] = big[e, 0:48, :]
        ao[...] = big[e, 48:64, :]
        aff[...] = big[e, 64:96, :]
        bqkv[...] = big[4 + e, 0:48, :]
        bo[...] = big[4 + e, 48:64, :]
        bdn[...] = big[4 + e, 64:80, :]
        for n in range(4):
            adn[n] = big[8 + e, 16 * n : 16 * n + 16, :]
        tag_ref[...] = jnp.where(iota((16, 128), 0) == e, 1.0, 0.0).astype(BF)
        for copy in facts[:3]:
            copy.start()
        for i in range(2):
            gb[2 * i : 2 * i + 1, :] = gain_ref[i : i + 1, :]
            gb[2 * i + 1 : 2 * i + 2, :] = shift_ref[i : i + 1, :]
        rank = iota((48, 1), 0)
        for p in range(3):
            keep = (rank >= 16 * p) & (rank < 16 * p + 16)
            bblk[p] = jnp.where(keep, bqkv[...], jnp.zeros_like(bqkv[...]))
        rank = iota((32, 1), 0)
        for n in range(4):
            piece = big[12 + e, 32 * n : 32 * n + 32, :]
            bg[n] = jnp.where(rank < 16, piece, jnp.zeros_like(piece))
            bu[n] = jnp.where(rank >= 16, piece, jnp.zeros_like(piece))
        head = lax.div(iota((D, 128), 0), HEAD_DIM)
        spot = iota((D, 128), 1)
        h2[...] = jnp.where(lax.div(spot - 40, 2) == head, jnp.where(spot >= 40, -1.0, 0.0), 0.0).astype(BF)
        mf[...] = jnp.zeros_like(mf)
        dtwo[...] = jnp.zeros_like(dtwo)
        for ref in (gao_ref, gaff_ref, gadn_ref, gbo_ref, gbdn_ref, gbf_ref):
            ref[...] = jnp.zeros_like(ref)
        for copy in loads:
            copy.wait()

    q_ref, k_ref, v_ref = (big.at[pl.ds(i * 6, 6)] for i in range(3))
    stage = big.at[pl.ds(18, 8)]
    keep_wq = pltpu.make_async_copy(wq, wq_out, osem.at[9])
    saves = [
        pltpu.make_async_copy(a, b, osem.at[i])
        for i, (a, b) in enumerate(
            ((q_ref, q_hbm), (k_ref, k_hbm), (v_ref, v_hbm), (lowq, lowq_hbm), (cos, cos_hbm), (sin, sin_hbm), (fq, fq_hbm), (fk, fk_hbm))
        )
    ]

    def qkv_page(p, first, last):
        def step(rb, _):
            qkv_rows(p, rb, xw, wq, aqkv, bblk, cos, sin, (q_ref, k_ref, v_ref)[p], lowq)
            return 0

        lax.fori_loop(first, last, step, 0)

    def attend(qb, first, last):
        def pair_step(pair, _):
            attend_pair(qb, pair, pair, q_ref, k_ref, v_ref, fq, fk, bias, att, linv, mf, p_hbm, stage, psem)
            return 0

        lax.fori_loop(first, last, pair_step, 0)
        if last == 6:
            drain_pairs(qb, p_hbm, stage, psem)

    def out_step(rb, _):
        out_rows(rb, xw, att, wo, ao, bo, gb, aff, xhat, rstd, act, lowo, lowf)
        return 0

    def in_step(i, _):
        ffn_in_tile(lax.div(i, 2), lax.rem(i, 2), 512, act, lowf, wi, wd, bg, bu, adn, big, lowd, dtwo)
        return 0

    for step in ORDER:
        kind, rest = step[0], step[1:]
        if kind in kinds:
            kinds[kind](int(rest))
        elif kind == "h":
            halo[int(rest)].start()
        elif step == "T":
            prepare()
        elif kind == "P":
            qkv_page(int(rest), 0, 2)
        elif step == "H":
            for copy in halo:
                copy.wait_recv()
            for p in range(3):
                qkv_page(p, 2, 3)
            for copy in saves:
                copy.start()
            keep_wq.start()
        elif kind == "A":
            attend(*(int(v) for v in rest))
        elif step == "O":
            for copy in saves:
                copy.wait()
            lowd[...] = jnp.zeros_like(lowd)
            lax.fori_loop(0, 4, out_step, 0)
        elif kind == "F":
            n = int(rest)
            lax.fori_loop(2 * n, 2 * n + 2, in_step, 0)

    def down_step(rb, _):
        ffn_out_rows(rb, flip, lowd, bdn, xhat, gb, cot, dtwo, db2, dlow, mixed_ref, gbdn_ref)
        return 0

    lax.fori_loop(0, 4, down_step, 0)
    outs = [pltpu.make_async_copy(mixed_ref, mixed_hbm, rsem.at[0])]
    outs[0].start()

    def row_copies(rb):
        rows = pl.ds(pl.multiple_of(rb * QB, QB), QB)
        return (
            pltpu.make_async_copy(do_ref.at[rows], do_hbm.at[rows], rsem.at[1 + rb]),
            pltpu.make_async_copy(dtwo.at[rows], done_hbm.at[rows], rsem.at[5 + rb]),
            pltpu.make_async_copy(hf_ref.at[rows], hf_hbm.at[rows], rsem.at[9 + rb]),
        )

    def back_step(half, _):
        off = pl.multiple_of(half * 512, 512)
        acc[...] = jnp.zeros_like(acc)
        dlf[...] = jnp.zeros_like(dlf)

        def tile(n, _):
            ffn_back_tile(
                n, off, 512, db2, dlow, wd, wi, adn, bg, bu, big, lowf, acc, dlf, gadn_ref, gbf_ref
            )
            return 0

        lax.fori_loop(0, 4, tile, 0)

        def rows(i, _):
            hidden_back_rows(
                half * 2 + i, off, acc, dlf, aff, act, dtwo, xhat, rstd, gb, bo, ao, lowo, att, wo, linv, h2, mf,
                do_ref, hf_ref, gaff_ref, gbo_ref, gao_ref,
            )
            for copy in row_copies(half * 2 + i):
                copy.start()
            return 0

        lax.fori_loop(0, 2, rows, 0)
        return 0

    lax.fori_loop(0, 2, back_step, 0)
    for rb in range(4):
        outs.extend(row_copies(rb))
    ge_ref[0:32] = gaff_ref[...].astype(BF)
    ge_ref[32:48] = gbo_ref[...].astype(BF)
    ge_ref[48:64] = gbdn_ref[...].astype(BF)
    ge_ref[64:128] = gadn_ref[...].reshape(64, D).astype(BF)
    ge_ref[128:256] = gbf_ref[...].reshape(128, D).astype(BF)
    for copy in facts[3:]:
        copy.start()
    keep_wq.wait()
    for copy in outs + facts:
        copy.wait()
    for copy in halo:
        copy.wait_send()
    for c in range(NCHUNK):
        g.finish(c)


def k3_kernel(
    x_hbm, q_hbm, k_hbm, v_hbm, p_hbm, do_hbm, hf_hbm, ge_hbm, gao_hbm, tag_hbm, lowq_hbm, done_hbm, cos_hbm, sin_hbm,
    fq_hbm, fk_hbm, aqkv_hbm, bqkv_hbm, wq_hbm,
    dx_hbm, eg_hbm, lg_hbm,
    ge, gao, tag, aqkv, bqkv, gsem,
    ga_ref, gbq_ref, dproj, eg, lg, e_in, e_half, rs_e, rs_t, gl_out, gl_in, l_half, rs_l, dx_ref,
    xw, q, k, v, do, hf, lowq, done, cos, sin, fq, fk, wq, stage, dq, dkT, dvT, bias, sem, psem, hs, hr,
    es, er, ts, tr, ls, lr, dsem, *sems,
):
    flip = lax.axis_index("seq")
    g = Gather(sems, diagonal=(1,))

    def part(src, dst, start, size):
        return src.at[pl.ds(start, size)], dst.at[pl.ds(start, size)]

    table = (
        part(q_hbm, q, 0, 256), part(k_hbm, k, 0, 768), part(v_hbm, v, 0, 768), part(do_hbm, do, 0, 256),
        part(hf_hbm, hf, 0, 1024),
        part(q_hbm, q, 256, 1280), part(k_hbm, k, 768, 768), part(v_hbm, v, 768, 768), part(do_hbm, do, 256, 768),
        (ge_hbm, ge), (tag_hbm, tag), (gao_hbm, gao), (aqkv_hbm, aqkv), (bqkv_hbm, bqkv),
        (lowq_hbm, lowq), (done_hbm, done), (cos_hbm, cos), (sin_hbm, sin), (fq_hbm, fq), (fk_hbm, fk), (wq_hbm, wq),
    )
    loads = [pltpu.make_async_copy(a, b, sem.at[i]) for i, (a, b) in enumerate(table)]
    for i in range(4):
        loads.append(
            pltpu.make_async_copy(
                x_hbm.at[pl.ds(block_at(flip, i), QB)], xw.at[pl.ds(i * QB, QB)], sem.at[21 + i]
            )
        )
    for copy in loads:
        copy.start()

    def view(c, za, zb, k, half):
        lanes = ALL if half is None else pl.ds(0, 256) if half == 0 else pl.ds(256, 128)
        return (eg, lg)[c].at[za, zb, k, :, lanes]

    g.view = view

    def plane(d):
        return lax.rem(g.b + d, 16)

    def scatter(src, dst, send, recv):
        def copy(d):
            to = plane(d)
            return pltpu.make_async_remote_copy(
                src(to), dst.at[g.b], send.at[d], recv.at[d], device_id=(to, g.s), device_id_type=MESH
            )

        def arrival(d):
            return pltpu.make_async_remote_copy(
                src(0), dst.at[plane(16 - d)], send.at[d], recv.at[d], device_id=(plane(d), g.s), device_id_type=MESH
            )

        def each(what):
            def step(d, _):
                what(d)
                return 0

            lax.fori_loop(1, 16, step, 0)

        return (
            lambda: each(lambda d: copy(d).start()),
            lambda: each(lambda d: arrival(d).wait_recv()),
            lambda: each(lambda d: copy(d).wait_send()),
        )

    def piece(ref, size):
        def at(to):
            rows = pl.ds(pl.multiple_of(lax.div(to, 2) * size, size), size)
            return ref.at[rows, pl.ds(pl.multiple_of(lax.rem(to, 2) * 384, 128), 384)]

        return at

    loads[9].wait()
    loads[10].wait()
    send_e, wait_e, end_e = scatter(piece(e_half, 16), rs_e, es, er)
    send_t, wait_t, end_t = scatter(lambda to: tag, rs_t, ts, tr)
    send_l, wait_l, end_l = scatter(piece(l_half, 8), rs_l, ls, lr)

    bar = pltpu.get_barrier_semaphore()

    def greet(d, _):
        pl.semaphore_signal(bar, inc=1, device_id=(plane(d), g.s), device_id_type=MESH)
        return 0

    lax.fori_loop(1, 16, greet, 0)
    for dev in (g.devy, g.devd):
        pl.semaphore_signal(bar, inc=1, device_id=dev, device_id_type=MESH)
    pl.semaphore_wait(bar, 17)
    halo = []
    for i, (src, dst) in enumerate(
        (
            (do_hbm.at[pl.ds(768, QB)], do.at[pl.ds(1024, QB)]),
            (do_hbm.at[pl.ds(512, QB)], do.at[pl.ds(1280, QB)]),
            (hf_hbm.at[pl.ds(768, QB)], hf.at[pl.ds(1024, QB)]),
            (hf_hbm.at[pl.ds(512, QB)], hf.at[pl.ds(1280, QB)]),
            (ge.at[pl.ds(pl.multiple_of((1 - flip) * 128, 16), 128)], e_in),
            (gl_out.at[pl.ds(pl.multiple_of((1 - flip) * 64, 16), 64)], gl_in),
        )
    ):
        halo.append(
            pltpu.make_async_remote_copy(
                src, dst, hs.at[i], hr.at[i], device_id=g.devy, device_id_type=MESH
            )
        )
    for copy in (halo[4], halo[0], halo[1], halo[2], halo[3]):
        copy.start()
    send_t()

    def total_of(ref):
        totals = [0.0] * ADAPTERS
        for b in range(16):
            value = ref[b].astype(F32)
            for e in range(ADAPTERS):
                weight = rs_t[b, e : e + 1, :].astype(F32)
                totals[e] = totals[e] + value * jnp.concatenate([weight] * 3, axis=1)
        return jnp.concatenate(totals, axis=0).astype(BF)

    def own_piece(ref, size):
        rows = pl.ds(pl.multiple_of(lax.div(g.b, 2) * size, size), size)
        return ref[rows, pl.ds(pl.multiple_of(g.core * 384, 128), 384)]

    dkT[...] = jnp.zeros_like(dkT)
    dvT[...] = jnp.zeros_like(dvT)
    ga_ref[...] = jnp.zeros_like(ga_ref)
    gbq_ref[...] = jnp.zeros_like(gbq_ref)
    gap = iota((QB, QB), 0) - iota((QB, QB), 1)
    gap = jnp.where(flip == 1, -gap, gap)
    bias[...] = jnp.where(gap <= 0, 0.0, NEG)
    half = iota((1, 128), 1) >= HEAD_DIM
    for copy in loads[:5]:
        copy.wait()

    def picks(pair, first, width):
        head = 2 * pair + lax.div(iota((128, 256), 1), 128)
        row = iota((128, 256), 0) - first - width * head
        return jnp.where((row >= 0) & (row < width), 1.0, 0.0).astype(BF)

    for qb in range(4):
        k0, n, _, _ = PLAN[qb]
        own = min(4 - k0, n)
        rows = pl.ds(qb * QB, QB)
        krows = pl.ds(k0 * QB, n * QB)

        def fetch(pair, s, qb=qb, n=n):
            return prob_copies(n, p_hbm.at[qb, pair], stage.at[s], psem, s)

        for one in fetch(0, 0):
            one.start()

        def pair_step(pair, _, k0=k0, n=n, own=own, rows=rows, krows=krows, fetch=fetch):
            slot = lax.rem(pair, 2)
            for one in fetch(pair, slot):
                one.wait()

            @pl.when(pair < 5)
            def _():
                for one in fetch(pair + 1, 1 - slot):
                    one.start()

            lanes = pl.ds(pl.multiple_of(pair * 128, 128), 128)
            do2 = do[rows, lanes]
            ndl = nn(hf[rows, :], picks(pair, 40, 2))
            k2 = k[krows, lanes]
            v2 = v[krows, lanes]
            qT = q[rows, lanes].T
            doT = do2.T
            dqs = []
            masks = (jnp.logical_not(half), half)
            dps = [nt(jnp.where(mine, do2, jnp.zeros_like(do2)), v2) for mine in masks]
            for h, dp in enumerate(dps):
                spots = [divmod(h * n + t, 3) for t in range(n)]
                p = jnp.concatenate([stage[slot, i, :, j * QB : j * QB + QB] for i, j in spots], axis=1)
                d = ndl[:, h * 128 : (h + 1) * 128]
                ds = (p.astype(F32) * (dp + jnp.concatenate([d] * (2 * n), axis=1))).astype(BF)
                hr = pl.ds(pl.multiple_of(pair * 128 + h * 64, 64), 64)
                kc = pl.ds(k0 * QB, own * QB)
                dvT[hr, kc] += nn(doT[h * 64 : (h + 1) * 64], p[:, 0 : own * QB])
                dqs.append(nn(ds, k2))
                dkT[hr, kc] += nn(qT[h * 64 : (h + 1) * 64], ds[:, 0 : own * QB])
            dq[rows, lanes] = jnp.where(half, dqs[1], dqs[0]) * 0.125
            return 0

        lax.fori_loop(0, 6, pair_step, 0)
        if qb == 0:
            halo[4].wait_recv()
            mine = ge[pl.ds(pl.multiple_of(flip * 128, 16), 128), :]
            e_half[...] = (mine.astype(F32) + e_in[...].astype(F32)).astype(BF)
            send_e()
            for copy in loads[5:9]:
                copy.wait()
        elif qb == 1:
            rs_e[g.b] = own_piece(e_half, 16)
            rs_t[g.b] = tag[...]
            wait_e()
            wait_t()
            eg[g.za, g.zb, g.column(0, 0, 0)] = total_of(rs_e)
            g.send_z(0)
        elif qb == 2:
            g.stage_z(0)
        else:
            g.stage_xy(0)

    for copy in loads[11:]:
        copy.wait()
    for copy in halo[:4]:
        copy.wait_recv()
    def halo_step(pair, _):
        lanes = pl.ds(pl.multiple_of(pair * 128, 128), 128)
        delta_picks = picks(pair, 40, 2)
        top_picks = picks(pair, 4, 3)
        masks = (jnp.logical_not(half), half)
        work = []
        for i, (k0, n) in enumerate(HALO_PLAN):
            rows = pl.ds(1024 + i * QB, QB)
            krows = pl.ds(k0 * QB, n * QB)
            do2 = do[rows, lanes]
            q2 = q[rows, lanes]
            feats = hf[rows, :]
            ndl = nn(feats, delta_picks)
            nm = nn(feats, top_picks)
            keys = jnp.concatenate([k[krows, lanes], fk[krows, :]], axis=1)
            v2 = v[krows, lanes]
            for h, mine in enumerate(masks):
                s = nt(jnp.concatenate([jnp.where(mine, q2, jnp.zeros_like(q2)), fq[rows, :]], axis=1), keys)
                dp = nt(jnp.where(mine, do2, jnp.zeros_like(do2)), v2)
                work.append((k0, n, h, s, dp, nm, ndl, q2.T, do2.T))
        for k0, n, h, s, dp, nm, ndl, qT, doT in work:
            parts = [s[:, t * QB : (t + 1) * QB] for t in range(n)]
            parts[0] = parts[0] + bias[...]
            s = jnp.concatenate(parts, axis=1)
            m = nm[:, h * 128 : (h + 1) * 128]
            p = jnp.exp(s + jnp.concatenate([m] * (2 * n), axis=1))
            d = ndl[:, h * 128 : (h + 1) * 128]
            ds = (p * (dp + jnp.concatenate([d] * (2 * n), axis=1))).astype(BF)
            hr = pl.ds(pl.multiple_of(pair * 128 + h * 64, 64), 64)
            kc = pl.ds(k0 * QB, n * QB)
            dvT[hr, kc] += nn(doT[h * 64 : (h + 1) * 64], p.astype(BF))
            dkT[hr, kc] += nn(qT[h * 64 : (h + 1) * 64], ds)
        return 0

    lax.fori_loop(0, 3, halo_step, 0)
    g.stage_corner(0)
    lax.fori_loop(3, 6, halo_step, 0)
    g.stage_pair(0)

    lane = lax.div(iota((1, 48), 1), 16)
    rank = lax.div(iota((48, 1), 0), 16)

    def proj_step(rb, _):
        start = pl.multiple_of(rb * QB, QB)
        rows = pl.ds(start, QB)
        cosine = cos[rows, :]
        sine = -sin[rows, :]
        low = lowq[rows, :]
        dlow = jnp.zeros((QB, 48), F32)
        for p in range(3):
            if p == 0:
                d = rope(dq[rows, :], cosine, sine)
            else:
                src = (dkT, dvT)[p - 1]
                d = jnp.concatenate([src[pl.ds(c * 128, 128), rows].T for c in range(6)], axis=1)
                if p == 1:
                    d = rope(d, cosine, sine)
            d = d.astype(BF)
            dproj[p, rows, :] = d
            dlow += jnp.where(lane == p, nt(d, bqkv[...]), 0.0)
            gbq_ref[...] += jnp.where(rank == p, tn(low, d), 0.0)
        dlow = dlow.astype(BF)
        lowq[rows, :] = dlow
        ga_ref[...] += tn(dlow, xw[rows, :])
        return 0

    lax.fori_loop(0, 4, proj_step, 0)
    gl_out[0:48] = ga_ref[...].astype(BF)
    gl_out[48:96] = gbq_ref[...].astype(BF)
    gl_out[96:112] = gao[...].astype(BF)
    gl_out[112:128] = jnp.zeros((16, D), BF)
    halo[5].start()

    def dx_rows(rb):
        rows = pl.ds(rb * QB, QB)
        total = done[rows, :] + nn(lowq[rows, :], aqkv[...])
        for p in range(3):
            total += nt(dproj[p, rows, :], wq[p].reshape(D, D))
        dx_ref[rows, :] = total.astype(BF)
        copy = pltpu.make_async_copy(dx_ref.at[rows], dx_hbm.at[pl.ds(block_at(flip, rb), QB)], dsem.at[rb])
        copy.start()
        return copy

    tails = [dx_rows(0)]
    halo[5].wait_recv()
    mine = gl_out[pl.ds(pl.multiple_of(flip * 64, 16), 64), :]
    l_half[...] = mine.astype(F32) + gl_in[...].astype(F32)
    send_l()
    tails.append(dx_rows(1))
    rs_l[g.b] = own_piece(l_half, 8)
    wait_l()
    lg[g.za, g.zb, g.column(0, 0, 0)] = total_of(rs_l)
    g.send_z(1)
    tails.append(dx_rows(2))
    g.stage_z(1)
    tails.append(dx_rows(3))
    g.stage_core(0)
    keep_e = pltpu.make_async_copy(eg, eg_hbm, gsem.at[0])
    keep_e.start()
    g.stage_xy(1)
    for copy in halo:
        copy.wait_send()
    end_e()
    end_t()
    end_l()
    g.finish(0)
    g.stage_core(1)
    keep_l = pltpu.make_async_copy(lg, lg_hbm, gsem.at[1])
    keep_l.start()
    g.finish(1)
    keep_e.wait()
    keep_l.wait()
    for copy in tails:
        copy.wait()


def k4_kernel(
    eg_hbm, lg_hbm, mixed_hbm, dx_hbm,
    mixed_out, dx_out, gin_hbm, gdn_hbm, gout_hbm, gff_hbm,
    eg, lg, gin_ref, gdn_ref, gout_ref, gff_ref, mixed, dx, sem,
):
    moves = [
        pltpu.make_async_copy(a, b, sem.at[i])
        for i, (a, b) in enumerate(
            (
                (eg_hbm, eg), (lg_hbm, lg), (mixed_hbm, mixed), (dx_hbm, dx),
                (gdn_ref, gdn_hbm), (gff_ref, gff_hbm), (gin_ref, gin_hbm), (gout_ref, gout_hbm),
                (mixed, mixed_out), (dx, dx_out),
            )
        )
    ]
    for copy in moves[:4]:
        copy.start()

    def blocks(ref):
        for z in range(4):
            for xx in range(2):
                for core in range(2):
                    for y in range(2):
                        yield (
                            y * 8 + z * 2 + xx, core * 384,
                            ref[z // 2, z % 2, (xx * 2 + core) * 2 + y].astype(F32),
                        )

    moves[0].wait()
    for group, lane0, value in blocks(eg):
        lanes = slice(lane0, lane0 + 384)
        for e in range(ADAPTERS):
            rows = value[16 * e : 16 * e + 16]
            if group < 2:
                gin_ref[e, 64 + 16 * group : 80 + 16 * group, lanes] = rows
            elif group < 4:
                gout_ref[e, 16 + 16 * group : 32 + 16 * group, lanes] = rows
            elif group < 8:
                at = (group - 4) * D + lane0
                gdn_ref[e, :, at : at + 384] = rows
            else:
                at = (group - 8) // 2 * D + lane0
                first = 16 * (group % 2)
                gff_ref[e, first : first + 16, at : at + 384] = rows

    for i in (2, 3):
        moves[i].wait()
    for i in (4, 5, 8, 9):
        moves[i].start()
    moves[1].wait()
    for group, lane0, value in blocks(lg):
        lanes = slice(lane0, lane0 + 384)
        for e in range(ADAPTERS):
            rows = value[8 * e : 8 * e + 8]
            if group < 6:
                gin_ref[e, 8 * group : 8 * group + 8, lanes] = rows
            elif group < 12:
                gout_ref[e, 8 * group - 48 : 8 * group - 40, lanes] = rows
            elif group < 14:
                gin_ref[e, 8 * group - 48 : 8 * group - 40, lanes] = rows

    for copy in moves[6:8]:
        copy.start()
    for copy in moves[4:]:
        copy.wait()


def sds(shape, dtype):
    return jax.ShapeDtypeStruct(shape, dtype)


ANY = functools.partial(pl.BlockSpec, memory_space=pl.ANY)
INV = functools.partial(pl.BlockSpec, memory_space=pltpu.VMEM)


def kf_call(*args):
    outs = [
        (ANY, (6, QB, D), BF), (ANY, (6, QB, D), BF), (ANY, (6, QB, D), BF), (ANY, (4, 6, 4, QB, D), BF),
        (ANY, (1024, D), BF), (ANY, (1024, D), BF), (ANY, (1024, 128), BF),
        (ANY, (1536, 48), BF), (ANY, (1024, D), F32), (ANY, (1536, 128), F32), (ANY, (1536, 128), F32),
        (ANY, (1536, 128), BF), (ANY, (1536, 128), BF),
        (ANY, (256, D), BF), (ANY, (16, D), F32), (ANY, (16, 128), BF), (ANY, (48, D), BF), (ANY, (48, D), BF),
        (ANY, (3, 2, 2, 8, 24, D), BF),
    ]
    V = pltpu.VMEM
    scratch = [
        V((1, 2048), jnp.int32), V((1, 128), F32), pltpu.SMEM((1, 1), jnp.int32), V((2, D), F32), V((2, D), F32),
        V((1024, 128), BF), V((256, D), BF), V((16, D), F32), V((16, 128), BF), V((48, D), BF), V((48, D), BF),
        pltpu.SemaphoreType.DMA((5,)), pltpu.SemaphoreType.DMA((5,)),
        V((16, D), BF), V((16, D), BF), V((32, D), BF), V((4, 16, D), BF), V((16, D), BF), V((4, D), F32),
        V((32, D), F32), V((4, 16, D), F32), V((16, D), F32), V((16, D), F32), V((4, 32, D), F32),
        V((3, 2, 2, 8, 24, D), BF), V((2, 2, 8, 24, D), BF), V((4, 2, 2, 2, 8, 24, D), BF), V((2, 2, 8, 96, D), BF),
        V((32, QB, D), BF), V((1536, D), BF), V((1024, D), BF), V((1024, D), F32),
        V((1024, D), F32), V((1024, D), F32), V((1024, D), BF), V((1024, D), BF),
        V((1536, 128), F32), V((1536, 128), F32), V((1536, 128), BF), V((1536, 128), BF), V((2, QB, QB), F32),
        V((1024, 128), F32), V((1536, 48), BF), V((1024, 16), BF), V((1024, 32), BF),
        V((1024, 16), BF), V((512, D), F32), V((512, 32), F32), V((3, 48, D), BF),
        V((4, 32, D), BF), V((4, 32, D), BF), V((D, 128), BF), V((1024, D), BF), V((1024, D), BF),
        pltpu.SemaphoreType.DMA((13,)), pltpu.SemaphoreType.DMA((10,)), pltpu.SemaphoreType.DMA((7,)), pltpu.SemaphoreType.DMA((8,)), pltpu.SemaphoreType.DMA((10,)),
        pltpu.SemaphoreType.DMA((4,)), pltpu.SemaphoreType.DMA((4,)), pltpu.SemaphoreType.DMA((4,)),
    ]
    scratch += gather_sems(NCHUNK)
    return pl.pallas_call(
        kf_kernel,
        out_shape=[sds(s, t) for _, s, t in outs],
        in_specs=[ANY()] * 15,
        out_specs=[m() for m, _, _ in outs],
        scratch_shapes=scratch,
        compiler_params=pltpu.CompilerParams(
            vmem_limit_bytes=VMEM_LIMIT, collective_id=1, has_side_effects=True
        ),
    )(*args)


def k3_call(*args):
    V = pltpu.VMEM
    S = pltpu.SemaphoreType.DMA
    scratch = [
        V((256, D), BF), V((16, D), F32), V((16, 128), BF), V((48, D), BF), V((48, D), BF), S((2,)),
        V((48, D), F32), V((48, D), F32), V((3, 1024, D), BF), V((2, 2, 8, 64, 384), BF), V((2, 2, 8, 32, 384), BF),
        V((128, D), BF), V((128, D), BF), V((16, 16, 384), BF), V((16, 16, 128), BF), V((128, D), BF), V((64, D), BF),
        V((64, D), F32), V((16, 8, 384), F32), V((1024, D), BF),
        V((1024, D), BF), V((1536, D), BF), V((1536, D), BF), V((1536, D), BF), V((1536, D), BF), V((1536, 128), BF),
        V((1536, 48), BF), V((1024, D), F32), V((1536, 128), F32), V((1536, 128), F32), V((1536, 128), BF),
        V((1536, 128), BF), V((3, 2, 2, 8, 24, D), BF), V((2, 4, QB, D), BF), V((1024, D), F32), V((D, 1024), F32),
        V((D, 1024), F32), V((QB, QB), F32), S((25,)), S((4,)), S((6,)), S((6,)),
        S((16,)), S((16,)), S((16,)), S((16,)), S((16,)), S((16,)), S((4,)),
    ]
    return pl.pallas_call(
        k3_kernel,
        out_shape=[
            sds((1024, D), BF), sds((2, 2, 8, 64, 384), BF), sds((2, 2, 8, 32, 384), BF),
        ],
        in_specs=[ANY()] * 19,
        out_specs=[ANY()] * 3,
        scratch_shapes=scratch + gather_sems(2),
        compiler_params=pltpu.CompilerParams(
            vmem_limit_bytes=VMEM_LIMIT, collective_id=2, has_side_effects=True
        ),
    )(*args)


def k4_call(*args):
    V = pltpu.VMEM
    grads = [(4, 96, D), (4, 16, FF), (4, 80, D), (4, 32, FF)]
    return pl.pallas_call(
        k4_kernel,
        out_shape=[sds((1024, D), BF), sds((1024, D), BF)] + [sds(s, F32) for s in grads],
        in_specs=[ANY()] * 4,
        out_specs=[ANY()] * 6,
        scratch_shapes=[V((2, 2, 8, 64, 384), BF), V((2, 2, 8, 32, 384), BF)]
        + [V(s, F32) for s in grads]
        + [V((1024, D), BF), V((1024, D), BF), pltpu.SemaphoreType.DMA((10,))],
        compiler_params=pltpu.CompilerParams(vmem_limit_bytes=VMEM_LIMIT),
    )(*args)


def fast(
    tokens, cotangent, segments, adapter_index, qkv_weight, out_weight, ffn_in_weight, ffn_out_weight,
    norm_gain, norm_bias, adapt_in, adapt_down, adapt_out, adapt_ffn,
):
    x = tokens[0]
    freq = np.power(np.float32(ROPE_BASE), np.float32(-2.0 / HEAD_DIM) * np.arange(HEAD_DIM // 2, dtype=np.float32))
    freq = np.tile(freq.astype(np.float32), 4)[None]
    q, k, v, p, mixed, do, hf, lowq, done, cos, sin, fq, fk, ge, gao, tag, aqkv, bqkv, wq = kf_call(
        x, cotangent[0], segments, freq, adapter_index, norm_gain[0], norm_bias[0],
        adapt_in[0].transpose(0, 1, 3, 2).reshape(ADAPTERS, 96, D), adapt_down[0].transpose(0, 2, 1),
        adapt_out[0].reshape(ADAPTERS, 80, D), adapt_ffn[0].reshape(ADAPTERS, 32, FF),
        qkv_weight[0], out_weight[0], ffn_in_weight[0], ffn_out_weight[0],
    )
    q, k, v = (a.reshape(1536, D) for a in (q, k, v))
    dx, eg, lg = k3_call(
        x, q, k, v, p, do, hf, ge, gao, tag, lowq, done, cos, sin, fq, fk, aqkv, bqkv, wq
    )
    mixed, dx, g_in, g_dn, g_out, g_ff = k4_call(eg, lg, mixed, dx)
    return (
        mixed[None], dx[None], g_in.reshape(ADAPTERS, 6, 16, D).transpose(0, 1, 3, 2)[None],
        g_dn.transpose(0, 2, 1)[None], g_out.reshape(ADAPTERS, 5, 16, D)[None], g_ff.reshape(ADAPTERS, 2, 16, FF)[None],
    )


def solution(mesh):
    here = fast if dict(mesh.shape) == {"batch": 16, "seq": 2} else shards
    return jax.shard_map(
        here,
        mesh=mesh,
        in_specs=(
            P("batch", "seq", None),
            P("batch", "seq", None),
            P("batch", None),
            P("batch", None),
            P(None, None, ("batch", "seq"), None),
            P(None, ("batch", "seq"), None),
            P(None, None, ("batch", "seq"), None),
            P(None, ("batch", "seq"), None),
            P(),
            P(),
            P(),
            P(),
            P(),
            P(),
        ),
        out_specs=(P("batch", "seq", None), P("batch", "seq", None), P(), P(), P(), P()),
        check_vma=False,
    )
```

```python
import functools
import math

import jax
import jax.numpy as jnp
import numpy as np
from jax import lax
from jax.experimental import pallas as pl
from jax.experimental.pallas import tpu as pltpu
from jax.sharding import PartitionSpec as P

HEADS = 12
HEAD_DIM = 64
ADAPTERS = 4
LAYERS = 1
HALF = 512
D = HEADS * HEAD_DIM
FF = 4 * D


EPSILON = 1e-06
ROPE_BASE = 1000.0
PRECISE = lax.Precision.HIGHEST


def shifted(array, axis, by):
    count = lax.axis_size(axis)
    pairs = [(i, i + by) for i in range(count) if 0 <= i + by < count]
    return lax.ppermute(array, axis, pairs)


def doc_positions(segment_ids):
    position_ids = jnp.arange(segment_ids.shape[-1], dtype=jnp.int32)
    starts_here = jnp.concatenate(
        [
            jnp.ones(segment_ids.shape[:-1] + (1,), dtype=jnp.bool_),
            segment_ids[..., 1:] != segment_ids[..., :-1],
        ],
        axis=-1,
    )
    doc_start = lax.cummax(jnp.where(starts_here, position_ids, 0), axis=segment_ids.ndim - 1)
    return (position_ids - doc_start).astype(jnp.float32)


def rope_tables(segment_ids):
    positions = doc_positions(segment_ids)
    frequency = jnp.power(ROPE_BASE, -2.0 * jnp.arange(HEAD_DIM // 2, dtype=jnp.float32) / HEAD_DIM)
    angles = positions[..., None] * frequency
    return (jnp.cos(angles), jnp.sin(angles))


def rotate(vectors, cosine_table, sine_table):
    half_dim = vectors.shape[-1] // 2
    first_half = vectors[..., :half_dim]
    second_half = vectors[..., half_dim:]
    cosine_rows = cosine_table[..., None, :]
    sine_rows = sine_table[..., None, :]
    return jnp.concatenate(
        [
            first_half * cosine_rows - second_half * sine_rows,
            second_half * cosine_rows + first_half * sine_rows,
        ],
        axis=-1,
    )


def norm_apply(residual, gain_row, bias_row):
    centre = residual - jnp.mean(residual, axis=-1, keepdims=True)
    spread = jnp.mean(centre * centre, axis=-1, keepdims=True)
    return centre * lax.rsqrt(spread + EPSILON) * gain_row + bias_row


def split_heads(merged, group_count):
    seqs_here, row_count, _ = merged.shape
    return merged.reshape(seqs_here, row_count, group_count, -1, HEAD_DIM).transpose(2, 0, 1, 3, 4)


def join_heads(grouped):
    group_count, seqs_here, row_count, heads_group, head_size = grouped.shape
    return grouped.transpose(1, 2, 0, 3, 4).reshape(
        seqs_here, row_count, group_count * heads_group * head_size
    )


def shards(
    tokens,
    cotangent,
    segments,
    adapter_index,
    qkv_weight,
    out_weight,
    ffn_in_weight,
    ffn_out_weight,
    norm_gain,
    norm_bias,
    adapt_in,
    adapt_down,
    adapt_out,
    adapt_ffn,
):
    seqs_here, tok_rows, model_width = tokens.shape
    heads_group = math.gcd(HEADS, 4)
    group_count = HEADS // heads_group
    score_scale = 1.0 / math.sqrt(HEAD_DIM)
    seq_count = lax.axis_size("seq")
    row_base = lax.axis_index("seq") * tok_rows
    shift_plan = []
    for distance in range(1, min(seq_count, HALF // tok_rows + 2)):
        row_count = min(tok_rows, HALF - (distance - 1) * tok_rows)
        if row_count > 0:
            shift_plan.append((distance, row_count))
            shift_plan.append((-distance, row_count))
    left_total = sum((plan_item[1] for plan_item in shift_plan if plan_item[0] > 0))
    key_rows = 2 * left_total + tok_rows
    key_places = {}
    passed_rows = 0
    for distance, row_count in shift_plan:
        if distance > 0:
            key_places[distance] = left_total - passed_rows - row_count
            key_places[-distance] = left_total + tok_rows + passed_rows
            passed_rows += row_count
    cosine_all, sine_all = rope_tables(segments)
    cosine_here = lax.dynamic_slice_in_dim(cosine_all, row_base, tok_rows, 1)
    sine_here = lax.dynamic_slice_in_dim(sine_all, row_base, tok_rows, 1)
    padded_ids = jnp.pad(segments, ((0, 0), (HALF, HALF)), constant_values=-1)
    key_ids = lax.dynamic_slice_in_dim(padded_ids, row_base - left_total + HALF, key_rows, 1)
    query_ids = lax.dynamic_slice_in_dim(segments, row_base, tok_rows, 1)
    offsets = (
        jnp.arange(tok_rows, dtype=jnp.int32)[:, None]
        - jnp.arange(key_rows, dtype=jnp.int32)[None, :]
        + left_total
    )
    visible = (query_ids[:, :, None] == key_ids[:, None, :]) & (jnp.abs(offsets) <= HALF)[None]
    slot_hits = adapter_index[:, 0][:, None] == jnp.arange(ADAPTERS, dtype=jnp.int32)[None, :]
    slot_low = slot_hits.astype(jnp.bfloat16)
    slot_full = slot_hits.astype(jnp.float32)

    def select_adapter(table):
        return jnp.einsum(
            "se,le...->ls...", slot_low, table, preferred_element_type=jnp.float32
        ).astype(jnp.bfloat16)

    def spread_slots(per_sequence):
        return jnp.einsum("se,s...->e...", slot_full, per_sequence, precision=PRECISE)

    chosen_in = select_adapter(adapt_in)
    chosen_down = select_adapter(adapt_down)
    chosen_out = select_adapter(adapt_out)
    chosen_ffn = select_adapter(adapt_ffn)

    def forward_group(items):
        query_block, key_block, value_block = items
        scores = (
            jnp.einsum(
                "sqhd,skhd->shqk", query_block, key_block, preferred_element_type=jnp.float32
            )
            * score_scale
        )
        scores = jnp.where(visible[:, None], scores, -1e30)
        biggest = jnp.max(scores, axis=-1, keepdims=True)
        lifted = jnp.exp(scores - biggest)
        row_total = jnp.sum(lifted, axis=-1, keepdims=True)
        probability = (lifted / row_total).astype(jnp.bfloat16)
        result = jnp.einsum(
            "shqk,skhd->sqhd", probability, value_block, preferred_element_type=jnp.float32
        )
        return (result.astype(jnp.bfloat16), (biggest + jnp.log(row_total))[..., 0])

    def backward_group(items):
        query_block, key_block, value_block, grad_block, log_total = items
        scores = (
            jnp.einsum(
                "sqhd,skhd->shqk", query_block, key_block, preferred_element_type=jnp.float32
            )
            * score_scale
        )
        scores = jnp.where(visible[:, None], scores, -1e30)
        probability = jnp.exp(scores - log_total[..., None])
        d_prob = jnp.einsum(
            "sqhd,skhd->shqk", grad_block, value_block, preferred_element_type=jnp.float32
        )
        delta = jnp.sum(probability * d_prob, axis=-1, keepdims=True)
        d_score = (probability * (d_prob - delta)).astype(jnp.bfloat16)
        d_query = (
            jnp.einsum("shqk,skhd->sqhd", d_score, key_block, preferred_element_type=jnp.float32)
            * score_scale
        )
        d_key = (
            jnp.einsum("shqk,sqhd->skhd", d_score, query_block, preferred_element_type=jnp.float32)
            * score_scale
        )
        d_value = jnp.einsum(
            "shqk,sqhd->skhd",
            probability.astype(jnp.bfloat16),
            grad_block,
            preferred_element_type=jnp.float32,
        )
        return (d_query, d_key, d_value)

    state = tokens.astype(jnp.float32)
    layer_index = 0
    w_qkv = lax.all_gather(qkv_weight[layer_index], ("batch", "seq"), axis=1, tiled=True)
    w_out = lax.all_gather(out_weight[layer_index], ("batch", "seq"), axis=0, tiled=True)
    w_in = lax.all_gather(ffn_in_weight[layer_index], ("batch", "seq"), axis=1, tiled=True)
    w_down = lax.all_gather(ffn_out_weight[layer_index], ("batch", "seq"), axis=0, tiled=True)
    held = [(w_qkv, w_out, w_in, w_down)]
    act_one = state.astype(jnp.bfloat16)
    low_qkv = jnp.einsum(
        "std,spdr->pstr",
        act_one,
        chosen_in[layer_index][:, 0:3],
        preferred_element_type=jnp.float32,
    ).astype(jnp.bfloat16)
    proj = jnp.einsum(
        "std,pde->pste", act_one, w_qkv, preferred_element_type=jnp.float32
    ) + jnp.einsum(
        "pstr,spre->pste",
        low_qkv,
        chosen_out[layer_index][:, 0:3],
        preferred_element_type=jnp.float32,
    )
    queries = (
        rotate(proj[0].reshape(seqs_here, tok_rows, HEADS, HEAD_DIM), cosine_here, sine_here)
        .astype(jnp.bfloat16)
        .reshape(seqs_here, tok_rows, model_width)
    )
    key_rot = (
        rotate(proj[1].reshape(seqs_here, tok_rows, HEADS, HEAD_DIM), cosine_here, sine_here)
        .astype(jnp.bfloat16)
        .reshape(seqs_here, tok_rows, model_width)
    )
    key_value = jnp.stack([key_rot, proj[2].astype(jnp.bfloat16)])
    edges = {}
    for step_by, row_count in shift_plan:
        if step_by > 0:
            outgoing = key_value[:, :, tok_rows - row_count :]
        else:
            outgoing = key_value[:, :, :row_count]
        edges[step_by] = shifted(outgoing, "seq", step_by)
    earlier = [edges[distance] for distance, row_count in reversed(shift_plan) if distance > 0]
    later = [edges[-distance] for distance, row_count in shift_plan if distance > 0]
    window = jnp.concatenate(earlier + [key_value] + later, axis=2)
    heads_out, log_total = lax.map(
        forward_group,
        (
            split_heads(queries, group_count),
            split_heads(window[0], group_count),
            split_heads(window[1], group_count),
        ),
    )
    attended = join_heads(heads_out)
    low_out = jnp.einsum(
        "std,sdr->str", attended, chosen_in[layer_index][:, 3], preferred_element_type=jnp.float32
    ).astype(jnp.bfloat16)
    branch = jnp.einsum(
        "std,de->ste", attended, w_out, preferred_element_type=jnp.float32
    ) + jnp.einsum(
        "str,sre->ste", low_out, chosen_out[layer_index][:, 3], preferred_element_type=jnp.float32
    )
    resid_one = state + branch
    hidden = norm_apply(resid_one, norm_gain[layer_index, 0], norm_bias[layer_index, 0])
    act_two = hidden.astype(jnp.bfloat16)
    low_ffn = jnp.einsum(
        "std,spdr->pstr",
        act_two,
        chosen_in[layer_index][:, 4:6],
        preferred_element_type=jnp.float32,
    ).astype(jnp.bfloat16)
    gate_up = jnp.einsum(
        "std,pdf->pstf", act_two, w_in, preferred_element_type=jnp.float32
    ) + jnp.einsum(
        "pstr,sprf->pstf", low_ffn, chosen_ffn[layer_index], preferred_element_type=jnp.float32
    )
    inner = (jax.nn.silu(gate_up[0]) * gate_up[1]).astype(jnp.bfloat16)
    low_down = jnp.einsum(
        "stf,sfr->str", inner, chosen_down[layer_index], preferred_element_type=jnp.float32
    ).astype(jnp.bfloat16)
    branch_two = jnp.einsum(
        "stf,fe->ste", inner, w_down, preferred_element_type=jnp.float32
    ) + jnp.einsum(
        "str,sre->ste", low_down, chosen_out[layer_index][:, 4], preferred_element_type=jnp.float32
    )
    resid_two = hidden + branch_two
    kept = [
        (
            act_one,
            low_qkv,
            queries,
            window,
            log_total,
            attended,
            low_out,
            resid_one,
            act_two,
            low_ffn,
            gate_up,
            inner,
            low_down,
            resid_two,
        )
    ]
    state = norm_apply(resid_two, norm_gain[layer_index, 1], norm_bias[layer_index, 1])
    mixed = state.astype(jnp.bfloat16)
    grad = cotangent.astype(jnp.float32)
    collected = [None] * LAYERS
    for layer_index in reversed(range(LAYERS)):
        (
            act_one,
            low_qkv,
            queries,
            window,
            log_total,
            attended,
            low_out,
            resid_one,
            act_two,
            low_ffn,
            gate_up,
            inner,
            low_down,
            resid_two,
        ) = kept[layer_index]
        w_qkv, w_out, w_in, w_down = held[layer_index]
        gain_two = norm_gain[layer_index, 1]
        bias_two = norm_bias[layer_index, 1]
        _, pull_two = jax.vjp(lambda residual: norm_apply(residual, gain_two, bias_two), resid_two)
        (d_resid_two,) = pull_two(grad)
        d_branch_two = d_resid_two.astype(jnp.bfloat16)
        d_low_down = jnp.einsum(
            "ste,sre->str",
            d_branch_two,
            chosen_out[layer_index][:, 4],
            preferred_element_type=jnp.float32,
        ).astype(jnp.bfloat16)
        g_out_down = jnp.einsum(
            "str,ste->sre", low_down, d_branch_two, preferred_element_type=jnp.float32
        )
        g_down = jnp.einsum("stf,str->sfr", inner, d_low_down, preferred_element_type=jnp.float32)
        d_inner = jnp.einsum(
            "ste,fe->stf", d_branch_two, w_down, preferred_element_type=jnp.float32
        ) + jnp.einsum(
            "str,sfr->stf", d_low_down, chosen_down[layer_index], preferred_element_type=jnp.float32
        )
        _, pull_act = jax.vjp(
            lambda gate_part, up_part: jax.nn.silu(gate_part) * up_part, gate_up[0], gate_up[1]
        )
        d_gate, d_up = pull_act(d_inner)
        d_gate_up = jnp.stack([d_gate, d_up]).astype(jnp.bfloat16)
        d_low_ffn = jnp.einsum(
            "pstf,sprf->pstr",
            d_gate_up,
            chosen_ffn[layer_index],
            preferred_element_type=jnp.float32,
        ).astype(jnp.bfloat16)
        g_ffn = jnp.einsum(
            "pstr,pstf->sprf", low_ffn, d_gate_up, preferred_element_type=jnp.float32
        )
        g_in_ffn = jnp.einsum(
            "std,pstr->spdr", act_two, d_low_ffn, preferred_element_type=jnp.float32
        )
        ffn_in_sum = spread_slots(g_in_ffn)
        ffn_down_sum = spread_slots(g_down)
        ffn_out_sum = spread_slots(g_out_down[:, None])
        ffn_ffn_sum = spread_slots(g_ffn)
        d_hidden = (
            d_resid_two
            + jnp.einsum("pstf,pdf->std", d_gate_up, w_in, preferred_element_type=jnp.float32)
            + jnp.einsum(
                "pstr,spdr->std",
                d_low_ffn,
                chosen_in[layer_index][:, 4:6],
                preferred_element_type=jnp.float32,
            )
        )
        gain_one = norm_gain[layer_index, 0]
        bias_one = norm_bias[layer_index, 0]
        _, pull_one = jax.vjp(lambda residual: norm_apply(residual, gain_one, bias_one), resid_one)
        (d_resid_one,) = pull_one(d_hidden)
        d_branch = d_resid_one.astype(jnp.bfloat16)
        d_low_out = jnp.einsum(
            "ste,sre->str",
            d_branch,
            chosen_out[layer_index][:, 3],
            preferred_element_type=jnp.float32,
        ).astype(jnp.bfloat16)
        g_out_att = jnp.einsum(
            "str,ste->sre", low_out, d_branch, preferred_element_type=jnp.float32
        )
        g_in_att = jnp.einsum(
            "std,str->sdr", attended, d_low_out, preferred_element_type=jnp.float32
        )
        d_attended = (
            jnp.einsum("ste,de->std", d_branch, w_out, preferred_element_type=jnp.float32)
            + jnp.einsum(
                "str,sdr->std",
                d_low_out,
                chosen_in[layer_index][:, 3],
                preferred_element_type=jnp.float32,
            )
        ).astype(jnp.bfloat16)
        d_query_heads, d_key_heads, d_value_heads = lax.map(
            backward_group,
            (
                split_heads(queries, group_count),
                split_heads(window[0], group_count),
                split_heads(window[1], group_count),
                split_heads(d_attended, group_count),
                log_total,
            ),
        )
        d_query = join_heads(d_query_heads)
        d_window = jnp.stack([join_heads(d_key_heads), join_heads(d_value_heads)])
        d_pair = d_window[:, :, left_total : left_total + tok_rows]
        for step_by, row_count in shift_plan:
            returning = lax.slice_in_dim(
                d_window, key_places[step_by], key_places[step_by] + row_count, axis=2
            )
            arrived = shifted(returning.astype(jnp.bfloat16), "seq", -step_by).astype(
                returning.dtype
            )
            if step_by > 0:
                d_pair = d_pair.at[:, :, tok_rows - row_count :].add(arrived)
            else:
                d_pair = d_pair.at[:, :, :row_count].add(arrived)
        d_query_rot = rotate(
            d_query.reshape(seqs_here, tok_rows, HEADS, HEAD_DIM), cosine_here, -sine_here
        ).reshape(seqs_here, tok_rows, model_width)
        d_key_rot = rotate(
            d_pair[0].reshape(seqs_here, tok_rows, HEADS, HEAD_DIM), cosine_here, -sine_here
        ).reshape(seqs_here, tok_rows, model_width)
        d_proj = jnp.stack([d_query_rot, d_key_rot, d_pair[1]]).astype(jnp.bfloat16)
        d_low_qkv = jnp.einsum(
            "pste,spre->pstr",
            d_proj,
            chosen_out[layer_index][:, 0:3],
            preferred_element_type=jnp.float32,
        ).astype(jnp.bfloat16)
        g_out_qkv = jnp.einsum(
            "pstr,pste->spre", low_qkv, d_proj, preferred_element_type=jnp.float32
        )
        g_in_qkv = jnp.einsum(
            "std,pstr->spdr", act_one, d_low_qkv, preferred_element_type=jnp.float32
        )
        grad = (
            d_resid_one
            + jnp.einsum("pste,pde->std", d_proj, w_qkv, preferred_element_type=jnp.float32)
            + jnp.einsum(
                "pstr,spdr->std",
                d_low_qkv,
                chosen_in[layer_index][:, 0:3],
                preferred_element_type=jnp.float32,
            )
        )
        att_in_sum = spread_slots(jnp.concatenate([g_in_qkv, g_in_att[:, None]], axis=1))
        att_out_sum = spread_slots(jnp.concatenate([g_out_qkv, g_out_att[:, None]], axis=1))
        collected[layer_index] = (
            jnp.concatenate([att_in_sum, ffn_in_sum], axis=1),
            ffn_down_sum,
            jnp.concatenate([att_out_sum, ffn_out_sum], axis=1),
            ffn_ffn_sum,
        )
    input_grad = grad.astype(jnp.bfloat16)
    stack_in = jnp.stack([collected[0][0]])
    stack_down = jnp.stack([collected[0][1]])
    stack_out = jnp.stack([collected[0][2]])
    stack_ffn = jnp.stack([collected[0][3]])
    stack_in, stack_down, stack_out, stack_ffn = lax.psum(
        (stack_in, stack_down, stack_out, stack_ffn), ("batch", "seq")
    )
    return (mixed, input_grad, stack_in, stack_down, stack_out, stack_ffn)


MESH = pl.DeviceIdType.MESH
NCHUNK = 10
ALL = slice(None)


class Gather:
    def __init__(self, sems, direct=(), diagonal=()):
        self.direct = direct
        self.diagonal = diagonal
        (
            self.zs, self.zr, self.xs, self.xr, self.ys, self.yr, self.ds, self.dr, self.es, self.er, self.fs, self.fr,
            self.cs, self.cr,
        ) = sems
        b = lax.axis_index("batch")
        self.b = b
        self.s = lax.axis_index("seq")
        self.core = lax.rem(b, 2)
        self.x = lax.rem(lax.div(b, 2), 2)
        self.z = lax.div(b, 4)
        self.za = lax.div(self.z, 2)
        self.zb = lax.rem(self.z, 2)
        self.devx = (b + 2 - 4 * self.x, self.s)
        self.devy = (b, 1 - self.s)
        self.devd = (b + 2 - 4 * self.x, 1 - self.s)
        self.devc = (b + 1 - 2 * self.core, self.s)
        self.devp = (b + 4 - 8 * self.zb, self.s)

    def column(self, dx, dy, dc):
        x = 1 - self.x if dx else self.x
        y = 1 - self.s if dy else self.s
        c = 1 - self.core if dc else self.core
        return (x * 2 + c) * 2 + y

    def devz(self, z):
        return (z * 4 + self.x * 2 + self.core, self.s)

    def copy(self, c, za, zb, k, half, dev, send, recv):
        v = self.view(c, za, zb, k, half)
        return pltpu.make_async_remote_copy(v, v, send, recv, device_id=dev, device_id_type=MESH)

    def to_z(self, c, z):
        return self.copy(
            c, self.za, self.zb, self.column(0, 0, 0), None, self.devz(z), self.zs.at[c, z], self.zr.at[c, self.z]
        )

    def from_z(self, c, z):
        return self.copy(
            c, lax.div(z, 2), lax.rem(z, 2), self.column(0, 0, 0), None, self.devz(z), self.zs.at[c, z], self.zr.at[c, z]
        )

    def on_x(self, c, arriving):
        return self.copy(c, ALL, ALL, self.column(arriving, 0, 0), None, self.devx, self.xs.at[c], self.xr.at[c])

    def on_y(self, c, arriving):
        return self.copy(c, ALL, ALL, self.column(0, arriving, 0), None, self.devy, self.ys.at[c], self.yr.at[c])

    def on_diagonal(self, c, arriving):
        return self.copy(c, ALL, ALL, self.column(arriving, arriving, 0), None, self.devd, self.ds.at[c], self.dr.at[c])

    def parity(self, c):
        return ALL if c in self.direct else self.zb

    def corner_x(self, c, arriving):
        k = self.column(arriving, 1, 0)
        return self.copy(c, ALL, self.parity(c), k, 0, self.devx, self.ds.at[c], self.dr.at[c])

    def corner_y(self, c, arriving):
        k = self.column(1, arriving, 0)
        return self.copy(c, ALL, self.parity(c), k, 1, self.devy, self.es.at[c], self.er.at[c])

    def corner_z(self, c, arriving):
        zb = 1 - self.zb if arriving else self.zb
        return self.copy(c, ALL, zb, self.column(1, 1, 0), None, self.devp, self.fs.at[c], self.fr.at[c])

    def on_core(self, c, kind, arriving):
        k = self.column(kind & 1, kind >> 1, arriving)
        return self.copy(c, ALL, ALL, k, None, self.devc, self.cs.at[c, kind], self.cr.at[c, kind])

    def others(self):
        z = self.z
        first = jnp.where(z == 0, 1, z - 1)
        second = jnp.where(z == 0, 2, jnp.where(z == 3, 1, z + 1))
        third = jnp.where(z <= 1, 3, 0)
        return first, second, third

    def partners(self):
        return [self.devx, self.devy, self.devc] + [self.devz(z) for z in self.others()]

    def barrier(self, devices):
        bar = pltpu.get_barrier_semaphore()
        for dev in devices:
            pl.semaphore_signal(bar, inc=1, device_id=dev, device_id_type=MESH)
        pl.semaphore_wait(bar, len(devices))

    def send_z(self, c):
        for z in self.others():
            self.to_z(c, z).start()

    def stage_z(self, c):
        for z in self.others():
            self.from_z(c, z).wait_recv()
        self.on_x(c, 0).start()
        self.on_y(c, 0).start()
        if c in self.diagonal:
            self.on_diagonal(c, 0).start()
        self.on_core(c, 0, 0).start()

    def stage_xy(self, c):
        self.on_x(c, 1).wait_recv()
        if c not in self.diagonal:
            self.corner_y(c, 0).start()
        self.on_core(c, 1, 0).start()
        self.on_y(c, 1).wait_recv()
        if c not in self.diagonal:
            self.corner_x(c, 0).start()
        self.on_core(c, 2, 0).start()
        if c in self.diagonal:
            self.on_diagonal(c, 1).wait_recv()
            self.on_core(c, 3, 0).start()

    def stage_corner(self, c):
        self.corner_x(c, 1).wait_recv()
        self.corner_y(c, 1).wait_recv()
        if c in self.direct:
            self.on_core(c, 3, 0).start()
        else:
            self.corner_z(c, 0).start()

    def stage_pair(self, c):
        self.corner_z(c, 1).wait_recv()
        self.on_core(c, 3, 0).start()

    def stage_core(self, c):
        for kind in range(4):
            self.on_core(c, kind, 1).wait_recv()

    def finish(self, c):
        for z in self.others():
            self.to_z(c, z).wait_send()
        self.on_x(c, 0).wait_send()
        self.on_y(c, 0).wait_send()
        for kind in range(4):
            self.on_core(c, kind, 0).wait_send()
        if c in self.diagonal:
            self.on_diagonal(c, 0).wait_send()
        else:
            self.corner_x(c, 0).wait_send()
            self.corner_y(c, 0).wait_send()
            if c not in self.direct:
                self.corner_z(c, 0).wait_send()


def gather_sems(chunks):
    one = pltpu.SemaphoreType.DMA((chunks,))
    four = pltpu.SemaphoreType.DMA((chunks, 4))
    return [four] * 2 + [one] * 10 + [four] * 2


BF = jnp.bfloat16
F32 = jnp.float32
QB = 256
PLAN = ((0, 3, False, True), (0, 4, False, True), (0, 5, True, True), (1, 5, True, True))
HALO_PLAN = ((2, 2), (3, 1))
NEG = -1e30
VMEM_LIMIT = int(63.9 * 2**20)
ORDER = (
    "h0", "z0", "z1", "z2", "x0", "T", "x1", "x2", "c0", "z4", "h2", "c2", "c1", "k0",
    "h3", "k2", "z3", "P0", "k1", "x4", "z6", "h1", "P1", "P2", "A003", "z5", "A036", "c4",
    "A103", "x6", "z7", "A136", "H", "x5", "x3", "p4", "c6", "z8", "A202", "A224", "p6", "c5",
    "A246", "x7", "c3", "k6", "z9", "A302", "p5", "x8", "c7", "k3", "k4", "A324", "A346", "p7",
    "k5", "O", "x9", "c8", "k7", "F0", "c9", "p8", "F1", "k8", "p9", "F2", "k9", "F3",
)


def nn(a, b):
    return jnp.dot(a, b, preferred_element_type=F32)


def nt(a, b):
    return lax.dot_general(a, b, (((1,), (1,)), ((), ())), preferred_element_type=F32)


def tn(a, b):
    return lax.dot_general(a, b, (((0,), (0,)), ((), ())), preferred_element_type=F32)


def iota(shape, dim):
    return lax.broadcasted_iota(jnp.int32, shape, dim)


def block_at(flip, block):
    return pl.multiple_of(jnp.where(flip == 1, 3 - block, block) * QB, QB)


def rope(vectors, cosine, sine):
    lane = iota((1, 128), 1)
    first = lax.rem(lane, HEAD_DIM) < HEAD_DIM // 2
    out = []
    for c in range(vectors.shape[1] // 128):
        part = vectors[:, c * 128 : (c + 1) * 128]
        other = jnp.where(first, pltpu.roll(part, 96, 1), pltpu.roll(part, 32, 1))
        out.append(part * cosine + other * sine)
    return jnp.concatenate(out, axis=1)


def fill_tables(flip, seg_ref, freq_ref, cos_ref, sin_ref, fq_ref, fk_ref, bias_ref):
    lane = iota((1, 128), 1)
    seg_row = seg_ref[...].astype(F32)
    starts = [
        jnp.sum((seg_row < float(d)).astype(F32), axis=1, keepdims=True) for d in (1, 2, 3)
    ]
    sign = jnp.where(lax.rem(lane, HEAD_DIM) < HEAD_DIM // 2, -1.0, 1.0)
    for w in range(12):
        block, part = divmod(w, 2)
        base = jnp.where(flip == 1, 7 - block, block) * QB + part * 128
        row = seg_ref[:, pl.ds(pl.multiple_of(base, 128), 128)].astype(F32)
        seg = jnp.broadcast_to(row, (128, 128)).T
        start = jnp.where(
            seg >= 3.0,
            starts[2],
            jnp.where(seg >= 2.0, starts[1], jnp.where(seg >= 1.0, starts[0], 0.0)),
        )
        pos = (iota((128, 128), 0) + base).astype(F32) - start
        angle = pos * freq_ref[...]
        rows = pl.ds(w * 128, 128)
        cos_ref[rows, :] = jnp.cos(angle)
        sin_ref[rows, :] = jnp.sin(angle) * sign
        hit = seg == lane.astype(F32)
        fq_ref[rows, :] = jnp.where(hit, 1.0, 0.0).astype(BF)
        fk_ref[rows, :] = jnp.where(hit | (lane >= 4), 0.0, NEG).astype(BF)
    gap = iota((QB, QB), 0) - iota((QB, QB), 1)
    gap = jnp.where(flip == 1, -gap, gap)
    bias_ref[0] = jnp.where(gap >= 0, 0.0, NEG)
    bias_ref[1] = jnp.where(gap <= 0, 0.0, NEG)


def qkv_rows(p, rb, xw, wq, aqkv, bblk, cos_ref, sin_ref, dest, low_ref):
    rows = pl.ds(pl.multiple_of(rb * 512, 512), 512)
    x = xw[rows, :]
    if p == 0:
        low = nt(x, aqkv[...]).astype(BF)
        low_ref[rows, :] = low
    else:
        low = low_ref[rows, :]
    proj = nn(x, wq[p].reshape(D, D)) + nn(low, bblk[p])
    if p < 2:
        proj = rope(proj, cos_ref[rows, :], sin_ref[rows, :])
    value = proj.astype(BF)
    if p == 0:
        value = value * jnp.asarray(0.125, BF)
    dest[pl.ds(rb * 2, 2)] = value.reshape(2, QB, D)


def prob_copies(n, src, dst, sem, s):
    full = (2 * n + 2) // 3
    cuts = ((0, 2), (2, full)) if full > 2 else ((0, 1), (1, 2))
    return [
        pltpu.make_async_copy(src.at[pl.ds(a, b - a)], dst.at[pl.ds(a, b - a)], sem.at[2 * s + i])
        for i, (a, b) in enumerate(cuts)
    ]


def attend_pair(
    qb, pair, step, q_ref, k_ref, v_ref, fq_ref, fk_ref, bias_ref, att_ref, linv_ref, mf_ref, p_hbm, stage, sem
):
    k0, n, tri_first, tri_last = PLAN[qb]
    rows = pl.ds(qb * QB, QB)
    kblocks = pl.ds(k0, n)
    krows = pl.ds(k0 * QB, n * QB)
    half = iota((1, 128), 1) >= HEAD_DIM
    lane = iota((1, 128), 1)
    slot = lax.rem(step, 2)

    def copy(s, tiles=n):
        return prob_copies(tiles, stage.at[pl.ds(s * 4, 4)], p_hbm.at[qb, pair], sem, s)

    @pl.when(pair >= 2)
    def _():
        for one in copy(slot):
            one.wait()

    if qb > 0:

        @pl.when(pair < 2)
        def _():
            for one in copy(slot, PLAN[qb - 1][1]):
                one.wait()

    lanes = pl.ds(pl.multiple_of(pair * 128, 128), 128)
    q2 = q_ref[qb, :, lanes]
    fq = fq_ref[rows, :]
    keys = jnp.concatenate([k_ref[kblocks, :, lanes].reshape(n * QB, 128), fk_ref[krows, :]], axis=1)
    v2 = v_ref[kblocks, :, lanes].reshape(n * QB, 128)
    masks = (jnp.logical_not(half), half)
    scores = [
        nt(jnp.concatenate([jnp.where(mine, q2, jnp.zeros_like(q2)), fq], axis=1), keys) for mine in masks
    ]
    outs = []
    for h, (mine, s) in enumerate(zip(masks, scores)):
        parts = [s[:, t * QB : (t + 1) * QB] for t in range(n)]
        if tri_last:
            parts[n - 1] = parts[n - 1] + bias_ref[0]
        if tri_first:
            parts[0] = parts[0] + bias_ref[1]
        s = jnp.concatenate(parts, axis=1)
        m = jnp.max(s, axis=1, keepdims=True)
        p = jnp.exp(s - m).astype(BF)
        for t in range(n):
            block, lane0 = divmod(h * n + t, 3)
            stage[slot * 4 + block, :, lane0 * QB : lane0 * QB + QB] = p[:, t * QB : (t + 1) * QB]
        if qb >= 2:
            low = 4 + 3 * (2 * pair + h)
            mf_ref[rows, :] = jnp.where((lane >= low) & (lane < low + 3), -m, mf_ref[rows, :])
        outs.append(nn(p, jnp.where(mine, v2, jnp.ones_like(v2))))
    inv = 1.0 / pltpu.roll(jnp.where(half, outs[0], outs[1]), HEAD_DIM, 1)
    att_ref[rows, lanes] = (jnp.where(half, outs[1], outs[0]) * inv).astype(BF)
    linv_ref[rows, lanes] = inv
    for one in copy(slot):
        one.start()


def drain_pairs(qb, p_hbm, stage, sem):
    for s in range(2):
        for one in prob_copies(PLAN[qb][1], stage.at[pl.ds(s * 4, 4)], p_hbm.at[qb, 0], sem, s):
            one.wait()


def sigmoid(v):
    return 0.5 * jnp.tanh(0.5 * v) + 0.5


def norm_stats(r):
    centre = r - jnp.mean(r, axis=1, keepdims=True)
    rstd = lax.rsqrt(jnp.mean(centre * centre, axis=1, keepdims=True) + EPSILON)
    return centre * rstd, rstd


def norm_back(grad, xhat, rstd):
    return rstd * (
        grad
        - jnp.mean(grad, axis=1, keepdims=True)
        - xhat * jnp.mean(grad * xhat, axis=1, keepdims=True)
    )


def out_rows(rb, xw, att_ref, wo, ao, bo, gb, aff, xhat_ref, rstd_ref, act_ref, lowo_ref, lowf_ref):
    rows = pl.ds(pl.multiple_of(rb * QB, QB), QB)
    att = att_ref[rows, :]
    low = nt(att, ao[...]).astype(BF)
    lowo_ref[rows, :] = low
    branch = nn(att, wo[...].reshape(D, D)) + nn(low, bo[...])
    xhat, rstd = norm_stats(xw[rows, :].astype(F32) + branch)
    xhat_ref[rows, :] = xhat
    rstd_ref[rows, :] = jnp.broadcast_to(rstd, (QB, 128))
    act = (xhat * gb[0:1, :] + gb[1:2, :]).astype(BF)
    act_ref[rows, :] = act
    lowf_ref[rows, :] = nt(act, aff[...]).astype(BF)


def ffn_in_tile(n, rb, size, act_ref, lowf_ref, wi, wd, bg, bu, adn, big, lowd_ref, total_ref):
    start = pl.multiple_of(rb * size, size)
    rows = pl.ds(start, size)
    act = act_ref[rows, :]
    low = lowf_ref[rows, :]
    blocks = size // QB
    here = n * 4 + rb * blocks
    parts = []
    for c in range(3):
        lanes = slice(c * 256, c * 256 + 256)
        gate = nn(act, wi[n, 0, :, :, :, :, lanes].reshape(D, 256)) + nn(low, bg[n, :, lanes])
        up = nn(act, wi[n, 1, :, :, :, :, lanes].reshape(D, 256)) + nn(low, bu[n, :, lanes])
        parts.append((gate * sigmoid(gate) * up).astype(BF))
        big[pl.ds(here, blocks), :, lanes] = gate.astype(BF).reshape(blocks, QB, 256)
        big[pl.ds(here + 16, blocks), :, lanes] = up.astype(BF).reshape(blocks, QB, 256)
    inner = jnp.concatenate(parts, axis=1)
    lowd_ref[rows, 0:16] += nt(inner, adn[n])
    for c in range(3):
        lanes = slice(c * 256, c * 256 + 256)
        total_ref[rows, lanes] += nn(inner, wd[lax.div(n, 2), lax.rem(n, 2), :, :, lanes].reshape(D, 256))


def ffn_out_rows(
    rb, flip, lowd_ref, bdn, xhat_ref, gb, cot, dtwo_ref, db2_ref, dlow_ref, mixed_ref, gbdn_ref
):
    start = pl.multiple_of(rb * QB, QB)
    rows = pl.ds(start, QB)
    low = lowd_ref[rows, 0:16].astype(BF)
    total = nn(low, bdn[...]) + dtwo_ref[rows, :]
    r = xhat_ref[rows, :] * gb[0:1, :] + gb[1:2, :] + total
    xhat, rstd = norm_stats(r)
    mixed_ref[pl.ds(block_at(flip, rb), QB), :] = (xhat * gb[2:3, :] + gb[3:4, :]).astype(BF)
    dtwo = norm_back(cot[rows, :].astype(F32) * gb[2:3, :], xhat, rstd)
    dtwo_ref[rows, :] = dtwo
    db2 = dtwo.astype(BF)
    db2_ref[rows, :] = db2
    dlow_ref[rows, :] = nt(db2, bdn[...]).astype(BF)
    gbdn_ref[...] += tn(low, db2)


def ffn_back_tile(
    n, start, size, db2_ref, dlow_ref, wd, wi, adn, bg, bu, big, lowf_ref, acc, dlf_ref, gadn_ref, gbf_ref
):
    rows = pl.ds(start, size)
    db2 = db2_ref[rows, :]
    dlow = dlow_ref[rows, :]
    blocks = size // QB
    here = n * 4 + lax.div(start, QB)
    down = wd[lax.div(n, 2), lax.rem(n, 2)].reshape(D, D)
    dgs, dus, inners = [], [], []
    for c in range(3):
        lanes = slice(c * 256, c * 256 + 256)
        dinner = nt(db2, down[lanes]) + nn(dlow, adn[n, :, lanes])
        gate = big[pl.ds(here, blocks), :, lanes].reshape(size, 256).astype(F32)
        up = big[pl.ds(here + 16, blocks), :, lanes].reshape(size, 256).astype(F32)
        sig = sigmoid(gate)
        silu = gate * sig
        inners.append((silu * up).astype(BF))
        dgs.append((dinner * up * (sig + silu * (1.0 - sig))).astype(BF))
        dus.append((dinner * silu).astype(BF))
    dg, du, inner = (jnp.concatenate(v, axis=1) for v in (dgs, dus, inners))
    acc[...] += nt(dg, wi[n, 0].reshape(D, D)) + nt(du, wi[n, 1].reshape(D, D))
    dlf_ref[...] += nt(bg[n], dg) + nt(bu[n], du)
    gadn_ref[n] += tn(dlow, inner)
    low = lowf_ref[rows, :]
    gbf_ref[n] += jnp.where(iota((32, 1), 0) < 16, tn(low, dg), tn(low, du))


def hidden_back_rows(
    rb, off, acc, dlf_ref, aff, act_ref, dtwo_ref, xhat_ref, rstd_ref, gb, bo, ao, lowo_ref, att_ref,
    wo, linv_ref, h2, mf_ref, do_ref, hf_ref, gaff_ref, gbo_ref, gao_ref,
):
    start = pl.multiple_of(rb * QB, QB)
    rows = pl.ds(start, QB)
    local = pl.ds(pl.multiple_of(start - off, QB), QB)
    dlf = dlf_ref[:, local].T.astype(BF)
    dhid = dtwo_ref[rows, :] + acc[local, :] + nn(dlf, aff[...])
    gaff_ref[...] += tn(dlf, act_ref[rows, :])
    done = norm_back(dhid * gb[0:1, :], xhat_ref[rows, :], rstd_ref[rows, 0:1])
    dtwo_ref[rows, :] = done
    dbr = done.astype(BF)
    dlo = nt(dbr, bo[...]).astype(BF)
    att = att_ref[rows, :]
    gbo_ref[...] += tn(lowo_ref[rows, :], dbr)
    gao_ref[...] += tn(dlo, att)
    datt = (nt(dbr, wo[...].reshape(D, D)) + nn(dlo, ao[...])).astype(BF)
    do = (datt.astype(F32) * linv_ref[rows, :]).astype(BF)
    do_ref[rows, :] = do
    value = nn(do * att, h2[...]) + mf_ref[rows, :]
    lane = iota((1, 128), 1)
    role = jnp.where(lane < 40, lax.rem(lane + 2, 3), lax.rem(lane, 2))
    high = value.astype(BF)
    rest = value - high.astype(F32)
    mid = rest.astype(BF)
    last = (rest - mid.astype(F32)).astype(BF)
    hf_ref[rows, :] = jnp.where(role == 0, high, jnp.where(role == 1, mid, last))


def kf_kernel(
    x_hbm, cot_hbm, seg_hbm, freq_hbm, pick_hbm, gain_hbm, shift_hbm, tin_hbm, tdn_hbm, tout_hbm, tff_hbm,
    wq_hbm, wo_hbm, wi_hbm, wd_hbm,
    q_hbm, k_hbm, v_hbm, p_hbm, mixed_hbm, do_hbm, hf_hbm, lowq_hbm, done_hbm, cos_hbm, sin_hbm, fq_hbm, fk_hbm,
    ge_hbm, gao_hbm, tag_hbm, aqkv_hbm, bqkv_hbm, wq_out,
    seg_ref, freq_ref, pick_ref, gain_ref, shift_ref, hf_ref, ge_ref, gao_ref, tag_ref, aqkv, bqkv, ssem, fsem,
    ao, bo, aff, adn, bdn, gb,
    gaff_ref, gadn_ref, gbo_ref, gbdn_ref, gbf_ref,
    wq, wo, wi, wd, big, xw, att, linv, xhat, dtwo, act, db2, cos, sin, fq, fk, bias, mf,
    lowq, lowo, lowf, dlow, acc, dlf, bblk, bg, bu, h2, rsem, tsem, wsem, xsem, osem, psem, hs, hr, *sems,
):
    flip = lax.axis_index("seq")
    cot = db2
    do_ref = db2
    mixed_ref = xw.at[pl.ds(0, 1024)]
    rstd = cos
    lowd = sin
    loads = []
    for i in range(4):
        loads.append(
            pltpu.make_async_copy(
                x_hbm.at[pl.ds(block_at(flip, i), QB)], xw.at[pl.ds(i * QB, QB)], xsem.at[i]
            )
        )
        loads.append(
            pltpu.make_async_copy(
                cot_hbm.at[pl.ds(block_at(flip, i), QB)], cot.at[pl.ds(i * QB, QB)], xsem.at[4 + i]
            )
        )
    small = [
        pltpu.make_async_copy(a, b, ssem.at[i])
        for i, (a, b) in enumerate(
            ((seg_hbm, seg_ref), (freq_hbm, freq_ref), (pick_hbm, pick_ref), (gain_hbm, gain_ref), (shift_hbm, shift_ref))
        )
    ]
    for copy in small:
        copy.start()
    facts = [
        pltpu.make_async_copy(a, b, fsem.at[i])
        for i, (a, b) in enumerate(
            ((tag_ref, tag_hbm), (aqkv, aqkv_hbm), (bqkv, bqkv_hbm), (ge_ref, ge_hbm), (gao_ref, gao_hbm))
        )
    ]
    tables = [
        (tin_hbm, big.at[pl.ds(0, ADAPTERS), pl.ds(0, 96)]),
        (tout_hbm, big.at[pl.ds(4, ADAPTERS), pl.ds(0, 80)]),
    ]
    for n in range(4):
        lanes = pl.ds(n * D, D)
        tables.append((tdn_hbm.at[:, :, lanes], big.at[pl.ds(8, ADAPTERS), pl.ds(16 * n, 16)]))
        tables.append((tff_hbm.at[:, :, lanes], big.at[pl.ds(12, ADAPTERS), pl.ds(32 * n, 32)]))
    tables = [pltpu.make_async_copy(a, b, tsem.at[i]) for i, (a, b) in enumerate(tables)]
    g = Gather(sems, direct=(0, 1, 2, 3))

    def view(c, za, zb, k, half):
        cut = 384 if c < 4 else 640
        lanes = ALL if half is None else pl.ds(0, cut) if half == 0 else pl.ds(cut, D - cut)
        if c < 3:
            return wq.at[c, za, zb, k, :, lanes]
        if c == 3:
            return wo.at[za, zb, k, :, lanes]
        if c < 6:
            return wd.at[za, zb, k, pl.ds((c - 4) * 48, 48), lanes]
        return wi.at[c - 6, :, za, zb, k, :, lanes]

    g.view = view
    here = g.column(0, 0, 0)
    weights = [
        pltpu.make_async_copy(a, b, wsem.at[i])
        for i, (a, b) in enumerate(
            [(wq_hbm, wq.at[:, g.za, g.zb, here]), (wo_hbm, wo.at[g.za, g.zb, here]), (wd_hbm, wd.at[g.za, g.zb, here])]
            + [(wi_hbm.at[:, :, pl.ds(D * n, D)], wi.at[n, :, g.za, g.zb, here]) for n in range(4)]
        )
    ]
    for copy in weights:
        copy.start()
    g.barrier(g.partners())
    for copy in weights:
        copy.wait()
    for c in range(NCHUNK):
        g.send_z(c)
    halo = [
        pltpu.make_async_remote_copy(
            x_hbm.at[pl.ds(block_at(flip, 3 - i // 2) + i % 2 * 128, 128)], xw.at[pl.ds(1024 + i * 128, 128)],
            hs.at[i], hr.at[i], device_id=g.devy, device_id_type=MESH,
        )
        for i in range(4)
    ]

    kinds = {
        "z": g.stage_z, "x": g.stage_xy, "c": g.stage_corner, "p": g.stage_pair, "k": g.stage_core,
    }

    for copy in loads + tables:
        copy.start()

    def prepare():
        for copy in small:
            copy.wait()
        fill_tables(flip, seg_ref, freq_ref, cos, sin, fq, fk, bias)
        for copy in tables:
            copy.wait()
        e = pick_ref[0, 0]
        aqkv[...] = big[e, 0:48, :]
        ao[...] = big[e, 48:64, :]
        aff[...] = big[e, 64:96, :]
        bqkv[...] = big[4 + e, 0:48, :]
        bo[...] = big[4 + e, 48:64, :]
        bdn[...] = big[4 + e, 64:80, :]
        for n in range(4):
            adn[n] = big[8 + e, 16 * n : 16 * n + 16, :]
        tag_ref[...] = jnp.where(iota((16, 128), 0) == e, 1.0, 0.0).astype(BF)
        for copy in facts[:3]:
            copy.start()
        for i in range(2):
            gb[2 * i : 2 * i + 1, :] = gain_ref[i : i + 1, :]
            gb[2 * i + 1 : 2 * i + 2, :] = shift_ref[i : i + 1, :]
        rank = iota((48, 1), 0)
        for p in range(3):
            keep = (rank >= 16 * p) & (rank < 16 * p + 16)
            bblk[p] = jnp.where(keep, bqkv[...], jnp.zeros_like(bqkv[...]))
        rank = iota((32, 1), 0)
        for n in range(4):
            piece = big[12 + e, 32 * n : 32 * n + 32, :]
            bg[n] = jnp.where(rank < 16, piece, jnp.zeros_like(piece))
            bu[n] = jnp.where(rank >= 16, piece, jnp.zeros_like(piece))
        head = lax.div(iota((D, 128), 0), HEAD_DIM)
        spot = iota((D, 128), 1)
        h2[...] = jnp.where(lax.div(spot - 40, 2) == head, jnp.where(spot >= 40, -1.0, 0.0), 0.0).astype(BF)
        mf[...] = jnp.zeros_like(mf)
        dtwo[...] = jnp.zeros_like(dtwo)
        for ref in (gao_ref, gaff_ref, gadn_ref, gbo_ref, gbdn_ref, gbf_ref):
            ref[...] = jnp.zeros_like(ref)
        for copy in loads:
            copy.wait()

    q_ref, k_ref, v_ref = (big.at[pl.ds(i * 6, 6)] for i in range(3))
    stage = big.at[pl.ds(18, 8)]
    keep_wq = pltpu.make_async_copy(wq, wq_out, osem.at[9])
    saves = [
        pltpu.make_async_copy(a, b, osem.at[i])
        for i, (a, b) in enumerate(
            ((q_ref, q_hbm), (k_ref, k_hbm), (v_ref, v_hbm), (lowq, lowq_hbm), (cos, cos_hbm), (sin, sin_hbm), (fq, fq_hbm), (fk, fk_hbm))
        )
    ]

    def qkv_page(p, first, last):
        def step(rb, _):
            qkv_rows(p, rb, xw, wq, aqkv, bblk, cos, sin, (q_ref, k_ref, v_ref)[p], lowq)
            return 0

        lax.fori_loop(first, last, step, 0)

    def attend(qb, first, last):
        def pair_step(pair, _):
            attend_pair(qb, pair, pair, q_ref, k_ref, v_ref, fq, fk, bias, att, linv, mf, p_hbm, stage, psem)
            return 0

        lax.fori_loop(first, last, pair_step, 0)
        if last == 6 and qb == 3:
            drain_pairs(qb, p_hbm, stage, psem)

    def out_step(rb, _):
        out_rows(rb, xw, att, wo, ao, bo, gb, aff, xhat, rstd, act, lowo, lowf)
        return 0

    def in_step(i, _):
        ffn_in_tile(i, 0, 1024, act, lowf, wi, wd, bg, bu, adn, big, lowd, dtwo)
        return 0

    for step in ORDER:
        kind, rest = step[0], step[1:]
        if kind in kinds:
            kinds[kind](int(rest))
        elif kind == "h":
            halo[int(rest)].start()
        elif step == "T":
            prepare()
        elif kind == "P":
            qkv_page(int(rest), 0, 2)
        elif step == "H":
            for copy in halo:
                copy.wait_recv()
            for p in range(3):
                qkv_page(p, 2, 3)
            for copy in saves:
                copy.start()
            keep_wq.start()
        elif kind == "A":
            attend(*(int(v) for v in rest))
        elif step == "O":
            for copy in saves:
                copy.wait()
            lowd[...] = jnp.zeros_like(lowd)
            lax.fori_loop(0, 4, out_step, 0)
        elif kind == "F":
            n = int(rest)
            lax.fori_loop(n, n + 1, in_step, 0)

    def down_step(rb, _):
        ffn_out_rows(rb, flip, lowd, bdn, xhat, gb, cot, dtwo, db2, dlow, mixed_ref, gbdn_ref)
        return 0

    lax.fori_loop(0, 4, down_step, 0)
    outs = [pltpu.make_async_copy(mixed_ref, mixed_hbm, rsem.at[0])]
    outs[0].start()

    def row_copies(rb):
        rows = pl.ds(pl.multiple_of(rb * QB, QB), QB)
        return (
            pltpu.make_async_copy(do_ref.at[rows], do_hbm.at[rows], rsem.at[1 + rb]),
            pltpu.make_async_copy(dtwo.at[rows], done_hbm.at[rows], rsem.at[5 + rb]),
            pltpu.make_async_copy(hf_ref.at[rows], hf_hbm.at[rows], rsem.at[9 + rb]),
        )

    def back_step(half, _):
        off = pl.multiple_of(half * 512, 512)
        acc[...] = jnp.zeros_like(acc)
        dlf[...] = jnp.zeros_like(dlf)

        def tile(n, _):
            ffn_back_tile(
                n, off, 512, db2, dlow, wd, wi, adn, bg, bu, big, lowf, acc, dlf, gadn_ref, gbf_ref
            )
            return 0

        lax.fori_loop(0, 4, tile, 0)

        def rows(i, _):
            hidden_back_rows(
                half * 2 + i, off, acc, dlf, aff, act, dtwo, xhat, rstd, gb, bo, ao, lowo, att, wo, linv, h2, mf,
                do_ref, hf_ref, gaff_ref, gbo_ref, gao_ref,
            )
            for copy in row_copies(half * 2 + i):
                copy.start()
            return 0

        lax.fori_loop(0, 2, rows, 0)
        return 0

    lax.fori_loop(0, 2, back_step, 0)
    for rb in range(4):
        outs.extend(row_copies(rb))
    ge_ref[0:32] = gaff_ref[...].astype(BF)
    ge_ref[32:48] = gbo_ref[...].astype(BF)
    ge_ref[48:64] = gbdn_ref[...].astype(BF)
    ge_ref[64:128] = gadn_ref[...].reshape(64, D).astype(BF)
    ge_ref[128:256] = gbf_ref[...].reshape(128, D).astype(BF)
    for copy in facts[3:]:
        copy.start()
    keep_wq.wait()
    for copy in outs + facts:
        copy.wait()
    for copy in halo:
        copy.wait_send()
    for c in range(NCHUNK):
        g.finish(c)


def k3_kernel(
    x_hbm, q_hbm, k_hbm, v_hbm, p_hbm, do_hbm, hf_hbm, ge_hbm, gao_hbm, tag_hbm, lowq_hbm, done_hbm, cos_hbm, sin_hbm,
    fq_hbm, fk_hbm, aqkv_hbm, bqkv_hbm, wq_hbm,
    dx_hbm, eg_hbm, lg_hbm,
    ge, gao, tag, aqkv, bqkv, gsem,
    ga_ref, gbq_ref, dproj, eg, lg, e_in, e_half, rs_e, rs_t, gl_out, gl_in, l_half, rs_l, dx_ref,
    xw, q, k, v, do, hf, lowq, done, cos, sin, fq, fk, wq, stage, dq, dkT, dvT, bias, sem, psem, hs, hr,
    es, er, ts, tr, ls, lr, dsem, *sems,
):
    flip = lax.axis_index("seq")
    g = Gather(sems, diagonal=(1,))

    def part(src, dst, start, size):
        return src.at[pl.ds(start, size)], dst.at[pl.ds(start, size)]

    table = (
        part(q_hbm, q, 0, 256), part(k_hbm, k, 0, 768), part(v_hbm, v, 0, 768), part(do_hbm, do, 0, 256),
        part(hf_hbm, hf, 0, 1024),
        part(q_hbm, q, 256, 1280), part(k_hbm, k, 768, 768), part(v_hbm, v, 768, 768), part(do_hbm, do, 256, 768),
        (ge_hbm, ge), (tag_hbm, tag), (gao_hbm, gao), (aqkv_hbm, aqkv), (bqkv_hbm, bqkv),
        (lowq_hbm, lowq), (done_hbm, done), (cos_hbm, cos), (sin_hbm, sin), (fq_hbm, fq), (fk_hbm, fk), (wq_hbm, wq),
    )
    loads = [pltpu.make_async_copy(a, b, sem.at[i]) for i, (a, b) in enumerate(table)]
    for i in range(4):
        loads.append(
            pltpu.make_async_copy(
                x_hbm.at[pl.ds(block_at(flip, i), QB)], xw.at[pl.ds(i * QB, QB)], sem.at[21 + i]
            )
        )
    def fetch(qb, pair, s):
        return prob_copies(PLAN[qb][1], p_hbm.at[qb, pair], stage.at[s], psem, s)

    for copy in loads[:5]:
        copy.start()
    for copy in fetch(0, 0, 0):
        copy.start()
    for copy in loads[5:]:
        copy.start()

    def view(c, za, zb, k, half):
        lanes = ALL if half is None else pl.ds(0, 256) if half == 0 else pl.ds(256, 128)
        return (eg, lg)[c].at[za, zb, k, :, lanes]

    g.view = view

    def plane(d):
        return lax.rem(g.b + d, 16)

    def scatter(src, dst, send, recv):
        def copy(d):
            to = plane(d)
            return pltpu.make_async_remote_copy(
                src(to), dst.at[g.b], send.at[d], recv.at[d], device_id=(to, g.s), device_id_type=MESH
            )

        def arrival(d):
            return pltpu.make_async_remote_copy(
                src(0), dst.at[plane(16 - d)], send.at[d], recv.at[d], device_id=(plane(d), g.s), device_id_type=MESH
            )

        def each(what):
            def step(d, _):
                what(d)
                return 0

            lax.fori_loop(1, 16, step, 0)

        return (
            lambda: each(lambda d: copy(d).start()),
            lambda: each(lambda d: arrival(d).wait_recv()),
            lambda: each(lambda d: copy(d).wait_send()),
        )

    def piece(ref, size):
        def at(to):
            rows = pl.ds(pl.multiple_of(lax.div(to, 2) * size, size), size)
            return ref.at[rows, pl.ds(pl.multiple_of(lax.rem(to, 2) * 384, 128), 384)]

        return at

    loads[9].wait()
    loads[10].wait()
    send_e, wait_e, end_e = scatter(piece(e_half, 16), rs_e, es, er)
    send_t, wait_t, end_t = scatter(lambda to: tag, rs_t, ts, tr)
    send_l, wait_l, end_l = scatter(piece(l_half, 8), rs_l, ls, lr)

    bar = pltpu.get_barrier_semaphore()

    def greet(d, _):
        pl.semaphore_signal(bar, inc=1, device_id=(plane(d), g.s), device_id_type=MESH)
        return 0

    lax.fori_loop(1, 16, greet, 0)
    for dev in (g.devy, g.devd):
        pl.semaphore_signal(bar, inc=1, device_id=dev, device_id_type=MESH)
    halo = []
    for i, (src, dst) in enumerate(
        (
            (do_hbm.at[pl.ds(768, QB)], do.at[pl.ds(1024, QB)]),
            (do_hbm.at[pl.ds(512, QB)], do.at[pl.ds(1280, QB)]),
            (hf_hbm.at[pl.ds(768, QB)], hf.at[pl.ds(1024, QB)]),
            (hf_hbm.at[pl.ds(512, QB)], hf.at[pl.ds(1280, QB)]),
            (ge.at[pl.ds(pl.multiple_of((1 - flip) * 128, 16), 128)], e_in),
            (gl_out.at[pl.ds(pl.multiple_of((1 - flip) * 64, 16), 64)], gl_in),
        )
    ):
        halo.append(
            pltpu.make_async_remote_copy(
                src, dst, hs.at[i], hr.at[i], device_id=g.devy, device_id_type=MESH
            )
        )

    def total_of(ref):
        totals = [0.0] * ADAPTERS
        for b in range(16):
            value = ref[b].astype(F32)
            for e in range(ADAPTERS):
                weight = rs_t[b, e : e + 1, :].astype(F32)
                totals[e] = totals[e] + value * jnp.concatenate([weight] * 3, axis=1)
        return jnp.concatenate(totals, axis=0).astype(BF)

    def own_piece(ref, size):
        rows = pl.ds(pl.multiple_of(lax.div(g.b, 2) * size, size), size)
        return ref[rows, pl.ds(pl.multiple_of(g.core * 384, 128), 384)]

    dkT[...] = jnp.zeros_like(dkT)
    dvT[...] = jnp.zeros_like(dvT)
    ga_ref[...] = jnp.zeros_like(ga_ref)
    gbq_ref[...] = jnp.zeros_like(gbq_ref)
    gap = iota((QB, QB), 0) - iota((QB, QB), 1)
    gap = jnp.where(flip == 1, -gap, gap)
    bias[...] = jnp.where(gap <= 0, 0.0, NEG)
    half = iota((1, 128), 1) >= HEAD_DIM
    for copy in loads[:5]:
        copy.wait()

    def picks(pair, first, width):
        head = 2 * pair + lax.div(iota((128, 256), 1), 128)
        row = iota((128, 256), 0) - first - width * head
        return jnp.where((row >= 0) & (row < width), 1.0, 0.0).astype(BF)

    for qb in range(4):
        k0, n, _, _ = PLAN[qb]
        own = min(4 - k0, n)
        rows = pl.ds(qb * QB, QB)
        krows = pl.ds(k0 * QB, n * QB)


        def pair_step(pair, _, qb=qb, k0=k0, n=n, own=own, rows=rows, krows=krows):
            slot = lax.rem(pair, 2)
            for one in fetch(qb, pair, slot):
                one.wait()

            @pl.when(pair < 5)
            def _():
                for one in fetch(qb, pair + 1, 1 - slot):
                    one.start()

            if qb < 3:

                @pl.when(pair == 5)
                def _():
                    for one in fetch(qb + 1, 0, 0):
                        one.start()

            lanes = pl.ds(pl.multiple_of(pair * 128, 128), 128)
            do2 = do[rows, lanes]
            ndl = nn(hf[rows, :], picks(pair, 40, 2))
            k2 = k[krows, lanes]
            v2 = v[krows, lanes]
            qT = q[rows, lanes].T
            doT = do2.T
            dqs = []
            masks = (jnp.logical_not(half), half)
            dps = [nt(jnp.where(mine, do2, jnp.zeros_like(do2)), v2) for mine in masks]
            for h, dp in enumerate(dps):
                spots = [divmod(h * n + t, 3) for t in range(n)]
                p = jnp.concatenate([stage[slot, i, :, j * QB : j * QB + QB] for i, j in spots], axis=1)
                d = ndl[:, h * 128 : (h + 1) * 128]
                ds = (p.astype(F32) * (dp + jnp.concatenate([d] * (2 * n), axis=1))).astype(BF)
                hr = pl.ds(pl.multiple_of(pair * 128 + h * 64, 64), 64)
                kc = pl.ds(k0 * QB, own * QB)
                dvT[hr, kc] += nn(doT[h * 64 : (h + 1) * 64], p[:, 0 : own * QB])
                dqs.append(nn(ds, k2))
                dkT[hr, kc] += nn(qT[h * 64 : (h + 1) * 64], ds[:, 0 : own * QB])
            dq[rows, lanes] = jnp.where(half, dqs[1], dqs[0]) * 0.125
            return 0

        lax.fori_loop(0, 6, pair_step, 0)
        if qb == 0:
            pl.semaphore_wait(bar, 17)
            for copy in (halo[4], halo[0], halo[1], halo[2], halo[3]):
                copy.start()
            send_t()
            for copy in loads[5:9]:
                copy.wait()
        elif qb == 1:
            halo[4].wait_recv()
            mine = ge[pl.ds(pl.multiple_of(flip * 128, 16), 128), :]
            e_half[...] = (mine.astype(F32) + e_in[...].astype(F32)).astype(BF)
            send_e()
        elif qb == 2:
            rs_e[g.b] = own_piece(e_half, 16)
            rs_t[g.b] = tag[...]
            wait_e()
            wait_t()
            eg[g.za, g.zb, g.column(0, 0, 0)] = total_of(rs_e)
            g.send_z(0)
        else:
            g.stage_z(0)

    for copy in loads[11:]:
        copy.wait()
    for copy in halo[:4]:
        copy.wait_recv()
    def halo_step(pair, _):
        lanes = pl.ds(pl.multiple_of(pair * 128, 128), 128)
        delta_picks = picks(pair, 40, 2)
        top_picks = picks(pair, 4, 3)
        masks = (jnp.logical_not(half), half)
        work = []
        for i, (k0, n) in enumerate(HALO_PLAN):
            rows = pl.ds(1024 + i * QB, QB)
            krows = pl.ds(k0 * QB, n * QB)
            do2 = do[rows, lanes]
            q2 = q[rows, lanes]
            feats = hf[rows, :]
            ndl = nn(feats, delta_picks)
            nm = nn(feats, top_picks)
            keys = jnp.concatenate([k[krows, lanes], fk[krows, :]], axis=1)
            v2 = v[krows, lanes]
            for h, mine in enumerate(masks):
                s = nt(jnp.concatenate([jnp.where(mine, q2, jnp.zeros_like(q2)), fq[rows, :]], axis=1), keys)
                dp = nt(jnp.where(mine, do2, jnp.zeros_like(do2)), v2)
                work.append((k0, n, h, s, dp, nm, ndl, q2.T, do2.T))
        for k0, n, h, s, dp, nm, ndl, qT, doT in work:
            parts = [s[:, t * QB : (t + 1) * QB] for t in range(n)]
            parts[0] = parts[0] + bias[...]
            s = jnp.concatenate(parts, axis=1)
            m = nm[:, h * 128 : (h + 1) * 128]
            p = jnp.exp(s + jnp.concatenate([m] * (2 * n), axis=1))
            d = ndl[:, h * 128 : (h + 1) * 128]
            ds = (p * (dp + jnp.concatenate([d] * (2 * n), axis=1))).astype(BF)
            hr = pl.ds(pl.multiple_of(pair * 128 + h * 64, 64), 64)
            kc = pl.ds(k0 * QB, n * QB)
            dvT[hr, kc] += nn(doT[h * 64 : (h + 1) * 64], p.astype(BF))
            dkT[hr, kc] += nn(qT[h * 64 : (h + 1) * 64], ds)
        return 0

    lax.fori_loop(0, 3, halo_step, 0)
    g.stage_xy(0)
    lax.fori_loop(3, 6, halo_step, 0)
    g.stage_corner(0)

    lane = lax.div(iota((1, 48), 1), 16)
    rank = lax.div(iota((48, 1), 0), 16)

    def proj_step(rb, _):
        start = pl.multiple_of(rb * QB, QB)
        rows = pl.ds(start, QB)
        cosine = cos[rows, :]
        sine = -sin[rows, :]
        low = lowq[rows, :]
        dlow = jnp.zeros((QB, 48), F32)
        for p in range(3):
            if p == 0:
                d = rope(dq[rows, :], cosine, sine)
            else:
                src = (dkT, dvT)[p - 1]
                d = [src[pl.ds(c * 128, 128), rows] for c in range(6)]
                if p == 2:
                    d = [v.astype(BF) for v in d]
                d = jnp.concatenate([v.T for v in d], axis=1)
                if p == 1:
                    d = rope(d, cosine, sine)
            d = d.astype(BF)
            dproj[p, rows, :] = d
            dlow += jnp.where(lane == p, nt(d, bqkv[...]), 0.0)
            gbq_ref[...] += jnp.where(rank == p, tn(low, d), 0.0)
        dlow = dlow.astype(BF)
        lowq[rows, :] = dlow
        ga_ref[...] += tn(dlow, xw[rows, :])
        return 0

    lax.fori_loop(0, 4, proj_step, 0)
    g.stage_pair(0)
    gl_out[0:48] = ga_ref[...].astype(BF)
    gl_out[48:96] = gbq_ref[...].astype(BF)
    gl_out[96:112] = gao[...].astype(BF)
    gl_out[112:128] = jnp.zeros((16, D), BF)
    halo[5].start()

    def dx_rows(rb):
        rows = pl.ds(rb * QB, QB)
        total = done[rows, :] + nn(lowq[rows, :], aqkv[...])
        for p in range(3):
            total += nt(dproj[p, rows, :], wq[p].reshape(D, D))
        dx_ref[rows, :] = total.astype(BF)
        copy = pltpu.make_async_copy(dx_ref.at[rows], dx_hbm.at[pl.ds(block_at(flip, rb), QB)], dsem.at[rb])
        copy.start()
        return copy

    tails = [dx_rows(0)]
    halo[5].wait_recv()
    mine = gl_out[pl.ds(pl.multiple_of(flip * 64, 16), 64), :]
    l_half[...] = mine.astype(F32) + gl_in[...].astype(F32)
    send_l()
    tails.append(dx_rows(1))
    rs_l[g.b] = own_piece(l_half, 8)
    wait_l()
    lg[g.za, g.zb, g.column(0, 0, 0)] = total_of(rs_l)
    g.send_z(1)
    tails.append(dx_rows(2))
    g.stage_z(1)
    tails.append(dx_rows(3))
    g.stage_core(0)
    keep_e = pltpu.make_async_copy(eg, eg_hbm, gsem.at[0])
    keep_e.start()
    g.stage_xy(1)
    for copy in halo:
        copy.wait_send()
    end_e()
    end_t()
    end_l()
    g.finish(0)
    g.stage_core(1)
    keep_l = pltpu.make_async_copy(lg, lg_hbm, gsem.at[1])
    keep_l.start()
    g.finish(1)
    keep_e.wait()
    keep_l.wait()
    for copy in tails:
        copy.wait()


def k4_kernel(
    eg_hbm, lg_hbm, mixed_hbm, dx_hbm,
    mixed_out, dx_out, gin_hbm, gdn_hbm, gout_hbm, gff_hbm,
    eg, lg, gin_ref, gdn_ref, gout_ref, gff_ref, mixed, dx, sem,
):
    moves = [
        pltpu.make_async_copy(a, b, sem.at[i])
        for i, (a, b) in enumerate(
            (
                (eg_hbm, eg), (lg_hbm, lg), (mixed_hbm, mixed), (dx_hbm, dx),
                (gdn_ref, gdn_hbm), (gff_ref, gff_hbm), (gin_ref, gin_hbm), (gout_ref, gout_hbm),
                (mixed, mixed_out), (dx, dx_out),
            )
        )
    ]
    for copy in moves[:4]:
        copy.start()

    def blocks(ref):
        for z in range(4):
            for xx in range(2):
                for core in range(2):
                    for y in range(2):
                        yield (
                            y * 8 + z * 2 + xx, core * 384,
                            ref[z // 2, z % 2, (xx * 2 + core) * 2 + y].astype(F32),
                        )

    moves[0].wait()
    for group, lane0, value in blocks(eg):
        lanes = slice(lane0, lane0 + 384)
        for e in range(ADAPTERS):
            rows = value[16 * e : 16 * e + 16]
            if group < 2:
                gin_ref[e, 64 + 16 * group : 80 + 16 * group, lanes] = rows
            elif group < 4:
                gout_ref[e, 16 + 16 * group : 32 + 16 * group, lanes] = rows
            elif group < 8:
                at = (group - 4) * D + lane0
                gdn_ref[e, :, at : at + 384] = rows
            else:
                at = (group - 8) // 2 * D + lane0
                first = 16 * (group % 2)
                gff_ref[e, first : first + 16, at : at + 384] = rows

    for i in (2, 3):
        moves[i].wait()
    for i in (4, 5, 8, 9):
        moves[i].start()
    moves[1].wait()
    for group, lane0, value in blocks(lg):
        lanes = slice(lane0, lane0 + 384)
        for e in range(ADAPTERS):
            rows = value[8 * e : 8 * e + 8]
            if group < 6:
                gin_ref[e, 8 * group : 8 * group + 8, lanes] = rows
            elif group < 12:
                gout_ref[e, 8 * group - 48 : 8 * group - 40, lanes] = rows
            elif group < 14:
                gin_ref[e, 8 * group - 48 : 8 * group - 40, lanes] = rows

    for copy in moves[6:8]:
        copy.start()
    for copy in moves[4:]:
        copy.wait()


def sds(shape, dtype):
    return jax.ShapeDtypeStruct(shape, dtype)


ANY = functools.partial(pl.BlockSpec, memory_space=pl.ANY)
INV = functools.partial(pl.BlockSpec, memory_space=pltpu.VMEM)


def kf_call(*args):
    outs = [
        (ANY, (6, QB, D), BF), (ANY, (6, QB, D), BF), (ANY, (6, QB, D), BF), (ANY, (4, 6, 4, QB, D), BF),
        (ANY, (1024, D), BF), (ANY, (1024, D), BF), (ANY, (1024, 128), BF),
        (ANY, (1536, 48), BF), (ANY, (1024, D), F32), (ANY, (1536, 128), F32), (ANY, (1536, 128), F32),
        (ANY, (1536, 128), BF), (ANY, (1536, 128), BF),
        (ANY, (256, D), BF), (ANY, (16, D), F32), (ANY, (16, 128), BF), (ANY, (48, D), BF), (ANY, (48, D), BF),
        (ANY, (3, 2, 2, 8, 24, D), BF),
    ]
    V = pltpu.VMEM
    scratch = [
        V((1, 2048), jnp.int32), V((1, 128), F32), pltpu.SMEM((1, 1), jnp.int32), V((2, D), F32), V((2, D), F32),
        V((1024, 128), BF), V((256, D), BF), V((16, D), F32), V((16, 128), BF), V((48, D), BF), V((48, D), BF),
        pltpu.SemaphoreType.DMA((5,)), pltpu.SemaphoreType.DMA((5,)),
        V((16, D), BF), V((16, D), BF), V((32, D), BF), V((4, 16, D), BF), V((16, D), BF), V((4, D), F32),
        V((32, D), F32), V((4, 16, D), F32), V((16, D), F32), V((16, D), F32), V((4, 32, D), F32),
        V((3, 2, 2, 8, 24, D), BF), V((2, 2, 8, 24, D), BF), V((4, 2, 2, 2, 8, 24, D), BF), V((2, 2, 8, 96, D), BF),
        V((32, QB, D), BF), V((1536, D), BF), V((1024, D), BF), V((1024, D), F32),
        V((1024, D), F32), V((1024, D), F32), V((1024, D), BF), V((1024, D), BF),
        V((1536, 128), F32), V((1536, 128), F32), V((1536, 128), BF), V((1536, 128), BF), V((2, QB, QB), F32),
        V((1024, 128), F32), V((1536, 48), BF), V((1024, 16), BF), V((1024, 32), BF),
        V((1024, 16), BF), V((512, D), F32), V((32, 512), F32), V((3, 48, D), BF),
        V((4, 32, D), BF), V((4, 32, D), BF), V((D, 128), BF),
        pltpu.SemaphoreType.DMA((13,)), pltpu.SemaphoreType.DMA((10,)), pltpu.SemaphoreType.DMA((7,)), pltpu.SemaphoreType.DMA((8,)), pltpu.SemaphoreType.DMA((10,)),
        pltpu.SemaphoreType.DMA((4,)), pltpu.SemaphoreType.DMA((4,)), pltpu.SemaphoreType.DMA((4,)),
    ]
    scratch += gather_sems(NCHUNK)
    return pl.pallas_call(
        kf_kernel,
        out_shape=[sds(s, t) for _, s, t in outs],
        in_specs=[ANY()] * 15,
        out_specs=[m() for m, _, _ in outs],
        scratch_shapes=scratch,
        compiler_params=pltpu.CompilerParams(
            vmem_limit_bytes=VMEM_LIMIT, collective_id=1, has_side_effects=True
        ),
    )(*args)


def k3_call(*args):
    V = pltpu.VMEM
    S = pltpu.SemaphoreType.DMA
    scratch = [
        V((256, D), BF), V((16, D), F32), V((16, 128), BF), V((48, D), BF), V((48, D), BF), S((2,)),
        V((48, D), F32), V((48, D), F32), V((3, 1024, D), BF), V((2, 2, 8, 64, 384), BF), V((2, 2, 8, 32, 384), BF),
        V((128, D), BF), V((128, D), BF), V((16, 16, 384), BF), V((16, 16, 128), BF), V((128, D), BF), V((64, D), BF),
        V((64, D), F32), V((16, 8, 384), F32), V((1024, D), BF),
        V((1024, D), BF), V((1536, D), BF), V((1536, D), BF), V((1536, D), BF), V((1536, D), BF), V((1536, 128), BF),
        V((1536, 48), BF), V((1024, D), F32), V((1536, 128), F32), V((1536, 128), F32), V((1536, 128), BF),
        V((1536, 128), BF), V((3, 2, 2, 8, 24, D), BF), V((2, 4, QB, D), BF), V((1024, D), F32), V((D, 1024), F32),
        V((D, 1024), F32), V((QB, QB), F32), S((25,)), S((4,)), S((6,)), S((6,)),
        S((16,)), S((16,)), S((16,)), S((16,)), S((16,)), S((16,)), S((4,)),
    ]
    return pl.pallas_call(
        k3_kernel,
        out_shape=[
            sds((1024, D), BF), sds((2, 2, 8, 64, 384), BF), sds((2, 2, 8, 32, 384), BF),
        ],
        in_specs=[ANY()] * 19,
        out_specs=[ANY()] * 3,
        scratch_shapes=scratch + gather_sems(2),
        compiler_params=pltpu.CompilerParams(
            vmem_limit_bytes=VMEM_LIMIT, collective_id=2, has_side_effects=True
        ),
    )(*args)


def k4_call(*args):
    V = pltpu.VMEM
    grads = [(4, 96, D), (4, 16, FF), (4, 80, D), (4, 32, FF)]
    return pl.pallas_call(
        k4_kernel,
        out_shape=[sds((1024, D), BF), sds((1024, D), BF)] + [sds(s, F32) for s in grads],
        in_specs=[ANY()] * 4,
        out_specs=[ANY()] * 6,
        scratch_shapes=[V((2, 2, 8, 64, 384), BF), V((2, 2, 8, 32, 384), BF)]
        + [V(s, F32) for s in grads]
        + [V((1024, D), BF), V((1024, D), BF), pltpu.SemaphoreType.DMA((10,))],
        compiler_params=pltpu.CompilerParams(vmem_limit_bytes=VMEM_LIMIT),
    )(*args)


def fast(
    tokens, cotangent, segments, adapter_index, qkv_weight, out_weight, ffn_in_weight, ffn_out_weight,
    norm_gain, norm_bias, adapt_in, adapt_down, adapt_out, adapt_ffn,
):
    x = tokens[0]
    freq = np.power(np.float32(ROPE_BASE), np.float32(-2.0 / HEAD_DIM) * np.arange(HEAD_DIM // 2, dtype=np.float32))
    freq = np.tile(freq.astype(np.float32), 4)[None]
    q, k, v, p, mixed, do, hf, lowq, done, cos, sin, fq, fk, ge, gao, tag, aqkv, bqkv, wq = kf_call(
        x, cotangent[0], segments, freq, adapter_index, norm_gain[0], norm_bias[0],
        adapt_in[0].transpose(0, 1, 3, 2).reshape(ADAPTERS, 96, D), adapt_down[0].transpose(0, 2, 1),
        adapt_out[0].reshape(ADAPTERS, 80, D), adapt_ffn[0].reshape(ADAPTERS, 32, FF),
        qkv_weight[0], out_weight[0], ffn_in_weight[0], ffn_out_weight[0],
    )
    q, k, v = (a.reshape(1536, D) for a in (q, k, v))
    dx, eg, lg = k3_call(
        x, q, k, v, p, do, hf, ge, gao, tag, lowq, done, cos, sin, fq, fk, aqkv, bqkv, wq
    )
    mixed, dx, g_in, g_dn, g_out, g_ff = k4_call(eg, lg, mixed, dx)
    return (
        mixed[None], dx[None], g_in.reshape(ADAPTERS, 6, 16, D).transpose(0, 1, 3, 2)[None],
        g_dn.transpose(0, 2, 1)[None], g_out.reshape(ADAPTERS, 5, 16, D)[None], g_ff.reshape(ADAPTERS, 2, 16, FF)[None],
    )


def solution(mesh):
    here = fast if dict(mesh.shape) == {"batch": 16, "seq": 2} else shards
    return jax.shard_map(
        here,
        mesh=mesh,
        in_specs=(
            P("batch", "seq", None),
            P("batch", "seq", None),
            P("batch", None),
            P("batch", None),
            P(None, None, ("batch", "seq"), None),
            P(None, ("batch", "seq"), None),
            P(None, None, ("batch", "seq"), None),
            P(None, ("batch", "seq"), None),
            P(),
            P(),
            P(),
            P(),
            P(),
            P(),
        ),
        out_specs=(P("batch", "seq", None), P("batch", "seq", None), P(), P(), P(), P()),
        check_vma=False,
    )
```

```python
import functools
import math

import jax
import jax.numpy as jnp
import numpy as np
from jax import lax
from jax.experimental import pallas as pl
from jax.experimental.pallas import tpu as pltpu
from jax.sharding import PartitionSpec as P

HEADS = 12
HEAD_DIM = 64
ADAPTERS = 4
LAYERS = 1
HALF = 512
D = HEADS * HEAD_DIM
FF = 4 * D


EPSILON = 1e-06
ROPE_BASE = 1000.0
PRECISE = lax.Precision.HIGHEST


def shifted(array, axis, by):
    count = lax.axis_size(axis)
    pairs = [(i, i + by) for i in range(count) if 0 <= i + by < count]
    return lax.ppermute(array, axis, pairs)


def doc_positions(segment_ids):
    position_ids = jnp.arange(segment_ids.shape[-1], dtype=jnp.int32)
    starts_here = jnp.concatenate(
        [
            jnp.ones(segment_ids.shape[:-1] + (1,), dtype=jnp.bool_),
            segment_ids[..., 1:] != segment_ids[..., :-1],
        ],
        axis=-1,
    )
    doc_start = lax.cummax(jnp.where(starts_here, position_ids, 0), axis=segment_ids.ndim - 1)
    return (position_ids - doc_start).astype(jnp.float32)


def rope_tables(segment_ids):
    positions = doc_positions(segment_ids)
    frequency = jnp.power(ROPE_BASE, -2.0 * jnp.arange(HEAD_DIM // 2, dtype=jnp.float32) / HEAD_DIM)
    angles = positions[..., None] * frequency
    return (jnp.cos(angles), jnp.sin(angles))


def rotate(vectors, cosine_table, sine_table):
    half_dim = vectors.shape[-1] // 2
    first_half = vectors[..., :half_dim]
    second_half = vectors[..., half_dim:]
    cosine_rows = cosine_table[..., None, :]
    sine_rows = sine_table[..., None, :]
    return jnp.concatenate(
        [
            first_half * cosine_rows - second_half * sine_rows,
            second_half * cosine_rows + first_half * sine_rows,
        ],
        axis=-1,
    )


def norm_apply(residual, gain_row, bias_row):
    centre = residual - jnp.mean(residual, axis=-1, keepdims=True)
    spread = jnp.mean(centre * centre, axis=-1, keepdims=True)
    return centre * lax.rsqrt(spread + EPSILON) * gain_row + bias_row


def split_heads(merged, group_count):
    seqs_here, row_count, _ = merged.shape
    return merged.reshape(seqs_here, row_count, group_count, -1, HEAD_DIM).transpose(2, 0, 1, 3, 4)


def join_heads(grouped):
    group_count, seqs_here, row_count, heads_group, head_size = grouped.shape
    return grouped.transpose(1, 2, 0, 3, 4).reshape(
        seqs_here, row_count, group_count * heads_group * head_size
    )


def shards(
    tokens,
    cotangent,
    segments,
    adapter_index,
    qkv_weight,
    out_weight,
    ffn_in_weight,
    ffn_out_weight,
    norm_gain,
    norm_bias,
    adapt_in,
    adapt_down,
    adapt_out,
    adapt_ffn,
):
    seqs_here, tok_rows, model_width = tokens.shape
    heads_group = math.gcd(HEADS, 4)
    group_count = HEADS // heads_group
    score_scale = 1.0 / math.sqrt(HEAD_DIM)
    seq_count = lax.axis_size("seq")
    row_base = lax.axis_index("seq") * tok_rows
    shift_plan = []
    for distance in range(1, min(seq_count, HALF // tok_rows + 2)):
        row_count = min(tok_rows, HALF - (distance - 1) * tok_rows)
        if row_count > 0:
            shift_plan.append((distance, row_count))
            shift_plan.append((-distance, row_count))
    left_total = sum((plan_item[1] for plan_item in shift_plan if plan_item[0] > 0))
    key_rows = 2 * left_total + tok_rows
    key_places = {}
    passed_rows = 0
    for distance, row_count in shift_plan:
        if distance > 0:
            key_places[distance] = left_total - passed_rows - row_count
            key_places[-distance] = left_total + tok_rows + passed_rows
            passed_rows += row_count
    cosine_all, sine_all = rope_tables(segments)
    cosine_here = lax.dynamic_slice_in_dim(cosine_all, row_base, tok_rows, 1)
    sine_here = lax.dynamic_slice_in_dim(sine_all, row_base, tok_rows, 1)
    padded_ids = jnp.pad(segments, ((0, 0), (HALF, HALF)), constant_values=-1)
    key_ids = lax.dynamic_slice_in_dim(padded_ids, row_base - left_total + HALF, key_rows, 1)
    query_ids = lax.dynamic_slice_in_dim(segments, row_base, tok_rows, 1)
    offsets = (
        jnp.arange(tok_rows, dtype=jnp.int32)[:, None]
        - jnp.arange(key_rows, dtype=jnp.int32)[None, :]
        + left_total
    )
    visible = (query_ids[:, :, None] == key_ids[:, None, :]) & (jnp.abs(offsets) <= HALF)[None]
    slot_hits = adapter_index[:, 0][:, None] == jnp.arange(ADAPTERS, dtype=jnp.int32)[None, :]
    slot_low = slot_hits.astype(jnp.bfloat16)
    slot_full = slot_hits.astype(jnp.float32)

    def select_adapter(table):
        return jnp.einsum(
            "se,le...->ls...", slot_low, table, preferred_element_type=jnp.float32
        ).astype(jnp.bfloat16)

    def spread_slots(per_sequence):
        return jnp.einsum("se,s...->e...", slot_full, per_sequence, precision=PRECISE)

    chosen_in = select_adapter(adapt_in)
    chosen_down = select_adapter(adapt_down)
    chosen_out = select_adapter(adapt_out)
    chosen_ffn = select_adapter(adapt_ffn)

    def forward_group(items):
        query_block, key_block, value_block = items
        scores = (
            jnp.einsum(
                "sqhd,skhd->shqk", query_block, key_block, preferred_element_type=jnp.float32
            )
            * score_scale
        )
        scores = jnp.where(visible[:, None], scores, -1e30)
        biggest = jnp.max(scores, axis=-1, keepdims=True)
        lifted = jnp.exp(scores - biggest)
        row_total = jnp.sum(lifted, axis=-1, keepdims=True)
        probability = (lifted / row_total).astype(jnp.bfloat16)
        result = jnp.einsum(
            "shqk,skhd->sqhd", probability, value_block, preferred_element_type=jnp.float32
        )
        return (result.astype(jnp.bfloat16), (biggest + jnp.log(row_total))[..., 0])

    def backward_group(items):
        query_block, key_block, value_block, grad_block, log_total = items
        scores = (
            jnp.einsum(
                "sqhd,skhd->shqk", query_block, key_block, preferred_element_type=jnp.float32
            )
            * score_scale
        )
        scores = jnp.where(visible[:, None], scores, -1e30)
        probability = jnp.exp(scores - log_total[..., None])
        d_prob = jnp.einsum(
            "sqhd,skhd->shqk", grad_block, value_block, preferred_element_type=jnp.float32
        )
        delta = jnp.sum(probability * d_prob, axis=-1, keepdims=True)
        d_score = (probability * (d_prob - delta)).astype(jnp.bfloat16)
        d_query = (
            jnp.einsum("shqk,skhd->sqhd", d_score, key_block, preferred_element_type=jnp.float32)
            * score_scale
        )
        d_key = (
            jnp.einsum("shqk,sqhd->skhd", d_score, query_block, preferred_element_type=jnp.float32)
            * score_scale
        )
        d_value = jnp.einsum(
            "shqk,sqhd->skhd",
            probability.astype(jnp.bfloat16),
            grad_block,
            preferred_element_type=jnp.float32,
        )
        return (d_query, d_key, d_value)

    state = tokens.astype(jnp.float32)
    layer_index = 0
    w_qkv = lax.all_gather(qkv_weight[layer_index], ("batch", "seq"), axis=1, tiled=True)
    w_out = lax.all_gather(out_weight[layer_index], ("batch", "seq"), axis=0, tiled=True)
    w_in = lax.all_gather(ffn_in_weight[layer_index], ("batch", "seq"), axis=1, tiled=True)
    w_down = lax.all_gather(ffn_out_weight[layer_index], ("batch", "seq"), axis=0, tiled=True)
    held = [(w_qkv, w_out, w_in, w_down)]
    act_one = state.astype(jnp.bfloat16)
    low_qkv = jnp.einsum(
        "std,spdr->pstr",
        act_one,
        chosen_in[layer_index][:, 0:3],
        preferred_element_type=jnp.float32,
    ).astype(jnp.bfloat16)
    proj = jnp.einsum(
        "std,pde->pste", act_one, w_qkv, preferred_element_type=jnp.float32
    ) + jnp.einsum(
        "pstr,spre->pste",
        low_qkv,
        chosen_out[layer_index][:, 0:3],
        preferred_element_type=jnp.float32,
    )
    queries = (
        rotate(proj[0].reshape(seqs_here, tok_rows, HEADS, HEAD_DIM), cosine_here, sine_here)
        .astype(jnp.bfloat16)
        .reshape(seqs_here, tok_rows, model_width)
    )
    key_rot = (
        rotate(proj[1].reshape(seqs_here, tok_rows, HEADS, HEAD_DIM), cosine_here, sine_here)
        .astype(jnp.bfloat16)
        .reshape(seqs_here, tok_rows, model_width)
    )
    key_value = jnp.stack([key_rot, proj[2].astype(jnp.bfloat16)])
    edges = {}
    for step_by, row_count in shift_plan:
        if step_by > 0:
            outgoing = key_value[:, :, tok_rows - row_count :]
        else:
            outgoing = key_value[:, :, :row_count]
        edges[step_by] = shifted(outgoing, "seq", step_by)
    earlier = [edges[distance] for distance, row_count in reversed(shift_plan) if distance > 0]
    later = [edges[-distance] for distance, row_count in shift_plan if distance > 0]
    window = jnp.concatenate(earlier + [key_value] + later, axis=2)
    heads_out, log_total = lax.map(
        forward_group,
        (
            split_heads(queries, group_count),
            split_heads(window[0], group_count),
            split_heads(window[1], group_count),
        ),
    )
    attended = join_heads(heads_out)
    low_out = jnp.einsum(
        "std,sdr->str", attended, chosen_in[layer_index][:, 3], preferred_element_type=jnp.float32
    ).astype(jnp.bfloat16)
    branch = jnp.einsum(
        "std,de->ste", attended, w_out, preferred_element_type=jnp.float32
    ) + jnp.einsum(
        "str,sre->ste", low_out, chosen_out[layer_index][:, 3], preferred_element_type=jnp.float32
    )
    resid_one = state + branch
    hidden = norm_apply(resid_one, norm_gain[layer_index, 0], norm_bias[layer_index, 0])
    act_two = hidden.astype(jnp.bfloat16)
    low_ffn = jnp.einsum(
        "std,spdr->pstr",
        act_two,
        chosen_in[layer_index][:, 4:6],
        preferred_element_type=jnp.float32,
    ).astype(jnp.bfloat16)
    gate_up = jnp.einsum(
        "std,pdf->pstf", act_two, w_in, preferred_element_type=jnp.float32
    ) + jnp.einsum(
        "pstr,sprf->pstf", low_ffn, chosen_ffn[layer_index], preferred_element_type=jnp.float32
    )
    inner = (jax.nn.silu(gate_up[0]) * gate_up[1]).astype(jnp.bfloat16)
    low_down = jnp.einsum(
        "stf,sfr->str", inner, chosen_down[layer_index], preferred_element_type=jnp.float32
    ).astype(jnp.bfloat16)
    branch_two = jnp.einsum(
        "stf,fe->ste", inner, w_down, preferred_element_type=jnp.float32
    ) + jnp.einsum(
        "str,sre->ste", low_down, chosen_out[layer_index][:, 4], preferred_element_type=jnp.float32
    )
    resid_two = hidden + branch_two
    kept = [
        (
            act_one,
            low_qkv,
            queries,
            window,
            log_total,
            attended,
            low_out,
            resid_one,
            act_two,
            low_ffn,
            gate_up,
            inner,
            low_down,
            resid_two,
        )
    ]
    state = norm_apply(resid_two, norm_gain[layer_index, 1], norm_bias[layer_index, 1])
    mixed = state.astype(jnp.bfloat16)
    grad = cotangent.astype(jnp.float32)
    collected = [None] * LAYERS
    for layer_index in reversed(range(LAYERS)):
        (
            act_one,
            low_qkv,
            queries,
            window,
            log_total,
            attended,
            low_out,
            resid_one,
            act_two,
            low_ffn,
            gate_up,
            inner,
            low_down,
            resid_two,
        ) = kept[layer_index]
        w_qkv, w_out, w_in, w_down = held[layer_index]
        gain_two = norm_gain[layer_index, 1]
        bias_two = norm_bias[layer_index, 1]
        _, pull_two = jax.vjp(lambda residual: norm_apply(residual, gain_two, bias_two), resid_two)
        (d_resid_two,) = pull_two(grad)
        d_branch_two = d_resid_two.astype(jnp.bfloat16)
        d_low_down = jnp.einsum(
            "ste,sre->str",
            d_branch_two,
            chosen_out[layer_index][:, 4],
            preferred_element_type=jnp.float32,
        ).astype(jnp.bfloat16)
        g_out_down = jnp.einsum(
            "str,ste->sre", low_down, d_branch_two, preferred_element_type=jnp.float32
        )
        g_down = jnp.einsum("stf,str->sfr", inner, d_low_down, preferred_element_type=jnp.float32)
        d_inner = jnp.einsum(
            "ste,fe->stf", d_branch_two, w_down, preferred_element_type=jnp.float32
        ) + jnp.einsum(
            "str,sfr->stf", d_low_down, chosen_down[layer_index], preferred_element_type=jnp.float32
        )
        _, pull_act = jax.vjp(
            lambda gate_part, up_part: jax.nn.silu(gate_part) * up_part, gate_up[0], gate_up[1]
        )
        d_gate, d_up = pull_act(d_inner)
        d_gate_up = jnp.stack([d_gate, d_up]).astype(jnp.bfloat16)
        d_low_ffn = jnp.einsum(
            "pstf,sprf->pstr",
            d_gate_up,
            chosen_ffn[layer_index],
            preferred_element_type=jnp.float32,
        ).astype(jnp.bfloat16)
        g_ffn = jnp.einsum(
            "pstr,pstf->sprf", low_ffn, d_gate_up, preferred_element_type=jnp.float32
        )
        g_in_ffn = jnp.einsum(
            "std,pstr->spdr", act_two, d_low_ffn, preferred_element_type=jnp.float32
        )
        ffn_in_sum = spread_slots(g_in_ffn)
        ffn_down_sum = spread_slots(g_down)
        ffn_out_sum = spread_slots(g_out_down[:, None])
        ffn_ffn_sum = spread_slots(g_ffn)
        d_hidden = (
            d_resid_two
            + jnp.einsum("pstf,pdf->std", d_gate_up, w_in, preferred_element_type=jnp.float32)
            + jnp.einsum(
                "pstr,spdr->std",
                d_low_ffn,
                chosen_in[layer_index][:, 4:6],
                preferred_element_type=jnp.float32,
            )
        )
        gain_one = norm_gain[layer_index, 0]
        bias_one = norm_bias[layer_index, 0]
        _, pull_one = jax.vjp(lambda residual: norm_apply(residual, gain_one, bias_one), resid_one)
        (d_resid_one,) = pull_one(d_hidden)
        d_branch = d_resid_one.astype(jnp.bfloat16)
        d_low_out = jnp.einsum(
            "ste,sre->str",
            d_branch,
            chosen_out[layer_index][:, 3],
            preferred_element_type=jnp.float32,
        ).astype(jnp.bfloat16)
        g_out_att = jnp.einsum(
            "str,ste->sre", low_out, d_branch, preferred_element_type=jnp.float32
        )
        g_in_att = jnp.einsum(
            "std,str->sdr", attended, d_low_out, preferred_element_type=jnp.float32
        )
        d_attended = (
            jnp.einsum("ste,de->std", d_branch, w_out, preferred_element_type=jnp.float32)
            + jnp.einsum(
                "str,sdr->std",
                d_low_out,
                chosen_in[layer_index][:, 3],
                preferred_element_type=jnp.float32,
            )
        ).astype(jnp.bfloat16)
        d_query_heads, d_key_heads, d_value_heads = lax.map(
            backward_group,
            (
                split_heads(queries, group_count),
                split_heads(window[0], group_count),
                split_heads(window[1], group_count),
                split_heads(d_attended, group_count),
                log_total,
            ),
        )
        d_query = join_heads(d_query_heads)
        d_window = jnp.stack([join_heads(d_key_heads), join_heads(d_value_heads)])
        d_pair = d_window[:, :, left_total : left_total + tok_rows]
        for step_by, row_count in shift_plan:
            returning = lax.slice_in_dim(
                d_window, key_places[step_by], key_places[step_by] + row_count, axis=2
            )
            arrived = shifted(returning.astype(jnp.bfloat16), "seq", -step_by).astype(
                returning.dtype
            )
            if step_by > 0:
                d_pair = d_pair.at[:, :, tok_rows - row_count :].add(arrived)
            else:
                d_pair = d_pair.at[:, :, :row_count].add(arrived)
        d_query_rot = rotate(
            d_query.reshape(seqs_here, tok_rows, HEADS, HEAD_DIM), cosine_here, -sine_here
        ).reshape(seqs_here, tok_rows, model_width)
        d_key_rot = rotate(
            d_pair[0].reshape(seqs_here, tok_rows, HEADS, HEAD_DIM), cosine_here, -sine_here
        ).reshape(seqs_here, tok_rows, model_width)
        d_proj = jnp.stack([d_query_rot, d_key_rot, d_pair[1]]).astype(jnp.bfloat16)
        d_low_qkv = jnp.einsum(
            "pste,spre->pstr",
            d_proj,
            chosen_out[layer_index][:, 0:3],
            preferred_element_type=jnp.float32,
        ).astype(jnp.bfloat16)
        g_out_qkv = jnp.einsum(
            "pstr,pste->spre", low_qkv, d_proj, preferred_element_type=jnp.float32
        )
        g_in_qkv = jnp.einsum(
            "std,pstr->spdr", act_one, d_low_qkv, preferred_element_type=jnp.float32
        )
        grad = (
            d_resid_one
            + jnp.einsum("pste,pde->std", d_proj, w_qkv, preferred_element_type=jnp.float32)
            + jnp.einsum(
                "pstr,spdr->std",
                d_low_qkv,
                chosen_in[layer_index][:, 0:3],
                preferred_element_type=jnp.float32,
            )
        )
        att_in_sum = spread_slots(jnp.concatenate([g_in_qkv, g_in_att[:, None]], axis=1))
        att_out_sum = spread_slots(jnp.concatenate([g_out_qkv, g_out_att[:, None]], axis=1))
        collected[layer_index] = (
            jnp.concatenate([att_in_sum, ffn_in_sum], axis=1),
            ffn_down_sum,
            jnp.concatenate([att_out_sum, ffn_out_sum], axis=1),
            ffn_ffn_sum,
        )
    input_grad = grad.astype(jnp.bfloat16)
    stack_in = jnp.stack([collected[0][0]])
    stack_down = jnp.stack([collected[0][1]])
    stack_out = jnp.stack([collected[0][2]])
    stack_ffn = jnp.stack([collected[0][3]])
    stack_in, stack_down, stack_out, stack_ffn = lax.psum(
        (stack_in, stack_down, stack_out, stack_ffn), ("batch", "seq")
    )
    return (mixed, input_grad, stack_in, stack_down, stack_out, stack_ffn)


MESH = pl.DeviceIdType.MESH
NCHUNK = 10
ALL = slice(None)


class Gather:
    def __init__(self, sems, direct=(), diagonal=()):
        self.direct = direct
        self.diagonal = diagonal
        (
            self.zs, self.zr, self.xs, self.xr, self.ys, self.yr, self.ds, self.dr, self.es, self.er, self.fs, self.fr,
            self.cs, self.cr,
        ) = sems
        b = lax.axis_index("batch")
        self.b = b
        self.s = lax.axis_index("seq")
        self.core = lax.rem(b, 2)
        self.x = lax.rem(lax.div(b, 2), 2)
        self.z = lax.div(b, 4)
        self.za = lax.div(self.z, 2)
        self.zb = lax.rem(self.z, 2)
        self.devx = (b + 2 - 4 * self.x, self.s)
        self.devy = (b, 1 - self.s)
        self.devd = (b + 2 - 4 * self.x, 1 - self.s)
        self.devc = (b + 1 - 2 * self.core, self.s)
        self.devp = (b + 4 - 8 * self.zb, self.s)

    def column(self, dx, dy, dc):
        x = 1 - self.x if dx else self.x
        y = 1 - self.s if dy else self.s
        c = 1 - self.core if dc else self.core
        return (x * 2 + c) * 2 + y

    def devz(self, z):
        return (z * 4 + self.x * 2 + self.core, self.s)

    def copy(self, c, za, zb, k, half, dev, send, recv):
        v = self.view(c, za, zb, k, half)
        return pltpu.make_async_remote_copy(v, v, send, recv, device_id=dev, device_id_type=MESH)

    def to_z(self, c, z):
        return self.copy(
            c, self.za, self.zb, self.column(0, 0, 0), None, self.devz(z), self.zs.at[c, z], self.zr.at[c, self.z]
        )

    def from_z(self, c, z):
        return self.copy(
            c, lax.div(z, 2), lax.rem(z, 2), self.column(0, 0, 0), None, self.devz(z), self.zs.at[c, z], self.zr.at[c, z]
        )

    def on_x(self, c, arriving):
        return self.copy(c, ALL, ALL, self.column(arriving, 0, 0), None, self.devx, self.xs.at[c], self.xr.at[c])

    def on_y(self, c, arriving):
        return self.copy(c, ALL, ALL, self.column(0, arriving, 0), None, self.devy, self.ys.at[c], self.yr.at[c])

    def on_diagonal(self, c, arriving):
        return self.copy(c, ALL, ALL, self.column(arriving, arriving, 0), None, self.devd, self.ds.at[c], self.dr.at[c])

    def parity(self, c):
        return ALL if c in self.direct else self.zb

    def corner_x(self, c, arriving):
        k = self.column(arriving, 1, 0)
        return self.copy(c, ALL, self.parity(c), k, 0, self.devx, self.ds.at[c], self.dr.at[c])

    def corner_y(self, c, arriving):
        k = self.column(1, arriving, 0)
        return self.copy(c, ALL, self.parity(c), k, 1, self.devy, self.es.at[c], self.er.at[c])

    def corner_z(self, c, arriving):
        zb = 1 - self.zb if arriving else self.zb
        return self.copy(c, ALL, zb, self.column(1, 1, 0), None, self.devp, self.fs.at[c], self.fr.at[c])

    def on_core(self, c, kind, arriving):
        k = self.column(kind & 1, kind >> 1, arriving)
        return self.copy(c, ALL, ALL, k, None, self.devc, self.cs.at[c, kind], self.cr.at[c, kind])

    def others(self):
        z = self.z
        first = jnp.where(z == 0, 1, z - 1)
        second = jnp.where(z == 0, 2, jnp.where(z == 3, 1, z + 1))
        third = jnp.where(z <= 1, 3, 0)
        return first, second, third

    def partners(self):
        return [self.devx, self.devy, self.devc] + [self.devz(z) for z in self.others()]

    def barrier(self, devices):
        bar = pltpu.get_barrier_semaphore()
        for dev in devices:
            pl.semaphore_signal(bar, inc=1, device_id=dev, device_id_type=MESH)
        pl.semaphore_wait(bar, len(devices))

    def send_z(self, c):
        for z in self.others():
            self.to_z(c, z).start()

    def stage_z(self, c):
        for z in self.others():
            self.from_z(c, z).wait_recv()
        self.on_x(c, 0).start()
        self.on_y(c, 0).start()
        if c in self.diagonal:
            self.on_diagonal(c, 0).start()
        self.on_core(c, 0, 0).start()

    def stage_xy(self, c):
        self.on_x(c, 1).wait_recv()
        if c not in self.diagonal:
            self.corner_y(c, 0).start()
        self.on_core(c, 1, 0).start()
        self.on_y(c, 1).wait_recv()
        if c not in self.diagonal:
            self.corner_x(c, 0).start()
        self.on_core(c, 2, 0).start()
        if c in self.diagonal:
            self.on_diagonal(c, 1).wait_recv()
            self.on_core(c, 3, 0).start()

    def stage_corner(self, c):
        self.corner_x(c, 1).wait_recv()
        self.corner_y(c, 1).wait_recv()
        if c in self.direct:
            self.on_core(c, 3, 0).start()
        else:
            self.corner_z(c, 0).start()

    def stage_pair(self, c):
        self.corner_z(c, 1).wait_recv()
        self.on_core(c, 3, 0).start()

    def stage_core(self, c):
        for kind in range(4):
            self.on_core(c, kind, 1).wait_recv()

    def finish(self, c):
        for z in self.others():
            self.to_z(c, z).wait_send()
        self.on_x(c, 0).wait_send()
        self.on_y(c, 0).wait_send()
        for kind in range(4):
            self.on_core(c, kind, 0).wait_send()
        if c in self.diagonal:
            self.on_diagonal(c, 0).wait_send()
        else:
            self.corner_x(c, 0).wait_send()
            self.corner_y(c, 0).wait_send()
            if c not in self.direct:
                self.corner_z(c, 0).wait_send()


def gather_sems(chunks):
    one = pltpu.SemaphoreType.DMA((chunks,))
    four = pltpu.SemaphoreType.DMA((chunks, 4))
    return [four] * 2 + [one] * 10 + [four] * 2


BF = jnp.bfloat16
F32 = jnp.float32
QB = 256
PLAN = ((0, 3, False, True), (0, 4, False, True), (0, 5, True, True), (1, 5, True, True))
HALO_PLAN = ((2, 2), (3, 1))
NEG = -1e30
VMEM_LIMIT = int(63.9 * 2**20)
ORDER = (
    "h0", "z0", "z1", "z2", "x0", "T", "x1", "x2", "c0", "z4", "h2", "c2", "c1", "k0",
    "h3", "k2", "z3", "P0", "k1", "x4", "z6", "h1", "P1", "P2", "A003", "z5", "A036", "c4",
    "A103", "x6", "z7", "A136", "H", "x5", "x3", "p4", "c6", "z8", "A202", "A224", "p6", "c5",
    "A246", "x7", "c3", "k6", "z9", "A302", "p5", "x8", "c7", "k3", "k4", "A324", "A346", "p7",
    "k5", "O", "x9", "c8", "k7", "F0", "c9", "p8", "F1", "k8", "p9", "F2", "k9", "F3",
)


def nn(a, b):
    return jnp.dot(a, b, preferred_element_type=F32)


def nt(a, b):
    return lax.dot_general(a, b, (((1,), (1,)), ((), ())), preferred_element_type=F32)


def tn(a, b):
    return lax.dot_general(a, b, (((0,), (0,)), ((), ())), preferred_element_type=F32)


def iota(shape, dim):
    return lax.broadcasted_iota(jnp.int32, shape, dim)


def block_at(flip, block):
    return pl.multiple_of(jnp.where(flip == 1, 3 - block, block) * QB, QB)


def rope(vectors, cosine, sine):
    lane = iota((1, 128), 1)
    first = lax.rem(lane, HEAD_DIM) < HEAD_DIM // 2
    out = []
    for c in range(vectors.shape[1] // 128):
        part = vectors[:, c * 128 : (c + 1) * 128]
        other = jnp.where(first, pltpu.roll(part, 96, 1), pltpu.roll(part, 32, 1))
        out.append(part * cosine + other * sine)
    return jnp.concatenate(out, axis=1)


def fill_tables(flip, seg_ref, freq_ref, cos_ref, sin_ref, fq_ref, fk_ref, bias_ref):
    lane = iota((1, 128), 1)
    seg_row = seg_ref[...].astype(F32)
    starts = [
        jnp.sum((seg_row < float(d)).astype(F32), axis=1, keepdims=True) for d in (1, 2, 3)
    ]
    sign = jnp.where(lax.rem(lane, HEAD_DIM) < HEAD_DIM // 2, -1.0, 1.0)
    for w in range(12):
        block, part = divmod(w, 2)
        base = jnp.where(flip == 1, 7 - block, block) * QB + part * 128
        row = seg_ref[:, pl.ds(pl.multiple_of(base, 128), 128)].astype(F32)
        seg = jnp.broadcast_to(row, (128, 128)).T
        start = jnp.where(
            seg >= 3.0,
            starts[2],
            jnp.where(seg >= 2.0, starts[1], jnp.where(seg >= 1.0, starts[0], 0.0)),
        )
        pos = (iota((128, 128), 0) + base).astype(F32) - start
        angle = pos * freq_ref[...]
        rows = pl.ds(w * 128, 128)
        cos_ref[rows, :] = jnp.cos(angle)
        sin_ref[rows, :] = jnp.sin(angle) * sign
        hit = seg == lane.astype(F32)
        fq_ref[rows, :] = jnp.where(hit, 1.0, 0.0).astype(BF)
        fk_ref[rows, :] = jnp.where(hit | (lane >= 4), 0.0, NEG).astype(BF)
    gap = iota((QB, QB), 0) - iota((QB, QB), 1)
    gap = jnp.where(flip == 1, -gap, gap)
    bias_ref[0] = jnp.where(gap >= 0, 0.0, NEG)
    bias_ref[1] = jnp.where(gap <= 0, 0.0, NEG)


def qkv_rows(p, rb, xw, wq, aqkv, bblk, cos_ref, sin_ref, dest, low_ref):
    rows = pl.ds(pl.multiple_of(rb * 512, 512), 512)
    x = xw[rows, :]
    if p == 0:
        low = nt(x, aqkv[...]).astype(BF)
        low_ref[rows, :] = low
    else:
        low = low_ref[rows, :]
    proj = nn(x, wq[p].reshape(D, D)) + nn(low, bblk[p])
    if p < 2:
        proj = rope(proj, cos_ref[rows, :], sin_ref[rows, :])
    value = proj.astype(BF)
    if p == 0:
        value = value * jnp.asarray(0.125, BF)
    dest[pl.ds(rb * 2, 2)] = value.reshape(2, QB, D)


def prob_copies(n, src, dst, sem, s):
    full = (2 * n + 2) // 3
    cuts = ((0, 2), (2, full)) if full > 2 else ((0, 1), (1, 2))
    return [
        pltpu.make_async_copy(src.at[pl.ds(a, b - a)], dst.at[pl.ds(a, b - a)], sem.at[2 * s + i])
        for i, (a, b) in enumerate(cuts)
    ]


def attend_pair(
    qb, pair, step, q_ref, k_ref, v_ref, fq_ref, fk_ref, bias_ref, att_ref, linv_ref, mf_ref, p_hbm, stage, sem
):
    k0, n, tri_first, tri_last = PLAN[qb]
    rows = pl.ds(qb * QB, QB)
    kblocks = pl.ds(k0, n)
    krows = pl.ds(k0 * QB, n * QB)
    half = iota((1, 128), 1) >= HEAD_DIM
    lane = iota((1, 128), 1)
    slot = lax.rem(step, 2)

    def copy(s, tiles=n):
        return prob_copies(tiles, stage.at[pl.ds(s * 4, 4)], p_hbm.at[qb, pair], sem, s)

    @pl.when(pair >= 2)
    def _():
        for one in copy(slot):
            one.wait()

    if qb > 0:

        @pl.when(pair < 2)
        def _():
            for one in copy(slot, PLAN[qb - 1][1]):
                one.wait()

    lanes = pl.ds(pl.multiple_of(pair * 128, 128), 128)
    q2 = q_ref[qb, :, lanes]
    fq = fq_ref[rows, :]
    keys = jnp.concatenate([k_ref[kblocks, :, lanes].reshape(n * QB, 128), fk_ref[krows, :]], axis=1)
    v2 = v_ref[kblocks, :, lanes].reshape(n * QB, 128)
    masks = (jnp.logical_not(half), half)
    scores = [
        nt(jnp.concatenate([jnp.where(mine, q2, jnp.zeros_like(q2)), fq], axis=1), keys) for mine in masks
    ]
    outs = []
    for h, (mine, s) in enumerate(zip(masks, scores)):
        parts = [s[:, t * QB : (t + 1) * QB] for t in range(n)]
        if tri_last:
            parts[n - 1] = parts[n - 1] + bias_ref[0]
        if tri_first:
            parts[0] = parts[0] + bias_ref[1]
        s = jnp.concatenate(parts, axis=1)
        m = jnp.max(s, axis=1, keepdims=True)
        p = jnp.exp(s - m).astype(BF)
        for t in range(n):
            block, lane0 = divmod(h * n + t, 3)
            stage[slot * 4 + block, :, lane0 * QB : lane0 * QB + QB] = p[:, t * QB : (t + 1) * QB]
        if qb >= 2:
            low = 4 + 3 * (2 * pair + h)
            mf_ref[rows, :] = jnp.where((lane >= low) & (lane < low + 3), -m, mf_ref[rows, :])
        outs.append(nn(p, jnp.where(mine, v2, jnp.ones_like(v2))))
    inv = 1.0 / pltpu.roll(jnp.where(half, outs[0], outs[1]), HEAD_DIM, 1)
    att_ref[rows, lanes] = (jnp.where(half, outs[1], outs[0]) * inv).astype(BF)
    linv_ref[rows, lanes] = inv
    for one in copy(slot):
        one.start()


def drain_pairs(qb, p_hbm, stage, sem):
    for s in range(2):
        for one in prob_copies(PLAN[qb][1], stage.at[pl.ds(s * 4, 4)], p_hbm.at[qb, 0], sem, s):
            one.wait()


def sigmoid(v):
    return 0.5 * jnp.tanh(0.5 * v) + 0.5


def norm_stats(r):
    centre = r - jnp.mean(r, axis=1, keepdims=True)
    rstd = lax.rsqrt(jnp.mean(centre * centre, axis=1, keepdims=True) + EPSILON)
    return centre * rstd, rstd


def norm_back(grad, xhat, rstd):
    return rstd * (
        grad
        - jnp.mean(grad, axis=1, keepdims=True)
        - xhat * jnp.mean(grad * xhat, axis=1, keepdims=True)
    )


def out_rows(rb, xw, att_ref, wo, ao, bo, gb, aff, xhat_ref, rstd_ref, act_ref, lowo_ref, lowf_ref):
    rows = pl.ds(pl.multiple_of(rb * 512, 512), 512)
    att = att_ref[rows, :]
    low = nt(att, ao[...]).astype(BF)
    lowo_ref[rows, :] = low
    branch = nn(att, wo[...].reshape(D, D)) + nn(low, bo[...])
    xhat, rstd = norm_stats(xw[rows, :].astype(F32) + branch)
    xhat_ref[rows, :] = xhat
    rstd_ref[rows, :] = jnp.broadcast_to(rstd, (512, 128))
    act = (xhat * gb[0:1, :] + gb[1:2, :]).astype(BF)
    act_ref[rows, :] = act
    lowf_ref[rows, :] = nt(act, aff[...]).astype(BF)


def ffn_in_tile(n, rb, size, act_ref, lowf_ref, wi, wd, bg, bu, adn, big, lowd_ref, total_ref):
    start = pl.multiple_of(rb * size, size)
    rows = pl.ds(start, size)
    act = act_ref[rows, :]
    low = lowf_ref[rows, :]
    blocks = size // QB
    here = n * 4 + rb * blocks
    parts = []
    for c in range(3):
        lanes = slice(c * 256, c * 256 + 256)
        gate = nn(act, wi[n, 0, :, :, :, :, lanes].reshape(D, 256)) + nn(low, bg[n, :, lanes])
        up = nn(act, wi[n, 1, :, :, :, :, lanes].reshape(D, 256)) + nn(low, bu[n, :, lanes])
        parts.append((gate * sigmoid(gate) * up).astype(BF))
        big[pl.ds(here, blocks), :, lanes] = gate.astype(BF).reshape(blocks, QB, 256)
        big[pl.ds(here + 16, blocks), :, lanes] = up.astype(BF).reshape(blocks, QB, 256)
    inner = jnp.concatenate(parts, axis=1)
    lowd_ref[rows, 0:16] += nt(inner, adn[n])
    for c in range(3):
        lanes = slice(c * 256, c * 256 + 256)
        total_ref[rows, lanes] += nn(inner, wd[lax.div(n, 2), lax.rem(n, 2), :, :, lanes].reshape(D, 256))


def ffn_out_rows(
    rb, flip, lowd_ref, bdn, xhat_ref, gb, cot, dtwo_ref, db2_ref, dlow_ref, mixed_ref, gbdn_ref
):
    start = pl.multiple_of(rb * QB, QB)
    rows = pl.ds(start, QB)
    low = lowd_ref[rows, 0:16].astype(BF)
    total = nn(low, bdn[...]) + dtwo_ref[rows, :]
    r = xhat_ref[rows, :] * gb[0:1, :] + gb[1:2, :] + total
    xhat, rstd = norm_stats(r)
    mixed_ref[pl.ds(block_at(flip, rb), QB), :] = (xhat * gb[2:3, :] + gb[3:4, :]).astype(BF)
    dtwo = norm_back(cot[rows, :].astype(F32) * gb[2:3, :], xhat, rstd)
    dtwo_ref[rows, :] = dtwo
    db2 = dtwo.astype(BF)
    db2_ref[rows, :] = db2
    dlow_ref[rows, :] = nt(db2, bdn[...]).astype(BF)
    gbdn_ref[...] += tn(low, db2)


def ffn_back_tile(
    n, start, size, db2_ref, dlow_ref, wd, wi, adn, bg, bu, big, lowf_ref, acc, dlf_ref, gadn_ref, gbf_ref
):
    rows = pl.ds(start, size)
    db2 = db2_ref[rows, :]
    dlow = dlow_ref[rows, :]
    blocks = size // QB
    here = n * 4 + lax.div(start, QB)
    down = wd[lax.div(n, 2), lax.rem(n, 2)].reshape(D, D)
    dgs, dus, inners = [], [], []
    for c in range(3):
        lanes = slice(c * 256, c * 256 + 256)
        dinner = nt(db2, down[lanes]) + nn(dlow, adn[n, :, lanes])
        gate = big[pl.ds(here, blocks), :, lanes].reshape(size, 256).astype(F32)
        up = big[pl.ds(here + 16, blocks), :, lanes].reshape(size, 256).astype(F32)
        sig = sigmoid(gate)
        silu = gate * sig
        inners.append((silu * up).astype(BF))
        dgs.append((dinner * up * (sig + silu * (1.0 - sig))).astype(BF))
        dus.append((dinner * silu).astype(BF))
    dg, du, inner = (jnp.concatenate(v, axis=1) for v in (dgs, dus, inners))
    acc[...] += nt(dg, wi[n, 0].reshape(D, D)) + nt(du, wi[n, 1].reshape(D, D))
    dlf_ref[...] += nt(bg[n], dg) + nt(bu[n], du)
    gadn_ref[n] += tn(dlow, inner)
    low = lowf_ref[rows, :]
    gbf_ref[n] += jnp.where(iota((32, 1), 0) < 16, tn(low, dg), tn(low, du))


def hidden_back_rows(
    rb, off, acc, dlf_ref, aff, act_ref, dtwo_ref, xhat_ref, rstd_ref, gb, bo, ao, lowo_ref, att_ref,
    wo, linv_ref, h2, mf_ref, do_ref, hf_ref, gaff_ref, gbo_ref, gao_ref,
):
    start = pl.multiple_of(rb * QB, QB)
    rows = pl.ds(start, QB)
    local = pl.ds(pl.multiple_of(start - off, QB), QB)
    dlf = dlf_ref[:, local].T.astype(BF)
    dhid = dtwo_ref[rows, :] + acc[local, :] + nn(dlf, aff[...])
    gaff_ref[...] += tn(dlf, act_ref[rows, :])
    done = norm_back(dhid * gb[0:1, :], xhat_ref[rows, :], rstd_ref[rows, 0:1])
    dtwo_ref[rows, :] = done
    dbr = done.astype(BF)
    dlo = nt(dbr, bo[...]).astype(BF)
    att = att_ref[rows, :]
    gbo_ref[...] += tn(lowo_ref[rows, :], dbr)
    gao_ref[...] += tn(dlo, att)
    datt = (nt(dbr, wo[...].reshape(D, D)) + nn(dlo, ao[...])).astype(BF)
    do = (datt.astype(F32) * linv_ref[rows, :]).astype(BF)
    do_ref[rows, :] = do
    value = nn(do * att, h2[...]) + mf_ref[rows, :]
    lane = iota((1, 128), 1)
    role = jnp.where(lane < 40, lax.rem(lane + 2, 3), lax.rem(lane, 2))
    high = value.astype(BF)
    rest = value - high.astype(F32)
    mid = rest.astype(BF)
    last = (rest - mid.astype(F32)).astype(BF)
    hf_ref[rows, :] = jnp.where(role == 0, high, jnp.where(role == 1, mid, last))


def kf_kernel(
    x_hbm, cot_hbm, seg_hbm, freq_hbm, pick_hbm, gain_hbm, shift_hbm, tin_hbm, tdn_hbm, tout_hbm, tff_hbm,
    wq_hbm, wo_hbm, wi_hbm, wd_hbm,
    q_hbm, k_hbm, v_hbm, p_hbm, mixed_hbm, do_hbm, hf_hbm, lowq_hbm, done_hbm, cos_hbm, sin_hbm, fq_hbm, fk_hbm,
    ge_hbm, gao_hbm, tag_hbm, aqkv_hbm, bqkv_hbm, wq_out,
    seg_ref, freq_ref, pick_ref, gain_ref, shift_ref, hf_ref, ge_ref, gao_ref, tag_ref, aqkv, bqkv, ssem, fsem,
    ao, bo, aff, adn, bdn, gb,
    gaff_ref, gadn_ref, gbo_ref, gbdn_ref, gbf_ref,
    wq, wo, wi, wd, big, xw, att, linv, xhat, dtwo, act, db2, cos, sin, fq, fk, bias, mf,
    lowq, lowo, lowf, dlow, acc, dlf, bblk, bg, bu, h2, rsem, tsem, wsem, xsem, osem, psem, hs, hr, *sems,
):
    flip = lax.axis_index("seq")
    cot = db2
    do_ref = db2
    mixed_ref = xw.at[pl.ds(0, 1024)]
    rstd = cos
    lowd = sin
    loads = []
    for i in range(4):
        loads.append(
            pltpu.make_async_copy(
                x_hbm.at[pl.ds(block_at(flip, i), QB)], xw.at[pl.ds(i * QB, QB)], xsem.at[i]
            )
        )
        loads.append(
            pltpu.make_async_copy(
                cot_hbm.at[pl.ds(block_at(flip, i), QB)], cot.at[pl.ds(i * QB, QB)], xsem.at[4 + i]
            )
        )
    small = [
        pltpu.make_async_copy(a, b, ssem.at[i])
        for i, (a, b) in enumerate(
            ((seg_hbm, seg_ref), (freq_hbm, freq_ref), (pick_hbm, pick_ref), (gain_hbm, gain_ref), (shift_hbm, shift_ref))
        )
    ]
    for copy in small:
        copy.start()
    facts = [
        pltpu.make_async_copy(a, b, fsem.at[i])
        for i, (a, b) in enumerate(
            ((tag_ref, tag_hbm), (aqkv, aqkv_hbm), (bqkv, bqkv_hbm), (ge_ref, ge_hbm), (gao_ref, gao_hbm))
        )
    ]
    tables = [
        (tin_hbm, big.at[pl.ds(0, ADAPTERS), pl.ds(0, 96)]),
        (tout_hbm, big.at[pl.ds(4, ADAPTERS), pl.ds(0, 80)]),
    ]
    for n in range(4):
        lanes = pl.ds(n * D, D)
        tables.append((tdn_hbm.at[:, :, lanes], big.at[pl.ds(8, ADAPTERS), pl.ds(16 * n, 16)]))
        tables.append((tff_hbm.at[:, :, lanes], big.at[pl.ds(12, ADAPTERS), pl.ds(32 * n, 32)]))
    tables = [pltpu.make_async_copy(a, b, tsem.at[i]) for i, (a, b) in enumerate(tables)]
    g = Gather(sems, direct=(0, 1, 2, 3))

    def view(c, za, zb, k, half):
        cut = 384 if c < 4 else 640
        lanes = ALL if half is None else pl.ds(0, cut) if half == 0 else pl.ds(cut, D - cut)
        if c < 3:
            return wq.at[c, za, zb, k, :, lanes]
        if c == 3:
            return wo.at[za, zb, k, :, lanes]
        if c < 6:
            return wd.at[za, zb, k, pl.ds((c - 4) * 48, 48), lanes]
        return wi.at[c - 6, :, za, zb, k, :, lanes]

    g.view = view
    here = g.column(0, 0, 0)
    weights = [
        pltpu.make_async_copy(a, b, wsem.at[i])
        for i, (a, b) in enumerate(
            [(wq_hbm, wq.at[:, g.za, g.zb, here]), (wo_hbm, wo.at[g.za, g.zb, here]), (wd_hbm, wd.at[g.za, g.zb, here])]
            + [(wi_hbm.at[:, :, pl.ds(D * n, D)], wi.at[n, :, g.za, g.zb, here]) for n in range(4)]
        )
    ]
    for copy in weights:
        copy.start()
    g.barrier(g.partners())
    for copy in weights:
        copy.wait()
    for c in range(NCHUNK):
        g.send_z(c)
    halo = [
        pltpu.make_async_remote_copy(
            x_hbm.at[pl.ds(block_at(flip, 3 - i // 2) + i % 2 * 128, 128)], xw.at[pl.ds(1024 + i * 128, 128)],
            hs.at[i], hr.at[i], device_id=g.devy, device_id_type=MESH,
        )
        for i in range(4)
    ]

    kinds = {
        "z": g.stage_z, "x": g.stage_xy, "c": g.stage_corner, "p": g.stage_pair, "k": g.stage_core,
    }

    for copy in loads + tables:
        copy.start()

    def prepare():
        for copy in small:
            copy.wait()
        fill_tables(flip, seg_ref, freq_ref, cos, sin, fq, fk, bias)
        for copy in tables:
            copy.wait()
        e = pick_ref[0, 0]
        aqkv[...] = big[e, 0:48, :]
        ao[...] = big[e, 48:64, :]
        aff[...] = big[e, 64:96, :]
        bqkv[...] = big[4 + e, 0:48, :]
        bo[...] = big[4 + e, 48:64, :]
        bdn[...] = big[4 + e, 64:80, :]
        for n in range(4):
            adn[n] = big[8 + e, 16 * n : 16 * n + 16, :]
        tag_ref[...] = jnp.where(iota((16, 128), 0) == e, 1.0, 0.0).astype(BF)
        for copy in facts[:3]:
            copy.start()
        for i in range(2):
            gb[2 * i : 2 * i + 1, :] = gain_ref[i : i + 1, :]
            gb[2 * i + 1 : 2 * i + 2, :] = shift_ref[i : i + 1, :]
        rank = iota((48, 1), 0)
        for p in range(3):
            keep = (rank >= 16 * p) & (rank < 16 * p + 16)
            bblk[p] = jnp.where(keep, bqkv[...], jnp.zeros_like(bqkv[...]))
        rank = iota((32, 1), 0)
        for n in range(4):
            piece = big[12 + e, 32 * n : 32 * n + 32, :]
            bg[n] = jnp.where(rank < 16, piece, jnp.zeros_like(piece))
            bu[n] = jnp.where(rank >= 16, piece, jnp.zeros_like(piece))
        head = lax.div(iota((D, 128), 0), HEAD_DIM)
        spot = iota((D, 128), 1)
        h2[...] = jnp.where(lax.div(spot - 40, 2) == head, jnp.where(spot >= 40, -1.0, 0.0), 0.0).astype(BF)
        mf[...] = jnp.zeros_like(mf)
        dtwo[...] = jnp.zeros_like(dtwo)
        for ref in (gao_ref, gaff_ref, gadn_ref, gbo_ref, gbdn_ref, gbf_ref):
            ref[...] = jnp.zeros_like(ref)
        for copy in loads:
            copy.wait()

    q_ref, k_ref, v_ref = (big.at[pl.ds(i * 6, 6)] for i in range(3))
    stage = big.at[pl.ds(18, 8)]
    keep_wq = pltpu.make_async_copy(wq, wq_out, osem.at[9])
    saves = [
        pltpu.make_async_copy(a, b, osem.at[i])
        for i, (a, b) in enumerate(
            ((q_ref, q_hbm), (k_ref, k_hbm), (v_ref, v_hbm), (lowq, lowq_hbm), (cos, cos_hbm), (sin, sin_hbm), (fq, fq_hbm), (fk, fk_hbm))
        )
    ]

    def qkv_page(p, first, last):
        def step(rb, _):
            qkv_rows(p, rb, xw, wq, aqkv, bblk, cos, sin, (q_ref, k_ref, v_ref)[p], lowq)
            return 0

        lax.fori_loop(first, last, step, 0)

    def attend(qb, first, last):
        def pair_step(pair, _):
            attend_pair(qb, pair, pair, q_ref, k_ref, v_ref, fq, fk, bias, att, linv, mf, p_hbm, stage, psem)
            return 0

        lax.fori_loop(first, last, pair_step, 0)
        if last == 6 and qb == 3:
            drain_pairs(qb, p_hbm, stage, psem)

    def out_step(rb, _):
        out_rows(rb, xw, att, wo, ao, bo, gb, aff, xhat, rstd, act, lowo, lowf)
        return 0

    def in_step(i, _):
        ffn_in_tile(i, 0, 1024, act, lowf, wi, wd, bg, bu, adn, big, lowd, dtwo)
        return 0

    for step in ORDER:
        kind, rest = step[0], step[1:]
        if kind in kinds:
            kinds[kind](int(rest))
        elif kind == "h":
            halo[int(rest)].start()
        elif step == "T":
            prepare()
        elif kind == "P":
            qkv_page(int(rest), 0, 2)
        elif step == "H":
            for copy in halo:
                copy.wait_recv()
            for p in range(3):
                qkv_page(p, 2, 3)
            for copy in saves:
                copy.start()
            keep_wq.start()
        elif kind == "A":
            attend(*(int(v) for v in rest))
        elif step == "O":
            for copy in saves:
                copy.wait()
            lowd[...] = jnp.zeros_like(lowd)
            lax.fori_loop(0, 2, out_step, 0)
        elif kind == "F":
            n = int(rest)
            lax.fori_loop(n, n + 1, in_step, 0)

    def down_step(rb, _):
        ffn_out_rows(rb, flip, lowd, bdn, xhat, gb, cot, dtwo, db2, dlow, mixed_ref, gbdn_ref)
        return 0

    lax.fori_loop(0, 4, down_step, 0)
    outs = [pltpu.make_async_copy(mixed_ref, mixed_hbm, rsem.at[0])]
    outs[0].start()

    def row_copies(rb):
        rows = pl.ds(pl.multiple_of(rb * QB, QB), QB)
        return (
            pltpu.make_async_copy(do_ref.at[rows], do_hbm.at[rows], rsem.at[1 + rb]),
            pltpu.make_async_copy(dtwo.at[rows], done_hbm.at[rows], rsem.at[5 + rb]),
            pltpu.make_async_copy(hf_ref.at[rows], hf_hbm.at[rows], rsem.at[9 + rb]),
        )

    def back_step(half, _):
        off = pl.multiple_of(half * 512, 512)
        acc[...] = jnp.zeros_like(acc)
        dlf[...] = jnp.zeros_like(dlf)

        def tile(n, _):
            ffn_back_tile(
                n, off, 512, db2, dlow, wd, wi, adn, bg, bu, big, lowf, acc, dlf, gadn_ref, gbf_ref
            )
            return 0

        lax.fori_loop(0, 4, tile, 0)

        def rows(i, _):
            hidden_back_rows(
                half * 2 + i, off, acc, dlf, aff, act, dtwo, xhat, rstd, gb, bo, ao, lowo, att, wo, linv, h2, mf,
                do_ref, hf_ref, gaff_ref, gbo_ref, gao_ref,
            )
            for copy in row_copies(half * 2 + i):
                copy.start()
            return 0

        lax.fori_loop(0, 2, rows, 0)
        return 0

    lax.fori_loop(0, 2, back_step, 0)
    for rb in range(4):
        outs.extend(row_copies(rb))
    ge_ref[0:32] = gaff_ref[...].astype(BF)
    ge_ref[32:48] = gbo_ref[...].astype(BF)
    ge_ref[48:64] = gbdn_ref[...].astype(BF)
    ge_ref[64:128] = gadn_ref[...].reshape(64, D).astype(BF)
    ge_ref[128:256] = gbf_ref[...].reshape(128, D).astype(BF)
    for copy in facts[3:]:
        copy.start()
    keep_wq.wait()
    for copy in outs + facts:
        copy.wait()
    for copy in halo:
        copy.wait_send()
    for c in range(NCHUNK):
        g.finish(c)


def k3_kernel(
    x_hbm, q_hbm, k_hbm, v_hbm, p_hbm, do_hbm, hf_hbm, ge_hbm, gao_hbm, tag_hbm, lowq_hbm, done_hbm, cos_hbm, sin_hbm,
    fq_hbm, fk_hbm, aqkv_hbm, bqkv_hbm, wq_hbm,
    dx_hbm, eg_hbm, lg_hbm,
    ge, gao, tag, aqkv, bqkv, gsem,
    ga_ref, gbq_ref, dproj, eg, lg, e_in, e_half, rs_e, rs_t, gl_out, gl_in, l_half, rs_l, dx_ref,
    xw, q, k, v, do, hf, lowq, done, cos, sin, fq, fk, wq, stage, dq, dkT, dvT, bias, sem, psem, hs, hr,
    es, er, ts, tr, ls, lr, dsem, *sems,
):
    flip = lax.axis_index("seq")
    g = Gather(sems, diagonal=(1,))

    def part(src, dst, start, size):
        return src.at[pl.ds(start, size)], dst.at[pl.ds(start, size)]

    table = (
        part(q_hbm, q, 0, 256), part(k_hbm, k, 0, 768), part(v_hbm, v, 0, 768), part(do_hbm, do, 0, 256),
        part(hf_hbm, hf, 0, 1024),
        part(q_hbm, q, 256, 1280), part(k_hbm, k, 768, 768), part(v_hbm, v, 768, 768), part(do_hbm, do, 256, 768),
        (ge_hbm, ge), (tag_hbm, tag), (gao_hbm, gao), (aqkv_hbm, aqkv), (bqkv_hbm, bqkv),
        (lowq_hbm, lowq), (done_hbm, done), (cos_hbm, cos), (sin_hbm, sin), (fq_hbm, fq), (fk_hbm, fk), (wq_hbm, wq),
    )
    loads = [pltpu.make_async_copy(a, b, sem.at[i]) for i, (a, b) in enumerate(table)]
    for i in range(4):
        loads.append(
            pltpu.make_async_copy(
                x_hbm.at[pl.ds(block_at(flip, i), QB)], xw.at[pl.ds(i * QB, QB)], sem.at[21 + i]
            )
        )
    def fetch(qb, pair, s):
        return prob_copies(PLAN[qb][1], p_hbm.at[qb, pair], stage.at[s], psem, s)

    for copy in loads[:5]:
        copy.start()
    for copy in fetch(0, 0, 0):
        copy.start()
    for copy in loads[5:]:
        copy.start()

    def view(c, za, zb, k, half):
        lanes = ALL if half is None else pl.ds(0, 256) if half == 0 else pl.ds(256, 128)
        return (eg, lg)[c].at[za, zb, k, :, lanes]

    g.view = view

    def plane(d):
        return lax.rem(g.b + d, 16)

    def scatter(src, dst, send, recv):
        def copy(d):
            to = plane(d)
            return pltpu.make_async_remote_copy(
                src(to), dst.at[g.b], send.at[d], recv.at[d], device_id=(to, g.s), device_id_type=MESH
            )

        def arrival(d):
            return pltpu.make_async_remote_copy(
                src(0), dst.at[plane(16 - d)], send.at[d], recv.at[d], device_id=(plane(d), g.s), device_id_type=MESH
            )

        def each(what):
            def step(d, _):
                what(d)
                return 0

            lax.fori_loop(1, 16, step, 0)

        return (
            lambda: each(lambda d: copy(d).start()),
            lambda: each(lambda d: arrival(d).wait_recv()),
            lambda: each(lambda d: copy(d).wait_send()),
        )

    def piece(ref, size):
        def at(to):
            rows = pl.ds(pl.multiple_of(lax.div(to, 2) * size, size), size)
            return ref.at[rows, pl.ds(pl.multiple_of(lax.rem(to, 2) * 384, 128), 384)]

        return at

    loads[9].wait()
    loads[10].wait()
    send_e, wait_e, end_e = scatter(piece(e_half, 16), rs_e, es, er)
    send_t, wait_t, end_t = scatter(lambda to: tag, rs_t, ts, tr)
    send_l, wait_l, end_l = scatter(piece(l_half, 8), rs_l, ls, lr)

    bar = pltpu.get_barrier_semaphore()

    def greet(d, _):
        pl.semaphore_signal(bar, inc=1, device_id=(plane(d), g.s), device_id_type=MESH)
        return 0

    lax.fori_loop(1, 16, greet, 0)
    for dev in (g.devy, g.devd):
        pl.semaphore_signal(bar, inc=1, device_id=dev, device_id_type=MESH)
    halo = []
    for i, (src, dst) in enumerate(
        (
            (do_hbm.at[pl.ds(768, QB)], do.at[pl.ds(1024, QB)]),
            (do_hbm.at[pl.ds(512, QB)], do.at[pl.ds(1280, QB)]),
            (hf_hbm.at[pl.ds(768, QB)], hf.at[pl.ds(1024, QB)]),
            (hf_hbm.at[pl.ds(512, QB)], hf.at[pl.ds(1280, QB)]),
            (ge.at[pl.ds(pl.multiple_of((1 - flip) * 128, 16), 128)], e_in),
            (gl_out.at[pl.ds(pl.multiple_of((1 - flip) * 64, 16), 64)], gl_in),
        )
    ):
        halo.append(
            pltpu.make_async_remote_copy(
                src, dst, hs.at[i], hr.at[i], device_id=g.devy, device_id_type=MESH
            )
        )

    def total_of(ref):
        totals = [0.0] * ADAPTERS
        for b in range(16):
            value = ref[b].astype(F32)
            for e in range(ADAPTERS):
                weight = rs_t[b, e : e + 1, :].astype(F32)
                totals[e] = totals[e] + value * jnp.concatenate([weight] * 3, axis=1)
        return jnp.concatenate(totals, axis=0).astype(BF)

    def own_piece(ref, size):
        rows = pl.ds(pl.multiple_of(lax.div(g.b, 2) * size, size), size)
        return ref[rows, pl.ds(pl.multiple_of(g.core * 384, 128), 384)]

    dkT[...] = jnp.zeros_like(dkT)
    dvT[...] = jnp.zeros_like(dvT)
    ga_ref[...] = jnp.zeros_like(ga_ref)
    gbq_ref[...] = jnp.zeros_like(gbq_ref)
    gap = iota((QB, QB), 0) - iota((QB, QB), 1)
    gap = jnp.where(flip == 1, -gap, gap)
    bias[...] = jnp.where(gap <= 0, 0.0, NEG)
    half = iota((1, 128), 1) >= HEAD_DIM
    for copy in loads[:5]:
        copy.wait()

    def picks(pair, first, width):
        head = 2 * pair + lax.div(iota((128, 256), 1), 128)
        row = iota((128, 256), 0) - first - width * head
        return jnp.where((row >= 0) & (row < width), 1.0, 0.0).astype(BF)

    for qb in range(4):
        k0, n, _, _ = PLAN[qb]
        own = min(4 - k0, n)
        rows = pl.ds(qb * QB, QB)
        krows = pl.ds(k0 * QB, n * QB)


        def pair_step(pair, _, qb=qb, k0=k0, n=n, own=own, rows=rows, krows=krows):
            slot = lax.rem(pair, 2)
            for one in fetch(qb, pair, slot):
                one.wait()

            @pl.when(pair < 5)
            def _():
                for one in fetch(qb, pair + 1, 1 - slot):
                    one.start()

            if qb < 3:

                @pl.when(pair == 5)
                def _():
                    for one in fetch(qb + 1, 0, 0):
                        one.start()

            lanes = pl.ds(pl.multiple_of(pair * 128, 128), 128)
            do2 = do[rows, lanes]
            ndl = nn(hf[rows, :], picks(pair, 40, 2))
            k2 = k[krows, lanes]
            v2 = v[krows, lanes]
            qT = q[rows, lanes].T
            doT = do2.T
            dqs = []
            masks = (jnp.logical_not(half), half)
            dps = [nt(jnp.where(mine, do2, jnp.zeros_like(do2)), v2) for mine in masks]
            for h, dp in enumerate(dps):
                spots = [divmod(h * n + t, 3) for t in range(n)]
                p = jnp.concatenate([stage[slot, i, :, j * QB : j * QB + QB] for i, j in spots], axis=1)
                d = ndl[:, h * 128 : (h + 1) * 128]
                ds = (p.astype(F32) * (dp + jnp.concatenate([d] * (2 * n), axis=1))).astype(BF)
                hr = pl.ds(pl.multiple_of(pair * 128 + h * 64, 64), 64)
                kc = pl.ds(k0 * QB, own * QB)
                dvT[hr, kc] += nn(doT[h * 64 : (h + 1) * 64], p[:, 0 : own * QB])
                dqs.append(nn(ds, k2))
                dkT[hr, kc] += nn(qT[h * 64 : (h + 1) * 64], ds[:, 0 : own * QB])
            dq[rows, lanes] = jnp.where(half, dqs[1], dqs[0]) * 0.125
            return 0

        lax.fori_loop(0, 6, pair_step, 0)
        if qb == 0:
            pl.semaphore_wait(bar, 17)
            for copy in (halo[4], halo[0], halo[1], halo[2], halo[3]):
                copy.start()
            send_t()
            for copy in loads[5:9]:
                copy.wait()
        elif qb == 1:
            halo[4].wait_recv()
            mine = ge[pl.ds(pl.multiple_of(flip * 128, 16), 128), :]
            e_half[...] = (mine.astype(F32) + e_in[...].astype(F32)).astype(BF)
            send_e()
        elif qb == 2:
            rs_e[g.b] = own_piece(e_half, 16)
            rs_t[g.b] = tag[...]
            wait_e()
            wait_t()
            eg[g.za, g.zb, g.column(0, 0, 0)] = total_of(rs_e)
            g.send_z(0)
        else:
            g.stage_z(0)

    for copy in loads[11:]:
        copy.wait()
    for copy in halo[:4]:
        copy.wait_recv()
    def halo_step(pair, _):
        lanes = pl.ds(pl.multiple_of(pair * 128, 128), 128)
        delta_picks = picks(pair, 40, 2)
        top_picks = picks(pair, 4, 3)
        masks = (jnp.logical_not(half), half)
        work = []
        for i, (k0, n) in enumerate(HALO_PLAN):
            rows = pl.ds(1024 + i * QB, QB)
            krows = pl.ds(k0 * QB, n * QB)
            do2 = do[rows, lanes]
            q2 = q[rows, lanes]
            feats = hf[rows, :]
            ndl = nn(feats, delta_picks)
            nm = nn(feats, top_picks)
            keys = jnp.concatenate([k[krows, lanes], fk[krows, :]], axis=1)
            v2 = v[krows, lanes]
            for h, mine in enumerate(masks):
                s = nt(jnp.concatenate([jnp.where(mine, q2, jnp.zeros_like(q2)), fq[rows, :]], axis=1), keys)
                dp = nt(jnp.where(mine, do2, jnp.zeros_like(do2)), v2)
                work.append((k0, n, h, s, dp, nm, ndl, q2.T, do2.T))
        for k0, n, h, s, dp, nm, ndl, qT, doT in work:
            parts = [s[:, t * QB : (t + 1) * QB] for t in range(n)]
            parts[0] = parts[0] + bias[...]
            s = jnp.concatenate(parts, axis=1)
            m = nm[:, h * 128 : (h + 1) * 128]
            p = jnp.exp(s + jnp.concatenate([m] * (2 * n), axis=1))
            d = ndl[:, h * 128 : (h + 1) * 128]
            ds = (p * (dp + jnp.concatenate([d] * (2 * n), axis=1))).astype(BF)
            hr = pl.ds(pl.multiple_of(pair * 128 + h * 64, 64), 64)
            kc = pl.ds(k0 * QB, n * QB)
            dvT[hr, kc] += nn(doT[h * 64 : (h + 1) * 64], p.astype(BF))
            dkT[hr, kc] += nn(qT[h * 64 : (h + 1) * 64], ds)
        return 0

    lax.fori_loop(0, 3, halo_step, 0)
    g.stage_xy(0)
    lax.fori_loop(3, 6, halo_step, 0)
    g.stage_corner(0)

    lane = lax.div(iota((1, 48), 1), 16)
    rank = lax.div(iota((48, 1), 0), 16)

    def proj_step(rb, _):
        start = pl.multiple_of(rb * 512, 512)
        rows = pl.ds(start, 512)
        cosine = cos[rows, :]
        sine = -sin[rows, :]
        low = lowq[rows, :]
        dlow = jnp.zeros((512, 48), F32)
        for p in range(3):
            if p == 0:
                d = rope(dq[rows, :], cosine, sine)
            else:
                src = (dkT, dvT)[p - 1]
                d = [src[pl.ds(c * 128, 128), rows] for c in range(6)]
                if p == 2:
                    d = [v.astype(BF) for v in d]
                d = jnp.concatenate([v.T for v in d], axis=1)
                if p == 1:
                    d = rope(d, cosine, sine)
            d = d.astype(BF)
            dproj[p, rows, :] = d
            dlow += jnp.where(lane == p, nt(d, bqkv[...]), 0.0)
            gbq_ref[...] += jnp.where(rank == p, tn(low, d), 0.0)
        dlow = dlow.astype(BF)
        lowq[rows, :] = dlow
        ga_ref[...] += tn(dlow, xw[rows, :])
        return 0

    lax.fori_loop(0, 2, proj_step, 0)
    g.stage_pair(0)
    gl_out[0:48] = ga_ref[...].astype(BF)
    gl_out[48:96] = gbq_ref[...].astype(BF)
    gl_out[96:112] = gao[...].astype(BF)
    gl_out[112:128] = jnp.zeros((16, D), BF)
    halo[5].start()

    def dx_rows(rb):
        rows = pl.ds(rb * QB, QB)
        total = done[rows, :] + nn(lowq[rows, :], aqkv[...])
        for p in range(3):
            total += nt(dproj[p, rows, :], wq[p].reshape(D, D))
        dx_ref[rows, :] = total.astype(BF)
        copy = pltpu.make_async_copy(dx_ref.at[rows], dx_hbm.at[pl.ds(block_at(flip, rb), QB)], dsem.at[rb])
        copy.start()
        return copy

    tails = [dx_rows(0)]
    halo[5].wait_recv()
    mine = gl_out[pl.ds(pl.multiple_of(flip * 64, 16), 64), :]
    l_half[...] = mine.astype(F32) + gl_in[...].astype(F32)
    send_l()
    tails.append(dx_rows(1))
    rs_l[g.b] = own_piece(l_half, 8)
    wait_l()
    lg[g.za, g.zb, g.column(0, 0, 0)] = total_of(rs_l)
    g.send_z(1)
    tails.append(dx_rows(2))
    g.stage_z(1)
    tails.append(dx_rows(3))
    g.stage_core(0)
    keep_e = pltpu.make_async_copy(eg, eg_hbm, gsem.at[0])
    keep_e.start()
    g.stage_xy(1)
    for copy in halo:
        copy.wait_send()
    end_e()
    end_t()
    end_l()
    g.finish(0)
    g.stage_core(1)
    keep_l = pltpu.make_async_copy(lg, lg_hbm, gsem.at[1])
    keep_l.start()
    g.finish(1)
    keep_e.wait()
    keep_l.wait()
    for copy in tails:
        copy.wait()


def k4_kernel(
    eg_hbm, lg_hbm, mixed_hbm, dx_hbm,
    mixed_out, dx_out, gin_hbm, gdn_hbm, gout_hbm, gff_hbm,
    eg, lg, gin_ref, gdn_ref, gout_ref, gff_ref, mixed, dx, sem,
):
    moves = [
        pltpu.make_async_copy(a, b, sem.at[i])
        for i, (a, b) in enumerate(
            (
                (eg_hbm, eg), (lg_hbm, lg), (mixed_hbm, mixed), (dx_hbm, dx),
                (gdn_ref, gdn_hbm), (gff_ref, gff_hbm), (gin_ref, gin_hbm), (gout_ref, gout_hbm),
                (mixed, mixed_out), (dx, dx_out),
            )
        )
    ]
    for copy in moves[:4]:
        copy.start()

    def blocks(ref):
        for z in range(4):
            for xx in range(2):
                for core in range(2):
                    for y in range(2):
                        yield (
                            y * 8 + z * 2 + xx, core * 384,
                            ref[z // 2, z % 2, (xx * 2 + core) * 2 + y].astype(F32),
                        )

    moves[0].wait()
    for group, lane0, value in blocks(eg):
        lanes = slice(lane0, lane0 + 384)
        for e in range(ADAPTERS):
            rows = value[16 * e : 16 * e + 16]
            if group < 2:
                gin_ref[e, 64 + 16 * group : 80 + 16 * group, lanes] = rows
            elif group < 4:
                gout_ref[e, 16 + 16 * group : 32 + 16 * group, lanes] = rows
            elif group < 8:
                at = (group - 4) * D + lane0
                gdn_ref[e, :, at : at + 384] = rows
            else:
                at = (group - 8) // 2 * D + lane0
                first = 16 * (group % 2)
                gff_ref[e, first : first + 16, at : at + 384] = rows

    for i in (2, 3):
        moves[i].wait()
    for i in (4, 5, 8, 9):
        moves[i].start()
    moves[1].wait()
    for group, lane0, value in blocks(lg):
        lanes = slice(lane0, lane0 + 384)
        for e in range(ADAPTERS):
            rows = value[8 * e : 8 * e + 8]
            if group < 6:
                gin_ref[e, 8 * group : 8 * group + 8, lanes] = rows
            elif group < 12:
                gout_ref[e, 8 * group - 48 : 8 * group - 40, lanes] = rows
            elif group < 14:
                gin_ref[e, 8 * group - 48 : 8 * group - 40, lanes] = rows

    for copy in moves[6:8]:
        copy.start()
    for copy in moves[4:]:
        copy.wait()


def sds(shape, dtype):
    return jax.ShapeDtypeStruct(shape, dtype)


ANY = functools.partial(pl.BlockSpec, memory_space=pl.ANY)
INV = functools.partial(pl.BlockSpec, memory_space=pltpu.VMEM)


def kf_call(*args):
    outs = [
        (ANY, (6, QB, D), BF), (ANY, (6, QB, D), BF), (ANY, (6, QB, D), BF), (ANY, (4, 6, 4, QB, D), BF),
        (ANY, (1024, D), BF), (ANY, (1024, D), BF), (ANY, (1024, 128), BF),
        (ANY, (1536, 48), BF), (ANY, (1024, D), F32), (ANY, (1536, 128), F32), (ANY, (1536, 128), F32),
        (ANY, (1536, 128), BF), (ANY, (1536, 128), BF),
        (ANY, (256, D), BF), (ANY, (16, D), F32), (ANY, (16, 128), BF), (ANY, (48, D), BF), (ANY, (48, D), BF),
        (ANY, (3, 2, 2, 8, 24, D), BF),
    ]
    V = pltpu.VMEM
    scratch = [
        V((1, 2048), jnp.int32), V((1, 128), F32), pltpu.SMEM((1, 1), jnp.int32), V((2, D), F32), V((2, D), F32),
        V((1024, 128), BF), V((256, D), BF), V((16, D), F32), V((16, 128), BF), V((48, D), BF), V((48, D), BF),
        pltpu.SemaphoreType.DMA((5,)), pltpu.SemaphoreType.DMA((5,)),
        V((16, D), BF), V((16, D), BF), V((32, D), BF), V((4, 16, D), BF), V((16, D), BF), V((4, D), F32),
        V((32, D), F32), V((4, 16, D), F32), V((16, D), F32), V((16, D), F32), V((4, 32, D), F32),
        V((3, 2, 2, 8, 24, D), BF), V((2, 2, 8, 24, D), BF), V((4, 2, 2, 2, 8, 24, D), BF), V((2, 2, 8, 96, D), BF),
        V((32, QB, D), BF), V((1536, D), BF), V((1024, D), BF), V((1024, D), F32),
        V((1024, D), F32), V((1024, D), F32), V((1024, D), BF), V((1024, D), BF),
        V((1536, 128), F32), V((1536, 128), F32), V((1536, 128), BF), V((1536, 128), BF), V((2, QB, QB), F32),
        V((1024, 128), F32), V((1536, 48), BF), V((1024, 16), BF), V((1024, 32), BF),
        V((1024, 16), BF), V((512, D), F32), V((32, 512), F32), V((3, 48, D), BF),
        V((4, 32, D), BF), V((4, 32, D), BF), V((D, 128), BF),
        pltpu.SemaphoreType.DMA((13,)), pltpu.SemaphoreType.DMA((10,)), pltpu.SemaphoreType.DMA((7,)), pltpu.SemaphoreType.DMA((8,)), pltpu.SemaphoreType.DMA((10,)),
        pltpu.SemaphoreType.DMA((4,)), pltpu.SemaphoreType.DMA((4,)), pltpu.SemaphoreType.DMA((4,)),
    ]
    scratch += gather_sems(NCHUNK)
    return pl.pallas_call(
        kf_kernel,
        out_shape=[sds(s, t) for _, s, t in outs],
        in_specs=[ANY()] * 15,
        out_specs=[m() for m, _, _ in outs],
        scratch_shapes=scratch,
        compiler_params=pltpu.CompilerParams(
            vmem_limit_bytes=VMEM_LIMIT, collective_id=1, has_side_effects=True
        ),
    )(*args)


def k3_call(*args):
    V = pltpu.VMEM
    S = pltpu.SemaphoreType.DMA
    scratch = [
        V((256, D), BF), V((16, D), F32), V((16, 128), BF), V((48, D), BF), V((48, D), BF), S((2,)),
        V((48, D), F32), V((48, D), F32), V((3, 1024, D), BF), V((2, 2, 8, 64, 384), BF), V((2, 2, 8, 32, 384), BF),
        V((128, D), BF), V((128, D), BF), V((16, 16, 384), BF), V((16, 16, 128), BF), V((128, D), BF), V((64, D), BF),
        V((64, D), F32), V((16, 8, 384), F32), V((1024, D), BF),
        V((1024, D), BF), V((1536, D), BF), V((1536, D), BF), V((1536, D), BF), V((1536, D), BF), V((1536, 128), BF),
        V((1536, 48), BF), V((1024, D), F32), V((1536, 128), F32), V((1536, 128), F32), V((1536, 128), BF),
        V((1536, 128), BF), V((3, 2, 2, 8, 24, D), BF), V((2, 4, QB, D), BF), V((1024, D), F32), V((D, 1024), F32),
        V((D, 1024), F32), V((QB, QB), F32), S((25,)), S((4,)), S((6,)), S((6,)),
        S((16,)), S((16,)), S((16,)), S((16,)), S((16,)), S((16,)), S((4,)),
    ]
    return pl.pallas_call(
        k3_kernel,
        out_shape=[
            sds((1024, D), BF), sds((2, 2, 8, 64, 384), BF), sds((2, 2, 8, 32, 384), BF),
        ],
        in_specs=[ANY()] * 19,
        out_specs=[ANY()] * 3,
        scratch_shapes=scratch + gather_sems(2),
        compiler_params=pltpu.CompilerParams(
            vmem_limit_bytes=VMEM_LIMIT, collective_id=2, has_side_effects=True
        ),
    )(*args)


def k4_call(*args):
    V = pltpu.VMEM
    grads = [(4, 96, D), (4, 16, FF), (4, 80, D), (4, 32, FF)]
    return pl.pallas_call(
        k4_kernel,
        out_shape=[sds((1024, D), BF), sds((1024, D), BF)] + [sds(s, F32) for s in grads],
        in_specs=[ANY()] * 4,
        out_specs=[ANY()] * 6,
        scratch_shapes=[V((2, 2, 8, 64, 384), BF), V((2, 2, 8, 32, 384), BF)]
        + [V(s, F32) for s in grads]
        + [V((1024, D), BF), V((1024, D), BF), pltpu.SemaphoreType.DMA((10,))],
        compiler_params=pltpu.CompilerParams(vmem_limit_bytes=VMEM_LIMIT),
    )(*args)


def fast(
    tokens, cotangent, segments, adapter_index, qkv_weight, out_weight, ffn_in_weight, ffn_out_weight,
    norm_gain, norm_bias, adapt_in, adapt_down, adapt_out, adapt_ffn,
):
    x = tokens[0]
    freq = np.power(np.float32(ROPE_BASE), np.float32(-2.0 / HEAD_DIM) * np.arange(HEAD_DIM // 2, dtype=np.float32))
    freq = np.tile(freq.astype(np.float32), 4)[None]
    q, k, v, p, mixed, do, hf, lowq, done, cos, sin, fq, fk, ge, gao, tag, aqkv, bqkv, wq = kf_call(
        x, cotangent[0], segments, freq, adapter_index, norm_gain[0], norm_bias[0],
        adapt_in[0].transpose(0, 1, 3, 2).reshape(ADAPTERS, 96, D), adapt_down[0].transpose(0, 2, 1),
        adapt_out[0].reshape(ADAPTERS, 80, D), adapt_ffn[0].reshape(ADAPTERS, 32, FF),
        qkv_weight[0], out_weight[0], ffn_in_weight[0], ffn_out_weight[0],
    )
    q, k, v = (a.reshape(1536, D) for a in (q, k, v))
    dx, eg, lg = k3_call(
        x, q, k, v, p, do, hf, ge, gao, tag, lowq, done, cos, sin, fq, fk, aqkv, bqkv, wq
    )
    mixed, dx, g_in, g_dn, g_out, g_ff = k4_call(eg, lg, mixed, dx)
    return (
        mixed[None], dx[None], g_in.reshape(ADAPTERS, 6, 16, D).transpose(0, 1, 3, 2)[None],
        g_dn.transpose(0, 2, 1)[None], g_out.reshape(ADAPTERS, 5, 16, D)[None], g_ff.reshape(ADAPTERS, 2, 16, FF)[None],
    )


def solution(mesh):
    here = fast if dict(mesh.shape) == {"batch": 16, "seq": 2} else shards
    return jax.shard_map(
        here,
        mesh=mesh,
        in_specs=(
            P("batch", "seq", None),
            P("batch", "seq", None),
            P("batch", None),
            P("batch", None),
            P(None, None, ("batch", "seq"), None),
            P(None, ("batch", "seq"), None),
            P(None, None, ("batch", "seq"), None),
            P(None, ("batch", "seq"), None),
            P(),
            P(),
            P(),
            P(),
            P(),
            P(),
        ),
        out_specs=(P("batch", "seq", None), P("batch", "seq", None), P(), P(), P(), P()),
        check_vma=False,
    )
```
